32 devices in a mesh: expert: 8 (over z, y), tensor: 4 (over x, core).
Axes of the slice: x: 2, y: 2, z: 4, core: 2. Of those that a mesh axis runs over, the one named last changes fastest.
Arguments:
- tokens: bfloat16 [4096, 2048], P('expert'), may hold values from -6 to 6
- segment_ids: int32 [4096], replicated, may hold values from 0 to 2, as said below
- attn_routes: int32 [4096, 2], P('expert'), may hold values from 0 to 7, all different within a row; in each aligned block of 512 rows (0 to 511, 512 to 1023, ...) at most 160 rows name the same one
- ffn_routes: int32 [4096, 2], P('expert'), may hold values from 0 to 7, all different within a row; in each aligned block of 512 rows (0 to 511, 512 to 1023, ...) at most 160 rows name the same one
- attn_gain: bfloat16 [2048], replicated, may hold values from 0.099609375 to 1.8984375
- ffn_gain: bfloat16 [2048], replicated, may hold values from 0.099609375 to 1.8984375
- routers: bfloat16 [2048, 16], replicated, may hold values from -0.09375 to 0.09375
- query_weight: bfloat16 [8, 2048, 2048], P(None, 'expert', 'tensor'), may hold values from -0.125 to 0.125
- output_weight: bfloat16 [8, 2048, 2048], P(None, 'expert', 'tensor'), may hold values from -2 to 2
- key_value_weight: bfloat16 [2, 2048, 2048], P(None, 'expert', 'tensor'), may hold values from -0.125 to 0.125
- gate_weight: bfloat16 [8, 2048, 5632], P('expert', None, 'tensor'), may hold values from -0.125 to 0.125
- up_weight: bfloat16 [8, 2048, 5632], P('expert', None, 'tensor'), may hold values from -0.125 to 0.125
- down_weight: bfloat16 [8, 5632, 2048], P('expert', 'tensor'), may hold values from -0.078125 to 0.078125
- cotangent: bfloat16 [4096, 2048], P('expert'), may hold values from -6 to 6
Outputs:
- mixed: bfloat16 [4096, 2048], P('expert', 'tensor')
- tokens_grad: float32 [4096, 2048], P('expert')
- attn_gain_grad: float32 [2048], P('expert')
- ffn_gain_grad: float32 [2048], P('expert')
- routers_grad: float32 [2048, 16], P('expert')
- query_grad: float32 [8, 2048, 2048], P(None, 'expert', 'tensor')
- output_grad: float32 [8, 2048, 2048], P(None, 'expert', 'tensor')
- key_value_grad: float32 [2, 2048, 2048], P(None, 'expert', 'tensor')
- gate_grad: float32 [8, 2048, 5632], P('expert', None, 'tensor')
- up_grad: float32 [8, 2048, 5632], P('expert', None, 'tensor')
- down_grad: float32 [8, 5632, 2048], P('expert', 'tensor')
The draws below stay inside these ranges and needn't reach their ends.
Inputs may be any that keep to these rules, and one draw needn't show every extreme that they name: `segment_ids`: ids start at 0 and rise by 0 or 1 from one token to the next; there are exactly three documents, the middle one begins among the first 512 tokens and ends among the last 512. `attn_routes`: each row names 2 different experts; among the rows of one device no expert is named more than 160 times, a bound that some block reaches. `ffn_routes`: each row names 2 different experts; among the rows of one device no expert is named more than 160 times, a bound that some block reaches.
All inputs are finite; a program needn't handle non-finite values.
Results may differ from the reference program's by a relative error of at most 0.019.
Values may be sent and summed in bfloat16 or wider, within the bound.
A program may use at most 384 MiB of HBM per device.

```python
import math
import jax
import jax.numpy as jnp
import numpy as np
from jax import lax

D = 2048
FF = 5632
KVH = 16
HQ = 16
HD = 128
EXPERTS = 8
TOPK = 2
WINDOW = 1024
TOK_DEV = 512
TOKENS = 4096
CAP = 160
SPLIT = 1
PIECE = 5632
N_EXPERT = 8


def draw_segment_ids(key, part):
    key = jax.random.fold_in(key, 11)
    first_key, second_key = jax.random.split(key, 2)
    begin = jax.random.randint(first_key, (), 1, TOK_DEV)
    finish = jax.random.randint(second_key, (), TOKENS - TOK_DEV + 1, TOKENS)
    places = jnp.arange(TOKENS, dtype=jnp.int32)
    starts = jnp.where((places == 0) | (places == begin) | (places == finish), 1, 0).astype(jnp.int32)
    return (jnp.cumsum(starts) - 1).astype(jnp.int32)


def steps_of(own_key, dims, cuts, low, top_value):
    def one(position, shards_of):
        heights = jax.random.uniform(jax.random.fold_in(jax.random.fold_in(own_key, 6), position), (shards_of,), jnp.float32, low / len(cuts), top_value / len(cuts))
        return jnp.repeat(jnp.exp(heights), dims[position] // shards_of).reshape((-1,) + (1,) * (len(dims) - position - 1))

    gain = one(*cuts[0])
    for cut in cuts[1:]:
        gain = gain * one(*cut)
    return gain


def assign_block(key, own, number, rows, amount, top, reach, slope):
    order = jax.random.permutation(key, amount)
    crowded, ordinary = portions_of(amount, rows * top, reach, slope, True), portions_of(amount, rows * top, reach, slope, False)
    places = jnp.arange(amount)

    def named(tallies, rotation):
        used = int((tallies > 0).sum())
        fixed = max(1, used // 4)
        moved = fixed + (places - fixed + rotation * (used - fixed)) % max(1, amount - fixed)
        return jnp.zeros((amount,), jnp.int32).at[order[jnp.where(places < fixed, places, moved)]].set(jnp.asarray(tallies, jnp.int32))

    tallies = jnp.where(number % 4 == 0, named(crowded, number // 4), named(ordinary, number - number // 4 - 1))
    mixed = jax.random.permutation(jax.random.fold_in(own, 3), amount)
    source_of, taker = mixed[0:amount // 2 * 2:2], mixed[1:amount // 2 * 2:2]
    slack = jnp.minimum(tallies[source_of] - 1, reach - tallies[taker]) // 2
    slack = jnp.where((source_of == order[0]) | (taker == order[0]) | (tallies[taker] == 0), 0, jnp.maximum(slack, 0))
    moved = jax.random.randint(jax.random.fold_in(own, 4), (amount // 2,), 0, 1 << 20) % (slack + 1)
    tallies = tallies.at[source_of].add(-moved).at[taker].add(moved)
    labels = jnp.searchsorted(jnp.cumsum(tallies), jnp.arange(rows * top), side="right").astype(jnp.int32)
    listing = labels.reshape(top, rows).T
    listing = listing[jax.random.permutation(jax.random.fold_in(own, 1), rows)]
    rotation = jax.random.randint(jax.random.fold_in(own, 2), (rows, 1), 0, top)
    return jnp.take_along_axis(listing, (jnp.arange(top)[None, :] + rotation) % top, axis=1)


def portions_of(count, total, bound, skew, full):
    portions = [(1 << 20) // math.isqrt(grade ** skew) + 1 for grade in range(1, count + 1)]
    largest = bound if full else min(bound, max(-(-total // count), total * portions[0] // sum(portions)))
    least = 1 if total - largest >= count - 1 else 0
    counts, spare = [largest] + [least] * (count - 1), total - largest - least * (count - 1)
    while spare > 0:
        candidates = [i for i in range(1, count) if counts[i] < largest] or [i for i in range(1, count) if counts[i] < bound]
        mass, budget = sum([portions[i] for i in candidates]), spare
        for i in candidates:
            extra = min(bound - counts[i], max(1, budget * portions[i] // mass), spare)
            counts[i] = counts[i] + extra
            spare = spare - extra
    return np.array(counts)


def noise(own_key, dims, deviation, bound, cuts=(), kind=jnp.bfloat16):
    entries = deviation * jax.random.normal(own_key, dims, jnp.float32)
    if cuts:
        entries = entries * steps_of(own_key, dims, cuts, -0.22, 0.18)
    return jnp.clip(entries, -bound, bound).astype(kind)


def setup_inputs(seed: int = 0) -> dict:
    key_list = jax.random.split(jax.random.key(seed), 15)
    tokens = noise(key_list[0], (TOKENS, D), 1.0, 6.0, ((0, 8),))
    segment_ids = draw_segment_ids(jax.random.fold_in(key_list[14], 71), 0)
    attn_routes_keys = jax.random.split(jax.random.fold_in(key_list[2], 1), TOKENS // TOK_DEV)
    attn_routes_turns = jax.random.permutation(jax.random.fold_in(key_list[2], 3), TOKENS // TOK_DEV)
    attn_routes = jax.vmap(lambda own, number: assign_block(jax.random.fold_in(key_list[2], 2), own, number, TOK_DEV, EXPERTS, TOPK, CAP, 1))(attn_routes_keys, attn_routes_turns).reshape((TOKENS, TOPK))
    ffn_routes_keys = jax.random.split(jax.random.fold_in(key_list[3], 1), TOKENS // TOK_DEV)
    ffn_routes_turns = jax.random.permutation(jax.random.fold_in(key_list[3], 3), TOKENS // TOK_DEV)
    ffn_routes = jax.vmap(lambda own, number: assign_block(jax.random.fold_in(key_list[3], 2), own, number, TOK_DEV, EXPERTS, TOPK, CAP, 2))(ffn_routes_keys, ffn_routes_turns).reshape((TOKENS, TOPK))
    attn_gain = jnp.clip(1.0 + 0.18 * jax.random.normal(key_list[4], (D,), jnp.float32), 0.099609375, 1.8984375).astype(jnp.bfloat16)
    ffn_gain = jnp.clip(1.0 + 0.18 * jax.random.normal(key_list[5], (D,), jnp.float32), 0.099609375, 1.8984375).astype(jnp.bfloat16)
    routers = noise(key_list[6], (D, 2 * EXPERTS), (2 * D) ** -0.5, 0.09375)
    query_weight = noise(key_list[7], (EXPERTS, D, HQ * HD), D ** -0.5, 0.125, ((1, 8), (2, 4)))
    output_weight = noise(key_list[8], (EXPERTS, D, HQ * HD), (max(HQ * HD // 256, 1)) ** -0.5, 2.0, ((1, 8), (2, 4)))
    key_value_weight = noise(key_list[9], (2, D, KVH * HD), D ** -0.5, 0.125, ((1, 8), (2, 4)))
    gate_weight = noise(key_list[10], (N_EXPERT, D, PIECE), D ** -0.5, 0.125, ((0, 8), (2, 4)))
    up_weight = noise(key_list[11], (N_EXPERT, D, PIECE), D ** -0.5, 0.125, ((0, 8), (2, 4)))
    down_weight = noise(key_list[12], (N_EXPERT, PIECE, D), FF ** -0.5, 0.078125, ((0, 8), (1, 4)))
    cotangent = noise(key_list[13], (TOKENS, D), 1.0, 6.0, ((0, 8),))
    return {"tokens": tokens, "segment_ids": segment_ids, "attn_routes": attn_routes, "ffn_routes": ffn_routes, "attn_gain": attn_gain, "ffn_gain": ffn_gain, "routers": routers, "query_weight": query_weight, "output_weight": output_weight, "key_value_weight": key_value_weight, "gate_weight": gate_weight, "up_weight": up_weight, "down_weight": down_weight, "cotangent": cotangent}


@jax.custom_vjp
def low(v):
    return lax.optimization_barrier(v.astype(jnp.bfloat16)).astype(jnp.float32)

@jax.custom_vjp
def low_back(v):
    return v

def low_keep(v):
    return (low(v), None)

def low_pass(kept, grad):
    return (grad,)

def back_keep(v):
    return (v, None)

def back_low(kept, grad):
    return (low(grad),)
low.defvjp(low_keep, low_pass)
low_back.defvjp(back_keep, back_low)
eps = 1e-06
masked_value = -1e+30
highest = lax.Precision.HIGHEST

def round_both(v):
    return low(low_back(v))

def rms_norm(source, gain_vec):
    factor = lax.rsqrt(lax.optimization_barrier(jnp.mean(source * source, axis=1, keepdims=True)) + eps)
    return source * factor * gain_vec

def slot_rows(routes, slot_cap):
    flat_routes = routes.reshape(-1)
    one_hot = (flat_routes[:, None] == jnp.arange(EXPERTS, dtype=jnp.int32)[None, :]).astype(jnp.int32)
    earlier = jnp.cumsum(one_hot, axis=0) - one_hot
    return (flat_routes * slot_cap + lax.optimization_barrier(jnp.sum(earlier * one_hot, axis=1))).astype(jnp.int32)

def group_rows(row_data, target, slots_all):
    return jnp.zeros((slots_all, row_data.shape[1]), row_data.dtype).at[target].set(row_data)

def pick_gates(logits, routes):
    chosen = jnp.take_along_axis(logits, routes, axis=1)
    row_max = lax.optimization_barrier(jnp.max(chosen, axis=1, keepdims=True))
    shifted = jnp.exp(chosen - row_max)
    return shifted / lax.optimization_barrier(jnp.sum(shifted, axis=1, keepdims=True))

def attention(queries, keys, values, segment_ids):
    row_count = queries.shape[0]
    pad_keys = jnp.concatenate([jnp.zeros((WINDOW,) + keys.shape[1:], keys.dtype), keys])
    pad_values = jnp.concatenate([jnp.zeros((WINDOW,) + values.shape[1:], values.dtype), values])
    pad_segments = jnp.concatenate([jnp.full((WINDOW,), -1, jnp.int32), segment_ids])
    distance = jnp.arange(WINDOW, dtype=jnp.int32)[:, None] + WINDOW - jnp.arange(2 * WINDOW, dtype=jnp.int32)[None, :]

    def one_block(block_index):
        first = block_index * WINDOW
        query_block = lax.dynamic_slice_in_dim(queries, first, WINDOW)
        key_block = lax.dynamic_slice_in_dim(pad_keys, first, 2 * WINDOW)
        value_block = lax.dynamic_slice_in_dim(pad_values, first, 2 * WINDOW)
        query_segment = lax.dynamic_slice_in_dim(segment_ids, first, WINDOW)
        key_segment = lax.dynamic_slice_in_dim(pad_segments, first, 2 * WINDOW)
        allowed = (distance >= 0) & (distance < WINDOW) & (query_segment[:, None] == key_segment[None, :])
        scores = low_back(jnp.einsum('qkhd,jhd->khqj', query_block, key_block, precision=highest) * HD ** (-0.5))
        scores = jnp.where(allowed[None, None], scores, masked_value)
        row_max = lax.optimization_barrier(jnp.max(scores, axis=-1, keepdims=True))
        shifted = jnp.exp(scores - row_max)
        attn_probs = shifted / lax.optimization_barrier(jnp.sum(shifted, axis=-1, keepdims=True))
        return jnp.einsum('khqj,jhd->qkhd', low(attn_probs), value_block, precision=highest)
    blocks = lax.map(jax.checkpoint(one_block), jnp.arange(row_count // WINDOW, dtype=jnp.int32))
    return blocks.reshape(queries.shape)

def reference(tokens, segment_ids, attn_routes, ffn_routes, attn_gain, ffn_gain, routers, query_weight, output_weight, key_value_weight, gate_weight, up_weight, down_weight, cotangent):
    row_count = tokens.shape[0]
    slot_cap = N_EXPERT * CAP
    slots_all = EXPERTS * slot_cap
    attn_slot = slot_rows(attn_routes, slot_cap)
    ffn_slot = slot_rows(ffn_routes, slot_cap)

    def forward(state_in, gain_one, gain_two, router_maps, query_maps, output_maps, pair_maps, gate_maps, up_maps, down_maps):
        normed_one = low(rms_norm(state_in, gain_one))
        attn_logits = low_back(jnp.dot(normed_one, router_maps[:, :EXPERTS], precision=highest))
        attn_gates = pick_gates(attn_logits, attn_routes)
        pair = round_both(jnp.einsum('td,cdf->ctf', normed_one, pair_maps, precision=highest))
        keys = pair[0].reshape(row_count, KVH, HD)
        values = pair[1].reshape(row_count, KVH, HD)
        spread_one = group_rows(jnp.repeat(normed_one, TOPK, axis=0), attn_slot, slots_all).reshape(EXPERTS, slot_cap, D)
        query_rows = jnp.einsum('ecd,edf->ecf', spread_one, query_maps, precision=highest).reshape(slots_all, HQ * HD)[attn_slot]
        queries = round_both(query_rows).reshape(row_count, TOPK, HQ, HD)
        heads_out = round_both(attention(queries, keys, values, segment_ids)).reshape(row_count * TOPK, HQ * HD)
        spread_attn = group_rows(heads_out, attn_slot, slots_all).reshape(EXPERTS, slot_cap, HQ * HD)
        attn_rows = jnp.einsum('ecf,edf->ecd', spread_attn, output_maps, precision=highest).reshape(slots_all, D)[attn_slot]
        attn_rows = low_back(attn_rows).reshape(row_count, TOPK, D)
        state = state_in + lax.optimization_barrier(jnp.sum(attn_gates[:, :, None] * attn_rows, axis=1))
        normed_two = low(rms_norm(state, gain_two))
        ffn_logits = low_back(jnp.dot(normed_two, router_maps[:, EXPERTS:], precision=highest))
        ffn_gates = pick_gates(ffn_logits, ffn_routes)
        spread_two = group_rows(jnp.repeat(normed_two, TOPK, axis=0), ffn_slot, slots_all).reshape(EXPERTS, slot_cap, D)
        gate_full = gate_maps.reshape(EXPERTS, SPLIT, D, PIECE).transpose(0, 2, 1, 3).reshape(EXPERTS, D, FF)
        up_full = up_maps.reshape(EXPERTS, SPLIT, D, PIECE).transpose(0, 2, 1, 3).reshape(EXPERTS, D, FF)
        down_full = down_maps.reshape(EXPERTS, FF, D)
        gate_pre = low_back(jnp.einsum('ecd,edf->ecf', spread_two, gate_full, precision=highest))
        up_pre = low_back(jnp.einsum('ecd,edf->ecf', spread_two, up_full, precision=highest))
        hidden = low(jax.nn.silu(gate_pre) * up_pre)
        ffn_rows = jnp.einsum('ecf,efd->ecd', hidden, down_full, precision=highest).reshape(slots_all, D)[ffn_slot]
        ffn_rows = low_back(ffn_rows).reshape(row_count, TOPK, D)
        return state + lax.optimization_barrier(jnp.sum(ffn_gates[:, :, None] * ffn_rows, axis=1))
    float_args = (tokens.astype(jnp.float32), attn_gain.astype(jnp.float32), ffn_gain.astype(jnp.float32), routers.astype(jnp.float32), query_weight.astype(jnp.float32), output_weight.astype(jnp.float32), key_value_weight.astype(jnp.float32), gate_weight.astype(jnp.float32), up_weight.astype(jnp.float32), down_weight.astype(jnp.float32))
    mixed, pullback = jax.vjp(forward, *float_args)
    gradients = pullback(cotangent.astype(jnp.float32))
    return (mixed.astype(jnp.bfloat16), gradients[0], gradients[1], gradients[2], gradients[3], gradients[4], gradients[5], gradients[6], gradients[7], gradients[8], gradients[9])
```

```python
import jax
import jax.numpy as jnp
from jax import lax
from jax.sharding import PartitionSpec as P

D = 2048
HD = 128
EXPERTS = 8
TOPK = 2
WINDOW = 1024
CAP = 160
SLOTS = EXPERTS * CAP

eps = 1e-06
masked_value = -1e30
F32 = jnp.float32
BF16 = jnp.bfloat16


def dot(left, right, dims):
    return lax.dot_general(left, right, ((dims[0], dims[1]), ((), ())), preferred_element_type=F32)


def mm(left, right):
    return dot(left, right, ((1,), (0,)))


def mm_nt(left, right):
    return dot(left, right, ((1,), (1,)))


def mm_tn(left, right):
    return dot(left, right, ((0,), (0,)))


def shifted_by(shard, axis, by):
    count = lax.axis_size(axis)
    pairs = [(i, i + by) for i in range(count) if 0 <= i + by < count]
    return lax.ppermute(shard, axis, pairs)


def swap(blocks):
    return lax.all_to_all(blocks, "expert", split_axis=0, concat_axis=0, tiled=True)


def columns_together(rows):
    return lax.all_gather(rows, "tensor", axis=1, tiled=True)


def columns_summed(rows):
    return lax.psum_scatter(rows, "tensor", scatter_dimension=1, tiled=True)


def slot_places(routes):
    flat = routes.T.reshape(-1)
    one_hot = (flat[:, None] == jnp.arange(EXPERTS, dtype=jnp.int32)[None, :]).astype(jnp.int32)
    earlier = jnp.cumsum(one_hot, axis=0) - one_hot
    slots = flat * CAP + jnp.sum(earlier * one_hot, axis=1)
    return (jnp.arange(SLOTS, dtype=jnp.int32)[:, None] == slots[None, :]).astype(BF16)


def to_pieces(rows, pieces):
    if pieces == 1:
        return rows
    experts, r, c = rows.shape
    return rows.reshape(experts, r, pieces, c // pieces).transpose(0, 2, 1, 3).reshape(experts * pieces, r, -1)


def from_pieces(rows, pieces):
    if pieces == 1:
        return rows
    both, r, c = rows.shape
    return rows.reshape(both // pieces, pieces, r, c).transpose(0, 2, 1, 3).reshape(both // pieces, r, -1)


def for_pieces(rows, pieces):
    return jnp.repeat(rows, pieces, axis=0) if pieces > 1 else rows


def own_gate(logits, own, other):
    places = jnp.arange(EXPERTS, dtype=F32)[None, :]
    mine = jnp.sum(jnp.where(places == own, logits, 0.0), axis=1)
    rival = jnp.sum(jnp.where(places == other[:, None], logits, 0.0), axis=1)
    top = jnp.maximum(mine, rival)
    mine, rival = jnp.exp(mine - top), jnp.exp(rival - top)
    return (mine / (mine + rival))[:, None]


def pick_gates(logits, routes):
    one_hot = (routes[:, :, None] == jnp.arange(EXPERTS, dtype=jnp.int32)[None, None, :]).astype(F32)
    return jax.nn.softmax(jnp.sum(one_hot * logits[:, None, :], axis=2), axis=-1)


def gate_back(gating, pulled, routes):
    inner_sum = gating * (pulled - jnp.sum(gating * pulled, axis=1, keepdims=True))
    one_hot = (routes[:, :, None] == jnp.arange(EXPERTS, dtype=jnp.int32)[None, None, :]).astype(F32)
    return jnp.sum(one_hot * inner_sum[:, :, None], axis=1).astype(BF16)


def score_block(query_block, key_block, allowed):
    scores = jnp.einsum(
        "kqhd,jhd->khqj", query_block, key_block, preferred_element_type=F32
    ) * HD ** (-0.5)
    return jnp.where(allowed[None, None], scores, masked_value)


def attend(query_block, key_block, value_block, allowed):
    scores = score_block(query_block, key_block, allowed)
    row_max = jnp.max(scores, axis=-1, keepdims=True)
    shifted = jnp.exp(scores - row_max)
    row_total = jnp.sum(shifted, axis=-1, keepdims=True)
    attn_probs = (shifted / row_total).astype(BF16)
    result = jnp.einsum("khqj,jhd->kqhd", attn_probs, value_block, preferred_element_type=F32)
    return (result.astype(BF16), (row_max + jnp.log(row_total))[..., 0])


def attend_back(query_block, key_block, value_block, allowed, log_total, grad_block):
    scores = score_block(query_block, key_block, allowed)
    attn_probs = jnp.exp(scores - log_total[..., None])
    pulled = jnp.einsum("kqhd,jhd->khqj", grad_block, value_block, preferred_element_type=F32)
    row_inner = jnp.sum(attn_probs * pulled, axis=-1, keepdims=True)
    score_back = (attn_probs * (pulled - row_inner)).astype(BF16)
    query_back = jnp.einsum(
        "khqj,jhd->kqhd", score_back, key_block, preferred_element_type=F32
    ) * HD ** (-0.5)
    key_back = jnp.einsum(
        "khqj,kqhd->jhd", score_back, query_block, preferred_element_type=F32
    ) * HD ** (-0.5)
    value_back = jnp.einsum(
        "khqj,kqhd->jhd", attn_probs.astype(BF16), grad_block, preferred_element_type=F32
    )
    return (query_back, key_back, value_back)


def per_device(
    tokens,
    segment_ids,
    attn_routes,
    ffn_routes,
    attn_gain,
    ffn_gain,
    routers,
    query_weight,
    output_weight,
    key_value_weight,
    gate_weight,
    up_weight,
    down_weight,
    cotangent,
):
    rows_here = tokens.shape[0]
    expert_count = lax.axis_size("expert")
    tensor_count = lax.axis_size("tensor")
    pieces = expert_count // EXPERTS
    column_count = D // tensor_count
    expert_index = lax.axis_index("expert")
    tensor_index = lax.axis_index("tensor")
    own = (expert_index // pieces).astype(F32)
    head_width = query_weight.shape[2]
    head_count = head_width // HD
    depth = (WINDOW + rows_here - 1) // rows_here

    def cols(whole):
        return lax.dynamic_slice_in_dim(whole, tensor_index * column_count, column_count, whole.ndim - 1)

    def tokens_to_experts(token_cols, places):
        grouped = mm(places, token_cols).astype(BF16).reshape(EXPERTS, CAP, -1)
        return columns_together(swap(for_pieces(grouped, pieces)).reshape(-1, column_count))

    def choices_to_experts(choice_rows, places):
        grouped = mm(places, choice_rows).astype(BF16).reshape(EXPERTS, CAP, -1)
        out = swap(to_pieces(grouped, pieces))
        return out.reshape(-1, out.shape[2])

    def choices_from_experts(rows, places):
        back = from_pieces(swap(rows.reshape(expert_count, CAP, -1)), pieces)
        return mm_tn(places, back.reshape(SLOTS, -1)).astype(BF16)

    def sums_from_experts(part_rows, places):
        back = swap(columns_summed(part_rows.astype(BF16)).reshape(expert_count, CAP, column_count))
        back = back.reshape(EXPERTS, pieces, CAP, column_count)
        if pieces > 1:
            total = sum(mm_tn(places, back[:, p].reshape(SLOTS, -1)) for p in range(pieces))
        else:
            total = mm_tn(places, back.reshape(SLOTS, -1))
        return total

    def scalars_from_experts(scalars, places):
        n = scalars.shape[1]
        back = swap(lax.psum(scalars, "tensor").reshape(expert_count, CAP, n))
        back = back.reshape(EXPERTS, pieces, CAP, n).sum(1).reshape(SLOTS, n)
        got = lax.dot_general(
            places.astype(F32), back, (((0,), (0,)), ((), ())), precision=lax.Precision.HIGHEST,
            preferred_element_type=F32)
        return got.reshape(TOPK, rows_here, n)

    state_in = tokens.astype(F32)
    gain_one = attn_gain.astype(F32)
    gain_two = cols(ffn_gain.astype(F32))
    routers_one, routers_two = routers[:, :EXPERTS], routers[:, EXPERTS:]
    dy_cols = cols(cotangent)
    token_cols = cols(tokens).astype(F32)

    attn_places = slot_places(attn_routes)
    ffn_places = slot_places(ffn_routes)
    attn_tokens = attn_places[:, :rows_here] + attn_places[:, rows_here:]
    ffn_tokens = ffn_places[:, :rows_here] + ffn_places[:, rows_here:]
    others = jnp.stack([
        mm(attn_places, attn_routes[:, ::-1].T.reshape(-1, 1).astype(BF16)),
        mm(ffn_places, ffn_routes[:, ::-1].T.reshape(-1, 1).astype(BF16)),
    ]).reshape(2, EXPERTS, CAP).transpose(1, 0, 2)
    others = swap(for_pieces(others, pieces)).transpose(1, 0, 2).reshape(2, -1)

    rate_one = lax.rsqrt(jnp.mean(state_in * state_in, axis=1, keepdims=True) + eps)
    normed_one = (state_in * rate_one * gain_one).astype(BF16)

    query_map = swap(to_pieces(query_weight, pieces)).reshape(D, -1)
    output_map = swap(to_pieces(output_weight, pieces)).reshape(D, -1)
    pair_map = lax.all_gather(key_value_weight, "expert", axis=1, tiled=True)

    pair = jnp.einsum("td,cdf->ctf", normed_one, pair_map, preferred_element_type=F32).astype(BF16)
    keys, values = pair[0], pair[1]
    rows_one = tokens_to_experts(cols(normed_one), attn_tokens)
    query_rows = mm(rows_one, query_map).astype(BF16)
    queries = choices_from_experts(query_rows, attn_places).reshape(TOPK, rows_here, head_count, HD)
    earlier_keys, earlier_values = [], []
    for step in range(depth):
        got_keys, got_values = shifted_by((keys, values), "expert", step + 1)
        earlier_keys.append(got_keys)
        earlier_values.append(got_values)
    span = (depth + 1) * rows_here
    key_cat = jnp.concatenate(earlier_keys[::-1] + [keys]).reshape(span, head_count, HD)
    value_cat = jnp.concatenate(earlier_values[::-1] + [values]).reshape(span, head_count, HD)
    padded_segments = jnp.concatenate([jnp.full((depth * rows_here,), -1, jnp.int32), segment_ids])
    segment_cat = lax.dynamic_slice_in_dim(padded_segments, expert_index * rows_here, span)
    own_segments = lax.dynamic_slice_in_dim(segment_ids, expert_index * rows_here, rows_here)
    distance = jnp.arange(rows_here)[:, None] + depth * rows_here - jnp.arange(span)[None, :]
    allowed = (distance >= 0) & (distance < WINDOW) & (own_segments[:, None] == segment_cat[None, :])
    heads, log_total = attend(queries, key_cat, value_cat, allowed)
    heads_rows = choices_to_experts(heads.reshape(TOPK * rows_here, head_width), attn_places)

    attn_logits_there = mm(rows_one, routers_one)
    attn_gate_rows = own_gate(attn_logits_there, own, others[0])
    attn_back = attn_gate_rows * mm_nt(heads_rows, output_map)
    state = token_cols + sums_from_experts(attn_back, attn_tokens)

    mean_two = lax.psum(jnp.sum(state * state, axis=1, keepdims=True), "tensor") / D
    rate_two = lax.rsqrt(mean_two + eps)
    normed_two = (state * rate_two * gain_two).astype(BF16)
    rows_dy = tokens_to_experts(dy_cols, ffn_tokens)
    rows_two = tokens_to_experts(normed_two, ffn_tokens)
    gate_map, up_map, down_map = gate_weight[0], up_weight[0], down_weight[0]
    ffn_gate_rows = own_gate(mm(rows_two, routers_two), own, others[1])
    hidden_grad = mm_nt(rows_dy, down_map)
    gate_pre = mm(rows_two, gate_map)
    up_pre = mm(rows_two, up_map)
    sigma = 1.0 / (1.0 + jnp.exp(-gate_pre))
    silu = gate_pre * sigma
    hidden = (silu * up_pre).astype(BF16)
    scaled_grad = hidden_grad * ffn_gate_rows
    gate_low = (scaled_grad * up_pre * (sigma * (1.0 + gate_pre * (1.0 - sigma)))).astype(BF16)
    up_low = (scaled_grad * silu).astype(BF16)
    ffn_pull_part = jnp.sum(hidden.astype(F32) * hidden_grad, axis=1, keepdims=True)
    gate_part = ffn_gate_rows / tensor_count
    ffn_scalars = scalars_from_experts(jnp.concatenate([ffn_pull_part, gate_part / pieces], axis=1), ffn_places)
    row_grad = mm_nt(gate_low, gate_map) + mm_nt(up_low, up_map)
    normed_two_grad = sums_from_experts(row_grad, ffn_tokens)
    ffn_pull, ffn_gates = ffn_scalars[:, :, 0].T, ffn_scalars[:, :, 1].T
    ffn_logit_grad = gate_back(ffn_gates, ffn_pull, ffn_routes)
    normed_two_grad = normed_two_grad + mm_nt(
        ffn_logit_grad, lax.dynamic_slice_in_dim(routers_two, tensor_index * column_count, column_count, 0))
    ffn_router_cols = mm_tn(normed_two, ffn_logit_grad)
    ffn_gain_cols = jnp.sum(normed_two_grad * state * rate_two, axis=0)
    ahead = normed_two_grad * gain_two
    centre = lax.psum(jnp.sum(ahead * state, axis=1, keepdims=True), "tensor") / D
    state_grad = dy_cols.astype(F32) + rate_two * ahead - state * rate_two * rate_two * rate_two * centre

    rows_state = tokens_to_experts(state_grad.astype(BF16), attn_tokens)
    heads_grad_rows = mm(rows_state, output_map)
    attn_pull_part = jnp.sum(heads_grad_rows * heads_rows.astype(F32), axis=1, keepdims=True)
    heads_grad = choices_from_experts((heads_grad_rows * attn_gate_rows).astype(BF16), attn_places)
    output_part = mm_tn((rows_state.astype(F32) * attn_gate_rows).astype(BF16), heads_rows)
    attn_pull = scalars_from_experts(attn_pull_part, attn_places)[:, :, 0].T

    query_back, key_back, value_back = attend_back(
        queries, key_cat, value_cat, allowed, log_total, heads_grad.reshape(TOPK, rows_here, head_count, HD))
    key_back = key_back.reshape(span, head_width)
    value_back = value_back.reshape(span, head_width)
    key_total, value_total = key_back[depth * rows_here:], value_back[depth * rows_here:]
    for step in range(1, depth + 1):
        lower = (depth - step) * rows_here
        key_total = key_total + shifted_by(
            key_back[lower : lower + rows_here].astype(BF16), "expert", -step).astype(F32)
        value_total = value_total + shifted_by(
            value_back[lower : lower + rows_here].astype(BF16), "expert", -step).astype(F32)
    keys_grad, values_grad = key_total.astype(BF16), value_total.astype(BF16)
    query_grad_rows = choices_to_experts(
        query_back.reshape(TOPK * rows_here, head_width).astype(BF16), attn_places)
    query_part = mm_tn(rows_one, query_grad_rows)
    normed_grad = sums_from_experts(mm_nt(query_grad_rows, query_map), attn_tokens)
    pair_grad = jnp.stack([keys_grad, values_grad])
    pair_part = jnp.einsum("td,ctf->cdf", normed_one, pair_grad, preferred_element_type=F32)
    pair_back = jnp.einsum("ctf,cdf->td", pair_grad, pair_map, preferred_element_type=F32)
    normed_grad = normed_grad + columns_summed(pair_back.astype(BF16)).astype(F32)
    attn_gates = pick_gates(mm(normed_one, routers_one), attn_routes)
    attn_logit_grad = gate_back(attn_gates, attn_pull, attn_routes)
    normed_grad = normed_grad + mm_nt(
        attn_logit_grad, lax.dynamic_slice_in_dim(routers_one, tensor_index * column_count, column_count, 0))
    attn_router_cols = mm_tn(cols(normed_one), attn_logit_grad)
    attn_gain_cols = jnp.sum(normed_grad * token_cols * rate_one, axis=0)
    ahead_one = normed_grad * cols(gain_one)
    centre_one = lax.psum(jnp.sum(ahead_one * token_cols, axis=1, keepdims=True), "tensor") / D
    tokens_grad = state_grad + rate_one * ahead_one - token_cols * rate_one * rate_one * rate_one * centre_one
    tokens_grad = columns_together(tokens_grad)

    def from_maps(part):
        got = swap(part.astype(BF16).reshape(expert_count, D // expert_count, -1))
        return from_pieces(got, pieces).astype(F32)

    query_grad, output_grad = from_maps(query_part), from_maps(output_part)
    key_value_grad = lax.psum_scatter(
        pair_part.astype(BF16), "expert", scatter_dimension=1, tiled=True).astype(F32)
    small = jnp.concatenate(
        [attn_router_cols, ffn_router_cols, attn_gain_cols[:, None], ffn_gain_cols[:, None]], axis=1)
    small = lax.all_gather(small, "tensor", axis=0, tiled=True)
    small = lax.psum_scatter(small, "expert", scatter_dimension=0, tiled=True)

    scaled_dy = (rows_dy.astype(F32) * ffn_gate_rows).astype(BF16)
    gate_grad = mm_tn(rows_two, gate_low)
    up_grad = mm_tn(rows_two, up_low)
    down_grad = mm_tn(hidden, scaled_dy)
    ffn_back = sums_from_experts(mm(hidden, down_map) * ffn_gate_rows, ffn_tokens)
    mixed = (state + ffn_back).astype(BF16)
    return (
        mixed,
        tokens_grad,
        small[:, 2 * EXPERTS],
        small[:, 2 * EXPERTS + 1],
        small[:, : 2 * EXPERTS],
        query_grad,
        output_grad,
        key_value_grad,
        gate_grad[None],
        up_grad[None],
        down_grad[None],
    )


def solution(mesh):
    in_specs = (
        P("expert", None),
        P(),
        P("expert", None),
        P("expert", None),
        P(),
        P(),
        P(),
        P(None, "expert", "tensor"),
        P(None, "expert", "tensor"),
        P(None, "expert", "tensor"),
        P("expert", None, "tensor"),
        P("expert", None, "tensor"),
        P("expert", "tensor", None),
        P("expert", None),
    )
    out_specs = (
        P("expert", "tensor"),
        P("expert", None),
        P("expert"),
        P("expert"),
        P("expert", None),
        P(None, "expert", "tensor"),
        P(None, "expert", "tensor"),
        P(None, "expert", "tensor"),
        P("expert", None, "tensor"),
        P("expert", None, "tensor"),
        P("expert", "tensor", None),
    )
    return jax.shard_map(
        per_device, mesh=mesh, in_specs=in_specs, out_specs=out_specs, check_vma=False
    )
```

```python
import functools
import math

import jax
import jax.numpy as jnp
from jax import lax
from jax.experimental import pallas as pl
from jax.experimental.pallas import tpu as pltpu
from jax.sharding import PartitionSpec as P

D = 2048
HD = 128
EXPERTS = 8
TOPK = 2
WINDOW = 1024
CAP = 160
SLOTS = EXPERTS * CAP

eps = 1e-06
masked_value = -1e30
SCALE = HD ** (-0.5)
LOG2E = math.log2(math.e)
Q_ROWS = 256
NOTES = 16
WINDOW_ORDER = (1, 0, 2)
F32 = jnp.float32
BF16 = jnp.bfloat16
MESH = pl.DeviceIdType.MESH
VMEM = pl.BlockSpec(memory_space=pltpu.VMEM)
ANY = pl.BlockSpec(memory_space=pl.ANY)


def remote(src, dst, send, recv, **device):
    return pltpu.make_async_remote_copy(
        src_ref=src, dst_ref=dst, send_sem=send, recv_sem=recv, device_id=device, device_id_type=MESH)


def meet(experts, bits):
    e, t = lax.axis_index("expert"), lax.axis_index("tensor")
    barrier = pltpu.get_barrier_semaphore()

    @pl.loop(1, experts)
    def _(s):
        pl.semaphore_signal(barrier, inc=1, device_id={"expert": e ^ s}, device_id_type=MESH)

    for b in range(bits):
        pl.semaphore_signal(barrier, inc=1, device_id={"tensor": t ^ (1 << b)}, device_id_type=MESH)
    pl.semaphore_wait(barrier, experts - 1 + bits)


def partners(e, experts, near):
    if near:
        return lambda s: e ^ s
    return lambda s: e ^ ((experts - s) & (experts - 1))


def low_bit(d):
    return (d & -d).bit_length() - 1


def gather_kernel(experts, bits, near, multiply, scale, *refs):
    refs = list(refs)
    x = refs.pop(0)
    w = refs.pop(0) if multiply else None
    gate = refs.pop(0) if scale else None
    rows = refs.pop(0)
    back = refs.pop(0) if multiply else None
    product = refs.pop(0) if scale else None
    y = refs.pop(0) if multiply else None
    z_send, z_recv, t_send, t_recv = refs[:4]
    refs = refs[4:]
    if multiply:
        y_send, y_recv = refs[:2]
    e, t = lax.axis_index("expert"), lax.axis_index("tensor")
    partner = partners(e, experts, near)
    width = x.shape[2]
    tensor = 1 << bits

    def cols(d):
        return pl.ds(pl.multiple_of((t ^ d) * width, 128), width)

    def arrive(j):
        return remote(x.at[j], rows.at[e, :, cols(0)], z_send.at[j], z_recv.at[e], expert=j)

    def arrived(j):
        return remote(x.at[j], rows.at[j, :, cols(0)], z_send.at[j], z_recv.at[j], expert=j)

    def pass_on(j, d, b):
        place = rows.at[j, :, cols(d)]
        far = d | (1 << b)
        return remote(place, place, t_send.at[j, far], t_recv.at[j, far], tensor=t ^ (1 << b))

    def passed(j, d):
        place = rows.at[j, :, cols(d)]
        return remote(place, place, t_send.at[j, d], t_recv.at[j, d], tensor=t ^ (1 << low_bit(d)))

    def hand_back(j):
        return remote(y.at[j], back.at[e], y_send.at[j], y_recv.at[e], expert=j)

    def handed(j):
        return remote(y.at[j], back.at[j], y_send.at[j], y_recv.at[j], expert=j)

    meet(experts, bits)

    @pl.loop(1, experts)
    def _(s):
        arrive(partner(s)).start()

    rows[e, :, cols(0)] = x[e]

    @pl.loop(0, experts + bits)
    def _(i):
        @pl.when(i < experts)
        def _():
            j = partner(i)

            @pl.when(i > 0)
            def _():
                arrived(j).wait_recv()

            for b in reversed(range(bits)):
                pass_on(j, 0, b).start()

        for k in range(1, bits + 1):
            @pl.when((i >= k) & (i < experts + k))
            def _():
                m = i - k
                j = partner(m)
                bit = bits - k
                for d in range(1, tensor):
                    if low_bit(d) == bit:
                        passed(j, d).wait_recv()
                        for b in reversed(range(bit)):
                            pass_on(j, d, b).start()
                if k == bits and multiply:
                    out = jnp.dot(rows[j], w[...], preferred_element_type=F32)
                    if scale:
                        product[j] = out.astype(BF16)
                        out = out * gate[j]
                    y[j] = out.astype(BF16)

                    @pl.when(m == 0)
                    def _():
                        back[e] = y[e]

                    @pl.when(m > 0)
                    def _():
                        hand_back(j).start()

    @pl.loop(1, experts)
    def _(s):
        j = partner(s)
        arrived(j).wait_send()
        if multiply:
            handed(j).wait_recv()
            handed(j).wait_send()

    @pl.loop(0, experts)
    def _(j):
        for d in range(1, tensor):
            passed(j, d).wait_send()


def gather_rows(x, w=None, gate=None, near=True, collective_id=0):
    experts, tensor = lax.axis_size("expert"), lax.axis_size("tensor")
    bits = tensor.bit_length() - 1
    cap, width = x.shape[1], x.shape[2]
    multiply = w is not None
    f = w.shape[-1] if multiply else 0
    ins, specs = [x], [VMEM]
    outs = [jax.ShapeDtypeStruct((experts, cap, width * tensor), BF16)]
    scratch = []
    if multiply:
        ins.append(w)
        specs.append(VMEM)
        outs.append(jax.ShapeDtypeStruct((experts, cap, f), BF16))
    if gate is not None:
        ins.append(gate)
        specs.append(VMEM)
        outs.append(jax.ShapeDtypeStruct((experts, cap, f), BF16))
    if multiply:
        scratch.append(pltpu.VMEM((experts, cap, f), BF16))
    scratch += [pltpu.SemaphoreType.DMA((experts,))] * 2 + [pltpu.SemaphoreType.DMA((experts, tensor))] * 2
    if multiply:
        scratch += [pltpu.SemaphoreType.DMA((experts,))] * 2
    return pl.pallas_call(
        functools.partial(gather_kernel, experts, bits, near, multiply, gate is not None),
        out_shape=outs,
        in_specs=specs,
        out_specs=[VMEM] * len(outs),
        scratch_shapes=scratch,
        compiler_params=pltpu.CompilerParams(
            collective_id=collective_id, has_side_effects=True, vmem_limit_bytes=48 * 2**20),
    )(*ins)


def front_kernel(experts, bits, *refs):
    (tokens, gain, slots, w_in, kv_in, rows, back, w, window, kv, keys, values, x, y,
     z_send, z_recv, t_send, t_recv, y_send, y_recv, w_send, w_recv, k_send, k_recv, n_send, n_recv, own_sem) = refs
    e, t = lax.axis_index("expert"), lax.axis_index("tensor")
    partner = partners(e, experts, True)
    width = x.shape[1]
    cap = rows.shape[1]
    here = tokens.shape[0]
    tensor = 1 << bits
    expert_bits = experts.bit_length() - 1
    pieces = experts * cap // x.shape[0]

    def x_part(j):
        return pl.ds(pl.multiple_of((j // pieces) * cap, cap), cap)

    def cols(d):
        return pl.ds(pl.multiple_of((t ^ d) * width, 128), width)

    def part(j):
        return pl.ds(j * (w.shape[0] // experts), w.shape[0] // experts)

    def block(q, d):
        if isinstance(q, int):
            return window.at[q - experts, :, cols(d)]
        return rows.at[q, :, cols(d)]

    def pass_on(q, d, b):
        far = d | (1 << b)
        return remote(block(q, d), block(q, d), t_send.at[q, far], t_recv.at[q, far], tensor=t ^ (1 << b))

    def passed(q, d):
        return remote(block(q, d), block(q, d), t_send.at[q, d], t_recv.at[q, d], tensor=t ^ (1 << low_bit(d)))

    def stage(q, k):
        bit = bits - k
        for d in range(1, tensor):
            if low_bit(d) == bit:
                passed(q, d).wait_recv()
                for b in reversed(range(bit)):
                    pass_on(q, d, b).start()

    def arrived(j):
        return remote(x.at[x_part(j)], rows.at[j, :, cols(0)], z_send.at[j], z_recv.at[j], expert=j)

    def handed(j):
        return remote(y.at[j], back.at[j], y_send.at[j], y_recv.at[j], expert=j)

    def chunk(d):
        return kv.at[:, part(e ^ d), :]

    def pass_chunk(d, b):
        far = d | (1 << b)
        return remote(chunk(d), chunk(d), k_send.at[far], k_recv.at[far], expert=e ^ (1 << b))

    def passed_chunk(d):
        return remote(chunk(d), chunk(d), k_send.at[d], k_recv.at[d], expert=e ^ (1 << low_bit(d)))

    def chunks(bit):
        for d in range(1, experts):
            if low_bit(d) == bit:
                passed_chunk(d).wait_recv()
                for b in reversed(range(bit)):
                    pass_chunk(d, b).start()

    def two_on(way):
        return remote(window.at[2, :, cols(0)], window.at[0, :, cols(0)], n_send.at[0], n_recv.at[0],
                      expert=lax.rem(e + experts + 2 * way, experts))

    def across():
        return remote(window.at[2 - 2 * (e & 1), :, cols(0)], window.at[1, :, cols(0)], n_send.at[1], n_recv.at[1],
                      expert=e ^ 1)

    own_kv = pltpu.make_async_copy(kv_in, chunk(0), own_sem.at[0])
    own_w = pltpu.make_async_copy(w_in.at[e], w.at[part(e)], own_sem.at[1])
    own_kv.start()
    own_w.start()
    meet(experts, bits)
    for b in reversed(range(expert_bits)):
        remote(kv_in, chunk(0), k_send.at[1 << b], k_recv.at[1 << b], expert=e ^ (1 << b)).start()

    state = tokens[...].astype(F32)
    rate = lax.rsqrt(jnp.mean(state * state, axis=1, keepdims=True) + eps)
    window[2] = (state * rate * gain[...]).astype(BF16)
    two_on(1).start()
    place = lax.broadcasted_iota(jnp.int32, (x.shape[0], here), 0)
    chosen = (place == slots[:, pl.ds(0, here)]) | (place == slots[:, pl.ds(here, here)])
    x[...] = jnp.dot(chosen.astype(F32).astype(BF16), window[2, :, cols(0)], preferred_element_type=F32).astype(BF16)

    @pl.loop(1, experts)
    def _(s):
        j = partner(s)
        remote(x.at[x_part(j)], rows.at[e, :, cols(0)], z_send.at[j], z_recv.at[e], expert=j).start()

    @pl.loop(1, experts)
    def _(s):
        j = partner(s)
        remote(w_in.at[j], w.at[part(e)], w_send.at[j], w_recv.at[e], expert=j).start()

    rows[e, :, cols(0)] = x[x_part(e), :]
    chunks(expert_bits - 1)

    @pl.loop(0, experts + bits)
    def _(i):
        @pl.when(i < experts)
        def _():
            j = partner(i)

            @pl.when(i > 0)
            def _():
                arrived(j).wait_recv()

            for b in reversed(range(bits)):
                pass_on(j, 0, b).start()

        for k in range(1, bits + 1):
            @pl.when((i >= k) & (i < experts + k))
            def _():
                stage(partner(i - k), k)

        @pl.when(i == experts // 2)
        def _():
            two_on(-1).wait_recv()
            across().start()
            for b in reversed(range(bits)):
                pass_on(experts, 0, b).start()

    for bit in reversed(range(1, expert_bits - 1)):
        chunks(bit)
    across().wait_recv()
    for b in reversed(range(bits)):
        pass_on(experts + 1, 0, b).start()
    own_w.wait()

    @pl.loop(1, experts)
    def _(s):
        q = partner(s)
        remote(w_in.at[q], w.at[part(q)], w_send.at[q], w_recv.at[q], expert=q).wait_recv()

    @pl.loop(0, experts)
    def _(i):
        j = partner(lax.rem(i + 1, experts))
        y[j] = jnp.dot(rows[j], w[...], preferred_element_type=F32).astype(BF16)

        @pl.when(i < experts - 1)
        def _():
            remote(y.at[j], back.at[e], y_send.at[j], y_recv.at[e], expert=j).start()

    back[e] = y[e]
    for k in range(1, bits + 1):
        for q in range(2):
            stage(experts + q, k)
    chunks(0)
    own_kv.wait()
    for q in range(3):
        for c, out in enumerate((keys, values)):
            out[pl.ds(q * here, here), :] = jnp.dot(window[q], kv[c], preferred_element_type=F32).astype(BF16)

    @pl.loop(1, experts)
    def _(s):
        j = partner(s)
        arrived(j).wait_send()
        handed(j).wait_recv()
        handed(j).wait_send()
        remote(w_in.at[j], w.at[part(j)], w_send.at[j], w_recv.at[j], expert=j).wait_send()

    for d in range(1, experts):
        passed_chunk(d).wait_send()
    two_on(1).wait_send()
    across().wait_send()
    for q in range(2):
        for d in range(1, tensor):
            passed(experts + q, d).wait_send()

    @pl.loop(0, experts)
    def _(j):
        for d in range(1, tensor):
            passed(j, d).wait_send()


def front(tokens, gain, slots, w, kv, collective_id):
    experts, tensor = lax.axis_size("expert"), lax.axis_size("tensor")
    bits = tensor.bit_length() - 1
    here = tokens.shape[0]
    f, f_kv = w.shape[2], kv.shape[2]
    dma = pltpu.SemaphoreType.DMA
    return pl.pallas_call(
        functools.partial(front_kernel, experts, bits),
        out_shape=[
            jax.ShapeDtypeStruct((experts, CAP, D), BF16),
            jax.ShapeDtypeStruct((experts, CAP, f), BF16),
            jax.ShapeDtypeStruct((D, f), BF16),
            jax.ShapeDtypeStruct((3, here, D), BF16),
            jax.ShapeDtypeStruct((2, D, f_kv), BF16),
            jax.ShapeDtypeStruct((3 * here, f_kv), BF16),
            jax.ShapeDtypeStruct((3 * here, f_kv), BF16),
        ],
        in_specs=[VMEM, VMEM, VMEM, ANY, ANY],
        out_specs=[VMEM] * 7,
        scratch_shapes=[pltpu.VMEM((SLOTS, D // tensor), BF16), pltpu.VMEM((experts, CAP, f), BF16)]
        + [dma((experts,))] * 2 + [dma((experts + 2, tensor))] * 2 + [dma((experts,))] * 6
        + [dma((2,))] * 3,
        compiler_params=pltpu.CompilerParams(
            collective_id=collective_id, has_side_effects=True, vmem_limit_bytes=56 * 2**20),
    )(tokens, gain, slots, w, kv)


def scatter_kernel(experts, bits, depth, near, multiply, terms, scale, noted, *refs):
    refs = list(refs)
    h_in = refs.pop(0) if multiply else None
    w = refs.pop(0) if multiply else None
    factors = [(refs.pop(0), refs.pop(0)) for _ in range(terms)]
    gate = refs.pop(0) if scale else None
    notes = refs.pop(0) if noted else None
    if depth:
        key_grad, value_grad, kv = refs[:3]
        refs = refs[3:]
    back = refs.pop(0)
    h = refs.pop(0) if multiply else None
    if multiply:
        factors = [(h, w)]
    owed = refs.pop(0) if depth else None
    keep, sent, got, y, t_send, t_recv, y_send, y_recv = refs[:8]
    refs = refs[8:]
    if multiply:
        h_send, h_recv = refs[:2]
        refs = refs[2:]
    if depth:
        n_keep, n_sent, n_got, n_y, n_in, n_send, n_recv, o_send, o_recv = refs
    e, t = lax.axis_index("expert"), lax.axis_index("tensor")
    partner = partners(e, experts, near)
    tensor = 1 << bits
    cap, width = factors[0][0].shape[1], y.shape[2]
    body = pl.ds(0, cap)
    foot = pl.ds(cap, NOTES)

    def slice_at(d):
        return pl.ds(pl.multiple_of((t ^ d) * width, 128), width)

    def handed(j):
        return remote(y.at[j], back.at[j], y_send.at[j], y_recv.at[j], expert=j)

    def give(j, d):
        return remote(sent.at[j, d], got.at[j, d], t_send.at[j, d], t_recv.at[j, d], tensor=t ^ (1 << low_bit(d)))

    def owe(q, d):
        return remote(n_sent.at[q, d], n_got.at[q, d], n_send.at[q, d], n_recv.at[q, d], tensor=t ^ (1 << low_bit(d)))

    def across():
        return remote(n_y.at[1], n_in, o_send.at[1], o_recv.at[1], expert=e ^ 1)

    def two_back(way):
        return remote(n_y.at[0], owed.at[1], o_send.at[0], o_recv.at[0],
                      expert=lax.rem(e + experts - 2 * way, experts))

    def window_stage(k):
        for q in WINDOW_ORDER:
            for d in range(tensor - 1, -1, -1):
                if d % (1 << k) == 0:
                    came = d | (1 << (k - 1))
                    owe(q, came).wait_recv()
                    total = n_keep[q, d // 2] + n_got[q, came].astype(F32)
                    if k == bits:
                        if q == 1:
                            n_y[1] = total.astype(BF16)
                            across().start()
                        else:
                            n_keep[q, 0] = total
                    elif d & (1 << k):
                        n_sent[q, d] = total.astype(BF16)
                        owe(q, d).start()
                    else:
                        n_keep[q, d // 2] = total

    meet(experts, bits)
    if multiply:
        @pl.loop(1, experts)
        def _(s):
            j = partner(s)
            remote(h_in.at[j], h.at[e], h_send.at[j], h_recv.at[e], expert=j).start()

        h[e] = h_in[e]
    if depth:
        here = key_grad.shape[0] // 3
        for q in WINDOW_ORDER:
            place = pl.ds(q * here, here)
            for d in range(tensor - 1, -1, -1):
                part = lax.dot_general(
                    key_grad[place, :], kv[0, slice_at(d), :], (((1,), (1,)), ((), ())), preferred_element_type=F32)
                part += lax.dot_general(
                    value_grad[place, :], kv[1, slice_at(d), :], (((1,), (1,)), ((), ())), preferred_element_type=F32)
                if d & 1:
                    n_sent[q, d] = part.astype(BF16)
                    owe(q, d).start()
                else:
                    n_keep[q, d // 2] = part
        window_stage(1)

    @pl.loop(0, experts + bits)
    def _(i):
        @pl.when(i < experts)
        def _():
            j = partner(i)
            slot = lax.rem(i, bits + 1)
            if multiply:
                @pl.when(i > 0)
                def _():
                    remote(h_in.at[j], h.at[j], h_send.at[j], h_recv.at[j], expert=j).wait_recv()
            for d in range(tensor - 1, -1, -1):
                part = None
                for left, right in factors:
                    term = lax.dot_general(
                        left[j], right[slice_at(d), :], (((1,), (1,)), ((), ())), preferred_element_type=F32)
                    part = term if part is None else part + term
                if scale:
                    part = part * gate[j]
                if d & 1:
                    sent[j, d, body, :] = part.astype(BF16)
                    if noted:
                        sent[j, d, foot, :] = notes[j].astype(BF16)
                    give(j, d).start()
                else:
                    keep[slot, d // 2, body, :] = part
                    if noted:
                        keep[slot, d // 2, foot, :] = notes[j]

        for k in range(1, bits + 1):
            @pl.when((i >= k) & (i < experts + k))
            def _():
                m = i - k
                slot = lax.rem(m, bits + 1)
                j = partner(m)
                for d in range(tensor - 1, -1, -1):
                    if d % (1 << k) == 0:
                        came = d | (1 << (k - 1))
                        give(j, came).wait_recv()
                        total = keep[slot, d // 2] + got[j, came].astype(F32)
                        if k == bits:
                            y[j] = total.astype(BF16)
                        elif d & (1 << k):
                            sent[j, d] = total.astype(BF16)
                            give(j, d).start()
                        else:
                            keep[slot, d // 2] = total
                if k == bits:
                    @pl.when(m == 0)
                    def _():
                        back[e] = y[e]

                    @pl.when(m > 0)
                    def _():
                        remote(y.at[j], back.at[e], y_send.at[j], y_recv.at[e], expert=j).start()

        if depth:
            for k in range(2, bits + 1):
                @pl.when(i == 2 * (k - 1))
                def _():
                    window_stage(k)

            @pl.when(i == 2 * bits)
            def _():
                across().wait_recv()
                passing = (e & 1).astype(F32)
                came = n_in[...].astype(F32)
                n_y[0] = (n_keep[0, 0] + passing * came).astype(BF16)
                owed[0] = (n_keep[2, 0] + (1.0 - passing) * came).astype(BF16)
                two_back(1).start()

    @pl.loop(1, experts)
    def _(s):
        j = partner(s)
        if multiply:
            remote(h_in.at[j], h.at[j], h_send.at[j], h_recv.at[j], expert=j).wait_send()
        handed(j).wait_recv()
        handed(j).wait_send()

    @pl.loop(0, experts)
    def _(j):
        for d in range(1, tensor):
            give(j, d).wait_send()

    if depth:
        for q in range(3):
            for d in range(1, tensor):
                owe(q, d).wait_send()
        across().wait_send()
        two_back(-1).wait_recv()
        two_back(1).wait_send()


def scatter_rows(h=None, w=None, gate=None, notes=None, products=(), windows=None, near=True, collective_id=0):
    experts, tensor = lax.axis_size("expert"), lax.axis_size("tensor")
    bits = tensor.bit_length() - 1
    multiply = w is not None
    high = CAP + (NOTES if notes is not None else 0)
    width = D // tensor
    dma = pltpu.SemaphoreType.DMA
    ins = [a for a in (h, w) if a is not None] + [a for pair in products for a in pair]
    ins += [a for a in (gate, notes) if a is not None]
    outs = [jax.ShapeDtypeStruct((experts, high, width), BF16)]
    scratch = [
        pltpu.VMEM((bits + 1, tensor // 2, high, width), F32),
        pltpu.VMEM((experts, tensor, high, width), BF16),
        pltpu.VMEM((experts, tensor, high, width), BF16),
        pltpu.VMEM((experts, high, width), BF16),
    ]
    scratch += [dma((experts, tensor))] * 2 + [dma((experts,))] * 2
    if multiply:
        outs.append(jax.ShapeDtypeStruct(h.shape, BF16))
        scratch += [dma((experts,))] * 2
    if windows is not None:
        ins += windows
        here = windows[0].shape[0] // 3
        outs.append(jax.ShapeDtypeStruct((2, here, width), BF16))
        scratch += [
            pltpu.VMEM((3, tensor // 2, here, width), F32),
            pltpu.VMEM((3, tensor, here, width), BF16),
            pltpu.VMEM((3, tensor, here, width), BF16),
            pltpu.VMEM((2, here, width), BF16),
            pltpu.VMEM((here, width), BF16),
        ] + [dma((3, tensor))] * 2 + [dma((2,))] * 2
    return pl.pallas_call(
        functools.partial(
            scatter_kernel, experts, bits, windows is not None, near, multiply, len(products), gate is not None,
            notes is not None),
        out_shape=outs,
        in_specs=[VMEM] * len(ins),
        out_specs=[VMEM] * len(outs),
        scratch_shapes=scratch,
        compiler_params=pltpu.CompilerParams(
            collective_id=collective_id, has_side_effects=True, vmem_limit_bytes=60 * 2**20),
    )(*ins)


def dot(left, right, dims):
    return lax.dot_general(left, right, ((dims[0], dims[1]), ((), ())), preferred_element_type=F32)


def mm(left, right):
    return dot(left, right, ((1,), (0,)))


def mm_nt(left, right):
    return dot(left, right, ((1,), (1,)))


def mm_tn(left, right):
    return dot(left, right, ((0,), (0,)))


def swap(blocks):
    return lax.all_to_all(blocks, "expert", split_axis=0, concat_axis=0, tiled=True)


def columns_together(rows):
    return lax.all_gather(rows, "tensor", axis=1, tiled=True)


def columns_summed(rows):
    return lax.psum_scatter(rows, "tensor", scatter_dimension=1, tiled=True)


def slot_numbers(routes):
    flat = routes.T.reshape(-1)
    place = jnp.arange(flat.shape[0], dtype=jnp.int32)
    earlier = (flat[:, None] == flat[None, :]) & (place[None, :] < place[:, None])
    return flat * CAP + jnp.sum(earlier.astype(jnp.int32), axis=1)


def place_matrix(slots, stride=CAP):
    wide = slots + (slots // CAP) * (stride - CAP)
    return (jnp.arange(EXPERTS * stride, dtype=jnp.int32)[:, None] == wide[None, :]).astype(BF16)


def to_pieces(rows, pieces):
    if pieces == 1:
        return rows
    experts, r, c = rows.shape
    return rows.reshape(experts, r, pieces, c // pieces).transpose(0, 2, 1, 3).reshape(experts * pieces, r, -1)


def from_pieces(rows, pieces):
    if pieces == 1:
        return rows
    both, r, c = rows.shape
    return rows.reshape(both // pieces, pieces, r, c).transpose(0, 2, 1, 3).reshape(both // pieces, r, -1)


def for_pieces(rows, pieces):
    return jnp.repeat(rows, pieces, axis=0) if pieces > 1 else rows


def own_gate(logits, own, other):
    places = jnp.arange(EXPERTS, dtype=F32)[None, :]
    mine = jnp.sum(jnp.where(places == own, logits, 0.0), axis=1)
    rival = jnp.sum(jnp.where(places == other[:, None], logits, 0.0), axis=1)
    top = jnp.maximum(mine, rival)
    mine, rival = jnp.exp(mine - top), jnp.exp(rival - top)
    return (mine / (mine + rival))[:, None]


def pick_gates(logits, routes):
    one_hot = (routes[:, :, None] == jnp.arange(EXPERTS, dtype=jnp.int32)[None, None, :]).astype(F32)
    return jax.nn.softmax(jnp.sum(one_hot * logits[:, None, :], axis=2), axis=-1)


def gate_back(gating, pulled, routes):
    inner_sum = gating * (pulled - jnp.sum(gating * pulled, axis=1, keepdims=True))
    one_hot = (routes[:, :, None] == jnp.arange(EXPERTS, dtype=jnp.int32)[None, None, :]).astype(F32)
    return jnp.sum(one_hot * inner_sum[:, :, None], axis=1).astype(BF16)


def place_matrices(slots_ref, spread, gathered):
    count, choices = spread.shape
    spread[...] = (lax.broadcasted_iota(jnp.int32, (count, choices), 0) == slots_ref[...]).astype(F32).astype(BF16)
    gathered[...] = spread[...].T


def mask_bias(query_ids, key_ids, bias):
    blocks, span, _ = bias.shape

    for block in range(blocks):
        first = block * Q_ROWS
        query_place = lax.broadcasted_iota(jnp.int32, (span, Q_ROWS), 1) + WINDOW
        distance = query_place - lax.broadcasted_iota(jnp.int32, (span, Q_ROWS), 0)
        same = key_ids[pl.ds(first, span), :] == query_ids[:, pl.ds(first, Q_ROWS)]
        allowed = (distance >= 0) & (distance < WINDOW) & same
        part = jnp.where(allowed, 0.0, masked_value)
        for k in range(TOPK):
            bias[block, :, pl.ds(k * Q_ROWS, Q_ROWS)] = part


def of_block(choices, block):
    rows = choices.shape[0] // TOPK
    return jnp.concatenate([choices[pl.ds(k * rows + block * Q_ROWS, Q_ROWS), :] for k in range(TOPK)], axis=0)


def attend_kernel(slots_ref, back_ref, key_ref, value_ref, query_ids, key_ids, grouped_ref, query_ref, lse_ref,
                  spread, gathered, bias, heads):
    @pl.when(pl.program_id(0) == 0)
    def _():
        place_matrices(slots_ref, spread, gathered)
        mask_bias(query_ids, key_ids, bias)

    query_ref[...] = jnp.dot(gathered[...], back_ref[...], preferred_element_type=F32).astype(BF16)
    blocks, span, _ = bias.shape
    rows = query_ref.shape[0] // TOPK
    for block in range(blocks):
        queries = of_block(query_ref, block)
        keys = key_ref[pl.ds(block * Q_ROWS, span), :]
        values = value_ref[pl.ds(block * Q_ROWS, span), :]
        scores = lax.dot_general(keys, queries, (((1,), (1,)), ((), ())), preferred_element_type=F32)
        scores = scores * (SCALE * LOG2E) + bias[block]
        top = jnp.max(scores, axis=0, keepdims=True)
        probs = jnp.exp2(scores - top)
        total = jnp.sum(probs, axis=0, keepdims=True)
        out = lax.dot_general(values, probs.astype(BF16), (((0,), (0,)), ((), ())), preferred_element_type=F32)
        out = (out * (1.0 / total)).T.astype(BF16)
        for k in range(TOPK):
            heads[pl.ds(k * rows + block * Q_ROWS, Q_ROWS), :] = out[k * Q_ROWS : (k + 1) * Q_ROWS]
        lse_ref[0, :, pl.ds(block * TOPK * Q_ROWS, TOPK * Q_ROWS)] = top + jnp.log2(total)
    grouped_ref[...] = jnp.dot(spread[...], heads[...], preferred_element_type=F32).astype(BF16)


def attend(slots, back, keys, values, query_ids, key_ids):
    choices, (count, width), span = slots.shape[1], back.shape, keys.shape[0]
    blocks = choices // TOPK // Q_ROWS
    head = lambda rows: pl.BlockSpec((rows, HD), lambda h: (0, h))
    whole = lambda a: pl.BlockSpec(a.shape, lambda h: (0, 0))
    return pl.pallas_call(
        attend_kernel,
        grid=(width // HD,),
        out_shape=[
            jax.ShapeDtypeStruct((count, width), BF16),
            jax.ShapeDtypeStruct((choices, width), BF16),
            jax.ShapeDtypeStruct((width // HD, 1, choices), F32),
        ],
        in_specs=[whole(slots), head(count), head(span), head(span), whole(query_ids), whole(key_ids)],
        out_specs=[head(count), head(choices), pl.BlockSpec((1, 1, choices), lambda h: (h, 0, 0))],
        scratch_shapes=[
            pltpu.VMEM((count, choices), BF16),
            pltpu.VMEM((choices, count), BF16),
            pltpu.VMEM((blocks, WINDOW + Q_ROWS, TOPK * Q_ROWS), F32),
            pltpu.VMEM((choices, HD), BF16),
        ],
        compiler_params=pltpu.CompilerParams(vmem_limit_bytes=48 * 2**20),
        cost_estimate=pl.CostEstimate(flops=16 * 10**9, bytes_accessed=10**7, transcendentals=10**7),
    )(slots, back, keys, values, query_ids, key_ids)


def attend_back_kernel(slots_ref, back_ref, query_ref, key_ref, value_ref, lse_ref, query_ids, key_ids,
                       grouped_ref, key_grad_ref, value_grad_ref,
                       spread, gathered, bias, key_acc, value_acc, query_grad, head_grad):
    @pl.when(pl.program_id(0) == 0)
    def _():
        place_matrices(slots_ref, spread, gathered)
        mask_bias(query_ids, key_ids, bias)

    head_grad[...] = jnp.dot(gathered[...], back_ref[...], preferred_element_type=F32).astype(BF16)
    key_acc[...] = jnp.zeros_like(key_acc)
    value_acc[...] = jnp.zeros_like(value_acc)
    blocks, span, _ = bias.shape
    rows = query_ref.shape[0] // TOPK
    for block in range(blocks):
        queries = of_block(query_ref, block)
        grads = of_block(head_grad, block)
        place = pl.ds(block * Q_ROWS, span)
        keys, values = key_ref[place, :], value_ref[place, :]
        scores = lax.dot_general(keys, queries, (((1,), (1,)), ((), ())), preferred_element_type=F32)
        lse = lse_ref[0, :, pl.ds(block * TOPK * Q_ROWS, TOPK * Q_ROWS)]
        probs = jnp.exp2(scores * (SCALE * LOG2E) + bias[block] - lse)
        pulled = lax.dot_general(values, grads, (((1,), (1,)), ((), ())), preferred_element_type=F32)
        pulled = probs * pulled
        inner = jnp.sum(pulled, axis=0, keepdims=True)
        score_grad = (pulled - probs * inner).astype(BF16)
        value_acc[place, :] += jnp.dot(probs.astype(BF16), grads, preferred_element_type=F32)
        key_acc[place, :] += jnp.dot(score_grad, queries, preferred_element_type=F32)
        out = lax.dot_general(keys, score_grad, (((0,), (0,)), ((), ())), preferred_element_type=F32)
        out = (out * SCALE).T.astype(BF16)
        for k in range(TOPK):
            query_grad[pl.ds(k * rows + block * Q_ROWS, Q_ROWS), :] = out[k * Q_ROWS : (k + 1) * Q_ROWS]
    grouped_ref[...] = jnp.dot(spread[...], query_grad[...], preferred_element_type=F32).astype(BF16)
    key_grad_ref[...] = (key_acc[...] * SCALE).astype(BF16)
    value_grad_ref[...] = value_acc[...].astype(BF16)


def attend_back(slots, back, queries, keys, values, lse, query_ids, key_ids):
    choices, (count, width), span = slots.shape[1], back.shape, keys.shape[0]
    blocks = choices // TOPK // Q_ROWS
    head = lambda rows: pl.BlockSpec((rows, HD), lambda h: (0, h))
    whole = lambda a: pl.BlockSpec(a.shape, lambda h: (0, 0))
    return pl.pallas_call(
        attend_back_kernel,
        grid=(width // HD,),
        out_shape=[jax.ShapeDtypeStruct((count, width), BF16)] + [jax.ShapeDtypeStruct((span, width), BF16)] * 2,
        in_specs=[
            whole(slots), head(count), head(choices), head(span), head(span),
            pl.BlockSpec((1, 1, choices), lambda h: (h, 0, 0)), whole(query_ids), whole(key_ids),
        ],
        out_specs=[head(count), head(span), head(span)],
        scratch_shapes=[
            pltpu.VMEM((count, choices), BF16),
            pltpu.VMEM((choices, count), BF16),
            pltpu.VMEM((blocks, WINDOW + Q_ROWS, TOPK * Q_ROWS), F32),
            pltpu.VMEM((span, HD), F32),
            pltpu.VMEM((span, HD), F32),
            pltpu.VMEM((choices, HD), BF16),
            pltpu.VMEM((choices, HD), BF16),
        ],
        compiler_params=pltpu.CompilerParams(vmem_limit_bytes=56 * 2**20),
        cost_estimate=pl.CostEstimate(flops=30 * 10**9, bytes_accessed=10**7, transcendentals=10**7),
    )(slots, back, queries, keys, values, lse, query_ids, key_ids)


def per_device(
    tokens,
    segment_ids,
    attn_routes,
    ffn_routes,
    attn_gain,
    ffn_gain,
    routers,
    query_weight,
    output_weight,
    key_value_weight,
    gate_weight,
    up_weight,
    down_weight,
    cotangent,
):
    rows_here = tokens.shape[0]
    expert_count = lax.axis_size("expert")
    tensor_count = lax.axis_size("tensor")
    pieces = expert_count // EXPERTS
    column_count = D // tensor_count
    expert_index = lax.axis_index("expert")
    tensor_index = lax.axis_index("tensor")
    own = (expert_index // pieces).astype(F32)
    head_width = query_weight.shape[2]
    head_count = head_width // HD

    def cols(whole):
        return lax.dynamic_slice_in_dim(whole, tensor_index * column_count, column_count, whole.ndim - 1)

    def group_tokens(token_cols, places):
        return for_pieces(mm(places, token_cols).astype(BF16).reshape(EXPERTS, CAP, -1), pieces)

    def tokens_to_experts(token_cols, places):
        return columns_together(swap(group_tokens(token_cols, places)).reshape(-1, column_count))

    def group_choices(choice_rows, places):
        return to_pieces(mm(places, choice_rows).astype(BF16).reshape(EXPERTS, CAP, -1), pieces)

    def choices_of(back, places):
        return mm_tn(places, from_pieces(back, pieces).reshape(SLOTS, -1)).astype(BF16)

    def sums_from_experts(part_rows, places):
        back = swap(columns_summed(part_rows.astype(BF16)).reshape(expert_count, CAP, column_count))
        return sums_of(back, places)

    def sums_of(back, places):
        stride = back.shape[1]
        back = back.reshape(EXPERTS, pieces, stride, column_count)
        if pieces > 1:
            total = sum(mm_tn(places, back[:, p].reshape(EXPERTS * stride, -1)) for p in range(pieces))
        else:
            total = mm_tn(places, back.reshape(EXPERTS * stride, -1))
        return total

    def notes_of(*scalars):
        rows = jnp.stack([v.reshape(expert_count, CAP) for v in scalars], axis=1)
        return jnp.pad(rows, ((0, 0), (0, NOTES - len(scalars)), (0, column_count - CAP)))

    def read_notes(back, places, count):
        noted = back[:, CAP : CAP + count, :CAP].astype(F32)
        noted = noted.reshape(EXPERTS, pieces, count, CAP).sum(1).transpose(0, 2, 1).reshape(SLOTS, count)
        return mm_tn(places, noted.astype(BF16)).reshape(TOPK, rows_here, count)

    state_in = tokens.astype(F32)
    gain_one = attn_gain.astype(F32)
    gain_two = cols(ffn_gain.astype(F32))
    routers_one, routers_two = routers[:, :EXPERTS], routers[:, EXPERTS:]
    dy_cols = cols(cotangent)
    token_cols = cols(tokens).astype(F32)

    def by_token(choices):
        return choices[:, :rows_here] + choices[:, rows_here:]

    attn_slots, ffn_slots = slot_numbers(attn_routes), slot_numbers(ffn_routes)
    attn_places, ffn_places = place_matrix(attn_slots), place_matrix(ffn_slots)
    attn_tokens, ffn_tokens = by_token(attn_places), by_token(ffn_places)
    attn_noted = by_token(place_matrix(attn_slots, CAP + NOTES))
    ffn_noted = by_token(place_matrix(ffn_slots, CAP + NOTES))
    others = jnp.stack([
        mm(attn_places, attn_routes[:, ::-1].T.reshape(-1, 1).astype(BF16)),
        mm(ffn_places, ffn_routes[:, ::-1].T.reshape(-1, 1).astype(BF16)),
    ]).reshape(2, EXPERTS, CAP).transpose(1, 0, 2)


    rows_one, query_rows, query_map, window, pair_map, keys, values = front(
        tokens, gain_one[None], attn_slots[None], to_pieces(query_weight, pieces), key_value_weight, collective_id=0)
    output_weight, others, rows_one = lax.optimization_barrier((output_weight, others, rows_one))
    rows_one = rows_one.reshape(-1, D)
    output_map = swap(to_pieces(output_weight, pieces)).reshape(D, -1)
    others = swap(for_pieces(others, pieces)).transpose(1, 0, 2).reshape(2, -1)
    normed_one = window[2]
    window = window.reshape(-1, D)
    padded_segments = jnp.concatenate([jnp.full((WINDOW,), -1, jnp.int32), segment_ids])
    key_ids = lax.dynamic_slice_in_dim(padded_segments, expert_index * rows_here, WINDOW + rows_here)
    query_ids = key_ids[None, WINDOW:]
    key_ids = key_ids[:, None]
    heads, queries, log_total = attend(
        attn_slots[None], from_pieces(query_rows, pieces).reshape(SLOTS, -1), keys, values, query_ids, key_ids)
    attn_gate_rows = own_gate(mm(rows_one, routers_one), own, others[0])
    attn_gate_blocks = attn_gate_rows.reshape(expert_count, CAP, 1)
    attn_back, heads_rows = scatter_rows(
        to_pieces(heads.reshape(EXPERTS, CAP, -1), pieces), output_map, attn_gate_blocks, collective_id=1)
    heads_rows = heads_rows.reshape(expert_count * CAP, -1)
    dy_cols, attn_back = lax.optimization_barrier((dy_cols, attn_back))
    state = token_cols + sums_of(attn_back, attn_tokens)

    mean_two = lax.psum(jnp.sum(state * state, axis=1, keepdims=True), "tensor") / D
    rate_two = lax.rsqrt(mean_two + eps)
    normed_two = (state * rate_two * gain_two).astype(BF16)
    rows_dy = tokens_to_experts(dy_cols, ffn_tokens)
    (rows_two,) = gather_rows(group_tokens(normed_two, ffn_tokens), collective_id=2)
    rows_two = rows_two.reshape(-1, D)
    gate_map, up_map, down_map = gate_weight[0], up_weight[0], down_weight[0]
    ffn_gate_rows = own_gate(mm(rows_two, routers_two), own, others[1])
    hidden_grad = mm_nt(rows_dy, down_map)
    gate_pre = mm(rows_two, gate_map)
    up_pre = mm(rows_two, up_map)
    sigma = 1.0 / (1.0 + jnp.exp(-gate_pre))
    silu = gate_pre * sigma
    hidden = (silu * up_pre).astype(BF16)
    scaled_grad = hidden_grad * ffn_gate_rows
    gate_low = (scaled_grad * up_pre * (sigma * (1.0 + gate_pre * (1.0 - sigma)))).astype(BF16)
    up_low = (scaled_grad * silu).astype(BF16)
    ffn_notes = notes_of(
        jnp.sum(hidden.astype(F32) * hidden_grad, axis=1), ffn_gate_rows[:, 0] / (tensor_count * pieces))
    (rows_back,) = scatter_rows(
        products=[(gate_low.reshape(expert_count, CAP, -1), gate_map), (up_low.reshape(expert_count, CAP, -1), up_map)],
        notes=ffn_notes, near=False, collective_id=3)
    normed_two_grad = sums_of(rows_back, ffn_noted)
    noted = read_notes(rows_back, ffn_places, 2)
    ffn_pull, ffn_gates = noted[:, :, 0].T, noted[:, :, 1].T
    ffn_logit_grad = gate_back(ffn_gates, ffn_pull, ffn_routes)
    normed_two_grad = normed_two_grad + mm_nt(
        ffn_logit_grad, lax.dynamic_slice_in_dim(routers_two, tensor_index * column_count, column_count, 0))
    ffn_router_cols = mm_tn(normed_two, ffn_logit_grad)
    ffn_gain_cols = jnp.sum(normed_two_grad * state * rate_two, axis=0)
    ahead = normed_two_grad * gain_two
    centre = lax.psum(jnp.sum(ahead * state, axis=1, keepdims=True), "tensor") / D
    state_grad = dy_cols.astype(F32) + rate_two * ahead - state * rate_two * rate_two * rate_two * centre

    rows_state, heads_grad, heads_grad_rows = gather_rows(
        group_tokens(state_grad.astype(BF16), attn_tokens), output_map, gate=attn_gate_blocks, collective_id=4)
    rows_state = rows_state.reshape(-1, D)
    heads_grad_rows = heads_grad_rows.reshape(expert_count * CAP, -1)
    attn_notes = notes_of(jnp.sum(heads_grad_rows.astype(F32) * heads_rows.astype(F32), axis=1))
    output_part = mm_tn((rows_state.astype(F32) * attn_gate_rows).astype(BF16), heads_rows).astype(BF16)
    heads_grad, output_part = lax.optimization_barrier((heads_grad, output_part))

    query_back, key_back, value_back = attend_back(
        attn_slots[None], from_pieces(heads_grad, pieces).reshape(SLOTS, -1), queries, keys, values, log_total,
        query_ids, key_ids)
    output_grad = swap(output_part.reshape(expert_count, D // expert_count, -1))
    query_back, output_grad = lax.optimization_barrier((query_back, output_grad))
    output_grad = from_pieces(output_grad, pieces).astype(F32)
    normed_back, query_grad_rows, owed = scatter_rows(
        to_pieces(query_back.reshape(EXPERTS, CAP, -1), pieces), query_map, notes=attn_notes,
        windows=[key_back, value_back, pair_map], collective_id=5)
    query_grad_rows = query_grad_rows.reshape(expert_count * CAP, -1)
    query_part = mm_tn(rows_one, query_grad_rows)
    normed_grad = sums_of(normed_back, attn_noted) + jnp.sum(owed.astype(F32), axis=0)
    attn_pull = read_notes(normed_back, attn_places, 1)[:, :, 0].T
    pair_grad = jnp.stack([key_back, value_back])
    pair_part = jnp.einsum("td,ctf->cdf", window, pair_grad, preferred_element_type=F32)
    attn_gates = pick_gates(mm(normed_one, routers_one), attn_routes)
    attn_logit_grad = gate_back(attn_gates, attn_pull, attn_routes)
    normed_grad = normed_grad + mm_nt(
        attn_logit_grad, lax.dynamic_slice_in_dim(routers_one, tensor_index * column_count, column_count, 0))
    attn_router_cols = mm_tn(cols(normed_one), attn_logit_grad)
    rate_one = lax.rsqrt(jnp.mean(state_in * state_in, axis=1, keepdims=True) + eps)
    attn_gain_cols = jnp.sum(normed_grad * token_cols * rate_one, axis=0)
    ahead_one = normed_grad * cols(gain_one)
    centre_one = lax.psum(jnp.sum(ahead_one * token_cols, axis=1, keepdims=True), "tensor") / D
    tokens_grad = state_grad + rate_one * ahead_one - token_cols * rate_one * rate_one * rate_one * centre_one
    tokens_grad = columns_together(tokens_grad.astype(BF16)).astype(F32)

    def from_maps(part):
        got = swap(part.astype(BF16).reshape(expert_count, D // expert_count, -1))
        return from_pieces(got, pieces).astype(F32)

    query_grad = from_maps(query_part)
    key_value_grad = lax.psum_scatter(
        pair_part.astype(BF16), "expert", scatter_dimension=1, tiled=True).astype(F32)
    small = jnp.concatenate(
        [attn_router_cols, ffn_router_cols, attn_gain_cols[:, None], ffn_gain_cols[:, None]], axis=1)
    small = lax.all_gather(small, "tensor", axis=0, tiled=True)
    small = lax.psum_scatter(small, "expert", scatter_dimension=0, tiled=True)

    scaled_dy = (rows_dy.astype(F32) * ffn_gate_rows).astype(BF16)
    gate_grad = mm_tn(rows_two, gate_low)
    up_grad = mm_tn(rows_two, up_low)
    down_grad = mm_tn(hidden, scaled_dy)
    ffn_back = sums_from_experts(mm(hidden, down_map) * ffn_gate_rows, ffn_tokens)
    mixed = (state + ffn_back).astype(BF16)
    return (
        mixed,
        tokens_grad,
        small[:, 2 * EXPERTS],
        small[:, 2 * EXPERTS + 1],
        small[:, : 2 * EXPERTS],
        query_grad,
        output_grad,
        key_value_grad,
        gate_grad[None],
        up_grad[None],
        down_grad[None],
    )


def solution(mesh):
    in_specs = (
        P("expert", None),
        P(),
        P("expert", None),
        P("expert", None),
        P(),
        P(),
        P(),
        P(None, "expert", "tensor"),
        P(None, "expert", "tensor"),
        P(None, "expert", "tensor"),
        P("expert", None, "tensor"),
        P("expert", None, "tensor"),
        P("expert", "tensor", None),
        P("expert", None),
    )
    out_specs = (
        P("expert", "tensor"),
        P("expert", None),
        P("expert"),
        P("expert"),
        P("expert", None),
        P(None, "expert", "tensor"),
        P(None, "expert", "tensor"),
        P(None, "expert", "tensor"),
        P("expert", None, "tensor"),
        P("expert", None, "tensor"),
        P("expert", "tensor", None),
    )
    return jax.shard_map(
        per_device, mesh=mesh, in_specs=in_specs, out_specs=out_specs, check_vma=False
    )
```

```python
import functools
import math

import jax
import jax.numpy as jnp
from jax import lax
from jax.experimental import pallas as pl
from jax.experimental.pallas import tpu as pltpu
from jax.sharding import PartitionSpec as P

D = 2048
HD = 128
EXPERTS = 8
TOPK = 2
WINDOW = 1024
CAP = 160
SLOTS = EXPERTS * CAP

eps = 1e-06
masked_value = -1e30
SCALE = HD ** (-0.5)
LOG2E = math.log2(math.e)
Q_ROWS = 256
NOTES = 16
WINDOW_ORDER = (1, 0, 2)
F32 = jnp.float32
BF16 = jnp.bfloat16
MESH = pl.DeviceIdType.MESH
VMEM = pl.BlockSpec(memory_space=pltpu.VMEM)
ANY = pl.BlockSpec(memory_space=pl.ANY)


def remote(src, dst, send, recv, **device):
    return pltpu.make_async_remote_copy(
        src_ref=src, dst_ref=dst, send_sem=send, recv_sem=recv, device_id=device, device_id_type=MESH)


def meet(experts, bits):
    e, t = lax.axis_index("expert"), lax.axis_index("tensor")
    barrier = pltpu.get_barrier_semaphore()

    @pl.loop(1, experts)
    def _(s):
        pl.semaphore_signal(barrier, inc=1, device_id={"expert": e ^ s}, device_id_type=MESH)

    for b in range(bits):
        pl.semaphore_signal(barrier, inc=1, device_id={"tensor": t ^ (1 << b)}, device_id_type=MESH)
    pl.semaphore_wait(barrier, experts - 1 + bits)


def partners(e, experts, near):
    if near:
        return lambda s: e ^ s
    return lambda s: e ^ ((experts - s) & (experts - 1))


def low_bit(d):
    return (d & -d).bit_length() - 1


def gather_kernel(experts, bits, near, multiply, scale, *refs):
    refs = list(refs)
    x = refs.pop(0)
    w = refs.pop(0) if multiply else None
    gate = refs.pop(0) if scale else None
    rows = refs.pop(0)
    back = refs.pop(0) if multiply else None
    product = refs.pop(0) if scale else None
    y = refs.pop(0) if multiply else None
    z_send, z_recv, t_send, t_recv = refs[:4]
    refs = refs[4:]
    if multiply:
        y_send, y_recv = refs[:2]
    e, t = lax.axis_index("expert"), lax.axis_index("tensor")
    partner = partners(e, experts, near)
    width = x.shape[2]
    tensor = 1 << bits

    def cols(d):
        return pl.ds(pl.multiple_of((t ^ d) * width, 128), width)

    def arrive(j):
        return remote(x.at[j], rows.at[e, :, cols(0)], z_send.at[j], z_recv.at[e], expert=j)

    def arrived(j):
        return remote(x.at[j], rows.at[j, :, cols(0)], z_send.at[j], z_recv.at[j], expert=j)

    def pass_on(j, d, b):
        place = rows.at[j, :, cols(d)]
        far = d | (1 << b)
        return remote(place, place, t_send.at[j, far], t_recv.at[j, far], tensor=t ^ (1 << b))

    def passed(j, d):
        place = rows.at[j, :, cols(d)]
        return remote(place, place, t_send.at[j, d], t_recv.at[j, d], tensor=t ^ (1 << low_bit(d)))

    def hand_back(j):
        return remote(y.at[j], back.at[e], y_send.at[j], y_recv.at[e], expert=j)

    def handed(j):
        return remote(y.at[j], back.at[j], y_send.at[j], y_recv.at[j], expert=j)

    meet(experts, bits)

    @pl.loop(1, experts)
    def _(s):
        arrive(partner(s)).start()

    rows[e, :, cols(0)] = x[e]

    @pl.loop(0, experts + bits)
    def _(i):
        @pl.when(i < experts)
        def _():
            j = partner(i)

            @pl.when(i > 0)
            def _():
                arrived(j).wait_recv()

            for b in reversed(range(bits)):
                pass_on(j, 0, b).start()

        for k in range(1, bits + 1):
            @pl.when((i >= k) & (i < experts + k))
            def _():
                m = i - k
                j = partner(m)
                bit = bits - k
                for d in range(1, tensor):
                    if low_bit(d) == bit:
                        passed(j, d).wait_recv()
                        for b in reversed(range(bit)):
                            pass_on(j, d, b).start()
                if k == bits and multiply:
                    out = jnp.dot(rows[j], w[...], preferred_element_type=F32)
                    if scale:
                        product[j] = out.astype(BF16)
                        out = out * gate[j]
                    y[j] = out.astype(BF16)

                    @pl.when(m == 0)
                    def _():
                        back[e] = y[e]

                    @pl.when(m > 0)
                    def _():
                        hand_back(j).start()

    @pl.loop(1, experts)
    def _(s):
        j = partner(s)
        arrived(j).wait_send()
        if multiply:
            handed(j).wait_recv()
            handed(j).wait_send()

    @pl.loop(0, experts)
    def _(j):
        for d in range(1, tensor):
            passed(j, d).wait_send()


def gather_rows(x, w=None, gate=None, near=True, collective_id=0):
    experts, tensor = lax.axis_size("expert"), lax.axis_size("tensor")
    bits = tensor.bit_length() - 1
    cap, width = x.shape[1], x.shape[2]
    multiply = w is not None
    f = w.shape[-1] if multiply else 0
    ins, specs = [x], [VMEM]
    outs = [jax.ShapeDtypeStruct((experts, cap, width * tensor), BF16)]
    scratch = []
    if multiply:
        ins.append(w)
        specs.append(VMEM)
        outs.append(jax.ShapeDtypeStruct((experts, cap, f), BF16))
    if gate is not None:
        ins.append(gate)
        specs.append(VMEM)
        outs.append(jax.ShapeDtypeStruct((experts, cap, f), BF16))
    if multiply:
        scratch.append(pltpu.VMEM((experts, cap, f), BF16))
    scratch += [pltpu.SemaphoreType.DMA((experts,))] * 2 + [pltpu.SemaphoreType.DMA((experts, tensor))] * 2
    if multiply:
        scratch += [pltpu.SemaphoreType.DMA((experts,))] * 2
    return pl.pallas_call(
        functools.partial(gather_kernel, experts, bits, near, multiply, gate is not None),
        out_shape=outs,
        in_specs=specs,
        out_specs=[VMEM] * len(outs),
        scratch_shapes=scratch,
        compiler_params=pltpu.CompilerParams(
            collective_id=collective_id, has_side_effects=True, vmem_limit_bytes=48 * 2**20),
        cost_estimate=pl.CostEstimate(flops=10**11, bytes_accessed=10**7, transcendentals=0),
    )(*ins)


def front_kernel(experts, bits, *refs):
    (tokens, gain, slots, wide, routes, routers, w_in, kv_in,
     rows, back, w, window, kv, keys, values, gates, rivals, x, y, facts, facts_in,
     f_send, f_recv, z_send, z_recv, t_send, t_recv, y_send, y_recv, w_send, w_recv, k_send, k_recv, n_send, n_recv, own_sem) = refs
    e, t = lax.axis_index("expert"), lax.axis_index("tensor")
    partner = partners(e, experts, True)
    width = x.shape[1]
    cap = rows.shape[1]
    here = tokens.shape[0]
    tensor = 1 << bits
    expert_bits = experts.bit_length() - 1
    pieces = experts * cap // x.shape[0]

    def x_part(j):
        return pl.ds(pl.multiple_of((j // pieces) * cap, cap), cap)

    def cols(d):
        return pl.ds(pl.multiple_of((t ^ d) * width, 128), width)

    def part(j):
        return pl.ds(j * (w.shape[0] // experts), w.shape[0] // experts)

    def block(q, d):
        if isinstance(q, int):
            return window.at[q - experts, :, cols(d)]
        return rows.at[q, :, cols(d)]

    def pass_on(q, d, b):
        far = d | (1 << b)
        return remote(block(q, d), block(q, d), t_send.at[q, far], t_recv.at[q, far], tensor=t ^ (1 << b))

    def passed(q, d):
        return remote(block(q, d), block(q, d), t_send.at[q, d], t_recv.at[q, d], tensor=t ^ (1 << low_bit(d)))

    def stage(q, k):
        bit = bits - k
        for d in range(1, tensor):
            if low_bit(d) == bit:
                passed(q, d).wait_recv()
                for b in reversed(range(bit)):
                    pass_on(q, d, b).start()

    def arrived(j):
        return remote(x.at[x_part(j)], rows.at[j, :, cols(0)], z_send.at[j], z_recv.at[j], expert=j)

    def handed(j):
        return remote(y.at[j], back.at[j], y_send.at[j], y_recv.at[j], expert=j)

    def chunk(d):
        return kv.at[:, part(e ^ d), :]

    def pass_chunk(d, b):
        far = d | (1 << b)
        return remote(chunk(d), chunk(d), k_send.at[far], k_recv.at[far], expert=e ^ (1 << b))

    def passed_chunk(d):
        return remote(chunk(d), chunk(d), k_send.at[d], k_recv.at[d], expert=e ^ (1 << low_bit(d)))

    def chunks(bit):
        for d in range(1, experts):
            if low_bit(d) == bit:
                passed_chunk(d).wait_recv()
                for b in reversed(range(bit)):
                    pass_chunk(d, b).start()

    def two_on(way):
        return remote(window.at[2, :, cols(0)], window.at[0, :, cols(0)], n_send.at[0], n_recv.at[0],
                      expert=lax.rem(e + experts + 2 * way, experts))

    def across():
        return remote(window.at[2 - 2 * (e & 1), :, cols(0)], window.at[1, :, cols(0)], n_send.at[1], n_recv.at[1],
                      expert=e ^ 1)

    own_kv = pltpu.make_async_copy(kv_in, chunk(0), own_sem.at[0])
    own_w = pltpu.make_async_copy(w_in.at[e], w.at[part(e)], own_sem.at[1])
    own_kv.start()
    own_w.start()
    meet(experts, bits)
    for b in reversed(range(expert_bits)):
        remote(kv_in, chunk(0), k_send.at[1 << b], k_recv.at[1 << b], expert=e ^ (1 << b)).start()

    state = tokens[...].astype(F32)
    rate = lax.rsqrt(jnp.mean(state * state, axis=1, keepdims=True) + eps)
    window[2] = (state * rate * gain[...]).astype(BF16)
    two_on(1).start()
    place = lax.broadcasted_iota(jnp.int32, (x.shape[0], here), 0)
    chosen = (place == slots[:, pl.ds(0, here)]) | (place == slots[:, pl.ds(here, here)])
    x[...] = jnp.dot(chosen.astype(F32).astype(BF16), window[2, :, cols(0)], preferred_element_type=F32).astype(BF16)

    @pl.loop(1, experts)
    def _(s):
        j = partner(s)
        remote(x.at[x_part(j)], rows.at[e, :, cols(0)], z_send.at[j], z_recv.at[e], expert=j).start()

    @pl.loop(1, experts)
    def _(s):
        j = partner(s)
        remote(w_in.at[j], w.at[part(e)], w_send.at[j], w_recv.at[e], expert=j).start()

    rows[e, :, cols(0)] = x[x_part(e), :]

    logits = jnp.dot(window[2], routers[...], preferred_element_type=F32)
    lane = lax.broadcasted_iota(jnp.int32, logits.shape, 1)
    first, second = (jnp.sum(jnp.where(lane == routes[:, k : k + 1], logits, 0.0), axis=1, keepdims=True) for k in (0, 1))
    top = jnp.maximum(first, second)
    first, second = jnp.exp(first - top), jnp.exp(second - top)
    gate = jnp.concatenate([first, second], axis=0) / jnp.concatenate([first + second] * 2, axis=0)
    other = jnp.concatenate([routes[:, 3:4], routes[:, 2:3]], axis=0).astype(F32)
    high = gate.astype(BF16).astype(F32)
    middle = (gate - high).astype(BF16).astype(F32)
    lane = lax.broadcasted_iota(jnp.int32, (2 * here, 128), 1)
    table = jnp.where(lane == 0, high, jnp.where(lane == 1, middle, jnp.where(lane == 2, gate - high - middle, 0.0)))
    fact = []
    for k, values_of in enumerate((table, jnp.where(lane == 0, other, 0.0))):
        spot = lax.broadcasted_iota(jnp.int32, (2 * here, EXPERTS * 256), 1) == wide[:, k : k + 1]
        fact.append(jnp.dot(values_of.T[:16].astype(BF16), spot.astype(F32).astype(BF16), preferred_element_type=F32))
    gate_row = fact[0][0:1] + fact[0][1:2] + fact[0][2:3]
    row = lax.broadcasted_iota(jnp.int32, (8, EXPERTS * 256), 0)
    fact = jnp.where(row == 0, gate_row, jnp.where(row == 1, fact[1][0:1], 0.0))
    for q in range(EXPERTS):
        facts[q] = fact[:, q * 256 : (q + 1) * 256]

    @pl.loop(1, experts)
    def _(s):
        j = partner(s)
        remote(facts.at[j // pieces], facts_in.at[e], f_send.at[j], f_recv.at[e], expert=j).start()

    facts_in[e] = facts[e // pieces]
    chunks(expert_bits - 1)

    @pl.loop(0, experts + bits)
    def _(i):
        @pl.when(i < experts)
        def _():
            j = partner(i)

            @pl.when(i > 0)
            def _():
                arrived(j).wait_recv()

            for b in reversed(range(bits)):
                pass_on(j, 0, b).start()

        for k in range(1, bits + 1):
            @pl.when((i >= k) & (i < experts + k))
            def _():
                stage(partner(i - k), k)

        @pl.when(i == experts // 2)
        def _():
            two_on(-1).wait_recv()
            across().start()
            for b in reversed(range(bits)):
                pass_on(experts, 0, b).start()

    for bit in reversed(range(1, expert_bits - 1)):
        chunks(bit)
    across().wait_recv()
    for b in reversed(range(bits)):
        pass_on(experts + 1, 0, b).start()
    own_w.wait()

    @pl.loop(1, experts)
    def _(s):
        q = partner(s)
        remote(w_in.at[q], w.at[part(q)], w_send.at[q], w_recv.at[q], expert=q).wait_recv()

    @pl.loop(0, experts)
    def _(i):
        j = partner(lax.rem(i + 1, experts))
        y[j] = jnp.dot(rows[j], w[...], preferred_element_type=F32).astype(BF16)

        @pl.when(i < experts - 1)
        def _():
            remote(y.at[j], back.at[e], y_send.at[j], y_recv.at[e], expert=j).start()

    back[e] = y[e]
    for k in range(1, bits + 1):
        for q in range(2):
            stage(experts + q, k)
    chunks(0)
    own_kv.wait()
    for q in range(3):
        for c, out in enumerate((keys, values)):
            out[pl.ds(q * here, here), :] = jnp.dot(window[q], kv[c], preferred_element_type=F32).astype(BF16)

    @pl.loop(1, experts)
    def _(s):
        j = partner(s)
        fact_from = remote(facts.at[j // pieces], facts_in.at[j], f_send.at[j], f_recv.at[j], expert=j)
        fact_from.wait_recv()
        fact_from.wait_send()

    @pl.loop(0, experts)
    def _(j):
        column = jnp.concatenate([facts_in[j], jnp.zeros((120, 256), F32)], axis=0).T[:cap]
        gates[j] = column[:, 0:1]
        rivals[j] = column[:, 1:2]

    @pl.loop(1, experts)
    def _(s):
        j = partner(s)
        arrived(j).wait_send()
        handed(j).wait_recv()
        handed(j).wait_send()
        remote(w_in.at[j], w.at[part(j)], w_send.at[j], w_recv.at[j], expert=j).wait_send()

    for d in range(1, experts):
        passed_chunk(d).wait_send()
    two_on(1).wait_send()
    across().wait_send()
    for q in range(2):
        for d in range(1, tensor):
            passed(experts + q, d).wait_send()

    @pl.loop(0, experts)
    def _(j):
        for d in range(1, tensor):
            passed(j, d).wait_send()


def front(tokens, gain, slots, wide, routes, routers, w, kv, collective_id):
    experts, tensor = lax.axis_size("expert"), lax.axis_size("tensor")
    bits = tensor.bit_length() - 1
    here = tokens.shape[0]
    f, f_kv = w.shape[2], kv.shape[2]
    dma = pltpu.SemaphoreType.DMA
    return pl.pallas_call(
        functools.partial(front_kernel, experts, bits),
        out_shape=[
            jax.ShapeDtypeStruct((experts, CAP, D), BF16),
            jax.ShapeDtypeStruct((experts, CAP, f), BF16),
            jax.ShapeDtypeStruct((D, f), BF16),
            jax.ShapeDtypeStruct((3, here, D), BF16),
            jax.ShapeDtypeStruct((2, D, f_kv), BF16),
            jax.ShapeDtypeStruct((3 * here, f_kv), BF16),
            jax.ShapeDtypeStruct((3 * here, f_kv), BF16),
            jax.ShapeDtypeStruct((experts, CAP, 1), F32),
            jax.ShapeDtypeStruct((experts, CAP, 1), F32),
        ],
        in_specs=[VMEM] * 6 + [ANY, ANY],
        out_specs=[VMEM] * 9,
        scratch_shapes=[
            pltpu.VMEM((SLOTS, D // tensor), BF16),
            pltpu.VMEM((experts, CAP, f), BF16),
            pltpu.VMEM((EXPERTS, 8, 256), F32),
            pltpu.VMEM((experts, 8, 256), F32),
        ] + [dma((experts,))] * 2 + [dma((experts,))] * 2 + [dma((experts + 2, tensor))] * 2 + [dma((experts,))] * 6
        + [dma((2,))] * 3,
        compiler_params=pltpu.CompilerParams(
            collective_id=collective_id, has_side_effects=True, vmem_limit_bytes=56 * 2**20),
        cost_estimate=pl.CostEstimate(flops=10**11, bytes_accessed=10**7, transcendentals=0),
    )(tokens, gain, slots, wide, routes, routers, w, kv)


def scatter_kernel(experts, bits, depth, near, scale, noted, *refs):
    refs = list(refs)
    h_in, w = refs[:2]
    refs = refs[2:]
    gate = refs.pop(0) if scale else None
    notes = refs.pop(0) if noted else None
    if depth:
        key_grad, value_grad, kv, rows, pair_part = refs[:5]
        refs = refs[5:]
    back, h = refs[:2]
    refs = refs[2:]
    if depth:
        owed, map_grad, pair_came = refs[:3]
        refs = refs[3:]
    keep, sent, got, y, t_send, t_recv, y_send, y_recv, h_send, h_recv = refs[:10]
    if depth:
        n_keep, n_sent, n_got, n_y, n_in, part_grad, n_send, n_recv, o_send, o_recv, g_send, g_recv, p_sem = refs[10:]
    e, t = lax.axis_index("expert"), lax.axis_index("tensor")
    partner = partners(e, experts, near)
    tensor = 1 << bits
    cap, width = h.shape[1], y.shape[2]
    body = pl.ds(0, cap)
    foot = pl.ds(cap, NOTES)

    def slice_at(d):
        return pl.ds(pl.multiple_of((t ^ d) * width, 128), width)

    def handed(j):
        return remote(y.at[j], back.at[j], y_send.at[j], y_recv.at[j], expert=j)

    def give(j, d):
        return remote(sent.at[j, d - 1], got.at[j, d - 1], t_send.at[j, d], t_recv.at[j, d], tensor=t ^ (1 << low_bit(d)))

    def owe(q, d):
        return remote(n_sent.at[q, d - 1], n_got.at[q, d - 1], n_send.at[q, d], n_recv.at[q, d],
                      tensor=t ^ (1 << low_bit(d)))

    def grad_to(j):
        return remote(part_grad.at[j], map_grad.at[e], g_send.at[j], g_recv.at[e], expert=j)

    def grad_from(j):
        return remote(part_grad.at[j], map_grad.at[j], g_send.at[j], g_recv.at[j], expert=j)

    def across():
        return remote(n_y.at[1], n_in, o_send.at[1], o_recv.at[1], expert=e ^ 1)

    def two_back(way):
        return remote(n_y.at[0], owed.at[1], o_send.at[0], o_recv.at[0],
                      expert=lax.rem(e + experts - 2 * way, experts))

    def window_stage(k):
        for q in WINDOW_ORDER:
            for d in range(tensor - 1, -1, -1):
                if d % (1 << k) == 0:
                    came = d | (1 << (k - 1))
                    owe(q, came).wait_recv()
                    total = n_keep[q, d // 2] + n_got[q, came - 1].astype(F32)
                    if k == bits:
                        if q == 1:
                            n_y[1] = total.astype(BF16)
                            across().start()
                        else:
                            n_keep[q, 0] = total
                    elif d & (1 << k):
                        n_sent[q, d - 1] = total.astype(BF16)
                        owe(q, d).start()
                    else:
                        n_keep[q, d // 2] = total

    def pair_half():
        half = pair_part.shape[0] // 2
        return remote(pair_part.at[pl.ds(half, half)], pair_came, p_sem.at[0], p_sem.at[1], expert=e ^ 1)

    def row_from(j):
        return remote(h_in.at[j], h.at[j], h_send.at[j], h_recv.at[j], expert=j)

    meet(experts, bits)

    @pl.loop(1, experts)
    def _(s):
        j = partner(s)
        remote(h_in.at[j], h.at[e], h_send.at[j], h_recv.at[e], expert=j).start()

    h[e] = h_in[e]
    if depth:
        pair_half().start()
        here = key_grad.shape[0] // 3
        for q in WINDOW_ORDER:
            place = pl.ds(q * here, here)
            for d in range(tensor - 1, -1, -1):
                part = lax.dot_general(
                    key_grad[place, :], kv[0, slice_at(d), :], (((1,), (1,)), ((), ())), preferred_element_type=F32)
                part += lax.dot_general(
                    value_grad[place, :], kv[1, slice_at(d), :], (((1,), (1,)), ((), ())), preferred_element_type=F32)
                if d & 1:
                    n_sent[q, d - 1] = part.astype(BF16)
                    owe(q, d).start()
                else:
                    n_keep[q, d // 2] = part
        window_stage(1)

        @pl.loop(1, experts)
        def _(s):
            row_from(partner(s)).wait_recv()

        @pl.loop(0, experts)
        def _(i):
            j = partner(lax.rem(i + 1, experts))
            share = part_grad.shape[1]
            some = rows[:, pl.ds(pl.multiple_of(j * share, share), share)]
            part_grad[j] = lax.dot_general(
                some, h[...].reshape(experts * cap, h.shape[2]), (((0,), (0,)), ((), ())),
                preferred_element_type=F32).astype(BF16)

            @pl.when(i < experts - 1)
            def _():
                grad_to(j).start()

        map_grad[e] = part_grad[e]

    @pl.loop(0, experts + bits)
    def _(i):
        @pl.when(i < experts)
        def _():
            j = partner(i)
            slot = lax.rem(i, bits + 1)
            if not depth:
                @pl.when(i > 0)
                def _():
                    row_from(j).wait_recv()
            for d in range(tensor - 1, -1, -1):
                part = lax.dot_general(
                    h[j], w[slice_at(d), :], (((1,), (1,)), ((), ())), preferred_element_type=F32)
                if scale:
                    part = part * gate[j]
                if d & 1:
                    sent[j, d - 1, body, :] = part.astype(BF16)
                    if noted:
                        sent[j, d - 1, foot, :] = notes[j].astype(BF16)
                    give(j, d).start()
                else:
                    keep[slot, d // 2, body, :] = part
                    if noted:
                        keep[slot, d // 2, foot, :] = notes[j]

        for k in range(1, bits + 1):
            @pl.when((i >= k) & (i < experts + k))
            def _():
                m = i - k
                slot = lax.rem(m, bits + 1)
                j = partner(m)
                for d in range(tensor - 1, -1, -1):
                    if d % (1 << k) == 0:
                        came = d | (1 << (k - 1))
                        give(j, came).wait_recv()
                        total = keep[slot, d // 2] + got[j, came - 1].astype(F32)
                        if k == bits:
                            y[j] = total.astype(BF16)
                        elif d & (1 << k):
                            sent[j, d - 1] = total.astype(BF16)
                            give(j, d).start()
                        else:
                            keep[slot, d // 2] = total
                if k == bits:
                    @pl.when(m == 0)
                    def _():
                        back[e] = y[e]

                    @pl.when(m > 0)
                    def _():
                        remote(y.at[j], back.at[e], y_send.at[j], y_recv.at[e], expert=j).start()

        if depth:
            for k in range(2, bits + 1):
                @pl.when(i == 2 * (k - 1))
                def _():
                    window_stage(k)

            @pl.when(i == 2 * bits)
            def _():
                across().wait_recv()
                passing = (e & 1).astype(F32)
                came = n_in[...].astype(F32)
                n_y[0] = (n_keep[0, 0] + passing * came).astype(BF16)
                owed[0] = (n_keep[2, 0] + (1.0 - passing) * came).astype(BF16)
                two_back(1).start()

    @pl.loop(1, experts)
    def _(s):
        j = partner(s)
        row_from(j).wait_send()
        handed(j).wait_recv()
        handed(j).wait_send()
        if depth:
            grad_from(j).wait_recv()
            grad_from(j).wait_send()

    @pl.loop(0, experts)
    def _(j):
        for d in range(1, tensor):
            give(j, d).wait_send()

    if depth:
        for q in range(3):
            for d in range(1, tensor):
                owe(q, d).wait_send()
        pair_half().wait_recv()
        pair_half().wait_send()
        across().wait_send()
        two_back(-1).wait_recv()
        two_back(1).wait_send()


def scatter_rows(h, w, gate=None, notes=None, windows=None, near=True, collective_id=0):
    experts, tensor = lax.axis_size("expert"), lax.axis_size("tensor")
    bits = tensor.bit_length() - 1
    high = CAP + (NOTES if notes is not None else 0)
    width, f = D // tensor, w.shape[1]
    dma = pltpu.SemaphoreType.DMA
    ins = [a for a in (h, w, gate, notes) if a is not None]
    outs = [jax.ShapeDtypeStruct((experts, high, width), BF16), jax.ShapeDtypeStruct(h.shape, BF16)]
    scratch = [
        pltpu.VMEM((bits + 1, tensor // 2, high, width), F32),
        pltpu.VMEM((experts, tensor - 1, high, width), BF16),
        pltpu.VMEM((experts, tensor - 1, high, width), BF16),
        pltpu.VMEM((experts, high, width), BF16),
    ] + [dma((experts, tensor))] * 2 + [dma((experts,))] * 4
    if windows is not None:
        ins += windows
        here = windows[0].shape[0] // 3
        outs.append(jax.ShapeDtypeStruct((2, here, width), BF16))
        outs.append(jax.ShapeDtypeStruct((experts, D // experts, f), BF16))
        outs.append(jax.ShapeDtypeStruct((windows[4].shape[0] // 2, windows[4].shape[1]), BF16))
        scratch += [
            pltpu.VMEM((3, tensor // 2, here, width), F32),
            pltpu.VMEM((3, tensor - 1, here, width), BF16),
            pltpu.VMEM((3, tensor - 1, here, width), BF16),
            pltpu.VMEM((2, here, width), BF16),
            pltpu.VMEM((here, width), BF16),
            pltpu.VMEM((experts, D // experts, f), BF16),
        ] + [dma((3, tensor))] * 2 + [dma((2,))] * 2 + [dma((experts,))] * 2 + [dma((2,))]
    return pl.pallas_call(
        functools.partial(scatter_kernel, experts, bits, windows is not None, near, gate is not None, notes is not None),
        out_shape=outs,
        in_specs=[VMEM] * (len(ins) - 1) + [VMEM if windows is None else ANY],
        out_specs=[VMEM] * (len(outs) - 1) + [VMEM if windows is None else ANY],
        scratch_shapes=scratch,
        compiler_params=pltpu.CompilerParams(
            collective_id=collective_id, has_side_effects=True, vmem_limit_bytes=63 * 2**20),
        cost_estimate=pl.CostEstimate(flops=10**11, bytes_accessed=10**7, transcendentals=0),
    )(*ins)


def ffn_kernel(experts, bits, pieces, *refs):
    (x_cols, dy_cols, slots, others, routers, gate_in, up_in, down_in,
     back, rows_out, dys_out, hidden_out, gate_out, up_out,
     x, dy, land, gate_map, up_map, down_map, gate_pre, up_pre, hidden_grad, gates, pulls, low, sent, got, keep, y,
     z_send, z_recv, t_send, t_recv, r_send, r_recv, y_send, y_recv, w_sem, o_sem) = refs
    e, t = lax.axis_index("expert"), lax.axis_index("tensor")
    tensor = 1 << bits
    pairs = experts // 2
    width = x.shape[1]
    pair_rows = 2 * CAP
    sources = (x, dy)
    results = ((low.at[0], hidden_out), (low.at[1], gate_out), (low.at[2], up_out))

    def first_block(u):
        return ((e >> 1) ^ u) * 2

    def block(j):
        return pl.ds(pl.multiple_of(j * CAP, CAP), CAP)

    def pair(j):
        return pl.ds(pl.multiple_of(j * CAP, pair_rows), pair_rows)

    def cols(d):
        return pl.ds(pl.multiple_of((t ^ d) * width, 128), width)

    def arrive(a, j):
        return remote(sources[a].at[block(j // pieces)], land.at[a, block(e), cols(0)], z_send.at[a, j], z_recv.at[a, e],
                      expert=j)

    def arrived(a, j):
        return remote(sources[a].at[block(j // pieces)], land.at[a, block(j), cols(0)], z_send.at[a, j], z_recv.at[a, j],
                      expert=j)

    def pass_on(a, j, d, b):
        place, far = land.at[a, block(j), cols(d)], d | (1 << b)
        return remote(place, place, t_send.at[a, j, far], t_recv.at[a, j, far], tensor=t ^ (1 << b))

    def passed(a, j, d):
        place = land.at[a, block(j), cols(d)]
        return remote(place, place, t_send.at[a, j, d], t_recv.at[a, j, d], tensor=t ^ (1 << low_bit(d)))

    def stage(j, k):
        for q in range(2):
            for a in range(2):
                for d in range(1, tensor):
                    if low_bit(d) == bits - k:
                        passed(a, j + q, d).wait_recv()
                        for b in reversed(range(bits - k)):
                            pass_on(a, j + q, d, b).start()

    def place_of(u, q):
        return 2 * (u & 1) + q

    def give(u, q, d):
        j = first_block(u) + q
        return remote(sent.at[place_of(u, q), d - 1], got.at[j, d - 1], r_send.at[place_of(u, q), d - 1],
                      r_recv.at[j, d - 1], tensor=t ^ (1 << low_bit(d)))

    def hand_back(j):
        return remote(y.at[j], back.at[e], y_send.at[j], y_recv.at[e], expert=j)

    def handed(j):
        return remote(y.at[j], back.at[j], y_send.at[j], y_recv.at[j], expert=j)

    def sum_stage(u, k):
        j = first_block(u)
        for q in range(2):
            for d in range(tensor - 1, -1, -1):
                if d % (1 << k) == 0:
                    came = d | (1 << (k - 1))
                    give(u, q, came).wait_recv()
                    total = keep[q, d // 2] + got[j + q, came - 1].astype(F32)
                    if k == bits:
                        y[j + q] = total.astype(BF16)
                    elif d & (1 << k):
                        sent[place_of(u, q), d - 1] = total.astype(BF16)
                        give(u, q, d).start()
                    else:
                        keep[q, d // 2] = total

    def finish(u):
        j = first_block(u)
        for k in range(2, bits + 1):
            sum_stage(u, k)
        for q in range(2):
            @pl.when(j + q == e)
            def _():
                back[e] = y[e]

            @pl.when(j + q != e)
            def _():
                hand_back(j + q).start()

    def to_memory(j):
        copies = [pltpu.make_async_copy(land.at[a, pair(j)], out.at[pair(j)], o_sem.at[a])
                  for a, out in enumerate((rows_out, dys_out))]
        return copies

    def results_to_memory(j):
        return [pltpu.make_async_copy(source, out.at[pair(j)], o_sem.at[2 + i])
                for i, (source, out) in enumerate(results)]

    weights = [pltpu.make_async_copy(a, b, w_sem.at[i])
               for i, (a, b) in enumerate(((gate_in, gate_map), (up_in, up_map), (down_in, down_map)))]
    for copy in weights:
        copy.start()
    here = x_cols.shape[0]
    place = lax.broadcasted_iota(jnp.int32, (x.shape[0], here), 0)
    chosen = (place == slots[:, pl.ds(0, here)]) | (place == slots[:, pl.ds(here, here)])
    chosen = chosen.astype(F32).astype(BF16)
    x[...] = jnp.dot(chosen, x_cols[...], preferred_element_type=F32).astype(BF16)
    dy[...] = jnp.dot(chosen, dy_cols[...], preferred_element_type=F32).astype(BF16)
    meet(experts, bits)
    for a in range(2):
        arrive(a, e ^ 1).start()

    def send_pair(u):
        for q in range(2):
            for a in range(2):
                arrive(a, first_block(u) + q).start()

    def forward_pair(u):
        for q in range(2):
            for a in range(2):
                arrived(a, first_block(u) + q).wait_recv()
                for b in reversed(range(bits)):
                    pass_on(a, first_block(u) + q, 0, b).start()

    send_pair(1)
    if pairs > 2:
        send_pair(2)
    own = first_block(0)
    for a in range(2):
        land[a, block(e), cols(0)] = sources[a][block(e // pieces), :]
        for b in reversed(range(bits)):
            pass_on(a, e, 0, b).start()
    foot = pl.ds(pair_rows, NOTES)
    for d in range(tensor):
        for q in range(4):
            if d:
                sent[q, d - 1, foot, :] = jnp.zeros((NOTES, width), BF16)
        for q in range(2):
            if d % 2 == 0:
                keep[q, d // 2, foot, :] = jnp.zeros((NOTES, width), F32)
    for a in range(2):
        arrived(a, e ^ 1).wait_recv()
        for b in reversed(range(bits)):
            pass_on(a, e ^ 1, 0, b).start()
    for k in range(1, bits):
        stage(own, k)
    forward_pair(1)
    for copy in weights:
        copy.wait()

    @pl.loop(0, pairs)
    def _(u):
        j = first_block(u)
        stage(j, bits)
        for copy in to_memory(j):
            copy.start()
        rows = land[0, pair(j), :]
        gate_pre[...] = jnp.dot(rows, gate_map[...], preferred_element_type=F32)
        up_pre[...] = jnp.dot(rows, up_map[...], preferred_element_type=F32)
        logits = jnp.dot(rows, routers[...], preferred_element_type=F32)
        lane = lax.broadcasted_iota(jnp.int32, logits.shape, 1)
        mine = jnp.sum(jnp.where(lane == EXPERTS + e // pieces, logits, 0.0), axis=1, keepdims=True)
        other = others[pair(j), :] + EXPERTS
        rival = jnp.sum(jnp.where(lane.astype(F32) == other, logits, 0.0), axis=1, keepdims=True)
        top = jnp.maximum(mine, rival)
        mine, rival = jnp.exp(mine - top), jnp.exp(rival - top)
        gates[...] = mine / (mine + rival)

        @pl.when(u < pairs - 1)
        def _():
            for k in range(1, bits):
                stage(first_block(u + 1), k)

        hidden_grad[...] = lax.dot_general(
            land[1, pair(j), :], down_map[...], (((1,), (1,)), ((), ())), preferred_element_type=F32)

        @pl.when(u > 0)
        def _():
            for copy in results_to_memory(j):
                copy.wait()

        @pl.loop(0, pair_rows // 16)
        def _(r):
            some = pl.ds(pl.multiple_of(r * 16, 16), 16)
            gate_here, up_here = gate_pre[some, :], up_pre[some, :]
            weight = gates[some, :]
            sigma = 1.0 / (1.0 + jnp.exp(-gate_here))
            silu = gate_here * sigma
            hidden = silu * up_here
            grad = hidden_grad[some, :]
            pulls[some, :] = jnp.sum(hidden * grad, axis=1, keepdims=True)
            grad = grad * weight
            low[0, some, :] = (hidden * weight).astype(BF16)
            low[1, some, :] = (grad * up_here * (sigma * (1.0 + gate_here * (1.0 - sigma)))).astype(BF16)
            low[2, some, :] = (grad * silu).astype(BF16)

        for copy in results_to_memory(j):
            copy.start()

        @pl.when(u < pairs - 2)
        def _():
            forward_pair(u + 2)

            @pl.when(u < pairs - 3)
            def _():
                send_pair(u + 3)

        @pl.when(u > 0)
        def _():
            finish(u - 1)

        @pl.when(u > 1)
        def _():
            for q in range(2):
                for d in range(1, tensor):
                    give(u - 2, q, d).wait_send()

        noted = []
        for q in range(2):
            some = pl.ds(q * CAP, CAP)
            lane = lax.broadcasted_iota(jnp.int32, (CAP, 128), 1)
            column = jnp.where(lane == 0, pulls[some, :], jnp.where(lane == 1, gates[some, :] / (tensor * pieces), 0.0))
            column = jnp.concatenate([column, jnp.zeros((256 - CAP, 128), F32)], axis=0)
            noted.append(column.T[:NOTES])
        for d in range(tensor - 1, -1, -1):
            grad = lax.dot_general(low[1], gate_map[cols(d), :], (((1,), (1,)), ((), ())), preferred_element_type=F32)
            grad += lax.dot_general(low[2], up_map[cols(d), :], (((1,), (1,)), ((), ())), preferred_element_type=F32)
            out = jnp.dot(low[0], down_map[:, cols(d)], preferred_element_type=F32)
            for q in range(2):
                part = pl.ds(q * CAP, CAP)
                parts = [(pl.ds(0, CAP), slice(None), grad[q * CAP : (q + 1) * CAP]),
                         (pl.ds(CAP, CAP), slice(None), out[q * CAP : (q + 1) * CAP]),
                         (foot, pl.ds(0, 256), noted[q])]
                for place, lanes, value in parts:
                    if d & 1:
                        sent[place_of(u, q), d - 1, place, lanes] = value.astype(BF16)
                    else:
                        keep[q, d // 2, place, lanes] = value
                if d & 1:
                    give(u, q, d).start()
        sum_stage(u, 1)
        for copy in to_memory(j):
            copy.wait()

    finish(pairs - 1)
    for copy in results_to_memory(0):
        copy.wait()
    for u in range(max(pairs - 2, 0), pairs):
        for q in range(2):
            for d in range(1, tensor):
                give(u, q, d).wait_send()

    @pl.loop(1, experts)
    def _(s):
        j = e ^ s
        for a in range(2):
            arrived(a, j).wait_send()
        handed(j).wait_recv()
        handed(j).wait_send()

    @pl.loop(0, experts)
    def _(j):
        for a in range(2):
            for d in range(1, tensor):
                passed(a, j, d).wait_send()


def feed_forward(x, dy, slots, others, routers, gate_map, up_map, down_map, collective_id):
    experts, tensor = lax.axis_size("expert"), lax.axis_size("tensor")
    bits = tensor.bit_length() - 1
    width, hidden = x.shape[1], gate_map.shape[1]
    high = 2 * CAP + NOTES
    count = experts * CAP
    dma = pltpu.SemaphoreType.DMA
    return pl.pallas_call(
        functools.partial(ffn_kernel, experts, bits, experts // EXPERTS),
        out_shape=[jax.ShapeDtypeStruct((experts, high, width), BF16)]
        + [jax.ShapeDtypeStruct((count, D), BF16)] * 2 + [jax.ShapeDtypeStruct((count, hidden), BF16)] * 3,
        in_specs=[VMEM] * 5 + [ANY] * 3,
        out_specs=[VMEM] + [ANY] * 5,
        scratch_shapes=[
            pltpu.VMEM((SLOTS, width), BF16),
            pltpu.VMEM((SLOTS, width), BF16),
            pltpu.VMEM((2, count, D), BF16),
            pltpu.VMEM((D, hidden), BF16),
            pltpu.VMEM((D, hidden), BF16),
            pltpu.VMEM((hidden, D), BF16),
            pltpu.VMEM((2 * CAP, hidden), F32),
            pltpu.VMEM((2 * CAP, hidden), F32),
            pltpu.VMEM((2 * CAP, hidden), F32),
            pltpu.VMEM((2 * CAP, 1), F32),
            pltpu.VMEM((2 * CAP, 1), F32),
            pltpu.VMEM((3, 2 * CAP, hidden), BF16),
            pltpu.VMEM((4, tensor - 1, high, width), BF16),
            pltpu.VMEM((experts, tensor - 1, high, width), BF16),
            pltpu.VMEM((2, tensor // 2, high, width), F32),
            pltpu.VMEM((experts, high, width), BF16),
        ] + [dma((2, experts))] * 2 + [dma((2, experts, tensor))] * 2
        + [dma((4, tensor - 1)), dma((experts, tensor - 1))] + [dma((experts,))] * 2 + [dma((3,)), dma((5,))],
        compiler_params=pltpu.CompilerParams(
            collective_id=collective_id, has_side_effects=True, vmem_limit_bytes=63 * 2**20),
        cost_estimate=pl.CostEstimate(flops=10**11, bytes_accessed=10**7, transcendentals=0),
    )(x, dy, slots, others, routers, gate_map, up_map, down_map)


def share_kernel(me, left_ref, right_ref, out_ref):
    out_ref[...] = lax.dot_general(
        left_ref[...], right_ref[...], (((0,), (0,)), ((), ())), preferred_element_type=F32).astype(BF16)


def share_products(left, right, expert_index, experts):
    share, f = D // experts, right.shape[1]

    def share_at(p, me):
        distance, last = 0, experts // 2
        for b in range(experts.bit_length() - 1):
            distance += ((p >> b) & 1) * (last >> b)
        return me[0] ^ distance

    return pl.pallas_call(
        share_kernel,
        grid_spec=pltpu.PrefetchScalarGridSpec(
            num_scalar_prefetch=1,
            grid=(experts,),
            in_specs=[
                pl.BlockSpec((left.shape[0], share), lambda p, me: (0, share_at(p, me))),
                pl.BlockSpec(right.shape, lambda p, me: (0, 0)),
            ],
            out_specs=pl.BlockSpec((share, f), lambda p, me: (p, 0)),
        ),
        out_shape=jax.ShapeDtypeStruct((D, f), BF16),
        compiler_params=pltpu.CompilerParams(vmem_limit_bytes=32 * 2**20),
        cost_estimate=pl.CostEstimate(flops=10**10, bytes_accessed=2 * 10**7, transcendentals=0),
    )(expert_index[None], left, right)


def small_kernel(experts, tensor, part, out, came, s_send, s_recv, b_send, b_recv):
    e, t = lax.axis_index("expert"), lax.axis_index("tensor")
    owners = experts // tensor
    width = out.shape[1]
    place = t * owners

    def to_owner(c):
        return remote(part.at[:, pl.ds(c * width, width)], came.at[e], s_send.at[c], s_recv.at[e], expert=place + c)

    barrier = pltpu.get_barrier_semaphore()

    @pl.loop(1, experts)
    def _(s):
        pl.semaphore_signal(barrier, inc=1, device_id={"expert": e ^ s}, device_id_type=MESH)

    @pl.loop(1, tensor)
    def _(s):
        pl.semaphore_signal(barrier, inc=1, device_id={"tensor": t ^ s}, device_id_type=MESH)

    pl.semaphore_wait(barrier, experts + tensor - 2)
    for c in range(owners):
        @pl.when(e != place + c)
        def _():
            to_owner(c).start()

        @pl.when(e == place + c)
        def _():
            came[e] = part[:, c * width : (c + 1) * width]

    @pl.when(e // owners == t)
    def _():
        @pl.loop(1, experts)
        def _(s):
            j = e ^ s
            remote(came.at[j], came.at[j], s_send.at[0], s_recv.at[j], expert=j).wait_recv()

        total = came[0]
        for j in range(1, experts):
            total += came[j]
        out[...] = total

        @pl.loop(1, tensor)
        def _(s):
            remote(out, out, b_send.at[s], b_recv, tensor=t ^ s).start()

        @pl.loop(1, tensor)
        def _(s):
            remote(out, out, b_send.at[s], b_recv, tensor=t ^ s).wait_send()

    @pl.when(e // owners != t)
    def _():
        remote(out, out, b_send.at[0], b_recv, tensor=e // owners).wait_recv()

    for c in range(owners):
        @pl.when(e != place + c)
        def _():
            to_owner(c).wait_send()


def small_sums(part, collective_id):
    experts, tensor = lax.axis_size("expert"), lax.axis_size("tensor")
    n, width = part.shape[0], D // experts
    dma = pltpu.SemaphoreType.DMA
    return pl.pallas_call(
        functools.partial(small_kernel, experts, tensor),
        out_shape=jax.ShapeDtypeStruct((n, width), F32),
        in_specs=[VMEM],
        out_specs=VMEM,
        scratch_shapes=[pltpu.VMEM((experts, n, width), F32), dma((experts // tensor,)), dma((experts,)), dma((tensor,)),
                        dma],
        compiler_params=pltpu.CompilerParams(collective_id=collective_id, has_side_effects=True),
        cost_estimate=pl.CostEstimate(flops=10**10, bytes_accessed=10**5, transcendentals=0),
    )(part)


def dot(left, right, dims):
    return lax.dot_general(left, right, ((dims[0], dims[1]), ((), ())), preferred_element_type=F32)


def mm(left, right):
    return dot(left, right, ((1,), (0,)))


def mm_nt(left, right):
    return dot(left, right, ((1,), (1,)))


def mm_tn(left, right):
    return dot(left, right, ((0,), (0,)))


def swap(blocks):
    return lax.all_to_all(blocks, "expert", split_axis=0, concat_axis=0, tiled=True)


def columns_together(rows):
    return lax.all_gather(rows, "tensor", axis=1, tiled=True)


def columns_summed(rows):
    return lax.psum_scatter(rows, "tensor", scatter_dimension=1, tiled=True)


def slot_numbers(routes):
    flat = routes.T.reshape(-1)
    place = jnp.arange(flat.shape[0], dtype=jnp.int32)
    earlier = (flat[:, None] == flat[None, :]) & (place[None, :] < place[:, None])
    return flat * CAP + jnp.sum(earlier.astype(jnp.int32), axis=1)


def spaced(slots, stride):
    return slots + (slots // CAP) * (stride - CAP)


def place_matrix(slots):
    return (jnp.arange(SLOTS, dtype=jnp.int32)[:, None] == slots[None, :]).astype(BF16)


def token_matrix(slots, stride=CAP, first=0):
    wide = (spaced(slots, stride) + first).reshape(TOPK, -1)
    place = jnp.arange(EXPERTS * stride, dtype=jnp.int32)[:, None]
    return ((place == wide[0][None, :]) | (place == wide[1][None, :])).astype(BF16)


def to_pieces(rows, pieces):
    if pieces == 1:
        return rows
    experts, r, c = rows.shape
    return rows.reshape(experts, r, pieces, c // pieces).transpose(0, 2, 1, 3).reshape(experts * pieces, r, -1)


def from_pieces(rows, pieces):
    if pieces == 1:
        return rows
    both, r, c = rows.shape
    return rows.reshape(both // pieces, pieces, r, c).transpose(0, 2, 1, 3).reshape(both // pieces, r, -1)


def for_pieces(rows, pieces):
    return jnp.repeat(rows, pieces, axis=0) if pieces > 1 else rows


def pick_gates(logits, routes):
    one_hot = (routes[:, :, None] == jnp.arange(EXPERTS, dtype=jnp.int32)[None, None, :]).astype(F32)
    return jax.nn.softmax(jnp.sum(one_hot * logits[:, None, :], axis=2), axis=-1)


def gate_back(gating, pulled, routes):
    inner_sum = gating * (pulled - jnp.sum(gating * pulled, axis=1, keepdims=True))
    one_hot = (routes[:, :, None] == jnp.arange(EXPERTS, dtype=jnp.int32)[None, None, :]).astype(F32)
    return jnp.sum(one_hot * inner_sum[:, :, None], axis=1).astype(BF16)


def place_matrices(slots_ref, spread, gathered):
    count, choices = spread.shape
    spread[...] = (lax.broadcasted_iota(jnp.int32, (count, choices), 0) == slots_ref[...]).astype(F32).astype(BF16)
    gathered[...] = spread[...].T


def mask_bias(query_ids, key_ids, bias):
    blocks, span, _ = bias.shape

    for block in range(blocks):
        first = block * Q_ROWS
        query_place = lax.broadcasted_iota(jnp.int32, (span, Q_ROWS), 1) + WINDOW
        distance = query_place - lax.broadcasted_iota(jnp.int32, (span, Q_ROWS), 0)
        same = key_ids[pl.ds(first, span), :] == query_ids[:, pl.ds(first, Q_ROWS)]
        allowed = (distance >= 0) & (distance < WINDOW) & same
        part = jnp.where(allowed, 0.0, masked_value)
        for k in range(TOPK):
            bias[block, :, pl.ds(k * Q_ROWS, Q_ROWS)] = part


def of_block(choices, block):
    rows = choices.shape[0] // TOPK
    return jnp.concatenate([choices[pl.ds(k * rows + block * Q_ROWS, Q_ROWS), :] for k in range(TOPK)], axis=0)


def attend_kernel(slots_ref, back_ref, key_ref, value_ref, query_ids, key_ids, grouped_ref, query_ref, lse_ref,
                  spread, gathered, bias, heads):
    @pl.when(pl.program_id(0) == 0)
    def _():
        place_matrices(slots_ref, spread, gathered)
        mask_bias(query_ids, key_ids, bias)

    query_ref[...] = jnp.dot(gathered[...], back_ref[...], preferred_element_type=F32).astype(BF16)
    blocks, span, _ = bias.shape
    rows = query_ref.shape[0] // TOPK
    for block in range(blocks):
        queries = of_block(query_ref, block)
        keys = key_ref[pl.ds(block * Q_ROWS, span), :]
        values = value_ref[pl.ds(block * Q_ROWS, span), :]
        scores = lax.dot_general(keys, queries, (((1,), (1,)), ((), ())), preferred_element_type=F32)
        scores = scores * (SCALE * LOG2E) + bias[block]
        top = jnp.max(scores, axis=0, keepdims=True)
        probs = jnp.exp2(scores - top)
        total = jnp.sum(probs, axis=0, keepdims=True)
        out = lax.dot_general(values, probs.astype(BF16), (((0,), (0,)), ((), ())), preferred_element_type=F32)
        out = (out * (1.0 / total)).T.astype(BF16)
        for k in range(TOPK):
            heads[pl.ds(k * rows + block * Q_ROWS, Q_ROWS), :] = out[k * Q_ROWS : (k + 1) * Q_ROWS]
        lse_ref[0, :, pl.ds(block * TOPK * Q_ROWS, TOPK * Q_ROWS)] = top + jnp.log2(total)
    grouped_ref[...] = jnp.dot(spread[...], heads[...], preferred_element_type=F32).astype(BF16)


def attend(slots, back, keys, values, query_ids, key_ids):
    choices, (count, width), span = slots.shape[1], back.shape, keys.shape[0]
    blocks = choices // TOPK // Q_ROWS
    head = lambda rows: pl.BlockSpec((rows, HD), lambda h: (0, h))
    whole = lambda a: pl.BlockSpec(a.shape, lambda h: (0, 0))
    return pl.pallas_call(
        attend_kernel,
        grid=(width // HD,),
        out_shape=[
            jax.ShapeDtypeStruct((count, width), BF16),
            jax.ShapeDtypeStruct((choices, width), BF16),
            jax.ShapeDtypeStruct((width // HD, 1, choices), F32),
        ],
        in_specs=[whole(slots), head(count), head(span), head(span), whole(query_ids), whole(key_ids)],
        out_specs=[head(count), head(choices), pl.BlockSpec((1, 1, choices), lambda h: (h, 0, 0))],
        scratch_shapes=[
            pltpu.VMEM((count, choices), BF16),
            pltpu.VMEM((choices, count), BF16),
            pltpu.VMEM((blocks, WINDOW + Q_ROWS, TOPK * Q_ROWS), F32),
            pltpu.VMEM((choices, HD), BF16),
        ],
        compiler_params=pltpu.CompilerParams(vmem_limit_bytes=48 * 2**20),
        cost_estimate=pl.CostEstimate(flops=16 * 10**9, bytes_accessed=10**7, transcendentals=10**7),
    )(slots, back, keys, values, query_ids, key_ids)


def attend_back_kernel(slots_ref, back_ref, query_ref, key_ref, value_ref, lse_ref, query_ids, key_ids,
                       grouped_ref, key_grad_ref, value_grad_ref,
                       spread, gathered, bias, key_acc, value_acc, query_grad, head_grad):
    @pl.when(pl.program_id(0) == 0)
    def _():
        place_matrices(slots_ref, spread, gathered)
        mask_bias(query_ids, key_ids, bias)

    head_grad[...] = jnp.dot(gathered[...], back_ref[...], preferred_element_type=F32).astype(BF16)
    key_acc[...] = jnp.zeros_like(key_acc)
    value_acc[...] = jnp.zeros_like(value_acc)
    blocks, span, _ = bias.shape
    rows = query_ref.shape[0] // TOPK
    for block in range(blocks):
        queries = of_block(query_ref, block)
        grads = of_block(head_grad, block)
        place = pl.ds(block * Q_ROWS, span)
        keys, values = key_ref[place, :], value_ref[place, :]
        scores = lax.dot_general(keys, queries, (((1,), (1,)), ((), ())), preferred_element_type=F32)
        lse = lse_ref[0, :, pl.ds(block * TOPK * Q_ROWS, TOPK * Q_ROWS)]
        probs = jnp.exp2(scores * (SCALE * LOG2E) + bias[block] - lse)
        pulled = lax.dot_general(values, grads, (((1,), (1,)), ((), ())), preferred_element_type=F32)
        pulled = probs * pulled
        inner = jnp.sum(pulled, axis=0, keepdims=True)
        score_grad = (pulled - probs * inner).astype(BF16)
        value_acc[place, :] += jnp.dot(probs.astype(BF16), grads, preferred_element_type=F32)
        key_acc[place, :] += jnp.dot(score_grad, queries, preferred_element_type=F32)
        out = lax.dot_general(keys, score_grad, (((0,), (0,)), ((), ())), preferred_element_type=F32)
        out = (out * SCALE).T.astype(BF16)
        for k in range(TOPK):
            query_grad[pl.ds(k * rows + block * Q_ROWS, Q_ROWS), :] = out[k * Q_ROWS : (k + 1) * Q_ROWS]
    grouped_ref[...] = jnp.dot(spread[...], query_grad[...], preferred_element_type=F32).astype(BF16)
    key_grad_ref[...] = (key_acc[...] * SCALE).astype(BF16)
    value_grad_ref[...] = value_acc[...].astype(BF16)


def attend_back(slots, back, queries, keys, values, lse, query_ids, key_ids):
    choices, (count, width), span = slots.shape[1], back.shape, keys.shape[0]
    blocks = choices // TOPK // Q_ROWS
    head = lambda rows: pl.BlockSpec((rows, HD), lambda h: (0, h))
    whole = lambda a: pl.BlockSpec(a.shape, lambda h: (0, 0))
    return pl.pallas_call(
        attend_back_kernel,
        grid=(width // HD,),
        out_shape=[jax.ShapeDtypeStruct((count, width), BF16)] + [jax.ShapeDtypeStruct((span, width), BF16)] * 2,
        in_specs=[
            whole(slots), head(count), head(choices), head(span), head(span),
            pl.BlockSpec((1, 1, choices), lambda h: (h, 0, 0)), whole(query_ids), whole(key_ids),
        ],
        out_specs=[head(count), head(span), head(span)],
        scratch_shapes=[
            pltpu.VMEM((count, choices), BF16),
            pltpu.VMEM((choices, count), BF16),
            pltpu.VMEM((blocks, WINDOW + Q_ROWS, TOPK * Q_ROWS), F32),
            pltpu.VMEM((span, HD), F32),
            pltpu.VMEM((span, HD), F32),
            pltpu.VMEM((choices, HD), BF16),
            pltpu.VMEM((choices, HD), BF16),
        ],
        compiler_params=pltpu.CompilerParams(vmem_limit_bytes=56 * 2**20),
        cost_estimate=pl.CostEstimate(flops=30 * 10**9, bytes_accessed=10**7, transcendentals=10**7),
    )(slots, back, queries, keys, values, lse, query_ids, key_ids)


def per_device(
    tokens,
    segment_ids,
    attn_routes,
    ffn_routes,
    attn_gain,
    ffn_gain,
    routers,
    query_weight,
    output_weight,
    key_value_weight,
    gate_weight,
    up_weight,
    down_weight,
    cotangent,
):
    rows_here = tokens.shape[0]
    expert_count = lax.axis_size("expert")
    tensor_count = lax.axis_size("tensor")
    pieces = expert_count // EXPERTS
    column_count = D // tensor_count
    expert_index = lax.axis_index("expert")
    tensor_index = lax.axis_index("tensor")
    own = (expert_index // pieces).astype(F32)
    head_width = query_weight.shape[2]
    head_count = head_width // HD

    def cols(whole):
        return lax.dynamic_slice_in_dim(whole, tensor_index * column_count, column_count, whole.ndim - 1)

    def group_tokens(token_cols, places):
        return for_pieces(mm(places, token_cols).astype(BF16).reshape(EXPERTS, CAP, -1), pieces)

    def group_choices(choice_rows, places):
        return to_pieces(mm(places, choice_rows).astype(BF16).reshape(EXPERTS, CAP, -1), pieces)

    def choices_of(back, places):
        return mm_tn(places, from_pieces(back, pieces).reshape(SLOTS, -1)).astype(BF16)

    def sums_of(back, places):
        stride = back.shape[1]
        back = back.reshape(EXPERTS, pieces, stride, column_count)
        if pieces > 1:
            total = sum(mm_tn(places, back[:, p].reshape(EXPERTS * stride, -1)) for p in range(pieces))
        else:
            total = mm_tn(places, back.reshape(EXPERTS * stride, -1))
        return total

    def notes_of(*scalars):
        rows = jnp.stack([v.reshape(expert_count, CAP) for v in scalars], axis=1)
        return jnp.pad(rows, ((0, 0), (0, NOTES - len(scalars)), (0, column_count - CAP)))

    def read_notes(back, places, count, first=CAP):
        noted = back[:, first : first + count, :CAP].astype(F32)
        noted = noted.reshape(EXPERTS, pieces, count, CAP).sum(1).transpose(0, 2, 1).reshape(SLOTS, count)
        return mm_tn(places, noted.astype(BF16)).reshape(TOPK, rows_here, count)

    def exchange(away, b):
        return lax.ppermute(away, "expert", [(i, i ^ (1 << b)) for i in range(expert_count)])

    state_in = tokens.astype(F32)
    gain_one = attn_gain.astype(F32)
    gain_two = cols(ffn_gain.astype(F32))
    routers_one, routers_two = routers[:, :EXPERTS], routers[:, EXPERTS:]
    dy_cols = cols(cotangent)
    token_cols = cols(tokens).astype(F32)

    attn_slots, ffn_slots = slot_numbers(attn_routes), slot_numbers(ffn_routes)
    attn_places, ffn_places = place_matrix(attn_slots), place_matrix(ffn_slots)


    wide_slots = jnp.stack([spaced(attn_slots, 256), spaced(ffn_slots, 256)], axis=1)
    rows_one, query_rows, query_map, window, pair_map, keys, values, attn_gate_blocks, rivals = front(
        tokens, gain_one[None], attn_slots[None], wide_slots, jnp.concatenate([attn_routes, ffn_routes], axis=1), routers,
        to_pieces(query_weight, pieces), key_value_weight, collective_id=0)
    output_weight, keys = lax.optimization_barrier((output_weight, keys))
    rows_one = rows_one.reshape(-1, D)
    output_map = swap(to_pieces(output_weight, pieces)).reshape(D, -1)
    normed_one = window[2]
    window = window.reshape(-1, D)
    padded_segments = jnp.concatenate([jnp.full((WINDOW,), -1, jnp.int32), segment_ids])
    key_ids = lax.dynamic_slice_in_dim(padded_segments, expert_index * rows_here, WINDOW + rows_here)
    query_ids = key_ids[None, WINDOW:]
    key_ids = key_ids[:, None]
    heads, queries, log_total = attend(
        attn_slots[None], from_pieces(query_rows, pieces).reshape(SLOTS, -1), keys, values, query_ids, key_ids)
    attn_back, heads_rows = scatter_rows(
        to_pieces(heads.reshape(EXPERTS, CAP, -1), pieces), output_map, attn_gate_blocks, collective_id=1)
    heads_rows = heads_rows.reshape(expert_count * CAP, -1)
    state = token_cols + sums_of(attn_back, token_matrix(attn_slots))

    mean_two = lax.psum(jnp.sum(state * state, axis=1, keepdims=True), "tensor") / D
    rate_two = lax.rsqrt(mean_two + eps)
    normed_two = (state * rate_two * gain_two).astype(BF16)
    gate_map, up_map, down_map = gate_weight[0], up_weight[0], down_weight[0]
    ffn_back, rows_two, rows_dy, hidden, gate_low, up_low = feed_forward(
        normed_two, dy_cols, ffn_slots[None], rivals.reshape(-1, 1), routers, gate_map, up_map, down_map, collective_id=2)
    normed_two_grad = sums_of(ffn_back, token_matrix(ffn_slots, 2 * CAP + NOTES))
    noted = read_notes(ffn_back, ffn_places, 2, 2 * CAP)
    ffn_pull, ffn_gates = noted[:, :, 0].T, noted[:, :, 1].T
    ffn_logit_grad = gate_back(ffn_gates, ffn_pull, ffn_routes)
    normed_two_grad = normed_two_grad + mm_nt(
        ffn_logit_grad, lax.dynamic_slice_in_dim(routers_two, tensor_index * column_count, column_count, 0))
    ffn_router_cols = mm_tn(normed_two, ffn_logit_grad)
    ffn_gain_cols = jnp.sum(normed_two_grad * state * rate_two, axis=0)
    ahead = normed_two_grad * gain_two
    centre = lax.psum(jnp.sum(ahead * state, axis=1, keepdims=True), "tensor") / D
    state_grad = dy_cols.astype(F32) + rate_two * ahead - state * rate_two * rate_two * rate_two * centre

    rows_state, heads_grad, heads_grad_rows = gather_rows(
        group_tokens(state_grad.astype(BF16), token_matrix(attn_slots)), output_map, gate=attn_gate_blocks, collective_id=4)
    rows_state = rows_state.reshape(-1, D)
    heads_grad_rows = heads_grad_rows.reshape(expert_count * CAP, -1)
    attn_notes = notes_of(jnp.sum(heads_grad_rows.astype(F32) * heads_rows.astype(F32), axis=1))
    output_part = mm_tn((rows_state.astype(F32) * attn_gate_blocks.reshape(-1, 1)).astype(BF16), heads_rows).astype(BF16)
    heads_grad, output_part = lax.optimization_barrier((heads_grad, output_part))

    query_back, key_back, value_back = attend_back(
        attn_slots[None], from_pieces(heads_grad, pieces).reshape(SLOTS, -1), queries, keys, values, log_total,
        query_ids, key_ids)
    output_grad = swap(output_part.reshape(expert_count, D // expert_count, -1))
    pair_part = share_products(window, jnp.concatenate([key_back, value_back], axis=1), expert_index, expert_count)
    query_back, output_grad = lax.optimization_barrier((query_back, output_grad))
    output_grad = from_pieces(output_grad, pieces).astype(F32)
    normed_back, unused_rows, owed, query_grad, pair_came = scatter_rows(
        to_pieces(query_back.reshape(EXPERTS, CAP, -1), pieces), query_map, notes=attn_notes,
        windows=[key_back, value_back, pair_map, rows_one, pair_part], collective_id=5)
    query_grad = from_pieces(query_grad, pieces).astype(F32)
    normed_grad = sums_of(normed_back, token_matrix(attn_slots, CAP + NOTES)) + jnp.sum(owed.astype(F32), axis=0)
    rows_two, rows_dy, normed_back = lax.optimization_barrier((rows_two, rows_dy, normed_back))
    attn_pull = read_notes(normed_back, attn_places, 1)[:, :, 0].T
    attn_gates = pick_gates(mm(normed_one, routers_one), attn_routes)
    attn_logit_grad = gate_back(attn_gates, attn_pull, attn_routes)
    normed_grad = normed_grad + mm_nt(
        attn_logit_grad, lax.dynamic_slice_in_dim(routers_one, tensor_index * column_count, column_count, 0))
    attn_router_cols = mm_tn(cols(normed_one), attn_logit_grad)
    rate_one = lax.rsqrt(jnp.mean(state_in * state_in, axis=1, keepdims=True) + eps)
    attn_gain_cols = jnp.sum(normed_grad * token_cols * rate_one, axis=0)
    ahead_one = normed_grad * cols(gain_one)
    centre_one = lax.psum(jnp.sum(ahead_one * token_cols, axis=1, keepdims=True), "tensor") / D
    tokens_grad = state_grad + rate_one * ahead_one - token_cols * rate_one * rate_one * rate_one * centre_one
    tokens_grad = columns_together(tokens_grad.astype(BF16)).astype(F32)

    small = jnp.concatenate(
        [attn_router_cols.T, ffn_router_cols.T, attn_gain_cols[None], ffn_gain_cols[None],
         jnp.zeros((6, column_count), F32)], axis=0)
    small = small_sums(small, collective_id=3)
    small, pair_came = lax.optimization_barrier((small, pair_came))
    small = small.T
    for b in range(1, expert_count.bit_length()):
        pair_part = pair_part[: pair_came.shape[0]].astype(F32) + pair_came.astype(F32)
        if b < expert_count.bit_length() - 1:
            pair_part = pair_part.astype(BF16)
            pair_came = exchange(pair_part[pair_part.shape[0] // 2 :], b)
    key_value_grad = pair_part.reshape(D // expert_count, 2, -1).transpose(1, 0, 2)

    gate_grad = mm_tn(rows_two, gate_low)
    up_grad = mm_tn(rows_two, up_low)
    down_grad = mm_tn(hidden, rows_dy)
    ffn_out = sums_of(ffn_back, token_matrix(ffn_slots, 2 * CAP + NOTES, CAP))
    mixed = (state + ffn_out).astype(BF16)
    return (
        mixed,
        tokens_grad,
        small[:, 2 * EXPERTS],
        small[:, 2 * EXPERTS + 1],
        small[:, : 2 * EXPERTS],
        query_grad,
        output_grad,
        key_value_grad,
        gate_grad[None],
        up_grad[None],
        down_grad[None],
    )


def solution(mesh):
    in_specs = (
        P("expert", None),
        P(),
        P("expert", None),
        P("expert", None),
        P(),
        P(),
        P(),
        P(None, "expert", "tensor"),
        P(None, "expert", "tensor"),
        P(None, "expert", "tensor"),
        P("expert", None, "tensor"),
        P("expert", None, "tensor"),
        P("expert", "tensor", None),
        P("expert", None),
    )
    out_specs = (
        P("expert", "tensor"),
        P("expert", None),
        P("expert"),
        P("expert"),
        P("expert", None),
        P(None, "expert", "tensor"),
        P(None, "expert", "tensor"),
        P(None, "expert", "tensor"),
        P("expert", None, "tensor"),
        P("expert", None, "tensor"),
        P("expert", "tensor", None),
    )
    return jax.shard_map(
        per_device, mesh=mesh, in_specs=in_specs, out_specs=out_specs, check_vma=False
    )
```

```python
import functools
import math

import jax
import jax.numpy as jnp
from jax import lax
from jax.experimental import pallas as pl
from jax.experimental.pallas import tpu as pltpu
from jax.sharding import PartitionSpec as P

D = 2048
HD = 128
EXPERTS = 8
TOPK = 2
WINDOW = 1024
CAP = 160
SLOTS = EXPERTS * CAP

eps = 1e-06
masked_value = -1e30
SCALE = HD ** (-0.5)
LOG2E = math.log2(math.e)
Q_ROWS = 256
NOTES = 16
F32 = jnp.float32
BF16 = jnp.bfloat16
MESH = pl.DeviceIdType.MESH
VMEM = pl.BlockSpec(memory_space=pltpu.VMEM)
ANY = pl.BlockSpec(memory_space=pl.ANY)


def remote(src, dst, send, recv, **device):
    return pltpu.make_async_remote_copy(
        src_ref=src, dst_ref=dst, send_sem=send, recv_sem=recv, device_id=device, device_id_type=MESH)


def meet(experts, bits):
    e, t = lax.axis_index("expert"), lax.axis_index("tensor")
    barrier = pltpu.get_barrier_semaphore()

    @pl.loop(1, experts)
    def _(s):
        pl.semaphore_signal(barrier, inc=1, device_id={"expert": e ^ s}, device_id_type=MESH)

    for b in range(bits):
        pl.semaphore_signal(barrier, inc=1, device_id={"tensor": t ^ (1 << b)}, device_id_type=MESH)
    pl.semaphore_wait(barrier, experts - 1 + bits)


def partners(e, experts, near):
    if near:
        return lambda s: e ^ s
    return lambda s: e ^ ((experts - s) & (experts - 1))


def low_bit(d):
    return (d & -d).bit_length() - 1


def gather_kernel(experts, bits, near, multiply, scale, *refs):
    refs = list(refs)
    x = refs.pop(0)
    w = refs.pop(0) if multiply else None
    gate = refs.pop(0) if scale else None
    rows = refs.pop(0)
    back = refs.pop(0) if multiply else None
    product = refs.pop(0) if scale else None
    y = refs.pop(0) if multiply else None
    z_send, z_recv, t_send, t_recv = refs[:4]
    refs = refs[4:]
    if multiply:
        y_send, y_recv = refs[:2]
    e, t = lax.axis_index("expert"), lax.axis_index("tensor")
    partner = partners(e, experts, near)
    width = x.shape[2]
    tensor = 1 << bits

    def cols(d):
        return pl.ds(pl.multiple_of((t ^ d) * width, 128), width)

    def arrive(j):
        return remote(x.at[j], rows.at[e, :, cols(0)], z_send.at[j], z_recv.at[e], expert=j)

    def arrived(j):
        return remote(x.at[j], rows.at[j, :, cols(0)], z_send.at[j], z_recv.at[j], expert=j)

    def pass_on(j, d, b):
        place = rows.at[j, :, cols(d)]
        far = d | (1 << b)
        return remote(place, place, t_send.at[j, far], t_recv.at[j, far], tensor=t ^ (1 << b))

    def passed(j, d):
        place = rows.at[j, :, cols(d)]
        return remote(place, place, t_send.at[j, d], t_recv.at[j, d], tensor=t ^ (1 << low_bit(d)))

    def hand_back(j):
        return remote(y.at[j], back.at[e], y_send.at[j], y_recv.at[e], expert=j)

    def handed(j):
        return remote(y.at[j], back.at[j], y_send.at[j], y_recv.at[j], expert=j)

    meet(experts, bits)

    @pl.loop(1, experts)
    def _(s):
        arrive(partner(s)).start()

    rows[e, :, cols(0)] = x[e]

    @pl.loop(0, experts + bits)
    def _(i):
        @pl.when(i < experts)
        def _():
            j = partner(i)

            @pl.when(i > 0)
            def _():
                arrived(j).wait_recv()

            for b in reversed(range(bits)):
                pass_on(j, 0, b).start()

        for k in range(1, bits + 1):
            @pl.when((i >= k) & (i < experts + k))
            def _():
                m = i - k
                j = partner(m)
                bit = bits - k
                for d in range(1, tensor):
                    if low_bit(d) == bit:
                        passed(j, d).wait_recv()
                        for b in reversed(range(bit)):
                            pass_on(j, d, b).start()
                if k == bits and multiply:
                    out = jnp.dot(rows[j], w[...], preferred_element_type=F32)
                    if scale:
                        product[j] = out.astype(BF16)
                        out = out * gate[j]
                    y[j] = out.astype(BF16)

                    @pl.when(m == 0)
                    def _():
                        back[e] = y[e]

                    @pl.when(m > 0)
                    def _():
                        hand_back(j).start()

    @pl.loop(1, experts)
    def _(s):
        j = partner(s)
        arrived(j).wait_send()
        if multiply:
            handed(j).wait_recv()
            handed(j).wait_send()

    @pl.loop(0, experts)
    def _(j):
        for d in range(1, tensor):
            passed(j, d).wait_send()


def gather_rows(x, w=None, gate=None, near=True, collective_id=0):
    experts, tensor = lax.axis_size("expert"), lax.axis_size("tensor")
    bits = tensor.bit_length() - 1
    cap, width = x.shape[1], x.shape[2]
    multiply = w is not None
    f = w.shape[-1] if multiply else 0
    ins, specs = [x], [VMEM]
    outs = [jax.ShapeDtypeStruct((experts, cap, width * tensor), BF16)]
    scratch = []
    if multiply:
        ins.append(w)
        specs.append(VMEM)
        outs.append(jax.ShapeDtypeStruct((experts, cap, f), BF16))
    if gate is not None:
        ins.append(gate)
        specs.append(VMEM)
        outs.append(jax.ShapeDtypeStruct((experts, cap, f), BF16))
    if multiply:
        scratch.append(pltpu.VMEM((experts, cap, f), BF16))
    scratch += [pltpu.SemaphoreType.DMA((experts,))] * 2 + [pltpu.SemaphoreType.DMA((experts, tensor))] * 2
    if multiply:
        scratch += [pltpu.SemaphoreType.DMA((experts,))] * 2
    return pl.pallas_call(
        functools.partial(gather_kernel, experts, bits, near, multiply, gate is not None),
        out_shape=outs,
        in_specs=specs,
        out_specs=[VMEM] * len(outs),
        scratch_shapes=scratch,
        compiler_params=pltpu.CompilerParams(
            collective_id=collective_id, has_side_effects=True, vmem_limit_bytes=48 * 2**20),
        cost_estimate=pl.CostEstimate(flops=10**11, bytes_accessed=10**7, transcendentals=0),
    )(*ins)


def place_matrices(slots_ref, spread, gathered):
    count, choices = spread.shape
    spread[...] = (lax.broadcasted_iota(jnp.int32, (count, choices), 0) == slots_ref[0:1, :]).astype(F32).astype(BF16)
    gathered[...] = spread[...].T


def mask_bias(segments, bias):
    blocks, span, _ = bias.shape
    here = blocks * Q_ROWS
    e = lax.axis_index("expert")
    query_ids = segments[:, pl.ds(pl.multiple_of(e * here + WINDOW, 128), here)]
    key_row = segments[:, pl.ds(pl.multiple_of(e * here, 128), WINDOW + here)].astype(F32)
    key_ids = jnp.concatenate([key_row, jnp.zeros((7, WINDOW + here), F32)], axis=0).T[:, 0:1].astype(jnp.int32)

    for block in range(blocks):
        first = block * Q_ROWS
        query_place = lax.broadcasted_iota(jnp.int32, (span, Q_ROWS), 1) + WINDOW
        distance = query_place - lax.broadcasted_iota(jnp.int32, (span, Q_ROWS), 0)
        same = key_ids[first : first + span] == query_ids[:, first : first + Q_ROWS]
        allowed = (distance >= 0) & (distance < WINDOW) & same
        part = jnp.where(allowed, 0.0, masked_value)
        for k in range(TOPK):
            bias[block, :, pl.ds(k * Q_ROWS, Q_ROWS)] = part


def of_block(choices, block, lanes):
    rows = choices.shape[0] // TOPK
    return jnp.concatenate([choices[pl.ds(k * rows + block * Q_ROWS, Q_ROWS), lanes] for k in range(TOPK)], axis=0)


def attend(back, keys_ref, values_ref, grouped, queries_ref, lse, spread, gathered, bias, packed, heads):
    blocks, span, _ = bias.shape
    rows = queries_ref.shape[0] // TOPK
    pieces, of_piece = back.shape[0] // EXPERTS, back.shape[2] // HD

    @pl.loop(0, queries_ref.shape[1] // HD)
    def _(head):
        lanes = pl.ds(pl.multiple_of(head * HD, HD), HD)
        inner = pl.ds(pl.multiple_of(lax.rem(head, of_piece) * HD, HD), HD)
        for q in range(EXPERTS):
            packed[pl.ds(q * CAP, CAP), :] = back[q * pieces + lax.div(head, of_piece), :, inner]
        queries_ref[:, lanes] = jnp.dot(gathered[...], packed[...], preferred_element_type=F32).astype(BF16)
        for block in range(blocks):
            place = pl.ds(block * Q_ROWS, span)
            queries = of_block(queries_ref, block, lanes)
            scores = lax.dot_general(
                keys_ref[place, lanes], queries, (((1,), (1,)), ((), ())), preferred_element_type=F32)
            scores = scores * (SCALE * LOG2E) + bias[block]
            top = jnp.max(scores, axis=0, keepdims=True)
            probs = jnp.exp2(scores - top)
            total = jnp.sum(probs, axis=0, keepdims=True)
            out = lax.dot_general(
                values_ref[place, lanes], probs.astype(BF16), (((0,), (0,)), ((), ())), preferred_element_type=F32)
            out = (out * (1.0 / total)).T.astype(BF16)
            for k in range(TOPK):
                heads[pl.ds(k * rows + block * Q_ROWS, Q_ROWS), :] = out[k * Q_ROWS : (k + 1) * Q_ROWS]
            lse[head, :, pl.ds(block * TOPK * Q_ROWS, TOPK * Q_ROWS)] = top + jnp.log2(total)
        grouped[:, lanes] = jnp.dot(spread[...], heads[...], preferred_element_type=F32).astype(BF16)


def attend_back_kernel(experts, *refs):
    (slots, back, queries_ref, keys_ref, values_ref, lse, segments, rows, heads_rows, gates,
     grouped, key_grad, value_grad, map_grad,
     spread, gathered, bias, key_acc, value_acc, query_grad, head_grad, scaled, part_grad,
     g_send, g_recv) = refs
    e = lax.axis_index("expert")
    blocks, span, _ = bias.shape
    here = queries_ref.shape[0] // TOPK
    share = part_grad.shape[1]

    def shares(q):
        return pl.ds(pl.multiple_of(q * share, share), share)

    def grad_from(j):
        return remote(part_grad.at[j], map_grad.at[j], g_send.at[j], g_recv.at[j], expert=j)

    barrier = pltpu.get_barrier_semaphore()

    @pl.loop(1, experts)
    def _(s):
        pl.semaphore_signal(barrier, inc=1, device_id={"expert": e ^ s}, device_id_type=MESH)

    scaled[...] = (heads_rows[...].astype(F32) * gates[...]).astype(BF16)
    pl.semaphore_wait(barrier, experts - 1)

    @pl.loop(0, experts)
    def _(s):
        j = e ^ lax.rem(s + 1, experts)
        part_grad[j] = lax.dot_general(
            rows[:, shares(j)], scaled[...], (((0,), (0,)), ((), ())), preferred_element_type=F32).astype(BF16)

        @pl.when(s < experts - 1)
        def _():
            remote(part_grad.at[j], map_grad.at[e], g_send.at[j], g_recv.at[e], expert=j).start()

    map_grad[e] = part_grad[e]
    place_matrices(slots, spread, gathered)
    mask_bias(segments, bias)

    @pl.loop(0, queries_ref.shape[1] // HD)
    def _(head):
        lanes = pl.ds(pl.multiple_of(head * HD, HD), HD)
        head_grad[...] = jnp.dot(gathered[...], back[:, lanes], preferred_element_type=F32).astype(BF16)
        key_acc[...] = jnp.zeros_like(key_acc)
        value_acc[...] = jnp.zeros_like(value_acc)
        for block in range(blocks):
            queries = of_block(queries_ref, block, lanes)
            grads = of_block(head_grad, block, slice(None))
            place = pl.ds(block * Q_ROWS, span)
            keys, values = keys_ref[place, lanes], values_ref[place, lanes]
            scores = lax.dot_general(keys, queries, (((1,), (1,)), ((), ())), preferred_element_type=F32)
            probs = jnp.exp2(scores * (SCALE * LOG2E) + bias[block]
                             - lse[head, :, pl.ds(block * TOPK * Q_ROWS, TOPK * Q_ROWS)])
            pulled = lax.dot_general(values, grads, (((1,), (1,)), ((), ())), preferred_element_type=F32)
            pulled = probs * pulled
            inner = jnp.sum(pulled, axis=0, keepdims=True)
            score_grad = (pulled - probs * inner).astype(BF16)
            value_acc[place, :] += jnp.dot(probs.astype(BF16), grads, preferred_element_type=F32)
            key_acc[place, :] += jnp.dot(score_grad, queries, preferred_element_type=F32)
            out = lax.dot_general(keys, score_grad, (((0,), (0,)), ((), ())), preferred_element_type=F32)
            out = (out * SCALE).T.astype(BF16)
            for k in range(TOPK):
                query_grad[pl.ds(k * here + block * Q_ROWS, Q_ROWS), :] = out[k * Q_ROWS : (k + 1) * Q_ROWS]
        grouped[:, lanes] = jnp.dot(spread[...], query_grad[...], preferred_element_type=F32).astype(BF16)
        key_grad[:, lanes] = (key_acc[...] * SCALE).astype(BF16)
        value_grad[:, lanes] = value_acc[...].astype(BF16)

    @pl.loop(1, experts)
    def _(s):
        grad_from(e ^ s).wait_recv()
        grad_from(e ^ s).wait_send()


def attend_back(slots, back, queries, keys, values, lse, segments, rows, heads_rows, gates, collective_id):
    experts = lax.axis_size("expert")
    choices, (count, width), span = queries.shape[0], back.shape, keys.shape[0]
    blocks = choices // TOPK // Q_ROWS
    f, share = heads_rows.shape[1], D // experts
    dma = pltpu.SemaphoreType.DMA
    return pl.pallas_call(
        functools.partial(attend_back_kernel, experts),
        out_shape=[
            jax.ShapeDtypeStruct((count, width), BF16),
            jax.ShapeDtypeStruct((span, width), BF16),
            jax.ShapeDtypeStruct((span, width), BF16),
            jax.ShapeDtypeStruct((experts, share, f), BF16),
        ],
        in_specs=[VMEM] * 10,
        out_specs=[VMEM] * 4,
        scratch_shapes=[
            pltpu.VMEM((count, choices), BF16),
            pltpu.VMEM((choices, count), BF16),
            pltpu.VMEM((blocks, WINDOW + Q_ROWS, TOPK * Q_ROWS), F32),
            pltpu.VMEM((span, HD), F32),
            pltpu.VMEM((span, HD), F32),
            pltpu.VMEM((choices, HD), BF16),
            pltpu.VMEM((choices, HD), BF16),
            pltpu.VMEM(heads_rows.shape, BF16),
            pltpu.VMEM((experts, share, f), BF16),
        ] + [dma((experts,))] * 2,
        compiler_params=pltpu.CompilerParams(
            collective_id=collective_id, has_side_effects=True, vmem_limit_bytes=63 * 2**20),
        cost_estimate=pl.CostEstimate(flops=10**11, bytes_accessed=10**7, transcendentals=0),
    )(slots, back, queries, keys, values, lse, segments, rows, heads_rows, gates)


def fact_column(facts, k):
    return jnp.concatenate([facts, jnp.zeros((120, 256), F32)], axis=0).T[:CAP, k : k + 1]


def front_kernel(experts, bits, *refs):
    (tokens, gain, slots, routes, routers, segments, w_in, kv_in, wo_in,
     rows, w, window, kv, keys, values, gates, facts_in, grouped, queries, lse, wo,
     back, x, y, facts, spread, gathered, bias, packed, heads,
     f_send, f_recv, v_send, v_recv, z_send, z_recv, t_send, t_recv, y_send, y_recv, w_send, w_recv, k_send, k_recv, n_send, n_recv, own_sem) = refs
    e, t = lax.axis_index("expert"), lax.axis_index("tensor")
    partner = partners(e, experts, True)
    width = x.shape[1]
    cap = rows.shape[1]
    here = tokens.shape[0]
    tensor = 1 << bits
    expert_bits = experts.bit_length() - 1
    pieces = experts * cap // x.shape[0]

    def x_part(j):
        return pl.ds(pl.multiple_of((j // pieces) * cap, cap), cap)

    def cols(d):
        return pl.ds(pl.multiple_of((t ^ d) * width, 128), width)

    def part(j):
        return pl.ds(j * (w.shape[0] // experts), w.shape[0] // experts)

    def block(q, d):
        if isinstance(q, int):
            return window.at[q - experts, :, cols(d)]
        return rows.at[q, :, cols(d)]

    def pass_on(q, d, b):
        far = d | (1 << b)
        return remote(block(q, d), block(q, d), t_send.at[q, far], t_recv.at[q, far], tensor=t ^ (1 << b))

    def passed(q, d):
        return remote(block(q, d), block(q, d), t_send.at[q, d], t_recv.at[q, d], tensor=t ^ (1 << low_bit(d)))

    def stage(q, k):
        bit = bits - k
        for d in range(1, tensor):
            if low_bit(d) == bit:
                passed(q, d).wait_recv()
                for b in reversed(range(bit)):
                    pass_on(q, d, b).start()

    def arrived(j):
        return remote(x.at[x_part(j)], rows.at[j, :, cols(0)], z_send.at[j], z_recv.at[j], expert=j)

    def handed(j):
        return remote(y.at[j], back.at[j], y_send.at[j], y_recv.at[j], expert=j)

    def chunk(d):
        return kv.at[:, part(e ^ d), :]

    def pass_chunk(d, b):
        far = d | (1 << b)
        return remote(chunk(d), chunk(d), k_send.at[far], k_recv.at[far], expert=e ^ (1 << b))

    def passed_chunk(d):
        return remote(chunk(d), chunk(d), k_send.at[d], k_recv.at[d], expert=e ^ (1 << low_bit(d)))

    def chunks(bit):
        for d in range(1, experts):
            if low_bit(d) == bit:
                passed_chunk(d).wait_recv()
                for b in reversed(range(bit)):
                    pass_chunk(d, b).start()

    def two_on(way):
        return remote(window.at[2, :, cols(0)], window.at[0, :, cols(0)], n_send.at[0], n_recv.at[0],
                      expert=lax.rem(e + experts + 2 * way, experts))

    def across():
        return remote(window.at[2 - 2 * (e & 1), :, cols(0)], window.at[1, :, cols(0)], n_send.at[1], n_recv.at[1],
                      expert=e ^ 1)

    own_kv = pltpu.make_async_copy(kv_in, chunk(0), own_sem.at[0])
    own_w = pltpu.make_async_copy(w_in.at[e], w.at[part(e)], own_sem.at[1])
    own_kv.start()
    own_w.start()
    meet(experts, bits)
    for b in reversed(range(expert_bits)):
        remote(kv_in, chunk(0), k_send.at[1 << b], k_recv.at[1 << b], expert=e ^ (1 << b)).start()

    state = tokens[...].astype(F32)
    rate = lax.rsqrt(jnp.mean(state * state, axis=1, keepdims=True) + eps)
    window[2] = (state * rate * gain[...].astype(F32)).astype(BF16)

    @pl.when(e < experts - 2)
    def _():
        two_on(1).start()

    @pl.when(e < 2)
    def _():
        window[0] = jnp.zeros((here, tensor * width), BF16)

    place = lax.broadcasted_iota(jnp.int32, (x.shape[0], here), 0)
    chosen = (place == slots[0:1, pl.ds(0, here)]) | (place == slots[0:1, pl.ds(here, here)])
    x[...] = jnp.dot(chosen.astype(F32).astype(BF16), window[2, :, cols(0)], preferred_element_type=F32).astype(BF16)

    @pl.loop(1, experts)
    def _(s):
        j = partner(s)
        remote(x.at[x_part(j)], rows.at[e, :, cols(0)], z_send.at[j], z_recv.at[e], expert=j).start()

    @pl.loop(1, experts)
    def _(s):
        j = partner(s)
        remote(w_in.at[j], w.at[part(e)], w_send.at[j], w_recv.at[e], expert=j).start()

    rows[e, :, cols(0)] = x[x_part(e), :]

    logits = lax.dot_general(routers[...], window[2], (((1,), (1,)), ((), ())), preferred_element_type=F32)
    row = lax.broadcasted_iota(jnp.int32, logits.shape, 0)
    first, second = (jnp.sum(jnp.where(row == routes[k : k + 1, :], logits, 0.0), axis=0, keepdims=True) for k in (0, 1))
    top = jnp.maximum(first, second)
    first, second = jnp.exp(first - top), jnp.exp(second - top)
    gate = jnp.concatenate([first / (first + second), second / (first + second)], axis=1)
    other = jnp.concatenate([routes[3:4, :], routes[2:3, :]], axis=1).astype(F32)
    high = gate.astype(BF16).astype(F32)
    middle = (gate - high).astype(BF16).astype(F32)
    empty = jnp.zeros((13, 2 * here), F32)
    tables = [jnp.concatenate([high, middle, gate - high - middle, empty], axis=0).astype(BF16),
              jnp.concatenate([other, empty, empty[:2]], axis=0).astype(BF16)]
    for q in range(EXPERTS):
        place = lax.broadcasted_iota(jnp.int32, (256, 2 * here), 0) + q * 256
        fact = [lax.dot_general(table, (place == slots[2 + k : 3 + k, :]).astype(F32).astype(BF16),
                                (((1,), (1,)), ((), ())), preferred_element_type=F32) for k, table in enumerate(tables)]
        row = lax.broadcasted_iota(jnp.int32, (8, 256), 0)
        facts[q] = jnp.where(row == 0, fact[0][0:1] + fact[0][1:2] + fact[0][2:3], jnp.where(row == 1, fact[1][0:1], 0.0))

    @pl.loop(1, experts)
    def _(s):
        j = partner(s)
        remote(facts.at[j // pieces], facts_in.at[e], f_send.at[j], f_recv.at[e], expert=j).start()

    facts_in[e] = facts[e // pieces]
    chunks(expert_bits - 1)
    place_matrices(slots, spread, gathered)
    mask_bias(segments, bias)

    @pl.loop(0, experts + bits)
    def _(i):
        @pl.when(i < experts)
        def _():
            j = partner(i)

            @pl.when(i > 0)
            def _():
                arrived(j).wait_recv()

            for b in reversed(range(bits)):
                pass_on(j, 0, b).start()

        for k in range(1, bits + 1):
            @pl.when((i >= k) & (i < experts + k))
            def _():
                stage(partner(i - k), k)

        @pl.when(i == experts // 2)
        def _():
            @pl.when(e >= 2)
            def _():
                two_on(-1).wait_recv()

            across().start()
            for b in reversed(range(bits)):
                pass_on(experts, 0, b).start()

    for bit in reversed(range(1, expert_bits - 1)):
        chunks(bit)
    across().wait_recv()
    for b in reversed(range(bits)):
        pass_on(experts + 1, 0, b).start()
    own_w.wait()

    @pl.loop(1, experts)
    def _(s):
        q = partner(s)
        remote(w_in.at[q], w.at[part(q)], w_send.at[q], w_recv.at[q], expert=q).wait_recv()

    @pl.loop(0, experts)
    def _(i):
        j = partner(lax.rem(i + 1, experts))
        y[j] = jnp.dot(rows[j], w[...], preferred_element_type=F32).astype(BF16)

        @pl.when(i < experts - 1)
        def _():
            remote(y.at[j], back.at[e], y_send.at[j], y_recv.at[e], expert=j).start()

    back[e] = y[e]

    def map_from(j):
        return remote(wo_in.at[j], wo.at[part(j)], v_send.at[j], v_recv.at[j], expert=j)

    own_wo = pltpu.make_async_copy(wo_in.at[e], wo.at[part(e)], own_sem.at[2])
    own_wo.start()

    @pl.loop(1, experts)
    def _(s):
        j = partner(s)
        remote(wo_in.at[j], wo.at[part(e)], v_send.at[j], v_recv.at[e], expert=j).start()

    for k in range(1, bits + 1):
        for q in range(2):
            stage(experts + q, k)
    chunks(0)
    own_kv.wait()
    for q in range(3):
        for c, out in enumerate((keys, values)):
            out[pl.ds(q * here, here), :] = jnp.dot(window[q], kv[c], preferred_element_type=F32).astype(BF16)

    @pl.loop(1, experts)
    def _(s):
        j = partner(s)
        fact_from = remote(facts.at[j // pieces], facts_in.at[j], f_send.at[j], f_recv.at[j], expert=j)
        fact_from.wait_recv()
        fact_from.wait_send()

    @pl.loop(0, experts)
    def _(j):
        gates[j] = fact_column(facts_in[j], 0)

    @pl.loop(1, experts)
    def _(s):
        handed(partner(s)).wait_recv()

    attend(back, keys, values, grouped, queries, lse, spread, gathered, bias, packed, heads)
    own_wo.wait()

    @pl.loop(1, experts)
    def _(s):
        j = partner(s)
        arrived(j).wait_send()
        handed(j).wait_send()
        remote(w_in.at[j], w.at[part(j)], w_send.at[j], w_recv.at[j], expert=j).wait_send()
        map_from(j).wait_recv()
        map_from(j).wait_send()

    for d in range(1, experts):
        passed_chunk(d).wait_send()
    @pl.when(e < experts - 2)
    def _():
        two_on(1).wait_send()

    across().wait_send()
    for q in range(2):
        for d in range(1, tensor):
            passed(experts + q, d).wait_send()

    @pl.loop(0, experts)
    def _(j):
        for d in range(1, tensor):
            passed(j, d).wait_send()


def front(tokens, gain, slots, routes, routers, segments, w, kv, wo, collective_id):
    experts, tensor = lax.axis_size("expert"), lax.axis_size("tensor")
    bits = tensor.bit_length() - 1
    here = tokens.shape[0]
    f, f_kv = w.shape[2], kv.shape[2]
    dma = pltpu.SemaphoreType.DMA
    outs = [
        ((experts, CAP, D), BF16),
        ((D, f), BF16),
        ((3, here, D), BF16),
        ((2, D, f_kv), BF16),
        ((3 * here, f_kv), BF16),
        ((3 * here, f_kv), BF16),
        ((experts, CAP, 1), F32),
        ((experts, 8, 256), F32),
        ((SLOTS, f_kv), BF16),
        ((TOPK * here, f_kv), BF16),
        ((f_kv // HD, 1, TOPK * here), F32),
        ((D, f), BF16),
    ]
    return pl.pallas_call(
        functools.partial(front_kernel, experts, bits),
        out_shape=[jax.ShapeDtypeStruct(*out) for out in outs],
        in_specs=[VMEM] * 6 + [ANY] * 3,
        out_specs=[VMEM] * 11 + [ANY],
        scratch_shapes=[
            pltpu.VMEM((experts, CAP, f), BF16),
            pltpu.VMEM((SLOTS, D // tensor), BF16),
            pltpu.VMEM((experts, CAP, f), BF16),
            pltpu.VMEM((EXPERTS, 8, 256), F32),
            pltpu.VMEM((SLOTS, TOPK * here), BF16),
            pltpu.VMEM((TOPK * here, SLOTS), BF16),
            pltpu.VMEM((here // Q_ROWS, WINDOW + Q_ROWS, TOPK * Q_ROWS), F32),
            pltpu.VMEM((SLOTS, HD), BF16),
            pltpu.VMEM((TOPK * here, HD), BF16),
        ] + [dma((experts,))] * 6 + [dma((experts + 2, tensor))] * 2 + [dma((experts,))] * 6
        + [dma((2,))] * 2 + [dma((3,))],
        compiler_params=pltpu.CompilerParams(
            collective_id=collective_id, has_side_effects=True, vmem_limit_bytes=63 * 2**20),
        cost_estimate=pl.CostEstimate(flops=10**11, bytes_accessed=10**7, transcendentals=0),
    )(tokens, gain, slots, routes, routers, segments, w, kv, wo)


def scatter_kernel(experts, bits, depth, near, scale, noted, *refs):
    refs = list(refs)
    h_in, w = refs[:2]
    refs = refs[2:]
    gate = refs.pop(0) if scale else None
    notes = refs.pop(0) if noted else None
    if depth:
        key_grad, value_grad, kv_in, rows_in, window_in = refs[:5]
        refs = refs[5:]
    back, h = refs[:2]
    refs = refs[2:]
    if depth:
        owed, map_grad, pair_kept, pair_came = refs[:4]
        refs = refs[4:]
    keep, sent, got, y, t_send, t_recv, y_send, y_recv, h_send, h_recv = refs[:10]
    if depth:
        (kv, rows, window, n_keep, n_sent, n_got, n_in, n_y, n_back, own, total_grad, pair_away,
         n_send, n_recv, o_send, o_recv, p_send, p_recv, l_sem) = refs[10:]
    e, t = lax.axis_index("expert"), lax.axis_index("tensor")
    partner = partners(e, experts, near)
    tensor = 1 << bits
    cap, width = h.shape[1], y.shape[2]
    body = pl.ds(0, cap)
    foot = pl.ds(cap, NOTES)

    def slice_at(d):
        return pl.ds(pl.multiple_of((t ^ d) * width, 128), width)

    def handed(j):
        return remote(y.at[j], back.at[j], y_send.at[j], y_recv.at[j], expert=j)

    def give(j, d):
        return remote(sent.at[j, d - 1], got.at[j, d - 1], t_send.at[j, d], t_recv.at[j, d], tensor=t ^ (1 << low_bit(d)))

    def owe(d):
        return remote(n_sent.at[d - 1], n_got.at[d - 1], n_send.at[d], n_recv.at[d], tensor=t ^ (1 << low_bit(d)))

    def across(c):
        grad = (key_grad, value_grad)[c]
        here = grad.shape[0] // 3
        return remote(grad.at[pl.ds(here, here)], n_in.at[c], o_send.at[c], o_recv.at[c], expert=e ^ 1)

    def two_back(way):
        return remote(n_y, n_back, o_send.at[2], o_recv.at[2], expert=lax.rem(e + experts - 2 * way, experts))

    def own_stage(k):
        for d in range(tensor - 1, -1, -1):
            if d % (1 << k) == 0:
                came = d | (1 << (k - 1))
                owe(came).wait_recv()
                total = n_keep[d // 2] + n_got[came - 1].astype(F32)
                if k == bits:
                    owed[...] = total.astype(BF16)
                elif d & (1 << k):
                    n_sent[d - 1] = total.astype(BF16)
                    owe(d).start()
                else:
                    n_keep[d // 2] = total

    def pair_product(p, c):
        distance = 0
        for b in range(experts.bit_length() - 1):
            distance += ((p >> b) & 1) * ((experts // 2) >> b)
        some = window[:, shares(e ^ distance)]
        return lax.dot_general(some, (key_grad, value_grad)[c][...], (((0,), (0,)), ((), ())),
                               preferred_element_type=F32).astype(BF16)

    def pair_chunk(p):
        return remote(pair_away.at[shares(p)], pair_came.at[shares(p)], p_send.at[p], p_recv.at[p], expert=e ^ 1)

    def shares(q):
        share = map_grad.shape[1]
        return pl.ds(pl.multiple_of(q * share, share), share)

    def row_from(j):
        return remote(h_in.at[j], h.at[j], h_send.at[j], h_recv.at[j], expert=j)

    if depth:
        loads = [pltpu.make_async_copy(a, b, l_sem.at[i])
                 for i, (a, b) in enumerate(((window_in, window), (rows_in, rows), (kv_in, kv)))]
        for load in loads:
            load.start()
    meet(experts, bits)

    @pl.loop(1, experts)
    def _(s):
        j = partner(s)
        remote(h_in.at[j], h.at[e], h_send.at[j], h_recv.at[e], expert=j).start()

    h[e] = h_in[e]
    if depth:
        here = n_in.shape[1]
        f = key_grad.shape[1]
        for c in range(2):
            across(c).start()
        loads[0].wait()

        @pl.loop(0, experts // 2)
        def _(p):
            for c in range(2):
                pair_away[shares(p), pl.ds(c * f, f)] = pair_product(p + experts // 2, c)
            pair_chunk(p).start()

        passing = (e & 1).astype(F32)
        for c, grad in enumerate((key_grad, value_grad)):
            across(c).wait_recv()
            came = n_in[c].astype(F32)
            n_y[c] = (grad[pl.ds(0, here), :].astype(F32) + passing * came).astype(BF16)
            own[c] = grad[pl.ds(2 * here, here), :].astype(F32) + (1.0 - passing) * came
        @pl.when(e >= 2)
        def _():
            two_back(1).start()

        @pl.when(e >= experts - 2)
        def _():
            n_back[...] = jnp.zeros_like(n_back)

        @pl.loop(0, experts // 2)
        def _(p):
            for c in range(2):
                pair_kept[shares(p), pl.ds(c * f, f)] = pair_product(p, c)

        loads[1].wait()

        @pl.loop(1, experts)
        def _(s):
            row_from(partner(s)).wait_recv()

        @pl.loop(0, experts)
        def _(i):
            map_grad[i] = lax.dot_general(
                rows[:, shares(i)], h[...].reshape(experts * cap, h.shape[2]), (((0,), (0,)), ((), ())),
                preferred_element_type=F32).astype(BF16)

    @pl.loop(0, experts + bits)
    def _(i):
        @pl.when(i < experts)
        def _():
            j = partner(i)
            slot = lax.rem(i, bits + 1)
            if not depth:
                @pl.when(i > 0)
                def _():
                    row_from(j).wait_recv()
            for d in range(tensor - 1, -1, -1):
                part = lax.dot_general(
                    h[j], w[slice_at(d), :], (((1,), (1,)), ((), ())), preferred_element_type=F32)
                if scale:
                    part = part * gate[j]
                if d & 1:
                    sent[j, d - 1, body, :] = part.astype(BF16)
                    if noted:
                        sent[j, d - 1, foot, :] = notes[j].astype(BF16)
                    give(j, d).start()
                else:
                    keep[slot, d // 2, body, :] = part
                    if noted:
                        keep[slot, d // 2, foot, :] = notes[j]

        for k in range(1, bits + 1):
            @pl.when((i >= k) & (i < experts + k))
            def _():
                m = i - k
                slot = lax.rem(m, bits + 1)
                j = partner(m)
                for d in range(tensor - 1, -1, -1):
                    if d % (1 << k) == 0:
                        came = d | (1 << (k - 1))
                        give(j, came).wait_recv()
                        total = keep[slot, d // 2] + got[j, came - 1].astype(F32)
                        if k == bits:
                            y[j] = total.astype(BF16)
                        elif d & (1 << k):
                            sent[j, d - 1] = total.astype(BF16)
                            give(j, d).start()
                        else:
                            keep[slot, d // 2] = total
                if k == bits:
                    @pl.when(m == 0)
                    def _():
                        back[e] = y[e]

                    @pl.when(m > 0)
                    def _():
                        remote(y.at[j], back.at[e], y_send.at[j], y_recv.at[e], expert=j).start()

        if depth:
            @pl.when(i == experts - 1)
            def _():
                @pl.when(e < experts - 2)
                def _():
                    two_back(-1).wait_recv()

                loads[2].wait()
                for c in range(2):
                    total_grad[c] = (own[c] + n_back[c].astype(F32)).astype(BF16)
                for d in range(tensor - 1, -1, -1):
                    part = None
                    for c in range(2):
                        term = lax.dot_general(total_grad[c], kv[c, slice_at(d), :], (((1,), (1,)), ((), ())),
                                               preferred_element_type=F32)
                        part = term if part is None else part + term
                    if d & 1:
                        n_sent[d - 1] = part.astype(BF16)
                        owe(d).start()
                    else:
                        n_keep[d // 2] = part

            @pl.when(i == experts)
            def _():
                own_stage(1)

    @pl.loop(1, experts)
    def _(s):
        j = partner(s)
        row_from(j).wait_send()
        handed(j).wait_recv()
        handed(j).wait_send()

    @pl.loop(0, experts)
    def _(j):
        for d in range(1, tensor):
            give(j, d).wait_send()

    if depth:
        for k in range(2, bits + 1):
            own_stage(k)
        for d in range(1, tensor):
            owe(d).wait_send()
        for c in range(2):
            across(c).wait_send()

        @pl.when(e >= 2)
        def _():
            two_back(1).wait_send()

        @pl.loop(0, experts // 2)
        def _(p):
            pair_chunk(p).wait_recv()
            pair_chunk(p).wait_send()


def scatter_rows(h, w, gate=None, notes=None, windows=None, near=True, collective_id=0):
    experts, tensor = lax.axis_size("expert"), lax.axis_size("tensor")
    bits = tensor.bit_length() - 1
    high = CAP + (NOTES if notes is not None else 0)
    width, f = D // tensor, w.shape[1]
    dma = pltpu.SemaphoreType.DMA
    ins = [a for a in (h, w, gate, notes) if a is not None]
    outs = [jax.ShapeDtypeStruct((experts, high, width), BF16), jax.ShapeDtypeStruct(h.shape, BF16)]
    scratch = [
        pltpu.VMEM((bits + 1, tensor // 2, high, width), F32),
        pltpu.VMEM((experts, tensor - 1, high, width), BF16),
        pltpu.VMEM((experts, tensor - 1, high, width), BF16),
        pltpu.VMEM((experts, high, width), BF16),
    ] + [dma((experts, tensor))] * 2 + [dma((experts,))] * 4
    if windows is not None:
        ins += windows
        here = windows[0].shape[0] // 3
        outs.append(jax.ShapeDtypeStruct((here, width), BF16))
        outs.append(jax.ShapeDtypeStruct((experts, D // experts, f), BF16))
        outs += [jax.ShapeDtypeStruct((D // 2, 2 * windows[0].shape[1]), BF16)] * 2
        pair = (2, here, windows[0].shape[1])
        scratch += [
            pltpu.VMEM(windows[2].shape, BF16),
            pltpu.VMEM(windows[3].shape, BF16),
            pltpu.VMEM(windows[4].shape, BF16),
            pltpu.VMEM((tensor // 2, here, width), F32),
            pltpu.VMEM((tensor - 1, here, width), BF16),
            pltpu.VMEM((tensor - 1, here, width), BF16),
            pltpu.VMEM(pair, BF16),
            pltpu.VMEM(pair, BF16),
            pltpu.VMEM(pair, BF16),
            pltpu.VMEM(pair, F32),
            pltpu.VMEM(pair, BF16),
            pltpu.VMEM((D // 2, 2 * windows[0].shape[1]), BF16),
        ] + [dma((tensor,))] * 2 + [dma((3,))] * 2 + [dma((experts,))] * 2 + [dma((3,))]
    return pl.pallas_call(
        functools.partial(scatter_kernel, experts, bits, windows is not None, near, gate is not None, notes is not None),
        out_shape=outs,
        in_specs=[VMEM] * (len(ins) - 3) + [VMEM if windows is None else ANY] * 3,
        out_specs=[VMEM] * (len(outs) - 1) + [VMEM if windows is None else ANY],
        scratch_shapes=scratch,
        compiler_params=pltpu.CompilerParams(
            collective_id=collective_id, has_side_effects=True, vmem_limit_bytes=63 * 2**20),
        cost_estimate=pl.CostEstimate(flops=10**11, bytes_accessed=10**7, transcendentals=0),
    )(*ins)


def ffn_kernel(experts, bits, pieces, *refs):
    (x_cols, dy_all, slots, facts, routers, gate_in, up_in, down_in,
     back, rows_out, dys_out, hidden_out, gate_out, up_out,
     x, dy, dy_near, land, gate_map, up_map, down_map, gate_pre, up_pre, hidden_grad, gates, pulls, low, sent, got, keep,
     z_send, z_recv, t_send, t_recv, r_send, r_recv, y_send, y_recv, w_sem, o_sem) = refs
    e, t = lax.axis_index("expert"), lax.axis_index("tensor")
    tensor = 1 << bits
    pairs = experts // 2
    width = x.shape[1]
    pair_rows = 2 * CAP
    sources = (x, dy)
    results = ((low.at[0], hidden_out), (low.at[1], gate_out), (low.at[2], up_out))

    def first_block(u):
        s = (lax.rem(u, pairs - 1) + 1) * lax.div(u + pairs - 1, pairs)
        return ((e >> 1) ^ s) * 2

    def block(j):
        return pl.ds(pl.multiple_of(j * CAP, CAP), CAP)

    def pair(j):
        return pl.ds(pl.multiple_of(j * CAP, pair_rows), pair_rows)

    def cols(d):
        return pl.ds(pl.multiple_of((t ^ d) * width, 128), width)

    def arrive(a, j):
        return remote(sources[a].at[block(j // pieces)], land.at[a, block(e), cols(0)], z_send.at[a, j], z_recv.at[a, e],
                      expert=j)

    def arrived(a, j):
        return remote(sources[a].at[block(j // pieces)], land.at[a, block(j), cols(0)], z_send.at[a, j], z_recv.at[a, j],
                      expert=j)

    def pass_on(a, j, d, b):
        place, far = land.at[a, block(j), cols(d)], d | (1 << b)
        return remote(place, place, t_send.at[a, j, far], t_recv.at[a, j, far], tensor=t ^ (1 << b))

    def passed(a, j, d):
        place = land.at[a, block(j), cols(d)]
        return remote(place, place, t_send.at[a, j, d], t_recv.at[a, j, d], tensor=t ^ (1 << low_bit(d)))

    def stage(j, k, arrays=(0, 1)):
        for q in range(2):
            for a in arrays:
                for d in range(1, tensor):
                    if low_bit(d) == bits - k:
                        passed(a, j + q, d).wait_recv()
                        for b in reversed(range(bits - k)):
                            pass_on(a, j + q, d, b).start()

    def place_of(u, q):
        return 2 * (u & 1) + q

    def give(u, q, d):
        j = first_block(u) + q
        return remote(sent.at[place_of(u, q), d - 1], got.at[j, d - 1], r_send.at[place_of(u, q), d - 1],
                      r_recv.at[j, d - 1], tensor=t ^ (1 << low_bit(d)))

    final = tensor // 2 - 1

    def hand_back(j):
        return remote(got.at[j, final], back.at[e], y_send.at[j], y_recv.at[e], expert=j)

    def handed(j):
        return remote(got.at[j, final], back.at[j], y_send.at[j], y_recv.at[j], expert=j)

    def sum_stage(u, k):
        j = first_block(u)
        for q in range(2):
            for d in range(tensor - 1, -1, -1):
                if d % (1 << k) == 0:
                    came = d | (1 << (k - 1))
                    give(u, q, came).wait_recv()
                    total = keep[q, d // 2] + got[j + q, came - 1].astype(F32)
                    if k == bits:
                        got[j + q, final] = total.astype(BF16)
                    elif d & (1 << k):
                        sent[place_of(u, q), d - 1] = total.astype(BF16)
                        give(u, q, d).start()
                    else:
                        keep[q, d // 2] = total

    def finish(u):
        j = first_block(u)
        for k in range(2, bits + 1):
            sum_stage(u, k)
        for q in range(2):
            @pl.when(j + q == e)
            def _():
                back[e] = got[e, final]

            @pl.when(j + q != e)
            def _():
                hand_back(j + q).start()

    def to_memory(j):
        copies = [pltpu.make_async_copy(land.at[a, pair(j)], out.at[pair(j)], o_sem.at[a])
                  for a, out in enumerate((rows_out, dys_out))]
        return copies

    def results_to_memory(j):
        return [pltpu.make_async_copy(source, out.at[pair(j)], o_sem.at[2 + i])
                for i, (source, out) in enumerate(results)]

    weights = [pltpu.make_async_copy(a, b, w_sem.at[i])
               for i, (a, b) in enumerate(((gate_in, gate_map), (up_in, up_map), (down_in, down_map)))]
    for copy in weights:
        copy.start()
    here = x_cols.shape[0]
    place = lax.broadcasted_iota(jnp.int32, (x.shape[0], here), 0)
    chosen = (place == slots[:, pl.ds(0, here)]) | (place == slots[:, pl.ds(here, here)])
    chosen = chosen.astype(F32).astype(BF16)
    x[...] = jnp.dot(chosen, x_cols[...], preferred_element_type=F32).astype(BF16)
    dy[...] = jnp.dot(chosen, dy_all[:, cols(0)], preferred_element_type=F32).astype(BF16)

    even = [d for d in range(2, tensor, 2)]

    def near_block(n):
        return first_block((n // 2) * (pairs - 1)) + n % 2

    for n in range(4):
        place = lax.broadcasted_iota(jnp.int32, (CAP, here), 0) + (near_block(n) // pieces) * CAP
        mine = (place == slots[:, pl.ds(0, here)]) | (place == slots[:, pl.ds(here, here)])
        mine = mine.astype(F32).astype(BF16)
        for i, d in enumerate(even):
            dy_near[n, i] = jnp.dot(mine, dy_all[:, cols(d)], preferred_element_type=F32).astype(BF16)

    def straight(n, i):
        j, d = near_block(n), even[i]
        return remote(dy_near.at[n, i], land.at[1, block(e), cols(d)], t_send.at[1, j, d], t_recv.at[1, e, d], expert=j)

    def came_straight(j, d):
        return remote(land.at[1, block(j), cols(d)], land.at[1, block(j), cols(d)], t_send.at[1, j, d], t_recv.at[1, j, d],
                      expert=j)

    meet(experts, bits)
    for a in range(2):
        arrive(a, e ^ 1).start()
    for n in range(2):
        @pl.when(near_block(n) != e)
        def _():
            for i in range(len(even)):
                straight(n, i).start()

    def send_pair(u):
        for q in range(2):
            for a in range(2):
                arrive(a, first_block(u) + q).start()

    def forward_pair(u):
        for q in range(2):
            for a in range(2):
                arrived(a, first_block(u) + q).wait_recv()
                for b in reversed(range(bits)):
                    pass_on(a, first_block(u) + q, 0, b).start()

    def forward_near(j):
        for a in range(2):
            arrived(a, j).wait_recv()
            for b in reversed(range(1 if a else bits)):
                pass_on(a, j, 0, b).start()
        for d in even:
            came_straight(j, d).wait_recv()
            pass_on(1, j, d, 0).start()

    send_pair(1)
    own = first_block(0)
    for a in range(2):
        land[a, block(e), cols(0)] = sources[a][block(e // pieces), :]
        for b in reversed(range(1 if a else bits)):
            pass_on(a, e, 0, b).start()
    for i, d in enumerate(even):
        land[1, block(e), cols(d)] = dy_near[e & 1, i]
        pass_on(1, e, d, 0).start()
    foot = pl.ds(pair_rows, NOTES)
    for d in range(tensor):
        for q in range(4):
            if d:
                sent[q, d - 1, foot, :] = jnp.zeros((NOTES, width), BF16)
        for q in range(2):
            if d % 2 == 0:
                keep[q, d // 2, foot, :] = jnp.zeros((NOTES, width), F32)
    forward_near(e ^ 1)
    for k in range(1, bits):
        stage(own, k, (0,))
    for copy in weights:
        copy.wait()

    @pl.loop(0, pairs)
    def _(u):
        j = first_block(u)
        stage(j, bits)
        for copy in to_memory(j):
            copy.start()
        rows = land[0, pair(j), :]
        gate_pre[...] = jnp.dot(rows, gate_map[...], preferred_element_type=F32)
        up_pre[...] = jnp.dot(rows, up_map[...], preferred_element_type=F32)
        logits = lax.dot_general(rows, routers[...], (((1,), (1,)), ((), ())), preferred_element_type=F32)
        lane = lax.broadcasted_iota(jnp.int32, logits.shape, 1)
        mine = jnp.sum(jnp.where(lane == EXPERTS + e // pieces, logits, 0.0), axis=1, keepdims=True)
        other = jnp.concatenate([fact_column(facts[j + q], 1) for q in range(2)], axis=0) + EXPERTS
        rival = jnp.sum(jnp.where(lane.astype(F32) == other, logits, 0.0), axis=1, keepdims=True)
        top = jnp.maximum(mine, rival)
        mine, rival = jnp.exp(mine - top), jnp.exp(rival - top)
        gates[...] = mine / (mine + rival)

        @pl.when(u < pairs - 2)
        def _():
            forward_pair(u + 1)
            send_pair(u + 2)

        @pl.when(u == pairs - 3)
        def _():
            for n in range(2, 4):
                for i in range(len(even)):
                    straight(n, i).start()

        @pl.when(u == pairs - 2)
        def _():
            for q in range(2):
                forward_near(first_block(u + 1) + q)

        hidden_grad[...] = lax.dot_general(
            land[1, pair(j), :], down_map[...], (((1,), (1,)), ((), ())), preferred_element_type=F32)

        @pl.when(u > 0)
        def _():
            for copy in results_to_memory(j):
                copy.wait()

        @pl.loop(0, pair_rows // 16)
        def _(r):
            some = pl.ds(pl.multiple_of(r * 16, 16), 16)
            gate_here, up_here = gate_pre[some, :], up_pre[some, :]
            weight = gates[some, :]
            sigma = 1.0 / (1.0 + jnp.exp(-gate_here))
            silu = gate_here * sigma
            hidden = silu * up_here
            grad = hidden_grad[some, :]
            pulls[some, :] = jnp.sum(hidden * grad, axis=1, keepdims=True)
            grad = grad * weight
            low[0, some, :] = (hidden * weight).astype(BF16)
            low[1, some, :] = (grad * up_here * (sigma * (1.0 + gate_here * (1.0 - sigma)))).astype(BF16)
            low[2, some, :] = (grad * silu).astype(BF16)

        for copy in results_to_memory(j):
            copy.start()

        @pl.when(u > 0)
        def _():
            finish(u - 1)

        @pl.when(u > 1)
        def _():
            for q in range(2):
                for d in range(1, tensor):
                    give(u - 2, q, d).wait_send()

        noted = []
        for q in range(2):
            some = pl.ds(q * CAP, CAP)
            lane = lax.broadcasted_iota(jnp.int32, (CAP, 128), 1)
            column = jnp.where(lane == 0, pulls[some, :], jnp.where(lane == 1, gates[some, :] / (tensor * pieces), 0.0))
            column = jnp.concatenate([column, jnp.zeros((256 - CAP, 128), F32)], axis=0)
            noted.append(column.T[:NOTES])
        for d in range(tensor - 1, -1, -1):
            grad = lax.dot_general(low[1], gate_map[cols(d), :], (((1,), (1,)), ((), ())), preferred_element_type=F32)
            grad += lax.dot_general(low[2], up_map[cols(d), :], (((1,), (1,)), ((), ())), preferred_element_type=F32)
            out = jnp.dot(low[0], down_map[:, cols(d)], preferred_element_type=F32)
            for q in range(2):
                part = pl.ds(q * CAP, CAP)
                parts = [(pl.ds(0, CAP), slice(None), grad[q * CAP : (q + 1) * CAP]),
                         (pl.ds(CAP, CAP), slice(None), out[q * CAP : (q + 1) * CAP]),
                         (foot, pl.ds(0, 256), noted[q])]
                for place, lanes, value in parts:
                    if d & 1:
                        sent[place_of(u, q), d - 1, place, lanes] = value.astype(BF16)
                    else:
                        keep[q, d // 2, place, lanes] = value
                if d & 1:
                    give(u, q, d).start()
        sum_stage(u, 1)

        @pl.when(u < pairs - 1)
        def _():
            for k in range(1, bits):
                stage(first_block(u + 1), k, (0,))

                @pl.when(u < pairs - 2)
                def _():
                    stage(first_block(u + 1), k, (1,))

        for copy in to_memory(j):
            copy.wait()

    finish(pairs - 1)
    for copy in results_to_memory(0):
        copy.wait()
    for u in range(max(pairs - 2, 0), pairs):
        for q in range(2):
            for d in range(1, tensor):
                give(u, q, d).wait_send()

    @pl.loop(1, experts)
    def _(s):
        j = e ^ s
        for a in range(2):
            arrived(a, j).wait_send()
        handed(j).wait_recv()
        handed(j).wait_send()

    @pl.loop(0, experts)
    def _(j):
        for a in range(2):
            for d in range(1, tensor):
                if a == 0 or d & 1:
                    passed(a, j, d).wait_send()

        @pl.when(j != e)
        def _():
            for d in even:
                passed(1, j, d).wait_send()


def feed_forward(x, dy, slots, facts, routers, gate_map, up_map, down_map, collective_id):
    experts, tensor = lax.axis_size("expert"), lax.axis_size("tensor")
    bits = tensor.bit_length() - 1
    width, hidden = x.shape[1], gate_map.shape[1]
    high = 2 * CAP + NOTES
    count = experts * CAP
    dma = pltpu.SemaphoreType.DMA
    return pl.pallas_call(
        functools.partial(ffn_kernel, experts, bits, experts // EXPERTS),
        out_shape=[jax.ShapeDtypeStruct((experts, high, width), BF16)]
        + [jax.ShapeDtypeStruct((count, D), BF16)] * 2 + [jax.ShapeDtypeStruct((count, hidden), BF16)] * 3,
        in_specs=[VMEM] * 5 + [ANY] * 3,
        out_specs=[VMEM] + [ANY] * 5,
        scratch_shapes=[
            pltpu.VMEM((SLOTS, width), BF16),
            pltpu.VMEM((SLOTS, width), BF16),
            pltpu.VMEM((4, tensor // 2 - 1, CAP, width), BF16),
            pltpu.VMEM((2, count, D), BF16),
            pltpu.VMEM((D, hidden), BF16),
            pltpu.VMEM((D, hidden), BF16),
            pltpu.VMEM((hidden, D), BF16),
            pltpu.VMEM((2 * CAP, hidden), F32),
            pltpu.VMEM((2 * CAP, hidden), F32),
            pltpu.VMEM((2 * CAP, hidden), F32),
            pltpu.VMEM((2 * CAP, 1), F32),
            pltpu.VMEM((2 * CAP, 1), F32),
            pltpu.VMEM((3, 2 * CAP, hidden), BF16),
            pltpu.VMEM((4, tensor - 1, high, width), BF16),
            pltpu.VMEM((experts, tensor - 1, high, width), BF16),
            pltpu.VMEM((2, tensor // 2, high, width), F32),
        ] + [dma((2, experts))] * 2 + [dma((2, experts, tensor))] * 2
        + [dma((4, tensor - 1)), dma((experts, tensor - 1))] + [dma((experts,))] * 2 + [dma((3,)), dma((5,))],
        compiler_params=pltpu.CompilerParams(
            collective_id=collective_id, has_side_effects=True, vmem_limit_bytes=63 * 2**20),
        cost_estimate=pl.CostEstimate(flops=10**11, bytes_accessed=10**7, transcendentals=0),
    )(x, dy, slots, facts, routers, gate_map, up_map, down_map)


def small_kernel(experts, tensor, part, out, came, s_send, s_recv, b_send, b_recv):
    e, t = lax.axis_index("expert"), lax.axis_index("tensor")
    owners = experts // tensor
    width = out.shape[1]
    place = t * owners

    def to_owner(c):
        return remote(part.at[:, pl.ds(c * width, width)], came.at[e], s_send.at[c], s_recv.at[e], expert=place + c)

    barrier = pltpu.get_barrier_semaphore()

    @pl.loop(1, experts)
    def _(s):
        pl.semaphore_signal(barrier, inc=1, device_id={"expert": e ^ s}, device_id_type=MESH)

    @pl.loop(1, tensor)
    def _(s):
        pl.semaphore_signal(barrier, inc=1, device_id={"tensor": t ^ s}, device_id_type=MESH)

    pl.semaphore_wait(barrier, experts + tensor - 2)
    for c in range(owners):
        @pl.when(e != place + c)
        def _():
            to_owner(c).start()

        @pl.when(e == place + c)
        def _():
            came[e] = part[:, c * width : (c + 1) * width]

    @pl.when(e // owners == t)
    def _():
        @pl.loop(1, experts)
        def _(s):
            j = e ^ s
            remote(came.at[j], came.at[j], s_send.at[0], s_recv.at[j], expert=j).wait_recv()

        total = came[0]
        for j in range(1, experts):
            total += came[j]
        out[...] = total

        @pl.loop(1, tensor)
        def _(s):
            remote(out, out, b_send.at[s], b_recv, tensor=t ^ s).start()

        @pl.loop(1, tensor)
        def _(s):
            remote(out, out, b_send.at[s], b_recv, tensor=t ^ s).wait_send()

    @pl.when(e // owners != t)
    def _():
        remote(out, out, b_send.at[0], b_recv, tensor=e // owners).wait_recv()

    for c in range(owners):
        @pl.when(e != place + c)
        def _():
            to_owner(c).wait_send()


def small_sums(part, collective_id):
    experts, tensor = lax.axis_size("expert"), lax.axis_size("tensor")
    n, width = part.shape[0], D // experts
    dma = pltpu.SemaphoreType.DMA
    return pl.pallas_call(
        functools.partial(small_kernel, experts, tensor),
        out_shape=jax.ShapeDtypeStruct((n, width), F32),
        in_specs=[VMEM],
        out_specs=VMEM,
        scratch_shapes=[pltpu.VMEM((experts, n, width), F32), dma((experts // tensor,)), dma((experts,)), dma((tensor,)),
                        dma],
        compiler_params=pltpu.CompilerParams(collective_id=collective_id, has_side_effects=True),
        cost_estimate=pl.CostEstimate(flops=10**10, bytes_accessed=10**5, transcendentals=0),
    )(part)


def dot(left, right, dims):
    return lax.dot_general(left, right, ((dims[0], dims[1]), ((), ())), preferred_element_type=F32)


def mm(left, right):
    return dot(left, right, ((1,), (0,)))


def mm_nt(left, right):
    return dot(left, right, ((1,), (1,)))


def mm_tn(left, right):
    return dot(left, right, ((0,), (0,)))


def swap(blocks):
    return lax.all_to_all(blocks, "expert", split_axis=0, concat_axis=0, tiled=True)


def columns_together(rows):
    return lax.all_gather(rows, "tensor", axis=1, tiled=True)


def columns_summed(rows):
    return lax.psum_scatter(rows, "tensor", scatter_dimension=1, tiled=True)


def slot_numbers(routes):
    flat = routes.T.reshape(-1)
    place = jnp.arange(flat.shape[0], dtype=jnp.int32)
    earlier = (flat[:, None] == flat[None, :]) & (place[None, :] < place[:, None])
    return flat * CAP + jnp.sum(earlier.astype(jnp.int32), axis=1)


def spaced(slots, stride):
    return slots + (slots // CAP) * (stride - CAP)


def place_matrix(slots):
    return (jnp.arange(SLOTS, dtype=jnp.int32)[:, None] == slots[None, :]).astype(BF16)


def token_matrix(slots, stride=CAP, first=0):
    wide = (spaced(slots, stride) + first).reshape(TOPK, -1)
    place = jnp.arange(EXPERTS * stride, dtype=jnp.int32)[:, None]
    return ((place == wide[0][None, :]) | (place == wide[1][None, :])).astype(BF16)


def to_pieces(rows, pieces):
    if pieces == 1:
        return rows
    experts, r, c = rows.shape
    return rows.reshape(experts, r, pieces, c // pieces).transpose(0, 2, 1, 3).reshape(experts * pieces, r, -1)


def from_pieces(rows, pieces):
    if pieces == 1:
        return rows
    both, r, c = rows.shape
    return rows.reshape(both // pieces, pieces, r, c).transpose(0, 2, 1, 3).reshape(both // pieces, r, -1)


def for_pieces(rows, pieces):
    return jnp.repeat(rows, pieces, axis=0) if pieces > 1 else rows


def pick_gates(logits, routes):
    one_hot = (routes[:, :, None] == jnp.arange(EXPERTS, dtype=jnp.int32)[None, None, :]).astype(F32)
    return jax.nn.softmax(jnp.sum(one_hot * logits[:, None, :], axis=2), axis=-1)


def gate_back(gating, pulled, routes):
    inner_sum = gating * (pulled - jnp.sum(gating * pulled, axis=1, keepdims=True))
    one_hot = (routes[:, :, None] == jnp.arange(EXPERTS, dtype=jnp.int32)[None, None, :]).astype(F32)
    return jnp.sum(one_hot * inner_sum[:, :, None], axis=1).astype(BF16)


def per_device(
    tokens,
    segment_ids,
    attn_routes,
    ffn_routes,
    attn_gain,
    ffn_gain,
    routers,
    query_weight,
    output_weight,
    key_value_weight,
    gate_weight,
    up_weight,
    down_weight,
    cotangent,
):
    rows_here = tokens.shape[0]
    expert_count = lax.axis_size("expert")
    tensor_count = lax.axis_size("tensor")
    pieces = expert_count // EXPERTS
    column_count = D // tensor_count
    expert_index = lax.axis_index("expert")
    tensor_index = lax.axis_index("tensor")
    own = (expert_index // pieces).astype(F32)
    head_width = query_weight.shape[2]
    head_count = head_width // HD

    def cols(whole):
        return lax.dynamic_slice_in_dim(whole, tensor_index * column_count, column_count, whole.ndim - 1)

    def group_tokens(token_cols, places):
        return for_pieces(mm(places, token_cols).astype(BF16).reshape(EXPERTS, CAP, -1), pieces)

    def group_choices(choice_rows, places):
        return to_pieces(mm(places, choice_rows).astype(BF16).reshape(EXPERTS, CAP, -1), pieces)

    def choices_of(back, places):
        return mm_tn(places, from_pieces(back, pieces).reshape(SLOTS, -1)).astype(BF16)

    def sums_of(back, places):
        stride = back.shape[1]
        back = back.reshape(EXPERTS, pieces, stride, column_count)
        if pieces > 1:
            total = sum(mm_tn(places, back[:, p].reshape(EXPERTS * stride, -1)) for p in range(pieces))
        else:
            total = mm_tn(places, back.reshape(EXPERTS * stride, -1))
        return total

    def notes_of(*scalars):
        rows = jnp.stack([v.reshape(expert_count, CAP) for v in scalars], axis=1)
        return jnp.pad(rows, ((0, 0), (0, NOTES - len(scalars)), (0, column_count - CAP)))

    def read_notes(back, places, count, first=CAP):
        noted = back[:, first : first + count, :CAP].astype(F32)
        noted = noted.reshape(EXPERTS, pieces, count, CAP).sum(1).transpose(0, 2, 1).reshape(SLOTS, count)
        return mm_tn(places, noted.astype(BF16)).reshape(TOPK, rows_here, count)

    def exchange(away, b):
        return lax.ppermute(away, "expert", [(i, i ^ (1 << b)) for i in range(expert_count)])

    attn_slots, ffn_slots = slot_numbers(attn_routes), slot_numbers(ffn_routes)

    slots = jnp.stack([attn_slots, ffn_slots, spaced(attn_slots, 256), spaced(ffn_slots, 256)])
    segments = jnp.concatenate([jnp.full((WINDOW,), -1, jnp.int32), segment_ids])[None]
    (rows_one, query_map, window, pair_map, keys, values, attn_gate_blocks, facts, heads, queries, log_total,
     output_map) = front(
        tokens, attn_gain[None], slots, jnp.concatenate([attn_routes.T, ffn_routes.T]), routers.T, segments,
        to_pieces(query_weight, pieces), key_value_weight, to_pieces(output_weight, pieces), collective_id=0)
    rows_one, attn_slots, ffn_slots, tokens, attn_gain, ffn_gain, routers, cotangent = lax.optimization_barrier(
        (rows_one, attn_slots, ffn_slots, tokens, attn_gain, ffn_gain, routers, cotangent))
    routers_one, routers_two = routers[:, :EXPERTS], routers[:, EXPERTS:]
    state_in = tokens.astype(F32)
    gain_one = attn_gain.astype(F32)
    gain_two = cols(ffn_gain.astype(F32))
    dy_cols = cols(cotangent)
    token_cols = cols(tokens).astype(F32)
    attn_places, ffn_places = place_matrix(attn_slots), place_matrix(ffn_slots)
    rows_one = rows_one.reshape(-1, D)
    normed_one = window[2]
    window = window.reshape(-1, D)
    attn_back, heads_rows = scatter_rows(
        to_pieces(heads.reshape(EXPERTS, CAP, -1), pieces), output_map, attn_gate_blocks, collective_id=1)
    heads_rows = heads_rows.reshape(expert_count * CAP, -1)
    state = token_cols + sums_of(attn_back, token_matrix(attn_slots))

    mean_two = lax.psum(jnp.sum(state * state, axis=1, keepdims=True), "tensor") / D
    rate_two = lax.rsqrt(mean_two + eps)
    normed_two = (state * rate_two * gain_two).astype(BF16)
    gate_map, up_map, down_map = gate_weight[0], up_weight[0], down_weight[0]
    ffn_back, rows_two, rows_dy, hidden, gate_low, up_low = feed_forward(
        normed_two, cotangent, ffn_slots[None], facts, routers.T, gate_map, up_map, down_map, collective_id=2)
    normed_two_grad = sums_of(ffn_back, token_matrix(ffn_slots, 2 * CAP + NOTES))
    noted = read_notes(ffn_back, ffn_places, 2, 2 * CAP)
    ffn_pull, ffn_gates = noted[:, :, 0].T, noted[:, :, 1].T
    ffn_logit_grad = gate_back(ffn_gates, ffn_pull, ffn_routes)
    normed_two_grad = normed_two_grad + mm_nt(
        ffn_logit_grad, lax.dynamic_slice_in_dim(routers_two, tensor_index * column_count, column_count, 0))
    ffn_router_cols = mm_tn(normed_two, ffn_logit_grad)
    ffn_gain_cols = jnp.sum(normed_two_grad * state * rate_two, axis=0)
    ahead = normed_two_grad * gain_two
    centre = lax.psum(jnp.sum(ahead * state, axis=1, keepdims=True), "tensor") / D
    state_grad = dy_cols.astype(F32) + rate_two * ahead - state * rate_two * rate_two * rate_two * centre

    rows_state, heads_grad, heads_grad_rows = gather_rows(
        group_tokens(state_grad.astype(BF16), token_matrix(attn_slots)), output_map, gate=attn_gate_blocks, collective_id=4)
    rows_state = rows_state.reshape(-1, D)
    heads_grad_rows = heads_grad_rows.reshape(expert_count * CAP, -1)
    attn_notes = notes_of(jnp.sum(heads_grad_rows.astype(F32) * heads_rows.astype(F32), axis=1))
    query_back, key_back, value_back, output_grad = attend_back(
        attn_slots[None], from_pieces(heads_grad, pieces).reshape(SLOTS, -1), queries, keys, values, log_total,
        segments, rows_state, heads_rows, attn_gate_blocks.reshape(-1, 1), collective_id=6)
    output_grad = from_pieces(output_grad, pieces).astype(F32)
    normed_back, unused_rows, owed, query_grad, pair_part, pair_came = scatter_rows(
        to_pieces(query_back.reshape(EXPERTS, CAP, -1), pieces), query_map, notes=attn_notes,
        windows=[key_back, value_back, pair_map, rows_one, window], collective_id=5)
    pair_part = (pair_part.astype(F32) + pair_came.astype(F32)).astype(BF16)
    pair_part, query_grad, rows_two, hidden = lax.optimization_barrier((pair_part, query_grad, rows_two, hidden))
    pair_came = exchange(pair_part[pair_part.shape[0] // 2 :], 1)
    query_grad = swap(query_grad)
    gate_grad = mm_tn(rows_two, gate_low)
    up_grad = mm_tn(rows_two, up_low)
    down_grad = mm_tn(hidden, rows_dy)
    normed_back, owed, gate_grad, up_grad, down_grad, pair_came = lax.optimization_barrier(
        (normed_back, owed, gate_grad, up_grad, down_grad, pair_came))
    normed_grad = sums_of(normed_back, token_matrix(attn_slots, CAP + NOTES)) + owed.astype(F32)
    attn_pull = read_notes(normed_back, attn_places, 1)[:, :, 0].T
    attn_gates = pick_gates(mm(normed_one, routers_one), attn_routes)
    attn_logit_grad = gate_back(attn_gates, attn_pull, attn_routes)
    normed_grad = normed_grad + mm_nt(
        attn_logit_grad, lax.dynamic_slice_in_dim(routers_one, tensor_index * column_count, column_count, 0))
    attn_router_cols = mm_tn(cols(normed_one), attn_logit_grad)
    rate_one = lax.rsqrt(jnp.mean(state_in * state_in, axis=1, keepdims=True) + eps)
    attn_gain_cols = jnp.sum(normed_grad * token_cols * rate_one, axis=0)
    ahead_one = normed_grad * cols(gain_one)
    centre_one = lax.psum(jnp.sum(ahead_one * token_cols, axis=1, keepdims=True), "tensor") / D
    tokens_grad = state_grad + rate_one * ahead_one - token_cols * rate_one * rate_one * rate_one * centre_one
    tokens_grad = columns_together(tokens_grad.astype(BF16)).astype(F32)

    small = jnp.concatenate(
        [attn_router_cols.T, ffn_router_cols.T, attn_gain_cols[None], ffn_gain_cols[None],
         jnp.zeros((6, column_count), F32)], axis=0)
    small = small_sums(small, collective_id=3)
    small = small.T
    query_grad = from_pieces(query_grad, pieces).astype(F32)
    for b in range(2, expert_count.bit_length() - 1):
        pair_part = pair_part[: pair_came.shape[0]].astype(F32) + pair_came.astype(F32)
        pair_part = pair_part.astype(BF16)
        pair_came = exchange(pair_part[pair_part.shape[0] // 2 :], b)
    pair_part = pair_part[: pair_came.shape[0]].astype(F32) + pair_came.astype(F32)
    key_value_grad = pair_part.reshape(D // expert_count, 2, -1).transpose(1, 0, 2)
    ffn_out = sums_of(ffn_back, token_matrix(ffn_slots, 2 * CAP + NOTES, CAP))
    mixed = (state + ffn_out).astype(BF16)
    return (
        mixed,
        tokens_grad,
        small[:, 2 * EXPERTS],
        small[:, 2 * EXPERTS + 1],
        small[:, : 2 * EXPERTS],
        query_grad,
        output_grad,
        key_value_grad,
        gate_grad[None],
        up_grad[None],
        down_grad[None],
    )


def solution(mesh):
    in_specs = (
        P("expert", None),
        P(),
        P("expert", None),
        P("expert", None),
        P(),
        P(),
        P(),
        P(None, "expert", "tensor"),
        P(None, "expert", "tensor"),
        P(None, "expert", "tensor"),
        P("expert", None, "tensor"),
        P("expert", None, "tensor"),
        P("expert", "tensor", None),
        P("expert", None),
    )
    out_specs = (
        P("expert", "tensor"),
        P("expert", None),
        P("expert"),
        P("expert"),
        P("expert", None),
        P(None, "expert", "tensor"),
        P(None, "expert", "tensor"),
        P(None, "expert", "tensor"),
        P("expert", None, "tensor"),
        P("expert", None, "tensor"),
        P("expert", "tensor", None),
    )
    return jax.shard_map(
        per_device, mesh=mesh, in_specs=in_specs, out_specs=out_specs, check_vma=False
    )
```

```python
import functools
import math

import jax
import jax.numpy as jnp
from jax import lax
from jax.experimental import pallas as pl
from jax.experimental.pallas import tpu as pltpu
from jax.sharding import PartitionSpec as P

D = 2048
HD = 128
EXPERTS = 8
TOPK = 2
WINDOW = 1024
CAP = 160
SLOTS = EXPERTS * CAP

eps = 1e-06
masked_value = -1e30
SCALE = HD ** (-0.5)
LOG2E = math.log2(math.e)
Q_ROWS = 256
NOTES = 16
F32 = jnp.float32
BF16 = jnp.bfloat16
MESH = pl.DeviceIdType.MESH
VMEM = pl.BlockSpec(memory_space=pltpu.VMEM)
ANY = pl.BlockSpec(memory_space=pl.ANY)


def remote(src, dst, send, recv, **device):
    return pltpu.make_async_remote_copy(
        src_ref=src, dst_ref=dst, send_sem=send, recv_sem=recv, device_id=device, device_id_type=MESH)


def meet(experts, bits):
    e, t = lax.axis_index("expert"), lax.axis_index("tensor")
    barrier = pltpu.get_barrier_semaphore()

    @pl.loop(1, experts)
    def _(s):
        pl.semaphore_signal(barrier, inc=1, device_id={"expert": e ^ s}, device_id_type=MESH)

    for b in range(bits):
        pl.semaphore_signal(barrier, inc=1, device_id={"tensor": t ^ (1 << b)}, device_id_type=MESH)
    pl.semaphore_wait(barrier, experts - 1 + bits)


def partners(e, experts, near):
    if near:
        return lambda s: e ^ s
    return lambda s: e ^ ((experts - s) & (experts - 1))


def low_bit(d):
    return (d & -d).bit_length() - 1


def gather_kernel(experts, bits, near, multiply, scale, *refs):
    refs = list(refs)
    x = refs.pop(0)
    w = refs.pop(0) if multiply else None
    gate = refs.pop(0) if scale else None
    others = refs.pop(0) if scale else None
    rows = refs.pop(0)
    back = refs.pop(0) if multiply else None
    product = refs.pop(0) if scale else None
    map_grad = refs.pop(0) if scale else None
    y = refs.pop(0) if multiply else None
    z_send, z_recv, t_send, t_recv = refs[:4]
    refs = refs[4:]
    if multiply:
        y_send, y_recv = refs[:2]
    e, t = lax.axis_index("expert"), lax.axis_index("tensor")
    partner = partners(e, experts, near)
    width = x.shape[2]
    tensor = 1 << bits

    def cols(d):
        return pl.ds(pl.multiple_of((t ^ d) * width, 128), width)

    def arrive(j):
        return remote(x.at[j], rows.at[e, :, cols(0)], z_send.at[j], z_recv.at[e], expert=j)

    def arrived(j):
        return remote(x.at[j], rows.at[j, :, cols(0)], z_send.at[j], z_recv.at[j], expert=j)

    def pass_on(j, d, b):
        place = rows.at[j, :, cols(d)]
        far = d | (1 << b)
        return remote(place, place, t_send.at[j, far], t_recv.at[j, far], tensor=t ^ (1 << b))

    def passed(j, d):
        place = rows.at[j, :, cols(d)]
        return remote(place, place, t_send.at[j, d], t_recv.at[j, d], tensor=t ^ (1 << low_bit(d)))

    def hand_back(j):
        return remote(y.at[j], back.at[e], y_send.at[j], y_recv.at[e], expert=j)

    def handed(j):
        return remote(y.at[j], back.at[j], y_send.at[j], y_recv.at[j], expert=j)

    meet(experts, bits)

    @pl.loop(1, experts)
    def _(s):
        arrive(partner(s)).start()

    rows[e, :, cols(0)] = x[e]

    @pl.loop(0, experts + bits)
    def _(i):
        @pl.when(i < experts)
        def _():
            j = partner(i)

            @pl.when(i > 0)
            def _():
                arrived(j).wait_recv()

            for b in reversed(range(bits)):
                pass_on(j, 0, b).start()

        for k in range(1, bits + 1):
            @pl.when((i >= k) & (i < experts + k))
            def _():
                m = i - k
                j = partner(m)
                bit = bits - k
                for d in range(1, tensor):
                    if low_bit(d) == bit:
                        passed(j, d).wait_recv()
                        for b in reversed(range(bit)):
                            pass_on(j, d, b).start()
                if k == bits and multiply:
                    out = jnp.dot(rows[j], w[...], preferred_element_type=F32)
                    if scale:
                        product[j] = out.astype(BF16)
                        out = out * gate[j]
                    y[j] = out.astype(BF16)

                    @pl.when(m == 0)
                    def _():
                        back[e] = y[e]

                    @pl.when(m > 0)
                    def _():
                        hand_back(j).start()

    if scale:
        cap, f = others.shape[1], others.shape[2]
        share = map_grad.shape[1]
        scaled = (others[...].astype(F32) * gate[...]).astype(BF16).reshape(experts * cap, f)

        @pl.loop(0, experts)
        def _(j):
            some = rows[:, :, pl.ds(pl.multiple_of(j * share, share), share)].reshape(experts * cap, share)
            map_grad[j] = lax.dot_general(
                some, scaled, (((0,), (0,)), ((), ())), preferred_element_type=F32).astype(BF16)

    @pl.loop(1, experts)
    def _(s):
        j = partner(s)
        arrived(j).wait_send()
        if multiply:
            handed(j).wait_recv()
            handed(j).wait_send()

    @pl.loop(0, experts)
    def _(j):
        for d in range(1, tensor):
            passed(j, d).wait_send()


def gather_rows(x, w=None, gate=None, others=None, near=True, collective_id=0):
    experts, tensor = lax.axis_size("expert"), lax.axis_size("tensor")
    bits = tensor.bit_length() - 1
    cap, width = x.shape[1], x.shape[2]
    multiply = w is not None
    f = w.shape[-1] if multiply else 0
    ins, specs = [x], [VMEM]
    outs = [jax.ShapeDtypeStruct((experts, cap, width * tensor), BF16)]
    scratch = []
    if multiply:
        ins.append(w)
        specs.append(VMEM)
        outs.append(jax.ShapeDtypeStruct((experts, cap, f), BF16))
    if gate is not None:
        ins += [gate, others]
        specs += [VMEM, VMEM]
        outs.append(jax.ShapeDtypeStruct((experts, cap, f), BF16))
        outs.append(jax.ShapeDtypeStruct((experts, D // experts, f), BF16))
    if multiply:
        scratch.append(pltpu.VMEM((experts, cap, f), BF16))
    scratch += [pltpu.SemaphoreType.DMA((experts,))] * 2 + [pltpu.SemaphoreType.DMA((experts, tensor))] * 2
    if multiply:
        scratch += [pltpu.SemaphoreType.DMA((experts,))] * 2
    return pl.pallas_call(
        functools.partial(gather_kernel, experts, bits, near, multiply, gate is not None),
        out_shape=outs,
        in_specs=specs,
        out_specs=[VMEM] * len(outs),
        scratch_shapes=scratch,
        compiler_params=pltpu.CompilerParams(
            collective_id=collective_id, has_side_effects=True, vmem_limit_bytes=48 * 2**20),
        cost_estimate=pl.CostEstimate(flops=10**11, bytes_accessed=10**7, transcendentals=0),
    )(*ins)


def place_matrices(slots_ref, spread, gathered):
    count, choices = spread.shape
    spread[...] = (lax.broadcasted_iota(jnp.int32, (count, choices), 0) == slots_ref[0:1, :]).astype(F32).astype(BF16)
    gathered[...] = spread[...].T


def mask_bias(segments, bias):
    blocks, span, _ = bias.shape
    here = blocks * Q_ROWS
    e = lax.axis_index("expert")
    query_ids = segments[:, pl.ds(pl.multiple_of(e * here + WINDOW, 128), here)]
    key_row = segments[:, pl.ds(pl.multiple_of(e * here, 128), WINDOW + here)].astype(F32)
    key_ids = jnp.concatenate([key_row, jnp.zeros((7, WINDOW + here), F32)], axis=0).T[:, 0:1].astype(jnp.int32)

    for block in range(blocks):
        first = block * Q_ROWS
        query_place = lax.broadcasted_iota(jnp.int32, (span, Q_ROWS), 1) + WINDOW
        distance = query_place - lax.broadcasted_iota(jnp.int32, (span, Q_ROWS), 0)
        same = key_ids[first : first + span] == query_ids[:, first : first + Q_ROWS]
        allowed = (distance >= 0) & (distance < WINDOW) & same
        part = jnp.where(allowed, 0.0, masked_value)
        for k in range(TOPK):
            bias[block, :, pl.ds(k * Q_ROWS, Q_ROWS)] = part


def of_block(choices, block, lanes):
    rows = choices.shape[0] // TOPK
    return jnp.concatenate([choices[pl.ds(k * rows + block * Q_ROWS, Q_ROWS), lanes] for k in range(TOPK)], axis=0)


def attend(back, keys_ref, values_ref, grouped, queries_ref, lse, spread, gathered, bias, packed, heads):
    blocks, span, _ = bias.shape
    rows = queries_ref.shape[0] // TOPK
    pieces, of_piece = back.shape[0] // EXPERTS, back.shape[2] // HD

    @pl.loop(0, queries_ref.shape[1] // HD)
    def _(head):
        lanes = pl.ds(pl.multiple_of(head * HD, HD), HD)
        inner = pl.ds(pl.multiple_of(lax.rem(head, of_piece) * HD, HD), HD)
        for q in range(EXPERTS):
            packed[pl.ds(q * CAP, CAP), :] = back[q * pieces + lax.div(head, of_piece), :, inner]
        queries_ref[:, lanes] = jnp.dot(gathered[...], packed[...], preferred_element_type=F32).astype(BF16)
        for block in range(blocks):
            place = pl.ds(block * Q_ROWS, span)
            queries = of_block(queries_ref, block, lanes)
            scores = lax.dot_general(
                keys_ref[place, lanes], queries, (((1,), (1,)), ((), ())), preferred_element_type=F32)
            scores = scores * (SCALE * LOG2E) + bias[block]
            top = jnp.max(scores, axis=0, keepdims=True)
            probs = jnp.exp2(scores - top)
            total = jnp.sum(probs, axis=0, keepdims=True)
            out = lax.dot_general(
                values_ref[place, lanes], probs.astype(BF16), (((0,), (0,)), ((), ())), preferred_element_type=F32)
            out = (out * (1.0 / total)).T.astype(BF16)
            for k in range(TOPK):
                heads[pl.ds(k * rows + block * Q_ROWS, Q_ROWS), :] = out[k * Q_ROWS : (k + 1) * Q_ROWS]
            lse[head, :, pl.ds(block * TOPK * Q_ROWS, TOPK * Q_ROWS)] = top + jnp.log2(total)
        grouped[:, lanes] = jnp.dot(spread[...], heads[...], preferred_element_type=F32).astype(BF16)


def attend_back_kernel(experts, *refs):
    (slots, back, queries_ref, keys_ref, values_ref, lse, segments, part_grad,
     grouped, key_grad, value_grad, map_grad,
     spread, gathered, bias, key_acc, value_acc, query_grad, head_grad,
     g_send, g_recv, own_sem) = refs
    e = lax.axis_index("expert")
    blocks, span, _ = bias.shape
    here = queries_ref.shape[0] // TOPK
    def grad_from(j):
        return remote(part_grad.at[j], map_grad.at[j], g_send.at[j], g_recv.at[j], expert=j)

    barrier = pltpu.get_barrier_semaphore()

    @pl.loop(1, experts)
    def _(s):
        pl.semaphore_signal(barrier, inc=1, device_id={"expert": e ^ s}, device_id_type=MESH)

    own = pltpu.make_async_copy(part_grad.at[e], map_grad.at[e], own_sem)
    own.start()
    pl.semaphore_wait(barrier, experts - 1)

    @pl.loop(1, experts)
    def _(s):
        j = e ^ s
        remote(part_grad.at[j], map_grad.at[e], g_send.at[j], g_recv.at[e], expert=j).start()

    place_matrices(slots, spread, gathered)
    mask_bias(segments, bias)

    @pl.loop(0, queries_ref.shape[1] // HD)
    def _(head):
        lanes = pl.ds(pl.multiple_of(head * HD, HD), HD)
        head_grad[...] = jnp.dot(gathered[...], back[:, lanes], preferred_element_type=F32).astype(BF16)
        key_acc[...] = jnp.zeros_like(key_acc)
        value_acc[...] = jnp.zeros_like(value_acc)
        for block in range(blocks):
            queries = of_block(queries_ref, block, lanes)
            grads = of_block(head_grad, block, slice(None))
            place = pl.ds(block * Q_ROWS, span)
            keys, values = keys_ref[place, lanes], values_ref[place, lanes]
            scores = lax.dot_general(keys, queries, (((1,), (1,)), ((), ())), preferred_element_type=F32)
            probs = jnp.exp2(scores * (SCALE * LOG2E) + bias[block]
                             - lse[head, :, pl.ds(block * TOPK * Q_ROWS, TOPK * Q_ROWS)])
            pulled = lax.dot_general(values, grads, (((1,), (1,)), ((), ())), preferred_element_type=F32)
            pulled = probs * pulled
            inner = jnp.sum(pulled, axis=0, keepdims=True)
            score_grad = (pulled - probs * inner).astype(BF16)
            value_acc[place, :] += jnp.dot(probs.astype(BF16), grads, preferred_element_type=F32)
            key_acc[place, :] += jnp.dot(score_grad, queries, preferred_element_type=F32)
            out = lax.dot_general(keys, score_grad, (((0,), (0,)), ((), ())), preferred_element_type=F32)
            out = (out * SCALE).T.astype(BF16)
            for k in range(TOPK):
                query_grad[pl.ds(k * here + block * Q_ROWS, Q_ROWS), :] = out[k * Q_ROWS : (k + 1) * Q_ROWS]
        grouped[:, lanes] = jnp.dot(spread[...], query_grad[...], preferred_element_type=F32).astype(BF16)
        key_grad[:, lanes] = (key_acc[...] * SCALE).astype(BF16)
        value_grad[:, lanes] = value_acc[...].astype(BF16)

    own.wait()

    @pl.loop(1, experts)
    def _(s):
        grad_from(e ^ s).wait_recv()
        grad_from(e ^ s).wait_send()


def attend_back(slots, back, queries, keys, values, lse, segments, map_grad, collective_id):
    experts = lax.axis_size("expert")
    choices, (count, width), span = queries.shape[0], back.shape, keys.shape[0]
    blocks = choices // TOPK // Q_ROWS
    dma = pltpu.SemaphoreType.DMA
    return pl.pallas_call(
        functools.partial(attend_back_kernel, experts),
        out_shape=[
            jax.ShapeDtypeStruct((count, width), BF16),
            jax.ShapeDtypeStruct((span, width), BF16),
            jax.ShapeDtypeStruct((span, width), BF16),
            jax.ShapeDtypeStruct(map_grad.shape, BF16),
        ],
        in_specs=[VMEM] * 7 + [ANY],
        out_specs=[VMEM] * 3 + [ANY],
        scratch_shapes=[
            pltpu.VMEM((count, choices), BF16),
            pltpu.VMEM((choices, count), BF16),
            pltpu.VMEM((blocks, WINDOW + Q_ROWS, TOPK * Q_ROWS), F32),
            pltpu.VMEM((span, HD), F32),
            pltpu.VMEM((span, HD), F32),
            pltpu.VMEM((choices, HD), BF16),
            pltpu.VMEM((choices, HD), BF16),
        ] + [dma((experts,))] * 2 + [dma],
        compiler_params=pltpu.CompilerParams(
            collective_id=collective_id, has_side_effects=True, vmem_limit_bytes=56 * 2**20),
        cost_estimate=pl.CostEstimate(flops=10**11, bytes_accessed=10**7, transcendentals=0),
    )(slots, back, queries, keys, values, lse, segments, map_grad)


def fact_column(facts, k):
    return jnp.concatenate([facts, jnp.zeros((120, 256), F32)], axis=0).T[:CAP, k : k + 1]


def front_kernel(experts, bits, *refs):
    (tokens, gain, slots, routes, routers, segments, w_in, kv_in, wo_in,
     rows, w, window, kv, keys, values, gates, facts_in, grouped, queries, lse, wo,
     back, x, y, facts, spread, gathered, bias, packed, heads,
     f_send, f_recv, v_send, v_recv, z_send, z_recv, t_send, t_recv, y_send, y_recv, w_send, w_recv, k_send, k_recv, n_send, n_recv, own_sem) = refs
    e, t = lax.axis_index("expert"), lax.axis_index("tensor")
    partner = partners(e, experts, True)
    width = x.shape[1]
    cap = rows.shape[1]
    here = tokens.shape[0]
    tensor = 1 << bits
    expert_bits = experts.bit_length() - 1
    pieces = experts * cap // x.shape[0]

    def x_part(j):
        return pl.ds(pl.multiple_of((j // pieces) * cap, cap), cap)

    def cols(d):
        return pl.ds(pl.multiple_of((t ^ d) * width, 128), width)

    def part(j):
        return pl.ds(j * (w.shape[0] // experts), w.shape[0] // experts)

    def block(q, d):
        if isinstance(q, int):
            return window.at[q - experts, :, cols(d)]
        return rows.at[q, :, cols(d)]

    def pass_on(q, d, b):
        far = d | (1 << b)
        return remote(block(q, d), block(q, d), t_send.at[q, far], t_recv.at[q, far], tensor=t ^ (1 << b))

    def passed(q, d):
        return remote(block(q, d), block(q, d), t_send.at[q, d], t_recv.at[q, d], tensor=t ^ (1 << low_bit(d)))

    def stage(q, k):
        bit = bits - k
        for d in range(1, tensor):
            if low_bit(d) == bit:
                passed(q, d).wait_recv()
                for b in reversed(range(bit)):
                    pass_on(q, d, b).start()

    def arrived(j):
        return remote(x.at[x_part(j)], rows.at[j, :, cols(0)], z_send.at[j], z_recv.at[j], expert=j)

    def handed(j):
        return remote(y.at[j], back.at[j], y_send.at[j], y_recv.at[j], expert=j)

    def chunk(d):
        return kv.at[:, part(e ^ d), :]

    def pass_chunk(d, b):
        far = d | (1 << b)
        return remote(chunk(d), chunk(d), k_send.at[far], k_recv.at[far], expert=e ^ (1 << b))

    def passed_chunk(d):
        return remote(chunk(d), chunk(d), k_send.at[d], k_recv.at[d], expert=e ^ (1 << low_bit(d)))

    def chunks(bit):
        for d in range(1, experts):
            if low_bit(d) == bit:
                passed_chunk(d).wait_recv()
                for b in reversed(range(bit)):
                    pass_chunk(d, b).start()

    def two_on(way):
        return remote(window.at[2, :, cols(0)], window.at[0, :, cols(0)], n_send.at[0], n_recv.at[0],
                      expert=lax.rem(e + experts + 2 * way, experts))

    def across():
        return remote(window.at[2 - 2 * (e & 1), :, cols(0)], window.at[1, :, cols(0)], n_send.at[1], n_recv.at[1],
                      expert=e ^ 1)

    own_kv = pltpu.make_async_copy(kv_in, chunk(0), own_sem.at[0])
    own_w = pltpu.make_async_copy(w_in.at[e], w.at[part(e)], own_sem.at[1])
    own_kv.start()
    own_w.start()
    meet(experts, bits)
    for b in reversed(range(expert_bits)):
        remote(kv_in, chunk(0), k_send.at[1 << b], k_recv.at[1 << b], expert=e ^ (1 << b)).start()

    state = tokens[...].astype(F32)
    rate = lax.rsqrt(jnp.mean(state * state, axis=1, keepdims=True) + eps)
    window[2] = (state * rate * gain[...].astype(F32)).astype(BF16)

    @pl.when(e < experts - 2)
    def _():
        two_on(1).start()

    @pl.when(e < 2)
    def _():
        window[0] = jnp.zeros((here, tensor * width), BF16)

    place = lax.broadcasted_iota(jnp.int32, (x.shape[0], here), 0)
    chosen = (place == slots[0:1, pl.ds(0, here)]) | (place == slots[0:1, pl.ds(here, here)])
    x[...] = jnp.dot(chosen.astype(F32).astype(BF16), window[2, :, cols(0)], preferred_element_type=F32).astype(BF16)

    @pl.loop(1, experts)
    def _(s):
        j = partner(s)
        remote(x.at[x_part(j)], rows.at[e, :, cols(0)], z_send.at[j], z_recv.at[e], expert=j).start()

    @pl.loop(1, experts)
    def _(s):
        j = partner(s)
        remote(w_in.at[j], w.at[part(e)], w_send.at[j], w_recv.at[e], expert=j).start()

    rows[e, :, cols(0)] = x[x_part(e), :]

    logits = lax.dot_general(routers[...], window[2], (((1,), (1,)), ((), ())), preferred_element_type=F32)
    row = lax.broadcasted_iota(jnp.int32, logits.shape, 0)
    first, second = (jnp.sum(jnp.where(row == routes[k : k + 1, :], logits, 0.0), axis=0, keepdims=True) for k in (0, 1))
    top = jnp.maximum(first, second)
    first, second = jnp.exp(first - top), jnp.exp(second - top)
    gate = jnp.concatenate([first / (first + second), second / (first + second)], axis=1)
    other = jnp.concatenate([routes[3:4, :], routes[2:3, :]], axis=1).astype(F32)
    high = gate.astype(BF16).astype(F32)
    middle = (gate - high).astype(BF16).astype(F32)
    empty = jnp.zeros((13, 2 * here), F32)
    tables = [jnp.concatenate([high, middle, gate - high - middle, empty], axis=0).astype(BF16),
              jnp.concatenate([other, empty, empty[:2]], axis=0).astype(BF16)]
    for q in range(EXPERTS):
        place = lax.broadcasted_iota(jnp.int32, (256, 2 * here), 0) + q * 256
        fact = [lax.dot_general(table, (place == slots[2 + k : 3 + k, :]).astype(F32).astype(BF16),
                                (((1,), (1,)), ((), ())), preferred_element_type=F32) for k, table in enumerate(tables)]
        row = lax.broadcasted_iota(jnp.int32, (8, 256), 0)
        facts[q] = jnp.where(row == 0, fact[0][0:1] + fact[0][1:2] + fact[0][2:3], jnp.where(row == 1, fact[1][0:1], 0.0))

    @pl.loop(1, experts)
    def _(s):
        j = partner(s)
        remote(facts.at[j // pieces], facts_in.at[e], f_send.at[j], f_recv.at[e], expert=j).start()

    facts_in[e] = facts[e // pieces]
    chunks(expert_bits - 1)
    place_matrices(slots, spread, gathered)
    mask_bias(segments, bias)

    @pl.loop(0, experts + bits)
    def _(i):
        @pl.when(i < experts)
        def _():
            j = partner(i)

            @pl.when(i > 0)
            def _():
                arrived(j).wait_recv()

            for b in reversed(range(bits)):
                pass_on(j, 0, b).start()

        for k in range(1, bits + 1):
            @pl.when((i >= k) & (i < experts + k))
            def _():
                stage(partner(i - k), k)

        @pl.when(i == experts // 2)
        def _():
            @pl.when(e >= 2)
            def _():
                two_on(-1).wait_recv()

            across().start()
            for b in reversed(range(bits)):
                pass_on(experts, 0, b).start()

    for bit in reversed(range(1, expert_bits - 1)):
        chunks(bit)
    across().wait_recv()
    for b in reversed(range(bits)):
        pass_on(experts + 1, 0, b).start()
    own_w.wait()

    @pl.loop(1, experts)
    def _(s):
        q = partner(s)
        remote(w_in.at[q], w.at[part(q)], w_send.at[q], w_recv.at[q], expert=q).wait_recv()

    @pl.loop(0, experts)
    def _(i):
        j = partner(lax.rem(i + 1, experts))
        y[j] = jnp.dot(rows[j], w[...], preferred_element_type=F32).astype(BF16)

        @pl.when(i < experts - 1)
        def _():
            remote(y.at[j], back.at[e], y_send.at[j], y_recv.at[e], expert=j).start()

    back[e] = y[e]

    def map_from(j):
        return remote(wo_in.at[j], wo.at[part(j)], v_send.at[j], v_recv.at[j], expert=j)

    own_wo = pltpu.make_async_copy(wo_in.at[e], wo.at[part(e)], own_sem.at[2])
    own_wo.start()

    @pl.loop(1, experts)
    def _(s):
        j = partner(s)
        remote(wo_in.at[j], wo.at[part(e)], v_send.at[j], v_recv.at[e], expert=j).start()

    for k in range(1, bits + 1):
        for q in range(2):
            stage(experts + q, k)
    chunks(0)
    own_kv.wait()
    for q in range(3):
        for c, out in enumerate((keys, values)):
            out[pl.ds(q * here, here), :] = jnp.dot(window[q], kv[c], preferred_element_type=F32).astype(BF16)

    @pl.loop(1, experts)
    def _(s):
        j = partner(s)
        fact_from = remote(facts.at[j // pieces], facts_in.at[j], f_send.at[j], f_recv.at[j], expert=j)
        fact_from.wait_recv()
        fact_from.wait_send()

    @pl.loop(0, experts)
    def _(j):
        gates[j] = fact_column(facts_in[j], 0)

    @pl.loop(1, experts)
    def _(s):
        handed(partner(s)).wait_recv()

    attend(back, keys, values, grouped, queries, lse, spread, gathered, bias, packed, heads)
    own_wo.wait()

    @pl.loop(1, experts)
    def _(s):
        j = partner(s)
        arrived(j).wait_send()
        handed(j).wait_send()
        remote(w_in.at[j], w.at[part(j)], w_send.at[j], w_recv.at[j], expert=j).wait_send()
        map_from(j).wait_recv()
        map_from(j).wait_send()

    for d in range(1, experts):
        passed_chunk(d).wait_send()
    @pl.when(e < experts - 2)
    def _():
        two_on(1).wait_send()

    across().wait_send()
    for q in range(2):
        for d in range(1, tensor):
            passed(experts + q, d).wait_send()

    @pl.loop(0, experts)
    def _(j):
        for d in range(1, tensor):
            passed(j, d).wait_send()


def front(tokens, gain, slots, routes, routers, segments, w, kv, wo, collective_id):
    experts, tensor = lax.axis_size("expert"), lax.axis_size("tensor")
    bits = tensor.bit_length() - 1
    here = tokens.shape[0]
    f, f_kv = w.shape[2], kv.shape[2]
    dma = pltpu.SemaphoreType.DMA
    outs = [
        ((experts, CAP, D), BF16),
        ((D, f), BF16),
        ((3, here, D), BF16),
        ((2, D, f_kv), BF16),
        ((3 * here, f_kv), BF16),
        ((3 * here, f_kv), BF16),
        ((experts, CAP, 1), F32),
        ((experts, 8, 256), F32),
        ((SLOTS, f_kv), BF16),
        ((TOPK * here, f_kv), BF16),
        ((f_kv // HD, 1, TOPK * here), F32),
        ((D, f), BF16),
    ]
    return pl.pallas_call(
        functools.partial(front_kernel, experts, bits),
        out_shape=[jax.ShapeDtypeStruct(*out) for out in outs],
        in_specs=[VMEM] * 6 + [ANY] * 3,
        out_specs=[VMEM] * 11 + [ANY],
        scratch_shapes=[
            pltpu.VMEM((experts, CAP, f), BF16),
            pltpu.VMEM((SLOTS, D // tensor), BF16),
            pltpu.VMEM((experts, CAP, f), BF16),
            pltpu.VMEM((EXPERTS, 8, 256), F32),
            pltpu.VMEM((SLOTS, TOPK * here), BF16),
            pltpu.VMEM((TOPK * here, SLOTS), BF16),
            pltpu.VMEM((here // Q_ROWS, WINDOW + Q_ROWS, TOPK * Q_ROWS), F32),
            pltpu.VMEM((SLOTS, HD), BF16),
            pltpu.VMEM((TOPK * here, HD), BF16),
        ] + [dma((experts,))] * 6 + [dma((experts + 2, tensor))] * 2 + [dma((experts,))] * 6
        + [dma((2,))] * 2 + [dma((3,))],
        compiler_params=pltpu.CompilerParams(
            collective_id=collective_id, has_side_effects=True, vmem_limit_bytes=63 * 2**20),
        cost_estimate=pl.CostEstimate(flops=10**11, bytes_accessed=10**7, transcendentals=0),
    )(tokens, gain, slots, routes, routers, segments, w, kv, wo)


def scatter_kernel(experts, bits, depth, near, scale, noted, *refs):
    refs = list(refs)
    h_in, w = refs[:2]
    refs = refs[2:]
    gate = refs.pop(0) if scale else None
    notes = refs.pop(0) if noted else None
    if depth:
        key_grad, value_grad, kv_in, rows_in, window_in = refs[:5]
        refs = refs[5:]
    back, h = refs[:2]
    refs = refs[2:]
    if depth:
        owed, map_grad, pair_kept, pair_came = refs[:4]
        refs = refs[4:]
    keep, sent, got, y, t_send, t_recv, y_send, y_recv, h_send, h_recv = refs[:10]
    if depth:
        (kv, rows, window, n_keep, n_sent, n_got, n_in, n_y, n_back, own, total_grad, pair_away,
         n_send, n_recv, o_send, o_recv, p_send, p_recv, l_sem) = refs[10:]
    e, t = lax.axis_index("expert"), lax.axis_index("tensor")
    partner = partners(e, experts, near)
    tensor = 1 << bits
    cap, width = h.shape[1], y.shape[2]
    body = pl.ds(0, cap)
    foot = pl.ds(cap, NOTES)

    def slice_at(d):
        return pl.ds(pl.multiple_of((t ^ d) * width, 128), width)

    def handed(j):
        return remote(y.at[j], back.at[j], y_send.at[j], y_recv.at[j], expert=j)

    def give(j, d):
        return remote(sent.at[j, d - 1], got.at[j, d - 1], t_send.at[j, d], t_recv.at[j, d], tensor=t ^ (1 << low_bit(d)))

    def owe(d):
        return remote(n_sent.at[d - 1], n_got.at[d - 1], n_send.at[d], n_recv.at[d], tensor=t ^ (1 << low_bit(d)))

    def across(c):
        grad = (key_grad, value_grad)[c]
        here = grad.shape[0] // 3
        return remote(grad.at[pl.ds(here, here)], n_in.at[c], o_send.at[c], o_recv.at[c], expert=e ^ 1)

    def two_back(way):
        return remote(n_y, n_back, o_send.at[2], o_recv.at[2], expert=lax.rem(e + experts - 2 * way, experts))

    def own_stage(k):
        for d in range(tensor - 1, -1, -1):
            if d % (1 << k) == 0:
                came = d | (1 << (k - 1))
                owe(came).wait_recv()
                total = n_keep[d // 2] + n_got[came - 1].astype(F32)
                if k == bits:
                    owed[...] = total.astype(BF16)
                elif d & (1 << k):
                    n_sent[d - 1] = total.astype(BF16)
                    owe(d).start()
                else:
                    n_keep[d // 2] = total

    order = [list(range(experts.bit_length() - 1)) for _ in range(2)]
    order[1][:2] = [1, 0]

    def pair_product(p, c):
        distance = 0
        for i, b in enumerate(reversed(order[c])):
            distance += ((p >> i) & 1) * (1 << b)
        some = window[:, shares(e ^ distance)]
        return lax.dot_general(some, (key_grad, value_grad)[c][...], (((0,), (0,)), ((), ())),
                               preferred_element_type=F32).astype(BF16)

    def pair_chunk(p, c):
        f = key_grad.shape[1]
        place, lanes = shares(p), pl.ds(c * f, f)
        return remote(pair_away.at[place, lanes], pair_came.at[place, lanes], p_send.at[c, p], p_recv.at[c, p],
                      expert=e ^ (1 << order[c][0]))

    def shares(q):
        share = map_grad.shape[1]
        return pl.ds(pl.multiple_of(q * share, share), share)

    def row_from(j):
        return remote(h_in.at[j], h.at[j], h_send.at[j], h_recv.at[j], expert=j)

    if depth:
        loads = [pltpu.make_async_copy(a, b, l_sem.at[i])
                 for i, (a, b) in enumerate(((window_in, window), (rows_in, rows), (kv_in, kv)))]
        for load in loads:
            load.start()
    meet(experts, bits)

    @pl.loop(1, experts)
    def _(s):
        j = partner(s)
        remote(h_in.at[j], h.at[e], h_send.at[j], h_recv.at[e], expert=j).start()

    h[e] = h_in[e]
    if depth:
        here = n_in.shape[1]
        f = key_grad.shape[1]
        for c in range(2):
            across(c).start()
        loads[0].wait()

        @pl.loop(0, experts // 2)
        def _(p):
            for c in range(2):
                pair_away[shares(p), pl.ds(c * f, f)] = pair_product(p + experts // 2, c)
                pair_chunk(p, c).start()

        passing = (e & 1).astype(F32)
        for c, grad in enumerate((key_grad, value_grad)):
            across(c).wait_recv()
            came = n_in[c].astype(F32)
            n_y[c] = (grad[pl.ds(0, here), :].astype(F32) + passing * came).astype(BF16)
            own[c] = grad[pl.ds(2 * here, here), :].astype(F32) + (1.0 - passing) * came
        @pl.when(e >= 2)
        def _():
            two_back(1).start()

        @pl.when(e >= experts - 2)
        def _():
            n_back[...] = jnp.zeros_like(n_back)

        @pl.loop(0, experts // 2)
        def _(p):
            for c in range(2):
                pair_kept[shares(p), pl.ds(c * f, f)] = pair_product(p, c)

    @pl.loop(0, experts + bits)
    def _(i):
        @pl.when(i < experts)
        def _():
            j = partner(i)
            slot = lax.rem(i, bits + 1)

            @pl.when(i > 0)
            def _():
                row_from(j).wait_recv()

            for d in range(tensor - 1, -1, -1):
                part = lax.dot_general(
                    h[j], w[slice_at(d), :], (((1,), (1,)), ((), ())), preferred_element_type=F32)
                if scale:
                    part = part * gate[j]
                if d & 1:
                    sent[j, d - 1, body, :] = part.astype(BF16)
                    if noted:
                        sent[j, d - 1, foot, :] = notes[j].astype(BF16)
                    give(j, d).start()
                else:
                    keep[slot, d // 2, body, :] = part
                    if noted:
                        keep[slot, d // 2, foot, :] = notes[j]

        for k in range(1, bits + 1):
            @pl.when((i >= k) & (i < experts + k))
            def _():
                m = i - k
                slot = lax.rem(m, bits + 1)
                j = partner(m)
                for d in range(tensor - 1, -1, -1):
                    if d % (1 << k) == 0:
                        came = d | (1 << (k - 1))
                        give(j, came).wait_recv()
                        total = keep[slot, d // 2] + got[j, came - 1].astype(F32)
                        if k == bits:
                            y[j] = total.astype(BF16)
                        elif d & (1 << k):
                            sent[j, d - 1] = total.astype(BF16)
                            give(j, d).start()
                        else:
                            keep[slot, d // 2] = total
                if k == bits:
                    @pl.when(m == 0)
                    def _():
                        back[e] = y[e]

                    @pl.when(m > 0)
                    def _():
                        remote(y.at[j], back.at[e], y_send.at[j], y_recv.at[e], expert=j).start()

        if depth:
            @pl.when(i == experts - 1)
            def _():
                @pl.when(e < experts - 2)
                def _():
                    two_back(-1).wait_recv()

                loads[2].wait()
                for c in range(2):
                    total_grad[c] = (own[c] + n_back[c].astype(F32)).astype(BF16)
                for d in range(tensor - 1, -1, -1):
                    part = None
                    for c in range(2):
                        term = lax.dot_general(total_grad[c], kv[c, slice_at(d), :], (((1,), (1,)), ((), ())),
                                               preferred_element_type=F32)
                        part = term if part is None else part + term
                    if d & 1:
                        n_sent[d - 1] = part.astype(BF16)
                        owe(d).start()
                    else:
                        n_keep[d // 2] = part

            @pl.when(i == experts)
            def _():
                own_stage(1)

    if depth:
        for k in range(2, bits + 1):
            own_stage(k)
        loads[1].wait()

        @pl.loop(0, experts)
        def _(i):
            map_grad[i] = lax.dot_general(
                rows[:, shares(i)], h[...].reshape(experts * cap, h.shape[2]), (((0,), (0,)), ((), ())),
                preferred_element_type=F32).astype(BF16)

    @pl.loop(1, experts)
    def _(s):
        j = partner(s)
        row_from(j).wait_send()
        handed(j).wait_recv()
        handed(j).wait_send()

    @pl.loop(0, experts)
    def _(j):
        for d in range(1, tensor):
            give(j, d).wait_send()

    if depth:
        for d in range(1, tensor):
            owe(d).wait_send()
        for c in range(2):
            across(c).wait_send()

        @pl.when(e >= 2)
        def _():
            two_back(1).wait_send()

        @pl.loop(0, experts // 2)
        def _(p):
            for c in range(2):
                pair_chunk(p, c).wait_recv()
                pair_chunk(p, c).wait_send()


def scatter_rows(h, w, gate=None, notes=None, windows=None, near=True, collective_id=0):
    experts, tensor = lax.axis_size("expert"), lax.axis_size("tensor")
    bits = tensor.bit_length() - 1
    high = CAP + (NOTES if notes is not None else 0)
    width, f = D // tensor, w.shape[1]
    dma = pltpu.SemaphoreType.DMA
    ins = [a for a in (h, w, gate, notes) if a is not None]
    outs = [jax.ShapeDtypeStruct((experts, high, width), BF16), jax.ShapeDtypeStruct(h.shape, BF16)]
    scratch = [
        pltpu.VMEM((bits + 1, tensor // 2, high, width), F32),
        pltpu.VMEM((experts, tensor - 1, high, width), BF16),
        pltpu.VMEM((experts, tensor - 1, high, width), BF16),
        pltpu.VMEM((experts, high, width), BF16),
    ] + [dma((experts, tensor))] * 2 + [dma((experts,))] * 4
    if windows is not None:
        ins += windows
        here = windows[0].shape[0] // 3
        outs.append(jax.ShapeDtypeStruct((here, width), BF16))
        outs.append(jax.ShapeDtypeStruct((experts, D // experts, f), BF16))
        outs += [jax.ShapeDtypeStruct((D // 2, 2 * windows[0].shape[1]), BF16)] * 2
        pair = (2, here, windows[0].shape[1])
        scratch += [
            pltpu.VMEM(windows[2].shape, BF16),
            pltpu.VMEM(windows[3].shape, BF16),
            pltpu.VMEM(windows[4].shape, BF16),
            pltpu.VMEM((tensor // 2, here, width), F32),
            pltpu.VMEM((tensor - 1, here, width), BF16),
            pltpu.VMEM((tensor - 1, here, width), BF16),
            pltpu.VMEM(pair, BF16),
            pltpu.VMEM(pair, BF16),
            pltpu.VMEM(pair, BF16),
            pltpu.VMEM(pair, F32),
            pltpu.VMEM(pair, BF16),
            pltpu.VMEM((D // 2, 2 * windows[0].shape[1]), BF16),
        ] + [dma((tensor,))] * 2 + [dma((3,))] * 2 + [dma((2, experts))] * 2 + [dma((3,))]
    return pl.pallas_call(
        functools.partial(scatter_kernel, experts, bits, windows is not None, near, gate is not None, notes is not None),
        out_shape=outs,
        in_specs=[VMEM] * (len(ins) - 3) + [VMEM if windows is None else ANY] * 3,
        out_specs=[VMEM] * (len(outs) - 1) + [VMEM if windows is None else ANY],
        scratch_shapes=scratch,
        compiler_params=pltpu.CompilerParams(
            collective_id=collective_id, has_side_effects=True, vmem_limit_bytes=63 * 2**20),
        cost_estimate=pl.CostEstimate(flops=10**11, bytes_accessed=10**7, transcendentals=0),
    )(*ins)


def ffn_kernel(experts, bits, pieces, *refs):
    (x_cols, dy_all, slots, facts, routers, gate_in, up_in, down_in,
     back, rows_out, dys_out, hidden_out, gate_out, up_out,
     x, dy, dy_near, land, gate_map, up_map, down_map, gate_pre, up_pre, hidden_grad, gates, pulls, moments, own_logits, low, sent, got, keep,
     z_send, z_recv, t_send, t_recv, r_send, r_recv, y_send, y_recv, w_sem, o_sem) = refs
    e, t = lax.axis_index("expert"), lax.axis_index("tensor")
    tensor = 1 << bits
    pairs = experts // 2
    width = x.shape[1]
    pair_rows = 2 * CAP
    sources = (x, dy)
    results = ((low.at[0], hidden_out), (low.at[1], gate_out), (low.at[2], up_out))

    def first_block(u):
        s = (lax.rem(u, pairs - 1) + 1) * lax.div(u + pairs - 1, pairs)
        return ((e >> 1) ^ s) * 2

    def block(j):
        return pl.ds(pl.multiple_of(j * CAP, CAP), CAP)

    def pair(j):
        return pl.ds(pl.multiple_of(j * CAP, pair_rows), pair_rows)

    def cols(d):
        return pl.ds(pl.multiple_of((t ^ d) * width, 128), width)

    def arrive(a, j):
        return remote(sources[a].at[block(j // pieces)], land.at[a, block(e), cols(0)], z_send.at[a, j], z_recv.at[a, e],
                      expert=j)

    def arrived(a, j):
        return remote(sources[a].at[block(j // pieces)], land.at[a, block(j), cols(0)], z_send.at[a, j], z_recv.at[a, j],
                      expert=j)

    def pass_on(a, j, d, b):
        place, far = land.at[a, block(j), cols(d)], d | (1 << b)
        return remote(place, place, t_send.at[a, j, far], t_recv.at[a, j, far], tensor=t ^ (1 << b))

    def passed(a, j, d):
        place = land.at[a, block(j), cols(d)]
        return remote(place, place, t_send.at[a, j, d], t_recv.at[a, j, d], tensor=t ^ (1 << low_bit(d)))

    def stage(j, k, arrays=(0, 1)):
        for q in range(2):
            for a in arrays:
                for d in range(1, tensor):
                    if low_bit(d) == bits - k:
                        passed(a, j + q, d).wait_recv()
                        for b in reversed(range(bits - k)):
                            pass_on(a, j + q, d, b).start()

    def place_of(u, q):
        return 2 * (u & 1) + q

    def give(u, q, d):
        j = first_block(u) + q
        return remote(sent.at[place_of(u, q), d - 1], got.at[j, d - 1], r_send.at[place_of(u, q), d - 1],
                      r_recv.at[j, d - 1], tensor=t ^ (1 << low_bit(d)))

    final = tensor // 2 - 1

    def hand_back(j):
        return remote(got.at[j, final], back.at[e], y_send.at[j], y_recv.at[e], expert=j)

    def handed(j):
        return remote(got.at[j, final], back.at[j], y_send.at[j], y_recv.at[j], expert=j)

    def sum_stage(u, k):
        j = first_block(u)
        for q in range(2):
            for d in range(tensor - 1, -1, -1):
                if d % (1 << k) == 0:
                    came = d | (1 << (k - 1))
                    give(u, q, came).wait_recv()
                    total = keep[q, d // 2] + got[j + q, came - 1].astype(F32)
                    if k == bits:
                        got[j + q, final] = total.astype(BF16)
                    elif d & (1 << k):
                        sent[place_of(u, q), d - 1] = total.astype(BF16)
                        give(u, q, d).start()
                    else:
                        keep[q, d // 2] = total

    def finish(u):
        j = first_block(u)
        for k in range(2, bits + 1):
            sum_stage(u, k)
        for q in range(2):
            @pl.when(j + q == e)
            def _():
                back[e] = got[e, final]

            @pl.when(j + q != e)
            def _():
                hand_back(j + q).start()

    def to_memory(j):
        copies = [pltpu.make_async_copy(land.at[a, pair(j)], out.at[pair(j)], o_sem.at[a])
                  for a, out in enumerate((rows_out, dys_out))]
        return copies

    def results_to_memory(j):
        return [pltpu.make_async_copy(source, out.at[pair(j)], o_sem.at[2 + i])
                for i, (source, out) in enumerate(results)]

    weights = [pltpu.make_async_copy(a, b, w_sem.at[i])
               for i, (a, b) in enumerate(((gate_in, gate_map), (up_in, up_map), (down_in, down_map)))]
    for copy in weights:
        copy.start()
    here = x_cols.shape[0]
    place = lax.broadcasted_iota(jnp.int32, (x.shape[0], here), 0)
    chosen = (place == slots[:, pl.ds(0, here)]) | (place == slots[:, pl.ds(here, here)])
    chosen = chosen.astype(F32).astype(BF16)
    x[...] = jnp.dot(chosen, x_cols[...], preferred_element_type=F32).astype(BF16)
    dy[...] = jnp.dot(chosen, dy_all[:, cols(0)], preferred_element_type=F32).astype(BF16)

    even = [d for d in range(2, tensor, 2)]

    def near_block(n):
        return first_block((n // 2) * (pairs - 1)) + n % 2

    for n in range(4):
        place = lax.broadcasted_iota(jnp.int32, (CAP, here), 0) + (near_block(n) // pieces) * CAP
        mine = (place == slots[:, pl.ds(0, here)]) | (place == slots[:, pl.ds(here, here)])
        mine = mine.astype(F32).astype(BF16)
        for i, d in enumerate(even):
            dy_near[n, i] = jnp.dot(mine, dy_all[:, cols(d)], preferred_element_type=F32).astype(BF16)

    def straight(n, i):
        j, d = near_block(n), even[i]
        return remote(dy_near.at[n, i], land.at[1, block(e), cols(d)], t_send.at[1, j, d], t_recv.at[1, e, d], expert=j)

    def came_straight(j, d):
        return remote(land.at[1, block(j), cols(d)], land.at[1, block(j), cols(d)], t_send.at[1, j, d], t_recv.at[1, j, d],
                      expert=j)

    meet(experts, bits)
    for a in range(2):
        arrive(a, e ^ 1).start()
    for n in range(2):
        @pl.when(near_block(n) != e)
        def _():
            for i in range(len(even)):
                straight(n, i).start()

    def send_pair(u):
        for q in range(2):
            for a in range(2):
                arrive(a, first_block(u) + q).start()

    def forward_pair(u):
        for q in range(2):
            for a in range(2):
                arrived(a, first_block(u) + q).wait_recv()
                for b in reversed(range(bits)):
                    pass_on(a, first_block(u) + q, 0, b).start()

    def forward_near(j):
        for a in range(2):
            arrived(a, j).wait_recv()
            for b in reversed(range(1 if a else bits)):
                pass_on(a, j, 0, b).start()
        for d in even:
            came_straight(j, d).wait_recv()
            pass_on(1, j, d, 0).start()

    send_pair(1)
    own = first_block(0)
    for a in range(2):
        land[a, block(e), cols(0)] = sources[a][block(e // pieces), :]
        for b in reversed(range(1 if a else bits)):
            pass_on(a, e, 0, b).start()
    for i, d in enumerate(even):
        land[1, block(e), cols(d)] = dy_near[e & 1, i]
        pass_on(1, e, d, 0).start()
    foot = pl.ds(pair_rows, NOTES)
    for d in range(tensor):
        for q in range(4):
            if d:
                sent[q, d - 1, foot, :] = jnp.zeros((NOTES, width), BF16)
        for q in range(2):
            if d % 2 == 0:
                keep[q, d // 2, foot, :] = jnp.zeros((NOTES, width), F32)
    forward_near(e ^ 1)
    for k in range(1, bits):
        stage(own, k, (0,))
    for copy in weights:
        copy.wait()

    @pl.loop(0, pairs)
    def _(u):
        j = first_block(u)
        stage(j, bits)
        for copy in to_memory(j):
            copy.start()
        rows = land[0, pair(j), :]
        gate_pre[...] = jnp.dot(rows, gate_map[...], preferred_element_type=F32)
        up_pre[...] = jnp.dot(rows, up_map[...], preferred_element_type=F32)
        logits = lax.dot_general(rows, routers[...], (((1,), (1,)), ((), ())), preferred_element_type=F32)
        lane = lax.broadcasted_iota(jnp.int32, logits.shape, 1)
        mine = jnp.sum(jnp.where(lane == EXPERTS + e // pieces, logits, 0.0), axis=1, keepdims=True)
        other = jnp.concatenate([fact_column(facts[j + q], 1) for q in range(2)], axis=0) + EXPERTS
        rival = jnp.sum(jnp.where(lane.astype(F32) == other, logits, 0.0), axis=1, keepdims=True)
        own_logits[...] = mine
        top = jnp.maximum(mine, rival)
        mine, rival = jnp.exp(mine - top), jnp.exp(rival - top)
        gates[...] = mine / (mine + rival)

        @pl.when(u < pairs - 2)
        def _():
            forward_pair(u + 1)
            send_pair(u + 2)

        @pl.when(u == pairs - 3)
        def _():
            for n in range(2, 4):
                for i in range(len(even)):
                    straight(n, i).start()

        @pl.when(u == pairs - 2)
        def _():
            for q in range(2):
                forward_near(first_block(u + 1) + q)

        hidden_grad[...] = lax.dot_general(
            land[1, pair(j), :], down_map[...], (((1,), (1,)), ((), ())), preferred_element_type=F32)

        @pl.when(u > 0)
        def _():
            for copy in results_to_memory(j):
                copy.wait()

        @pl.loop(0, pair_rows // 32)
        def _(r):
            some = pl.ds(pl.multiple_of(r * 32, 32), 32)
            gate_here, up_here = gate_pre[some, :], up_pre[some, :]
            weight = gates[some, :]
            sigma = 1.0 / (1.0 + jnp.exp(-gate_here))
            silu = gate_here * sigma
            hidden = silu * up_here
            grad = hidden_grad[some, :]
            pulls[some, :] = jnp.sum(hidden * grad, axis=1, keepdims=True)
            grad = grad * weight
            low[0, some, :] = (hidden * weight).astype(BF16)
            gate_low = (grad * up_here * (sigma * (1.0 + gate_here * (1.0 - sigma)))).astype(BF16)
            up_low = (grad * silu).astype(BF16)
            low[1, some, :] = gate_low
            low[2, some, :] = up_low
            moments[some, :] = jnp.sum(
                gate_low.astype(F32) * gate_here + up_low.astype(F32) * up_here, axis=1, keepdims=True)

        for copy in results_to_memory(j):
            copy.start()

        @pl.when(u > 0)
        def _():
            finish(u - 1)

        @pl.when(u > 1)
        def _():
            for q in range(2):
                for d in range(1, tensor):
                    give(u - 2, q, d).wait_send()

        noted = []
        for q in range(2):
            some = pl.ds(q * CAP, CAP)
            lane = lax.broadcasted_iota(jnp.int32, (CAP, 128), 1)
            shared = tensor * pieces
            column = jnp.where(lane == 0, pulls[some, :], jnp.where(lane == 1, gates[some, :] / shared, 0.0))
            column = jnp.where(lane == 2, moments[some, :], jnp.where(lane == 3, own_logits[some, :] / shared, column))
            column = jnp.concatenate([column, jnp.zeros((256 - CAP, 128), F32)], axis=0)
            noted.append(column.T[:NOTES])
        for d in range(tensor - 1, -1, -1):
            grad = lax.dot_general(low[1], gate_map[cols(d), :], (((1,), (1,)), ((), ())), preferred_element_type=F32)
            grad += lax.dot_general(low[2], up_map[cols(d), :], (((1,), (1,)), ((), ())), preferred_element_type=F32)
            out = jnp.dot(low[0], down_map[:, cols(d)], preferred_element_type=F32)
            for q in range(2):
                part = pl.ds(q * CAP, CAP)
                parts = [(pl.ds(0, CAP), slice(None), grad[q * CAP : (q + 1) * CAP]),
                         (pl.ds(CAP, CAP), slice(None), out[q * CAP : (q + 1) * CAP]),
                         (foot, pl.ds(0, 256), noted[q])]
                for place, lanes, value in parts:
                    if d & 1:
                        sent[place_of(u, q), d - 1, place, lanes] = value.astype(BF16)
                    else:
                        keep[q, d // 2, place, lanes] = value
                if d & 1:
                    give(u, q, d).start()
        sum_stage(u, 1)

        @pl.when(u < pairs - 1)
        def _():
            for k in range(1, bits):
                stage(first_block(u + 1), k, (0,))

                @pl.when(u < pairs - 2)
                def _():
                    stage(first_block(u + 1), k, (1,))

        for copy in to_memory(j):
            copy.wait()

    finish(pairs - 1)
    for copy in results_to_memory(0):
        copy.wait()
    for u in range(max(pairs - 2, 0), pairs):
        for q in range(2):
            for d in range(1, tensor):
                give(u, q, d).wait_send()

    @pl.loop(1, experts)
    def _(s):
        j = e ^ s
        for a in range(2):
            arrived(a, j).wait_send()
        handed(j).wait_recv()
        handed(j).wait_send()

    @pl.loop(0, experts)
    def _(j):
        for a in range(2):
            for d in range(1, tensor):
                if a == 0 or d & 1:
                    passed(a, j, d).wait_send()

        @pl.when(j != e)
        def _():
            for d in even:
                passed(1, j, d).wait_send()


def feed_forward(x, dy, slots, facts, routers, gate_map, up_map, down_map, collective_id):
    experts, tensor = lax.axis_size("expert"), lax.axis_size("tensor")
    bits = tensor.bit_length() - 1
    width, hidden = x.shape[1], gate_map.shape[1]
    high = 2 * CAP + NOTES
    count = experts * CAP
    dma = pltpu.SemaphoreType.DMA
    return pl.pallas_call(
        functools.partial(ffn_kernel, experts, bits, experts // EXPERTS),
        out_shape=[jax.ShapeDtypeStruct((experts, high, width), BF16)]
        + [jax.ShapeDtypeStruct((count, D), BF16)] * 2 + [jax.ShapeDtypeStruct((count, hidden), BF16)] * 3,
        in_specs=[VMEM] * 5 + [ANY] * 3,
        out_specs=[VMEM] + [ANY] * 5,
        scratch_shapes=[
            pltpu.VMEM((SLOTS, width), BF16),
            pltpu.VMEM((SLOTS, width), BF16),
            pltpu.VMEM((4, tensor // 2 - 1, CAP, width), BF16),
            pltpu.VMEM((2, count, D), BF16),
            pltpu.VMEM((D, hidden), BF16),
            pltpu.VMEM((D, hidden), BF16),
            pltpu.VMEM((hidden, D), BF16),
            pltpu.VMEM((2 * CAP, hidden), F32),
            pltpu.VMEM((2 * CAP, hidden), F32),
            pltpu.VMEM((2 * CAP, hidden), F32),
            pltpu.VMEM((2 * CAP, 1), F32),
            pltpu.VMEM((2 * CAP, 1), F32),
            pltpu.VMEM((2 * CAP, 1), F32),
            pltpu.VMEM((2 * CAP, 1), F32),
            pltpu.VMEM((3, 2 * CAP, hidden), BF16),
            pltpu.VMEM((4, tensor - 1, high, width), BF16),
            pltpu.VMEM((experts, tensor - 1, high, width), BF16),
            pltpu.VMEM((2, tensor // 2, high, width), F32),
        ] + [dma((2, experts))] * 2 + [dma((2, experts, tensor))] * 2
        + [dma((4, tensor - 1)), dma((experts, tensor - 1))] + [dma((experts,))] * 2 + [dma((3,)), dma((5,))],
        compiler_params=pltpu.CompilerParams(
            collective_id=collective_id, has_side_effects=True, vmem_limit_bytes=63 * 2**20),
        cost_estimate=pl.CostEstimate(flops=10**11, bytes_accessed=10**7, transcendentals=0),
    )(x, dy, slots, facts, routers, gate_map, up_map, down_map)


def small_kernel(experts, tensor, part, out, came, s_send, s_recv, b_send, b_recv):
    e, t = lax.axis_index("expert"), lax.axis_index("tensor")
    owners = experts // tensor
    width = out.shape[1]
    place = t * owners

    def to_owner(c):
        return remote(part.at[:, pl.ds(c * width, width)], came.at[e], s_send.at[c], s_recv.at[e], expert=place + c)

    barrier = pltpu.get_barrier_semaphore()

    @pl.loop(1, experts)
    def _(s):
        pl.semaphore_signal(barrier, inc=1, device_id={"expert": e ^ s}, device_id_type=MESH)

    @pl.loop(1, tensor)
    def _(s):
        pl.semaphore_signal(barrier, inc=1, device_id={"tensor": t ^ s}, device_id_type=MESH)

    pl.semaphore_wait(barrier, experts + tensor - 2)
    for c in range(owners):
        @pl.when(e != place + c)
        def _():
            to_owner(c).start()

        @pl.when(e == place + c)
        def _():
            came[e] = part[:, c * width : (c + 1) * width]

    @pl.when(e // owners == t)
    def _():
        @pl.loop(1, experts)
        def _(s):
            j = e ^ s
            remote(came.at[j], came.at[j], s_send.at[0], s_recv.at[j], expert=j).wait_recv()

        total = came[0]
        for j in range(1, experts):
            total += came[j]
        out[...] = total

        @pl.loop(1, tensor)
        def _(s):
            remote(out, out, b_send.at[s], b_recv, tensor=t ^ s).start()

        @pl.loop(1, tensor)
        def _(s):
            remote(out, out, b_send.at[s], b_recv, tensor=t ^ s).wait_send()

    @pl.when(e // owners != t)
    def _():
        remote(out, out, b_send.at[0], b_recv, tensor=e // owners).wait_recv()

    for c in range(owners):
        @pl.when(e != place + c)
        def _():
            to_owner(c).wait_send()


def small_sums(part, collective_id):
    experts, tensor = lax.axis_size("expert"), lax.axis_size("tensor")
    n, width = part.shape[0], D // experts
    dma = pltpu.SemaphoreType.DMA
    return pl.pallas_call(
        functools.partial(small_kernel, experts, tensor),
        out_shape=jax.ShapeDtypeStruct((n, width), F32),
        in_specs=[VMEM],
        out_specs=VMEM,
        scratch_shapes=[pltpu.VMEM((experts, n, width), F32), dma((experts // tensor,)), dma((experts,)), dma((tensor,)),
                        dma],
        compiler_params=pltpu.CompilerParams(collective_id=collective_id, has_side_effects=True),
        cost_estimate=pl.CostEstimate(flops=10**10, bytes_accessed=10**5, transcendentals=0),
    )(part)


def dot(left, right, dims):
    return lax.dot_general(left, right, ((dims[0], dims[1]), ((), ())), preferred_element_type=F32)


def mm(left, right):
    return dot(left, right, ((1,), (0,)))


def mm_nt(left, right):
    return dot(left, right, ((1,), (1,)))


def mm_tn(left, right):
    return dot(left, right, ((0,), (0,)))


def swap(blocks):
    return lax.all_to_all(blocks, "expert", split_axis=0, concat_axis=0, tiled=True)


def columns_together(rows):
    return lax.all_gather(rows, "tensor", axis=1, tiled=True)


def columns_summed(rows):
    return lax.psum_scatter(rows, "tensor", scatter_dimension=1, tiled=True)


def slot_numbers(routes):
    flat = routes.T.reshape(-1)
    place = jnp.arange(flat.shape[0], dtype=jnp.int32)
    earlier = (flat[:, None] == flat[None, :]) & (place[None, :] < place[:, None])
    return flat * CAP + jnp.sum(earlier.astype(jnp.int32), axis=1)


def spaced(slots, stride):
    return slots + (slots // CAP) * (stride - CAP)


def place_matrix(slots):
    return (jnp.arange(SLOTS, dtype=jnp.int32)[:, None] == slots[None, :]).astype(BF16)


def token_matrix(slots, stride=CAP, first=0):
    wide = (spaced(slots, stride) + first).reshape(TOPK, -1)
    place = jnp.arange(EXPERTS * stride, dtype=jnp.int32)[:, None]
    return ((place == wide[0][None, :]) | (place == wide[1][None, :])).astype(BF16)


def to_pieces(rows, pieces):
    if pieces == 1:
        return rows
    experts, r, c = rows.shape
    return rows.reshape(experts, r, pieces, c // pieces).transpose(0, 2, 1, 3).reshape(experts * pieces, r, -1)


def from_pieces(rows, pieces):
    if pieces == 1:
        return rows
    both, r, c = rows.shape
    return rows.reshape(both // pieces, pieces, r, c).transpose(0, 2, 1, 3).reshape(both // pieces, r, -1)


def for_pieces(rows, pieces):
    return jnp.repeat(rows, pieces, axis=0) if pieces > 1 else rows


def pick_gates(logits, routes):
    one_hot = (routes[:, :, None] == jnp.arange(EXPERTS, dtype=jnp.int32)[None, None, :]).astype(F32)
    return jax.nn.softmax(jnp.sum(one_hot * logits[:, None, :], axis=2), axis=-1)


def gate_back(gating, pulled, routes):
    inner_sum = gating * (pulled - jnp.sum(gating * pulled, axis=1, keepdims=True))
    one_hot = (routes[:, :, None] == jnp.arange(EXPERTS, dtype=jnp.int32)[None, None, :]).astype(F32)
    return jnp.sum(one_hot * inner_sum[:, :, None], axis=1).astype(BF16)


def per_device(
    tokens,
    segment_ids,
    attn_routes,
    ffn_routes,
    attn_gain,
    ffn_gain,
    routers,
    query_weight,
    output_weight,
    key_value_weight,
    gate_weight,
    up_weight,
    down_weight,
    cotangent,
):
    rows_here = tokens.shape[0]
    expert_count = lax.axis_size("expert")
    tensor_count = lax.axis_size("tensor")
    pieces = expert_count // EXPERTS
    column_count = D // tensor_count
    expert_index = lax.axis_index("expert")
    tensor_index = lax.axis_index("tensor")
    own = (expert_index // pieces).astype(F32)
    head_width = query_weight.shape[2]
    head_count = head_width // HD

    def cols(whole):
        return lax.dynamic_slice_in_dim(whole, tensor_index * column_count, column_count, whole.ndim - 1)

    def group_tokens(token_cols, places):
        return for_pieces(mm(places, token_cols).astype(BF16).reshape(EXPERTS, CAP, -1), pieces)

    def group_choices(choice_rows, places):
        return to_pieces(mm(places, choice_rows).astype(BF16).reshape(EXPERTS, CAP, -1), pieces)

    def choices_of(back, places):
        return mm_tn(places, from_pieces(back, pieces).reshape(SLOTS, -1)).astype(BF16)

    def sums_of(back, places):
        stride = back.shape[1]
        back = back.reshape(EXPERTS, pieces, stride, column_count)
        if pieces > 1:
            total = sum(mm_tn(places, back[:, p].reshape(EXPERTS * stride, -1)) for p in range(pieces))
        else:
            total = mm_tn(places, back.reshape(EXPERTS * stride, -1))
        return total

    def notes_of(*scalars):
        rows = jnp.stack([v.reshape(expert_count, CAP) for v in scalars], axis=1)
        return jnp.pad(rows, ((0, 0), (0, NOTES - len(scalars)), (0, column_count - CAP)))

    def read_notes(back, places, count, first=CAP):
        noted = back[:, first : first + count, :CAP].astype(F32)
        noted = noted.reshape(EXPERTS, pieces, count, CAP).sum(1).transpose(0, 2, 1).reshape(SLOTS, count)
        return mm_tn(places, noted.astype(BF16)).reshape(TOPK, rows_here, count)

    def exchange(away, b):
        return lax.ppermute(away, "expert", [(i, i ^ (1 << b)) for i in range(expert_count)])

    attn_slots, ffn_slots = slot_numbers(attn_routes), slot_numbers(ffn_routes)

    slots = jnp.stack([attn_slots, ffn_slots, spaced(attn_slots, 256), spaced(ffn_slots, 256)])
    segments = jnp.concatenate([jnp.full((WINDOW,), -1, jnp.int32), segment_ids])[None]
    (rows_one, query_map, window, pair_map, keys, values, attn_gate_blocks, facts, heads, queries, log_total,
     output_map) = front(
        tokens, attn_gain[None], slots, jnp.concatenate([attn_routes.T, ffn_routes.T]), routers.T, segments,
        to_pieces(query_weight, pieces), key_value_weight, to_pieces(output_weight, pieces), collective_id=0)
    rows_one, attn_slots, ffn_slots, tokens, attn_gain, ffn_gain, routers, cotangent = lax.optimization_barrier(
        (rows_one, attn_slots, ffn_slots, tokens, attn_gain, ffn_gain, routers, cotangent))
    routers_one, routers_two = routers[:, :EXPERTS], routers[:, EXPERTS:]
    state_in = tokens.astype(F32)
    gain_one = attn_gain.astype(F32)
    gain_two = cols(ffn_gain.astype(F32))
    dy_cols = cols(cotangent)
    token_cols = cols(tokens).astype(F32)
    attn_places, ffn_places = place_matrix(attn_slots), place_matrix(ffn_slots)
    rows_one = rows_one.reshape(-1, D)
    normed_one = window[2]
    window = window.reshape(-1, D)
    attn_back, heads_rows = scatter_rows(
        to_pieces(heads.reshape(EXPERTS, CAP, -1), pieces), output_map, attn_gate_blocks, collective_id=1)
    heads_rows = heads_rows.reshape(expert_count * CAP, -1)
    state = token_cols + sums_of(attn_back, token_matrix(attn_slots))

    mean_two = lax.psum(jnp.sum(state * state, axis=1, keepdims=True), "tensor") / D
    rate_two = lax.rsqrt(mean_two + eps)
    normed_two = (state * rate_two * gain_two).astype(BF16)
    gate_map, up_map, down_map = gate_weight[0], up_weight[0], down_weight[0]
    ffn_back, rows_two, rows_dy, hidden, gate_low, up_low = feed_forward(
        normed_two, cotangent, ffn_slots[None], facts, routers.T, gate_map, up_map, down_map, collective_id=2)
    normed_two_grad = sums_of(ffn_back, token_matrix(ffn_slots, 2 * CAP + NOTES))
    ffn_pull, ffn_gates, moments, own_logits = (
        note.T for note in jnp.moveaxis(read_notes(ffn_back, ffn_places, 4, 2 * CAP), 2, 0))
    ffn_logit_grad = gate_back(ffn_gates, ffn_pull, ffn_routes)
    normed_two_grad = normed_two_grad + mm_nt(
        ffn_logit_grad, lax.dynamic_slice_in_dim(routers_two, tensor_index * column_count, column_count, 0))
    ffn_router_cols = mm_tn(normed_two, ffn_logit_grad)
    ffn_gain_cols = jnp.sum(normed_two_grad * state * rate_two, axis=0)
    ahead = normed_two_grad * gain_two
    chosen_grad = jnp.sum(
        jnp.where(ffn_routes[:, :, None] == jnp.arange(EXPERTS, dtype=jnp.int32), ffn_logit_grad[:, None].astype(F32), 0.0),
        axis=2)
    centre = jnp.sum(moments + chosen_grad * own_logits, axis=1, keepdims=True) / (rate_two * D)
    state_grad = dy_cols.astype(F32) + rate_two * ahead - state * rate_two * rate_two * rate_two * centre

    unused_rows, heads_grad, heads_grad_rows, output_grad = gather_rows(
        group_tokens(state_grad.astype(BF16), token_matrix(attn_slots)), output_map, gate=attn_gate_blocks,
        others=heads_rows.reshape(expert_count, CAP, -1), collective_id=4)
    heads_grad_rows = heads_grad_rows.reshape(expert_count * CAP, -1)
    attn_notes = notes_of(jnp.sum(heads_grad_rows.astype(F32) * heads_rows.astype(F32), axis=1))
    query_back, key_back, value_back, output_grad = attend_back(
        attn_slots[None], from_pieces(heads_grad, pieces).reshape(SLOTS, -1), queries, keys, values, log_total,
        segments, output_grad, collective_id=6)
    output_grad = from_pieces(output_grad, pieces).astype(F32)
    normed_back, unused_rows, owed, query_grad, pair_part, pair_came = scatter_rows(
        to_pieces(query_back.reshape(EXPERTS, CAP, -1), pieces), query_map, notes=attn_notes,
        windows=[key_back, value_back, pair_map, rows_one, window], collective_id=5)
    pair_part = (pair_part.astype(F32) + pair_came.astype(F32)).astype(BF16)
    pair_part, query_grad, rows_two, hidden = lax.optimization_barrier((pair_part, query_grad, rows_two, hidden))
    quarter = D // 4
    pair_came = jnp.concatenate(
        [exchange(pair_part[quarter:, :head_width], 1), exchange(pair_part[quarter:, head_width:], 0)], axis=1)
    query_grad = swap(query_grad)
    gate_grad = mm_tn(rows_two, gate_low)
    up_grad = mm_tn(rows_two, up_low)
    pair_came, hidden, gate_grad, up_grad = lax.optimization_barrier((pair_came, hidden, gate_grad, up_grad))
    pair_part = pair_part[:quarter].astype(F32) + pair_came.astype(F32)
    for b in range(2, expert_count.bit_length() - 1):
        rest = pair_part.shape[0] // 2
        pair_part = pair_part.astype(BF16)
        if b == 2:
            pair_part, hidden = lax.optimization_barrier((pair_part, hidden))
        pair_part = pair_part[:rest].astype(F32) + exchange(pair_part[rest:], b).astype(F32)
    down_grad = mm_tn(hidden, rows_dy)
    normed_back, owed, down_grad = lax.optimization_barrier((normed_back, owed, down_grad))
    normed_grad = sums_of(normed_back, token_matrix(attn_slots, CAP + NOTES)) + owed.astype(F32)
    attn_pull = read_notes(normed_back, attn_places, 1)[:, :, 0].T
    attn_gates = pick_gates(mm(normed_one, routers_one), attn_routes)
    attn_logit_grad = gate_back(attn_gates, attn_pull, attn_routes)
    normed_grad = normed_grad + mm_nt(
        attn_logit_grad, lax.dynamic_slice_in_dim(routers_one, tensor_index * column_count, column_count, 0))
    attn_router_cols = mm_tn(cols(normed_one), attn_logit_grad)
    rate_one = lax.rsqrt(jnp.mean(state_in * state_in, axis=1, keepdims=True) + eps)
    attn_gain_cols = jnp.sum(normed_grad * token_cols * rate_one, axis=0)
    ahead_one = normed_grad * cols(gain_one)
    centre_one = jnp.sum(ahead_one * token_cols, axis=1, keepdims=True)
    centre_one = lax.psum(centre_one, "tensor") / D
    tokens_grad = state_grad + rate_one * ahead_one - token_cols * rate_one * rate_one * rate_one * centre_one
    tokens_grad = columns_together(tokens_grad.astype(BF16)).astype(F32)

    small = jnp.concatenate(
        [attn_router_cols.T, ffn_router_cols.T, attn_gain_cols[None], ffn_gain_cols[None],
         jnp.zeros((6, column_count), F32)], axis=0)
    small, pair_part = lax.optimization_barrier((small, pair_part))
    small = small_sums(small, collective_id=3).T
    query_grad = from_pieces(query_grad, pieces).astype(F32)
    key_value_grad = pair_part.reshape(D // expert_count, 2, -1).transpose(1, 0, 2)
    ffn_out = sums_of(ffn_back, token_matrix(ffn_slots, 2 * CAP + NOTES, CAP))
    mixed = (state + ffn_out).astype(BF16)
    return (
        mixed,
        tokens_grad,
        small[:, 2 * EXPERTS],
        small[:, 2 * EXPERTS + 1],
        small[:, : 2 * EXPERTS],
        query_grad,
        output_grad,
        key_value_grad,
        gate_grad[None],
        up_grad[None],
        down_grad[None],
    )


def solution(mesh):
    in_specs = (
        P("expert", None),
        P(),
        P("expert", None),
        P("expert", None),
        P(),
        P(),
        P(),
        P(None, "expert", "tensor"),
        P(None, "expert", "tensor"),
        P(None, "expert", "tensor"),
        P("expert", None, "tensor"),
        P("expert", None, "tensor"),
        P("expert", "tensor", None),
        P("expert", None),
    )
    out_specs = (
        P("expert", "tensor"),
        P("expert", None),
        P("expert"),
        P("expert"),
        P("expert", None),
        P(None, "expert", "tensor"),
        P(None, "expert", "tensor"),
        P(None, "expert", "tensor"),
        P("expert", None, "tensor"),
        P("expert", None, "tensor"),
        P("expert", "tensor", None),
    )
    return jax.shard_map(
        per_device, mesh=mesh, in_specs=in_specs, out_specs=out_specs, check_vma=False
    )
```

```python
import functools
import math

import jax
import jax.numpy as jnp
from jax import lax
from jax.experimental import pallas as pl
from jax.experimental.pallas import tpu as pltpu
from jax.sharding import PartitionSpec as P

D = 2048
HD = 128
EXPERTS = 8
TOPK = 2
WINDOW = 1024
CAP = 160
SLOTS = EXPERTS * CAP

eps = 1e-06
masked_value = -1e30
SCALE = HD ** (-0.5)
LOG2E = math.log2(math.e)
Q_ROWS = 256
NOTES = 16
F32 = jnp.float32
BF16 = jnp.bfloat16
MESH = pl.DeviceIdType.MESH
VMEM = pl.BlockSpec(memory_space=pltpu.VMEM)
ANY = pl.BlockSpec(memory_space=pl.ANY)


def remote(src, dst, send, recv, **device):
    return pltpu.make_async_remote_copy(
        src_ref=src, dst_ref=dst, send_sem=send, recv_sem=recv, device_id=device, device_id_type=MESH)


def meet(experts, bits):
    e, t = lax.axis_index("expert"), lax.axis_index("tensor")
    barrier = pltpu.get_barrier_semaphore()

    @pl.loop(1, experts)
    def _(s):
        pl.semaphore_signal(barrier, inc=1, device_id={"expert": e ^ s}, device_id_type=MESH)

    for b in range(bits):
        pl.semaphore_signal(barrier, inc=1, device_id={"tensor": t ^ (1 << b)}, device_id_type=MESH)
    pl.semaphore_wait(barrier, experts - 1 + bits)


def partners(e, experts, near):
    if near:
        return lambda s: e ^ s
    return lambda s: e ^ ((experts - s) & (experts - 1))


def low_bit(d):
    return (d & -d).bit_length() - 1


def gather_kernel(experts, bits, near, multiply, scale, *refs):
    refs = list(refs)
    x = refs.pop(0)
    w = refs.pop(0) if multiply else None
    gate = refs.pop(0) if scale else None
    others = refs.pop(0) if scale else None
    rows = refs.pop(0)
    back = refs.pop(0) if multiply else None
    product = refs.pop(0) if scale else None
    map_grad = refs.pop(0) if scale else None
    y = refs.pop(0) if multiply else None
    z_send, z_recv, t_send, t_recv = refs[:4]
    refs = refs[4:]
    if multiply:
        y_send, y_recv = refs[:2]
    e, t = lax.axis_index("expert"), lax.axis_index("tensor")
    partner = partners(e, experts, near)
    width = x.shape[2]
    tensor = 1 << bits

    def cols(d):
        return pl.ds(pl.multiple_of((t ^ d) * width, 128), width)

    def arrive(j):
        return remote(x.at[j], rows.at[e, :, cols(0)], z_send.at[j], z_recv.at[e], expert=j)

    def arrived(j):
        return remote(x.at[j], rows.at[j, :, cols(0)], z_send.at[j], z_recv.at[j], expert=j)

    def pass_on(j, d, b):
        place = rows.at[j, :, cols(d)]
        far = d | (1 << b)
        return remote(place, place, t_send.at[j, far], t_recv.at[j, far], tensor=t ^ (1 << b))

    def passed(j, d):
        place = rows.at[j, :, cols(d)]
        return remote(place, place, t_send.at[j, d], t_recv.at[j, d], tensor=t ^ (1 << low_bit(d)))

    def hand_back(j):
        return remote(y.at[j], back.at[e], y_send.at[j], y_recv.at[e], expert=j)

    def handed(j):
        return remote(y.at[j], back.at[j], y_send.at[j], y_recv.at[j], expert=j)

    meet(experts, bits)

    @pl.loop(1, experts)
    def _(s):
        arrive(partner(s)).start()

    rows[e, :, cols(0)] = x[e]

    @pl.loop(0, experts + bits)
    def _(i):
        @pl.when(i < experts)
        def _():
            j = partner(i)

            @pl.when(i > 0)
            def _():
                arrived(j).wait_recv()

            for b in reversed(range(bits)):
                pass_on(j, 0, b).start()

        for k in range(1, bits + 1):
            @pl.when((i >= k) & (i < experts + k))
            def _():
                m = i - k
                j = partner(m)
                bit = bits - k
                for d in range(1, tensor):
                    if low_bit(d) == bit:
                        passed(j, d).wait_recv()
                        for b in reversed(range(bit)):
                            pass_on(j, d, b).start()
                if k == bits and multiply:
                    out = jnp.dot(rows[j], w[...], preferred_element_type=F32)
                    if scale:
                        product[j] = out.astype(BF16)
                        out = out * gate[j]
                    y[j] = out.astype(BF16)

                    @pl.when(m == 0)
                    def _():
                        back[e] = y[e]

                    @pl.when(m > 0)
                    def _():
                        hand_back(j).start()

    if scale:
        cap, f = others.shape[1], others.shape[2]
        share = map_grad.shape[1]
        scaled = (others[...].astype(F32) * gate[...]).astype(BF16).reshape(experts * cap, f)

        @pl.loop(0, experts)
        def _(j):
            some = rows[:, :, pl.ds(pl.multiple_of(j * share, share), share)].reshape(experts * cap, share)
            map_grad[j] = lax.dot_general(
                some, scaled, (((0,), (0,)), ((), ())), preferred_element_type=F32).astype(BF16)

    @pl.loop(1, experts)
    def _(s):
        j = partner(s)
        arrived(j).wait_send()
        if multiply:
            handed(j).wait_recv()
            handed(j).wait_send()

    @pl.loop(0, experts)
    def _(j):
        for d in range(1, tensor):
            passed(j, d).wait_send()


def gather_rows(x, w=None, gate=None, others=None, near=True, collective_id=0):
    experts, tensor = lax.axis_size("expert"), lax.axis_size("tensor")
    bits = tensor.bit_length() - 1
    cap, width = x.shape[1], x.shape[2]
    multiply = w is not None
    f = w.shape[-1] if multiply else 0
    ins, specs = [x], [VMEM]
    outs = [jax.ShapeDtypeStruct((experts, cap, width * tensor), BF16)]
    scratch = []
    if multiply:
        ins.append(w)
        specs.append(VMEM)
        outs.append(jax.ShapeDtypeStruct((experts, cap, f), BF16))
    if gate is not None:
        ins += [gate, others]
        specs += [VMEM, VMEM]
        outs.append(jax.ShapeDtypeStruct((experts, cap, f), BF16))
        outs.append(jax.ShapeDtypeStruct((experts, D // experts, f), BF16))
    if multiply:
        scratch.append(pltpu.VMEM((experts, cap, f), BF16))
    scratch += [pltpu.SemaphoreType.DMA((experts,))] * 2 + [pltpu.SemaphoreType.DMA((experts, tensor))] * 2
    if multiply:
        scratch += [pltpu.SemaphoreType.DMA((experts,))] * 2
    return pl.pallas_call(
        functools.partial(gather_kernel, experts, bits, near, multiply, gate is not None),
        out_shape=outs,
        in_specs=specs,
        out_specs=[VMEM] * len(outs),
        scratch_shapes=scratch,
        compiler_params=pltpu.CompilerParams(
            collective_id=collective_id, has_side_effects=True, vmem_limit_bytes=48 * 2**20),
        cost_estimate=pl.CostEstimate(flops=10**11, bytes_accessed=10**7, transcendentals=0),
    )(*ins)


def place_matrices(slots_ref, spread, gathered):
    count, choices = spread.shape
    spread[...] = (lax.broadcasted_iota(jnp.int32, (count, choices), 0) == slots_ref[0:1, :]).astype(F32).astype(BF16)
    gathered[...] = spread[...].T


def mask_bias(segments, bias):
    blocks, span, _ = bias.shape
    here = blocks * Q_ROWS
    e, experts = lax.axis_index("expert"), lax.axis_size("expert")
    parts = []
    for back in range(WINDOW // here, -1, -1):
        device = lax.rem(e + experts - back, experts)
        part = segments[:, pl.ds(pl.multiple_of(device * here, 128), here)]
        parts.append(jnp.where(e >= back, part, -1))
    query_ids = parts[-1]
    key_row = jnp.concatenate(parts, axis=1).astype(F32)
    key_ids = jnp.concatenate([key_row, jnp.zeros((7, WINDOW + here), F32)], axis=0).T[:, 0:1].astype(jnp.int32)

    for block in range(blocks):
        first = block * Q_ROWS
        query_place = lax.broadcasted_iota(jnp.int32, (span, Q_ROWS), 1) + WINDOW
        distance = query_place - lax.broadcasted_iota(jnp.int32, (span, Q_ROWS), 0)
        same = key_ids[first : first + span] == query_ids[:, first : first + Q_ROWS]
        allowed = (distance >= 0) & (distance < WINDOW) & same
        part = jnp.where(allowed, 0.0, masked_value)
        for k in range(TOPK):
            bias[block, :, pl.ds(k * Q_ROWS, Q_ROWS)] = part


def of_block(choices, block, lanes):
    rows = choices.shape[0] // TOPK
    return jnp.concatenate([choices[pl.ds(k * rows + block * Q_ROWS, Q_ROWS), lanes] for k in range(TOPK)], axis=0)


def attend(back, keys_ref, values_ref, grouped, queries_ref, lse, spread, gathered, bias, packed, heads):
    blocks, span, _ = bias.shape
    rows = queries_ref.shape[0] // TOPK
    pieces, of_piece = back.shape[0] // EXPERTS, back.shape[2] // HD

    @pl.loop(0, queries_ref.shape[1] // HD)
    def _(head):
        lanes = pl.ds(pl.multiple_of(head * HD, HD), HD)
        inner = pl.ds(pl.multiple_of(lax.rem(head, of_piece) * HD, HD), HD)
        for q in range(EXPERTS):
            packed[pl.ds(q * CAP, CAP), :] = back[q * pieces + lax.div(head, of_piece), :, inner]
        queries_ref[:, lanes] = jnp.dot(gathered[...], packed[...], preferred_element_type=F32).astype(BF16)
        for block in range(blocks):
            place = pl.ds(block * Q_ROWS, span)
            queries = of_block(queries_ref, block, lanes)
            scores = lax.dot_general(
                keys_ref[place, lanes], queries, (((1,), (1,)), ((), ())), preferred_element_type=F32)
            scores = scores * (SCALE * LOG2E) + bias[block]
            top = jnp.max(scores, axis=0, keepdims=True)
            probs = jnp.exp2(scores - top)
            total = jnp.sum(probs, axis=0, keepdims=True)
            out = lax.dot_general(
                values_ref[place, lanes], probs.astype(BF16), (((0,), (0,)), ((), ())), preferred_element_type=F32)
            out = (out * (1.0 / total)).T.astype(BF16)
            for k in range(TOPK):
                heads[pl.ds(k * rows + block * Q_ROWS, Q_ROWS), :] = out[k * Q_ROWS : (k + 1) * Q_ROWS]
            lse[head, :, pl.ds(block * TOPK * Q_ROWS, TOPK * Q_ROWS)] = top + jnp.log2(total)
        grouped[:, lanes] = jnp.dot(spread[...], heads[...], preferred_element_type=F32).astype(BF16)


def attend_back_kernel(experts, *refs):
    (slots, back, queries_ref, keys_ref, values_ref, lse, segments, part_grad,
     grouped, key_grad, value_grad, map_grad,
     spread, gathered, bias, key_acc, value_acc, query_grad, head_grad,
     g_send, g_recv, own_sem) = refs
    e = lax.axis_index("expert")
    blocks, span, _ = bias.shape
    here = queries_ref.shape[0] // TOPK
    def grad_from(j):
        return remote(part_grad.at[j], map_grad.at[j], g_send.at[j], g_recv.at[j], expert=j)

    barrier = pltpu.get_barrier_semaphore()

    @pl.loop(1, experts)
    def _(s):
        pl.semaphore_signal(barrier, inc=1, device_id={"expert": e ^ s}, device_id_type=MESH)

    own = pltpu.make_async_copy(part_grad.at[e], map_grad.at[e], own_sem)
    own.start()
    pl.semaphore_wait(barrier, experts - 1)

    @pl.loop(1, experts)
    def _(s):
        j = e ^ s
        remote(part_grad.at[j], map_grad.at[e], g_send.at[j], g_recv.at[e], expert=j).start()

    place_matrices(slots, spread, gathered)
    mask_bias(segments, bias)

    @pl.loop(0, queries_ref.shape[1] // HD)
    def _(head):
        lanes = pl.ds(pl.multiple_of(head * HD, HD), HD)
        head_grad[...] = jnp.dot(gathered[...], back[:, lanes], preferred_element_type=F32).astype(BF16)
        key_acc[...] = jnp.zeros_like(key_acc)
        value_acc[...] = jnp.zeros_like(value_acc)
        for block in range(blocks):
            queries = of_block(queries_ref, block, lanes)
            grads = of_block(head_grad, block, slice(None))
            place = pl.ds(block * Q_ROWS, span)
            keys, values = keys_ref[place, lanes], values_ref[place, lanes]
            scores = lax.dot_general(keys, queries, (((1,), (1,)), ((), ())), preferred_element_type=F32)
            probs = jnp.exp2(scores * (SCALE * LOG2E) + bias[block]
                             - lse[head, :, pl.ds(block * TOPK * Q_ROWS, TOPK * Q_ROWS)])
            pulled = lax.dot_general(values, grads, (((1,), (1,)), ((), ())), preferred_element_type=F32)
            pulled = probs * pulled
            inner = jnp.sum(pulled, axis=0, keepdims=True)
            score_grad = (pulled - probs * inner).astype(BF16)
            value_acc[place, :] += jnp.dot(probs.astype(BF16), grads, preferred_element_type=F32)
            key_acc[place, :] += jnp.dot(score_grad, queries, preferred_element_type=F32)
            out = lax.dot_general(keys, score_grad, (((0,), (0,)), ((), ())), preferred_element_type=F32)
            out = (out * SCALE).T.astype(BF16)
            for k in range(TOPK):
                query_grad[pl.ds(k * here + block * Q_ROWS, Q_ROWS), :] = out[k * Q_ROWS : (k + 1) * Q_ROWS]
        grouped[:, lanes] = jnp.dot(spread[...], query_grad[...], preferred_element_type=F32).astype(BF16)
        key_grad[:, lanes] = (key_acc[...] * SCALE).astype(BF16)
        value_grad[:, lanes] = value_acc[...].astype(BF16)

    own.wait()

    @pl.loop(1, experts)
    def _(s):
        grad_from(e ^ s).wait_recv()
        grad_from(e ^ s).wait_send()


def attend_back(slots, back, queries, keys, values, lse, segments, map_grad, collective_id):
    experts = lax.axis_size("expert")
    choices, (count, width), span = queries.shape[0], back.shape, keys.shape[0]
    blocks = choices // TOPK // Q_ROWS
    dma = pltpu.SemaphoreType.DMA
    return pl.pallas_call(
        functools.partial(attend_back_kernel, experts),
        out_shape=[
            jax.ShapeDtypeStruct((count, width), BF16),
            jax.ShapeDtypeStruct((span, width), BF16),
            jax.ShapeDtypeStruct((span, width), BF16),
            jax.ShapeDtypeStruct(map_grad.shape, BF16),
        ],
        in_specs=[VMEM] * 7 + [ANY],
        out_specs=[VMEM] * 3 + [ANY],
        scratch_shapes=[
            pltpu.VMEM((count, choices), BF16),
            pltpu.VMEM((choices, count), BF16),
            pltpu.VMEM((blocks, WINDOW + Q_ROWS, TOPK * Q_ROWS), F32),
            pltpu.VMEM((span, HD), F32),
            pltpu.VMEM((span, HD), F32),
            pltpu.VMEM((choices, HD), BF16),
            pltpu.VMEM((choices, HD), BF16),
        ] + [dma((experts,))] * 2 + [dma],
        compiler_params=pltpu.CompilerParams(
            collective_id=collective_id, has_side_effects=True, vmem_limit_bytes=56 * 2**20),
        cost_estimate=pl.CostEstimate(flops=10**11, bytes_accessed=10**7, transcendentals=0),
    )(slots, back, queries, keys, values, lse, segments, map_grad)


def fact_column(facts, k):
    return jnp.concatenate([facts, jnp.zeros((120, 256), F32)], axis=0).T[:CAP, k : k + 1]


def front_kernel(experts, bits, *refs):
    (tokens, gain, slots, routes, next_routes, routers, segments, w_in, kv_in, wo_in,
     rows, w, window, kv, keys, values, gates, facts_in, grouped, queries, lse, gate_row, rate_out, wo,
     back, x, y, facts, spread, gathered, bias, packed, heads,
     f_send, f_recv, v_send, v_recv, z_send, z_recv, t_send, t_recv, y_send, y_recv, w_send, w_recv, k_send, k_recv, n_send, n_recv, own_sem) = refs
    e, t = lax.axis_index("expert"), lax.axis_index("tensor")
    partner = partners(e, experts, True)
    width = x.shape[1]
    cap = rows.shape[1]
    here = tokens.shape[0]
    tensor = 1 << bits
    expert_bits = experts.bit_length() - 1
    pieces = experts * cap // x.shape[0]

    def x_part(j):
        return pl.ds(pl.multiple_of((j // pieces) * cap, cap), cap)

    def cols(d):
        return pl.ds(pl.multiple_of((t ^ d) * width, 128), width)

    def part(j):
        return pl.ds(j * (w.shape[0] // experts), w.shape[0] // experts)

    def block(q, d):
        if isinstance(q, int):
            return window.at[q - experts, :, cols(d)]
        return rows.at[q, :, cols(d)]

    def pass_on(q, d, b):
        far = d | (1 << b)
        return remote(block(q, d), block(q, d), t_send.at[q, far], t_recv.at[q, far], tensor=t ^ (1 << b))

    def passed(q, d):
        return remote(block(q, d), block(q, d), t_send.at[q, d], t_recv.at[q, d], tensor=t ^ (1 << low_bit(d)))

    def stage(q, k):
        bit = bits - k
        for d in range(1, tensor):
            if low_bit(d) == bit:
                passed(q, d).wait_recv()
                for b in reversed(range(bit)):
                    pass_on(q, d, b).start()

    def arrived(j):
        return remote(x.at[x_part(j)], rows.at[j, :, cols(0)], z_send.at[j], z_recv.at[j], expert=j)

    def handed(j):
        return remote(y.at[j], back.at[j], y_send.at[j], y_recv.at[j], expert=j)

    def chunk(d):
        return kv.at[:, part(e ^ d), :]

    def pass_chunk(d, b):
        far = d | (1 << b)
        return remote(chunk(d), chunk(d), k_send.at[far], k_recv.at[far], expert=e ^ (1 << b))

    def passed_chunk(d):
        return remote(chunk(d), chunk(d), k_send.at[d], k_recv.at[d], expert=e ^ (1 << low_bit(d)))

    def chunks(bit):
        for d in range(1, experts):
            if low_bit(d) == bit:
                passed_chunk(d).wait_recv()
                for b in reversed(range(bit)):
                    pass_chunk(d, b).start()

    def two_on(way):
        return remote(window.at[2, :, cols(0)], window.at[0, :, cols(0)], n_send.at[0], n_recv.at[0],
                      expert=lax.rem(e + experts + 2 * way, experts))

    def across():
        return remote(window.at[2 - 2 * (e & 1), :, cols(0)], window.at[1, :, cols(0)], n_send.at[1], n_recv.at[1],
                      expert=e ^ 1)

    own_kv = pltpu.make_async_copy(kv_in, chunk(0), own_sem.at[0])
    own_w = pltpu.make_async_copy(w_in.at[e], w.at[part(e)], own_sem.at[1])
    own_kv.start()
    own_w.start()
    meet(experts, bits)
    for b in reversed(range(expert_bits)):
        remote(kv_in, chunk(0), k_send.at[1 << b], k_recv.at[1 << b], expert=e ^ (1 << b)).start()

    state = tokens[...].astype(F32)
    rate = lax.rsqrt(jnp.mean(state * state, axis=1, keepdims=True) + eps)
    rate_out[...] = rate
    window[2] = (state * rate * gain[...].astype(F32)).astype(BF16)

    @pl.when(e < experts - 2)
    def _():
        two_on(1).start()

    @pl.when(e < 2)
    def _():
        window[0] = jnp.zeros((here, tensor * width), BF16)

    place = lax.broadcasted_iota(jnp.int32, (x.shape[0], here), 0)
    chosen = (place == slots[0:1, pl.ds(0, here)]) | (place == slots[0:1, pl.ds(here, here)])
    x[...] = jnp.dot(chosen.astype(F32).astype(BF16), window[2, :, cols(0)], preferred_element_type=F32).astype(BF16)

    @pl.loop(1, experts)
    def _(s):
        j = partner(s)
        remote(x.at[x_part(j)], rows.at[e, :, cols(0)], z_send.at[j], z_recv.at[e], expert=j).start()

    @pl.loop(1, experts)
    def _(s):
        j = partner(s)
        remote(w_in.at[j], w.at[part(e)], w_send.at[j], w_recv.at[e], expert=j).start()

    rows[e, :, cols(0)] = x[x_part(e), :]

    logits = lax.dot_general(routers[...], window[2], (((1,), (1,)), ((), ())), preferred_element_type=F32)
    row = lax.broadcasted_iota(jnp.int32, logits.shape, 0)
    first, second = (jnp.sum(jnp.where(row == routes[k : k + 1, :], logits, 0.0), axis=0, keepdims=True) for k in (0, 1))
    top = jnp.maximum(first, second)
    first, second = jnp.exp(first - top), jnp.exp(second - top)
    gate = jnp.concatenate([first / (first + second), second / (first + second)], axis=1)
    gate_row[...] = gate
    other = jnp.concatenate([next_routes[1:2, :], next_routes[0:1, :]], axis=1).astype(F32)
    high = gate.astype(BF16).astype(F32)
    middle = (gate - high).astype(BF16).astype(F32)
    empty = jnp.zeros((13, 2 * here), F32)
    tables = [jnp.concatenate([high, middle, gate - high - middle, empty], axis=0).astype(BF16),
              jnp.concatenate([other, empty, empty[:2]], axis=0).astype(BF16)]
    for q in range(EXPERTS):
        place = lax.broadcasted_iota(jnp.int32, (256, 2 * here), 0) + q * 256
        fact = [lax.dot_general(table, (place == slots[2 + k : 3 + k, :]).astype(F32).astype(BF16),
                                (((1,), (1,)), ((), ())), preferred_element_type=F32) for k, table in enumerate(tables)]
        row = lax.broadcasted_iota(jnp.int32, (8, 256), 0)
        facts[q] = jnp.where(row == 0, fact[0][0:1] + fact[0][1:2] + fact[0][2:3], jnp.where(row == 1, fact[1][0:1], 0.0))

    @pl.loop(1, experts)
    def _(s):
        j = partner(s)
        remote(facts.at[j // pieces], facts_in.at[e], f_send.at[j], f_recv.at[e], expert=j).start()

    facts_in[e] = facts[e // pieces]
    chunks(expert_bits - 1)
    place_matrices(slots, spread, gathered)
    mask_bias(segments, bias)

    @pl.loop(0, experts + bits)
    def _(i):
        @pl.when(i < experts)
        def _():
            j = partner(i)

            @pl.when(i > 0)
            def _():
                arrived(j).wait_recv()

            for b in reversed(range(bits)):
                pass_on(j, 0, b).start()

        for k in range(1, bits + 1):
            @pl.when((i >= k) & (i < experts + k))
            def _():
                stage(partner(i - k), k)

        @pl.when(i == experts // 2)
        def _():
            @pl.when(e >= 2)
            def _():
                two_on(-1).wait_recv()

            across().start()
            for b in reversed(range(bits)):
                pass_on(experts, 0, b).start()

    for bit in reversed(range(1, expert_bits - 1)):
        chunks(bit)
    across().wait_recv()
    for b in reversed(range(bits)):
        pass_on(experts + 1, 0, b).start()
    own_w.wait()

    @pl.loop(1, experts)
    def _(s):
        q = partner(s)
        remote(w_in.at[q], w.at[part(q)], w_send.at[q], w_recv.at[q], expert=q).wait_recv()

    @pl.loop(0, experts)
    def _(i):
        j = partner(lax.rem(i + 1, experts))
        y[j] = jnp.dot(rows[j], w[...], preferred_element_type=F32).astype(BF16)

        @pl.when(i < experts - 1)
        def _():
            remote(y.at[j], back.at[e], y_send.at[j], y_recv.at[e], expert=j).start()

    back[e] = y[e]

    def map_from(j):
        return remote(wo_in.at[j], wo.at[part(j)], v_send.at[j], v_recv.at[j], expert=j)

    own_wo = pltpu.make_async_copy(wo_in.at[e], wo.at[part(e)], own_sem.at[2])
    own_wo.start()

    @pl.loop(1, experts)
    def _(s):
        j = partner(s)
        remote(wo_in.at[j], wo.at[part(e)], v_send.at[j], v_recv.at[e], expert=j).start()

    for k in range(1, bits + 1):
        for q in range(2):
            stage(experts + q, k)
    chunks(0)
    own_kv.wait()
    for q in range(3):
        for c, out in enumerate((keys, values)):
            out[pl.ds(q * here, here), :] = jnp.dot(window[q], kv[c], preferred_element_type=F32).astype(BF16)

    @pl.loop(1, experts)
    def _(s):
        j = partner(s)
        fact_from = remote(facts.at[j // pieces], facts_in.at[j], f_send.at[j], f_recv.at[j], expert=j)
        fact_from.wait_recv()
        fact_from.wait_send()

    @pl.loop(0, experts)
    def _(j):
        gates[j] = fact_column(facts_in[j], 0)

    @pl.loop(1, experts)
    def _(s):
        handed(partner(s)).wait_recv()

    attend(back, keys, values, grouped, queries, lse, spread, gathered, bias, packed, heads)
    own_wo.wait()

    @pl.loop(1, experts)
    def _(s):
        j = partner(s)
        arrived(j).wait_send()
        handed(j).wait_send()
        remote(w_in.at[j], w.at[part(j)], w_send.at[j], w_recv.at[j], expert=j).wait_send()
        map_from(j).wait_recv()
        map_from(j).wait_send()

    for d in range(1, experts):
        passed_chunk(d).wait_send()
    @pl.when(e < experts - 2)
    def _():
        two_on(1).wait_send()

    across().wait_send()
    for q in range(2):
        for d in range(1, tensor):
            passed(experts + q, d).wait_send()

    @pl.loop(0, experts)
    def _(j):
        for d in range(1, tensor):
            passed(j, d).wait_send()


def front(tokens, gain, slots, routes, next_routes, routers, segments, w, kv, wo, collective_id):
    experts, tensor = lax.axis_size("expert"), lax.axis_size("tensor")
    bits = tensor.bit_length() - 1
    here = tokens.shape[0]
    f, f_kv = w.shape[2], kv.shape[2]
    dma = pltpu.SemaphoreType.DMA
    outs = [
        ((experts, CAP, D), BF16),
        ((D, f), BF16),
        ((3, here, D), BF16),
        ((2, D, f_kv), BF16),
        ((3 * here, f_kv), BF16),
        ((3 * here, f_kv), BF16),
        ((experts, CAP, 1), F32),
        ((experts, 8, 256), F32),
        ((SLOTS, f_kv), BF16),
        ((TOPK * here, f_kv), BF16),
        ((f_kv // HD, 1, TOPK * here), F32),
        ((1, TOPK * here), F32),
        ((here, 1), F32),
        ((D, f), BF16),
    ]
    return pl.pallas_call(
        functools.partial(front_kernel, experts, bits),
        out_shape=[jax.ShapeDtypeStruct(*out) for out in outs],
        in_specs=[VMEM] * 7 + [ANY] * 3,
        out_specs=[VMEM] * 13 + [ANY],
        scratch_shapes=[
            pltpu.VMEM((experts, CAP, f), BF16),
            pltpu.VMEM((SLOTS, D // tensor), BF16),
            pltpu.VMEM((experts, CAP, f), BF16),
            pltpu.VMEM((EXPERTS, 8, 256), F32),
            pltpu.VMEM((SLOTS, TOPK * here), BF16),
            pltpu.VMEM((TOPK * here, SLOTS), BF16),
            pltpu.VMEM((here // Q_ROWS, WINDOW + Q_ROWS, TOPK * Q_ROWS), F32),
            pltpu.VMEM((SLOTS, HD), BF16),
            pltpu.VMEM((TOPK * here, HD), BF16),
        ] + [dma((experts,))] * 6 + [dma((experts + 2, tensor))] * 2 + [dma((experts,))] * 6
        + [dma((2,))] * 2 + [dma((3,))],
        compiler_params=pltpu.CompilerParams(
            collective_id=collective_id, has_side_effects=True, vmem_limit_bytes=63 * 2**20),
        cost_estimate=pl.CostEstimate(flops=10**11, bytes_accessed=10**7, transcendentals=0),
    )(tokens, gain, slots, routes, next_routes, routers, segments, w, kv, wo)


def scatter_kernel(experts, bits, depth, near, scale, noted, *refs):
    refs = list(refs)
    h_in, w = refs[:2]
    refs = refs[2:]
    gate = refs.pop(0) if scale else None
    notes = refs.pop(0) if noted else None
    if depth:
        key_grad, value_grad, kv_in, rows_in, window_in = refs[:5]
        refs = refs[5:]
    back, h = refs[:2]
    refs = refs[2:]
    if depth:
        owed, map_grad, pair_kept, pair_came = refs[:4]
        refs = refs[4:]
    keep, sent, got, y, t_send, t_recv, y_send, y_recv, h_send, h_recv = refs[:10]
    if depth:
        (kv, rows, window, n_keep, n_sent, n_got, n_in, n_y, n_back, own, total_grad, pair_away,
         n_send, n_recv, o_send, o_recv, p_send, p_recv, l_sem) = refs[10:]
    e, t = lax.axis_index("expert"), lax.axis_index("tensor")
    partner = partners(e, experts, near)
    tensor = 1 << bits
    cap, width = h.shape[1], y.shape[2]
    body = pl.ds(0, cap)
    foot = pl.ds(cap, NOTES)

    def slice_at(d):
        return pl.ds(pl.multiple_of((t ^ d) * width, 128), width)

    def handed(j):
        return remote(y.at[j], back.at[j], y_send.at[j], y_recv.at[j], expert=j)

    def give(j, d):
        return remote(sent.at[j, d - 1], got.at[j, d - 1], t_send.at[j, d], t_recv.at[j, d], tensor=t ^ (1 << low_bit(d)))

    def owe(d):
        return remote(n_sent.at[d - 1], n_got.at[d - 1], n_send.at[d], n_recv.at[d], tensor=t ^ (1 << low_bit(d)))

    def across(c):
        grad = (key_grad, value_grad)[c]
        here = grad.shape[0] // 3
        return remote(grad.at[pl.ds(here, here)], n_in.at[c], o_send.at[c], o_recv.at[c], expert=e ^ 1)

    def two_back(way):
        return remote(n_y, n_back, o_send.at[2], o_recv.at[2], expert=lax.rem(e + experts - 2 * way, experts))

    def own_stage(k):
        for d in range(tensor - 1, -1, -1):
            if d % (1 << k) == 0:
                came = d | (1 << (k - 1))
                owe(came).wait_recv()
                total = n_keep[d // 2] + n_got[came - 1].astype(F32)
                if k == bits:
                    owed[...] = total.astype(BF16)
                elif d & (1 << k):
                    n_sent[d - 1] = total.astype(BF16)
                    owe(d).start()
                else:
                    n_keep[d // 2] = total

    order = [list(range(experts.bit_length() - 1)) for _ in range(2)]
    order[1][:2] = [1, 0]

    def pair_product(p, c):
        distance = 0
        for i, b in enumerate(reversed(order[c])):
            distance += ((p >> i) & 1) * (1 << b)
        some = window[:, shares(e ^ distance)]
        return lax.dot_general(some, (key_grad, value_grad)[c][...], (((0,), (0,)), ((), ())),
                               preferred_element_type=F32).astype(BF16)

    def pair_chunk(p, c):
        f = key_grad.shape[1]
        place, lanes = shares(p), pl.ds(c * f, f)
        return remote(pair_away.at[place, lanes], pair_came.at[place, lanes], p_send.at[c, p], p_recv.at[c, p],
                      expert=e ^ (1 << order[c][0]))

    def shares(q):
        share = map_grad.shape[1]
        return pl.ds(pl.multiple_of(q * share, share), share)

    def row_from(j):
        return remote(h_in.at[j], h.at[j], h_send.at[j], h_recv.at[j], expert=j)

    if depth:
        loads = [pltpu.make_async_copy(a, b, l_sem.at[i])
                 for i, (a, b) in enumerate(((window_in, window), (rows_in, rows), (kv_in, kv)))]
        for load in loads:
            load.start()
    meet(experts, bits)

    @pl.loop(1, experts)
    def _(s):
        j = partner(s)
        remote(h_in.at[j], h.at[e], h_send.at[j], h_recv.at[e], expert=j).start()

    h[e] = h_in[e]
    if depth:
        here = n_in.shape[1]
        f = key_grad.shape[1]
        for c in range(2):
            across(c).start()
        loads[0].wait()

        @pl.loop(0, experts // 2)
        def _(p):
            for c in range(2):
                pair_away[shares(p), pl.ds(c * f, f)] = pair_product(p + experts // 2, c)
                pair_chunk(p, c).start()

        passing = (e & 1).astype(F32)
        for c, grad in enumerate((key_grad, value_grad)):
            across(c).wait_recv()
            came = n_in[c].astype(F32)
            n_y[c] = (grad[pl.ds(0, here), :].astype(F32) + passing * came).astype(BF16)
            own[c] = grad[pl.ds(2 * here, here), :].astype(F32) + (1.0 - passing) * came
        @pl.when(e >= 2)
        def _():
            two_back(1).start()

        @pl.when(e >= experts - 2)
        def _():
            n_back[...] = jnp.zeros_like(n_back)

        @pl.loop(0, experts // 2)
        def _(p):
            for c in range(2):
                pair_kept[shares(p), pl.ds(c * f, f)] = pair_product(p, c)

    @pl.loop(0, experts + bits)
    def _(i):
        @pl.when(i < experts)
        def _():
            j = partner(i)
            slot = lax.rem(i, bits + 1)

            @pl.when(i > 0)
            def _():
                row_from(j).wait_recv()

            for d in range(tensor - 1, -1, -1):
                part = lax.dot_general(
                    h[j], w[slice_at(d), :], (((1,), (1,)), ((), ())), preferred_element_type=F32)
                if scale:
                    part = part * gate[j]
                if d & 1:
                    sent[j, d - 1, body, :] = part.astype(BF16)
                    if noted:
                        sent[j, d - 1, foot, :] = notes[j].astype(BF16)
                    give(j, d).start()
                else:
                    keep[slot, d // 2, body, :] = part
                    if noted:
                        keep[slot, d // 2, foot, :] = notes[j]

        for k in range(1, bits + 1):
            @pl.when((i >= k) & (i < experts + k))
            def _():
                m = i - k
                slot = lax.rem(m, bits + 1)
                j = partner(m)
                for d in range(tensor - 1, -1, -1):
                    if d % (1 << k) == 0:
                        came = d | (1 << (k - 1))
                        give(j, came).wait_recv()
                        total = keep[slot, d // 2] + got[j, came - 1].astype(F32)
                        if k == bits:
                            y[j] = total.astype(BF16)
                        elif d & (1 << k):
                            sent[j, d - 1] = total.astype(BF16)
                            give(j, d).start()
                        else:
                            keep[slot, d // 2] = total
                if k == bits:
                    @pl.when(m == 0)
                    def _():
                        back[e] = y[e]

                    @pl.when(m > 0)
                    def _():
                        remote(y.at[j], back.at[e], y_send.at[j], y_recv.at[e], expert=j).start()

        if depth:
            @pl.when(i == experts - 1)
            def _():
                @pl.when(e < experts - 2)
                def _():
                    two_back(-1).wait_recv()

                loads[2].wait()
                for c in range(2):
                    total_grad[c] = (own[c] + n_back[c].astype(F32)).astype(BF16)
                for d in range(tensor - 1, -1, -1):
                    part = None
                    for c in range(2):
                        term = lax.dot_general(total_grad[c], kv[c, slice_at(d), :], (((1,), (1,)), ((), ())),
                                               preferred_element_type=F32)
                        part = term if part is None else part + term
                    if d & 1:
                        n_sent[d - 1] = part.astype(BF16)
                        owe(d).start()
                    else:
                        n_keep[d // 2] = part

            @pl.when(i == experts)
            def _():
                own_stage(1)

    if depth:
        for k in range(2, bits + 1):
            own_stage(k)
        loads[1].wait()

        @pl.loop(0, experts)
        def _(i):
            map_grad[i] = lax.dot_general(
                rows[:, shares(i)], h[...].reshape(experts * cap, h.shape[2]), (((0,), (0,)), ((), ())),
                preferred_element_type=F32).astype(BF16)

    @pl.loop(1, experts)
    def _(s):
        j = partner(s)
        row_from(j).wait_send()
        handed(j).wait_recv()
        handed(j).wait_send()

    @pl.loop(0, experts)
    def _(j):
        for d in range(1, tensor):
            give(j, d).wait_send()

    if depth:
        for d in range(1, tensor):
            owe(d).wait_send()
        for c in range(2):
            across(c).wait_send()

        @pl.when(e >= 2)
        def _():
            two_back(1).wait_send()

        @pl.loop(0, experts // 2)
        def _(p):
            for c in range(2):
                pair_chunk(p, c).wait_recv()
                pair_chunk(p, c).wait_send()


def scatter_rows(h, w, gate=None, notes=None, windows=None, near=True, collective_id=0):
    experts, tensor = lax.axis_size("expert"), lax.axis_size("tensor")
    bits = tensor.bit_length() - 1
    high = CAP + (NOTES if notes is not None else 0)
    width, f = D // tensor, w.shape[1]
    dma = pltpu.SemaphoreType.DMA
    ins = [a for a in (h, w, gate, notes) if a is not None]
    outs = [jax.ShapeDtypeStruct((experts, high, width), BF16), jax.ShapeDtypeStruct(h.shape, BF16)]
    scratch = [
        pltpu.VMEM((bits + 1, tensor // 2, high, width), F32),
        pltpu.VMEM((experts, tensor - 1, high, width), BF16),
        pltpu.VMEM((experts, tensor - 1, high, width), BF16),
        pltpu.VMEM((experts, high, width), BF16),
    ] + [dma((experts, tensor))] * 2 + [dma((experts,))] * 4
    if windows is not None:
        ins += windows
        here = windows[0].shape[0] // 3
        outs.append(jax.ShapeDtypeStruct((here, width), BF16))
        outs.append(jax.ShapeDtypeStruct((experts, D // experts, f), BF16))
        outs += [jax.ShapeDtypeStruct((D // 2, 2 * windows[0].shape[1]), BF16)] * 2
        pair = (2, here, windows[0].shape[1])
        scratch += [
            pltpu.VMEM(windows[2].shape, BF16),
            pltpu.VMEM(windows[3].shape, BF16),
            pltpu.VMEM(windows[4].shape, BF16),
            pltpu.VMEM((tensor // 2, here, width), F32),
            pltpu.VMEM((tensor - 1, here, width), BF16),
            pltpu.VMEM((tensor - 1, here, width), BF16),
            pltpu.VMEM(pair, BF16),
            pltpu.VMEM(pair, BF16),
            pltpu.VMEM(pair, BF16),
            pltpu.VMEM(pair, F32),
            pltpu.VMEM(pair, BF16),
            pltpu.VMEM((D // 2, 2 * windows[0].shape[1]), BF16),
        ] + [dma((tensor,))] * 2 + [dma((3,))] * 2 + [dma((2, experts))] * 2 + [dma((3,))]
    return pl.pallas_call(
        functools.partial(scatter_kernel, experts, bits, windows is not None, near, gate is not None, notes is not None),
        out_shape=outs,
        in_specs=[VMEM] * (len(ins) - 3) + [VMEM if windows is None else ANY] * 3,
        out_specs=[VMEM] * (len(outs) - 1) + [VMEM if windows is None else ANY],
        scratch_shapes=scratch,
        compiler_params=pltpu.CompilerParams(
            collective_id=collective_id, has_side_effects=True, vmem_limit_bytes=63 * 2**20),
        cost_estimate=pl.CostEstimate(flops=10**11, bytes_accessed=10**7, transcendentals=0),
    )(*ins)


def ffn_kernel(experts, bits, pieces, *refs):
    (x_cols, dy_all, slots, facts, routers, gate_in, up_in, down_in,
     back, rows_out, dys_out, hidden_out, gate_out, up_out,
     x, dy, dy_near, land, gate_map, up_map, down_map, gate_pre, up_pre, hidden_grad, gates, pulls, moments, own_logits, low, sent, got, keep,
     z_send, z_recv, t_send, t_recv, r_send, r_recv, y_send, y_recv, w_sem, o_sem) = refs
    e, t = lax.axis_index("expert"), lax.axis_index("tensor")
    tensor = 1 << bits
    pairs = experts // 2
    width = x.shape[1]
    pair_rows = 2 * CAP
    sources = (x, dy)
    results = ((low.at[0], hidden_out), (low.at[1], gate_out), (low.at[2], up_out))

    def first_block(u):
        s = (lax.rem(u, pairs - 1) + 1) * lax.div(u + pairs - 1, pairs)
        return ((e >> 1) ^ s) * 2

    def block(j):
        return pl.ds(pl.multiple_of(j * CAP, CAP), CAP)

    def pair(j):
        return pl.ds(pl.multiple_of(j * CAP, pair_rows), pair_rows)

    def cols(d):
        return pl.ds(pl.multiple_of((t ^ d) * width, 128), width)

    def arrive(a, j):
        return remote(sources[a].at[block(j // pieces)], land.at[a, block(e), cols(0)], z_send.at[a, j], z_recv.at[a, e],
                      expert=j)

    def arrived(a, j):
        return remote(sources[a].at[block(j // pieces)], land.at[a, block(j), cols(0)], z_send.at[a, j], z_recv.at[a, j],
                      expert=j)

    def pass_on(a, j, d, b):
        place, far = land.at[a, block(j), cols(d)], d | (1 << b)
        return remote(place, place, t_send.at[a, j, far], t_recv.at[a, j, far], tensor=t ^ (1 << b))

    def passed(a, j, d):
        place = land.at[a, block(j), cols(d)]
        return remote(place, place, t_send.at[a, j, d], t_recv.at[a, j, d], tensor=t ^ (1 << low_bit(d)))

    def stage(j, k, arrays=(0, 1)):
        for q in range(2):
            for a in arrays:
                for d in range(1, tensor):
                    if low_bit(d) == bits - k:
                        passed(a, j + q, d).wait_recv()
                        for b in reversed(range(bits - k)):
                            pass_on(a, j + q, d, b).start()

    def place_of(u, q):
        return 2 * (u & 1) + q

    def give(u, q, d):
        j = first_block(u) + q
        return remote(sent.at[place_of(u, q), d - 1], got.at[j, d - 1], r_send.at[place_of(u, q), d - 1],
                      r_recv.at[j, d - 1], tensor=t ^ (1 << low_bit(d)))

    final = tensor // 2 - 1

    def hand_back(j):
        return remote(got.at[j, final], back.at[e], y_send.at[j], y_recv.at[e], expert=j)

    def handed(j):
        return remote(got.at[j, final], back.at[j], y_send.at[j], y_recv.at[j], expert=j)

    def sum_stage(u, k):
        j = first_block(u)
        for q in range(2):
            for d in range(tensor - 1, -1, -1):
                if d % (1 << k) == 0:
                    came = d | (1 << (k - 1))
                    give(u, q, came).wait_recv()
                    total = keep[q, d // 2] + got[j + q, came - 1].astype(F32)
                    if k == bits:
                        got[j + q, final] = total.astype(BF16)
                    elif d & (1 << k):
                        sent[place_of(u, q), d - 1] = total.astype(BF16)
                        give(u, q, d).start()
                    else:
                        keep[q, d // 2] = total

    def finish(u):
        j = first_block(u)
        for k in range(2, bits + 1):
            sum_stage(u, k)
        for q in range(2):
            @pl.when(j + q == e)
            def _():
                back[e] = got[e, final]

            @pl.when(j + q != e)
            def _():
                hand_back(j + q).start()

    def to_memory(j):
        copies = [pltpu.make_async_copy(land.at[a, pair(j)], out.at[pair(j)], o_sem.at[a])
                  for a, out in enumerate((rows_out, dys_out))]
        return copies

    def results_to_memory(j):
        return [pltpu.make_async_copy(source, out.at[pair(j)], o_sem.at[2 + i])
                for i, (source, out) in enumerate(results)]

    weights = [pltpu.make_async_copy(a, b, w_sem.at[i])
               for i, (a, b) in enumerate(((gate_in, gate_map), (up_in, up_map), (down_in, down_map)))]
    for copy in weights:
        copy.start()
    here = x_cols.shape[0]
    place = lax.broadcasted_iota(jnp.int32, (x.shape[0], here), 0)
    chosen = (place == slots[:, pl.ds(0, here)]) | (place == slots[:, pl.ds(here, here)])
    chosen = chosen.astype(F32).astype(BF16)
    x[...] = jnp.dot(chosen, x_cols[...], preferred_element_type=F32).astype(BF16)
    dy[...] = jnp.dot(chosen, dy_all[:, cols(0)], preferred_element_type=F32).astype(BF16)

    even = [d for d in range(2, tensor, 2)]

    def near_block(n):
        return first_block((n // 2) * (pairs - 1)) + n % 2

    for n in range(4):
        place = lax.broadcasted_iota(jnp.int32, (CAP, here), 0) + (near_block(n) // pieces) * CAP
        mine = (place == slots[:, pl.ds(0, here)]) | (place == slots[:, pl.ds(here, here)])
        mine = mine.astype(F32).astype(BF16)
        for i, d in enumerate(even):
            dy_near[n, i] = jnp.dot(mine, dy_all[:, cols(d)], preferred_element_type=F32).astype(BF16)

    def straight(n, i):
        j, d = near_block(n), even[i]
        return remote(dy_near.at[n, i], land.at[1, block(e), cols(d)], t_send.at[1, j, d], t_recv.at[1, e, d], expert=j)

    def came_straight(j, d):
        return remote(land.at[1, block(j), cols(d)], land.at[1, block(j), cols(d)], t_send.at[1, j, d], t_recv.at[1, j, d],
                      expert=j)

    meet(experts, bits)
    for a in range(2):
        arrive(a, e ^ 1).start()
    for n in range(2):
        @pl.when(near_block(n) != e)
        def _():
            for i in range(len(even)):
                straight(n, i).start()

    def send_pair(u):
        for q in range(2):
            for a in range(2):
                arrive(a, first_block(u) + q).start()

    def forward_pair(u):
        for q in range(2):
            for a in range(2):
                arrived(a, first_block(u) + q).wait_recv()
                for b in reversed(range(bits)):
                    pass_on(a, first_block(u) + q, 0, b).start()

    def forward_near(j):
        for a in range(2):
            arrived(a, j).wait_recv()
            for b in reversed(range(1 if a else bits)):
                pass_on(a, j, 0, b).start()
        for d in even:
            came_straight(j, d).wait_recv()
            pass_on(1, j, d, 0).start()

    send_pair(1)
    own = first_block(0)
    for a in range(2):
        land[a, block(e), cols(0)] = sources[a][block(e // pieces), :]
        for b in reversed(range(1 if a else bits)):
            pass_on(a, e, 0, b).start()
    for i, d in enumerate(even):
        land[1, block(e), cols(d)] = dy_near[e & 1, i]
        pass_on(1, e, d, 0).start()
    foot = pl.ds(pair_rows, NOTES)
    for d in range(tensor):
        for q in range(4):
            if d:
                sent[q, d - 1, foot, :] = jnp.zeros((NOTES, width), BF16)
        for q in range(2):
            if d % 2 == 0:
                keep[q, d // 2, foot, :] = jnp.zeros((NOTES, width), F32)
    forward_near(e ^ 1)
    for k in range(1, bits):
        stage(own, k, (0,))
    for copy in weights:
        copy.wait()

    @pl.loop(0, pairs)
    def _(u):
        j = first_block(u)
        stage(j, bits)
        for copy in to_memory(j):
            copy.start()
        rows = land[0, pair(j), :]
        gate_pre[...] = jnp.dot(rows, gate_map[...], preferred_element_type=F32)
        up_pre[...] = jnp.dot(rows, up_map[...], preferred_element_type=F32)
        logits = lax.dot_general(rows, routers[...], (((1,), (1,)), ((), ())), preferred_element_type=F32)
        lane = lax.broadcasted_iota(jnp.int32, logits.shape, 1)
        mine = jnp.sum(jnp.where(lane == EXPERTS + e // pieces, logits, 0.0), axis=1, keepdims=True)
        other = jnp.concatenate([fact_column(facts[j + q], 1) for q in range(2)], axis=0) + EXPERTS
        rival = jnp.sum(jnp.where(lane.astype(F32) == other, logits, 0.0), axis=1, keepdims=True)
        own_logits[...] = mine
        top = jnp.maximum(mine, rival)
        mine, rival = jnp.exp(mine - top), jnp.exp(rival - top)
        gates[...] = mine / (mine + rival)

        @pl.when(u < pairs - 2)
        def _():
            forward_pair(u + 1)
            send_pair(u + 2)

        @pl.when(u == pairs - 3)
        def _():
            for n in range(2, 4):
                for i in range(len(even)):
                    straight(n, i).start()

        @pl.when(u == pairs - 2)
        def _():
            for q in range(2):
                forward_near(first_block(u + 1) + q)

        hidden_grad[...] = lax.dot_general(
            land[1, pair(j), :], down_map[...], (((1,), (1,)), ((), ())), preferred_element_type=F32)

        @pl.when(u > 0)
        def _():
            for copy in results_to_memory(j):
                copy.wait()

        @pl.loop(0, pair_rows // 32)
        def _(r):
            some = pl.ds(pl.multiple_of(r * 32, 32), 32)
            gate_here, up_here = gate_pre[some, :], up_pre[some, :]
            weight = gates[some, :]
            sigma = 1.0 / (1.0 + jnp.exp(-gate_here))
            silu = gate_here * sigma
            hidden = silu * up_here
            grad = hidden_grad[some, :]
            pulls[some, :] = jnp.sum(hidden * grad, axis=1, keepdims=True)
            grad = grad * weight
            low[0, some, :] = (hidden * weight).astype(BF16)
            gate_low = (grad * up_here * (sigma * (1.0 + gate_here * (1.0 - sigma)))).astype(BF16)
            up_low = (grad * silu).astype(BF16)
            low[1, some, :] = gate_low
            low[2, some, :] = up_low
            moments[some, :] = jnp.sum(
                gate_low.astype(F32) * gate_here + up_low.astype(F32) * up_here, axis=1, keepdims=True)

        for copy in results_to_memory(j):
            copy.start()

        @pl.when(u > 0)
        def _():
            finish(u - 1)

        @pl.when(u > 1)
        def _():
            for q in range(2):
                for d in range(1, tensor):
                    give(u - 2, q, d).wait_send()

        noted = []
        for q in range(2):
            some = pl.ds(q * CAP, CAP)
            lane = lax.broadcasted_iota(jnp.int32, (CAP, 128), 1)
            shared = tensor * pieces
            column = jnp.where(lane == 0, pulls[some, :], jnp.where(lane == 1, gates[some, :] / shared, 0.0))
            column = jnp.where(lane == 2, moments[some, :], jnp.where(lane == 3, own_logits[some, :] / shared, column))
            column = jnp.concatenate([column, jnp.zeros((256 - CAP, 128), F32)], axis=0)
            noted.append(column.T[:NOTES])
        for d in range(tensor - 1, -1, -1):
            grad = lax.dot_general(low[1], gate_map[cols(d), :], (((1,), (1,)), ((), ())), preferred_element_type=F32)
            grad += lax.dot_general(low[2], up_map[cols(d), :], (((1,), (1,)), ((), ())), preferred_element_type=F32)
            out = jnp.dot(low[0], down_map[:, cols(d)], preferred_element_type=F32)
            for q in range(2):
                part = pl.ds(q * CAP, CAP)
                parts = [(pl.ds(0, CAP), slice(None), grad[q * CAP : (q + 1) * CAP]),
                         (pl.ds(CAP, CAP), slice(None), out[q * CAP : (q + 1) * CAP]),
                         (foot, pl.ds(0, 256), noted[q])]
                for place, lanes, value in parts:
                    if d & 1:
                        sent[place_of(u, q), d - 1, place, lanes] = value.astype(BF16)
                    else:
                        keep[q, d // 2, place, lanes] = value
                if d & 1:
                    give(u, q, d).start()
        sum_stage(u, 1)

        @pl.when(u < pairs - 1)
        def _():
            for k in range(1, bits):
                stage(first_block(u + 1), k, (0,))

                @pl.when(u < pairs - 2)
                def _():
                    stage(first_block(u + 1), k, (1,))

        for copy in to_memory(j):
            copy.wait()

    finish(pairs - 1)
    for copy in results_to_memory(0):
        copy.wait()
    for u in range(max(pairs - 2, 0), pairs):
        for q in range(2):
            for d in range(1, tensor):
                give(u, q, d).wait_send()

    @pl.loop(1, experts)
    def _(s):
        j = e ^ s
        for a in range(2):
            arrived(a, j).wait_send()
        handed(j).wait_recv()
        handed(j).wait_send()

    @pl.loop(0, experts)
    def _(j):
        for a in range(2):
            for d in range(1, tensor):
                if a == 0 or d & 1:
                    passed(a, j, d).wait_send()

        @pl.when(j != e)
        def _():
            for d in even:
                passed(1, j, d).wait_send()


def feed_forward(x, dy, slots, facts, routers, gate_map, up_map, down_map, collective_id):
    experts, tensor = lax.axis_size("expert"), lax.axis_size("tensor")
    bits = tensor.bit_length() - 1
    width, hidden = x.shape[1], gate_map.shape[1]
    high = 2 * CAP + NOTES
    count = experts * CAP
    dma = pltpu.SemaphoreType.DMA
    return pl.pallas_call(
        functools.partial(ffn_kernel, experts, bits, experts // EXPERTS),
        out_shape=[jax.ShapeDtypeStruct((experts, high, width), BF16)]
        + [jax.ShapeDtypeStruct((count, D), BF16)] * 2 + [jax.ShapeDtypeStruct((count, hidden), BF16)] * 3,
        in_specs=[VMEM] * 5 + [ANY] * 3,
        out_specs=[VMEM] + [ANY] * 5,
        scratch_shapes=[
            pltpu.VMEM((SLOTS, width), BF16),
            pltpu.VMEM((SLOTS, width), BF16),
            pltpu.VMEM((4, tensor // 2 - 1, CAP, width), BF16),
            pltpu.VMEM((2, count, D), BF16),
            pltpu.VMEM((D, hidden), BF16),
            pltpu.VMEM((D, hidden), BF16),
            pltpu.VMEM((hidden, D), BF16),
            pltpu.VMEM((2 * CAP, hidden), F32),
            pltpu.VMEM((2 * CAP, hidden), F32),
            pltpu.VMEM((2 * CAP, hidden), F32),
            pltpu.VMEM((2 * CAP, 1), F32),
            pltpu.VMEM((2 * CAP, 1), F32),
            pltpu.VMEM((2 * CAP, 1), F32),
            pltpu.VMEM((2 * CAP, 1), F32),
            pltpu.VMEM((3, 2 * CAP, hidden), BF16),
            pltpu.VMEM((4, tensor - 1, high, width), BF16),
            pltpu.VMEM((experts, tensor - 1, high, width), BF16),
            pltpu.VMEM((2, tensor // 2, high, width), F32),
        ] + [dma((2, experts))] * 2 + [dma((2, experts, tensor))] * 2
        + [dma((4, tensor - 1)), dma((experts, tensor - 1))] + [dma((experts,))] * 2 + [dma((3,)), dma((5,))],
        compiler_params=pltpu.CompilerParams(
            collective_id=collective_id, has_side_effects=True, vmem_limit_bytes=63 * 2**20),
        cost_estimate=pl.CostEstimate(flops=10**11, bytes_accessed=10**7, transcendentals=0),
    )(x, dy, slots, facts, routers, gate_map, up_map, down_map)


def small_kernel(experts, tensor, part, out, came, s_send, s_recv, b_send, b_recv):
    e, t = lax.axis_index("expert"), lax.axis_index("tensor")
    owners = experts // tensor
    width = out.shape[1]
    place = t * owners

    def to_owner(c):
        return remote(part.at[:, pl.ds(c * width, width)], came.at[e], s_send.at[c], s_recv.at[e], expert=place + c)

    barrier = pltpu.get_barrier_semaphore()

    @pl.loop(1, experts)
    def _(s):
        pl.semaphore_signal(barrier, inc=1, device_id={"expert": e ^ s}, device_id_type=MESH)

    @pl.loop(1, tensor)
    def _(s):
        pl.semaphore_signal(barrier, inc=1, device_id={"tensor": t ^ s}, device_id_type=MESH)

    pl.semaphore_wait(barrier, experts + tensor - 2)
    for c in range(owners):
        @pl.when(e != place + c)
        def _():
            to_owner(c).start()

        @pl.when(e == place + c)
        def _():
            came[e] = part[:, c * width : (c + 1) * width]

    @pl.when(e // owners == t)
    def _():
        @pl.loop(1, experts)
        def _(s):
            j = e ^ s
            remote(came.at[j], came.at[j], s_send.at[0], s_recv.at[j], expert=j).wait_recv()

        total = came[0]
        for j in range(1, experts):
            total += came[j]
        out[...] = total

        @pl.loop(1, tensor)
        def _(s):
            remote(out, out, b_send.at[s], b_recv, tensor=t ^ s).start()

        @pl.loop(1, tensor)
        def _(s):
            remote(out, out, b_send.at[s], b_recv, tensor=t ^ s).wait_send()

    @pl.when(e // owners != t)
    def _():
        remote(out, out, b_send.at[0], b_recv, tensor=e // owners).wait_recv()

    for c in range(owners):
        @pl.when(e != place + c)
        def _():
            to_owner(c).wait_send()


def small_sums(part, collective_id):
    experts, tensor = lax.axis_size("expert"), lax.axis_size("tensor")
    n, width = part.shape[0], D // experts
    dma = pltpu.SemaphoreType.DMA
    return pl.pallas_call(
        functools.partial(small_kernel, experts, tensor),
        out_shape=jax.ShapeDtypeStruct((n, width), F32),
        in_specs=[VMEM],
        out_specs=VMEM,
        scratch_shapes=[pltpu.VMEM((experts, n, width), F32), dma((experts // tensor,)), dma((experts,)), dma((tensor,)),
                        dma],
        compiler_params=pltpu.CompilerParams(collective_id=collective_id, has_side_effects=True),
        cost_estimate=pl.CostEstimate(flops=10**10, bytes_accessed=10**5, transcendentals=0),
    )(part)


def dot(left, right, dims):
    return lax.dot_general(left, right, ((dims[0], dims[1]), ((), ())), preferred_element_type=F32)


def mm(left, right):
    return dot(left, right, ((1,), (0,)))


def mm_nt(left, right):
    return dot(left, right, ((1,), (1,)))


def mm_tn(left, right):
    return dot(left, right, ((0,), (0,)))


def swap(blocks):
    return lax.all_to_all(blocks, "expert", split_axis=0, concat_axis=0, tiled=True)


def columns_together(rows):
    return lax.all_gather(rows, "tensor", axis=1, tiled=True)


def columns_summed(rows):
    return lax.psum_scatter(rows, "tensor", scatter_dimension=1, tiled=True)


def slot_numbers(routes):
    flat = routes.T.reshape(-1)
    place = jnp.arange(flat.shape[0], dtype=jnp.int32)
    earlier = (flat[:, None] == flat[None, :]) & (place[None, :] < place[:, None])
    return flat * CAP + jnp.sum(earlier.astype(jnp.int32), axis=1)


def spaced(slots, stride):
    return slots + (slots // CAP) * (stride - CAP)


def place_matrix(slots):
    return (jnp.arange(SLOTS, dtype=jnp.int32)[:, None] == slots[None, :]).astype(BF16)


def token_matrix(slots, stride=CAP, first=0):
    wide = (spaced(slots, stride) + first).reshape(TOPK, -1)
    place = jnp.arange(EXPERTS * stride, dtype=jnp.int32)[:, None]
    return ((place == wide[0][None, :]) | (place == wide[1][None, :])).astype(BF16)


def to_pieces(rows, pieces):
    if pieces == 1:
        return rows
    experts, r, c = rows.shape
    return rows.reshape(experts, r, pieces, c // pieces).transpose(0, 2, 1, 3).reshape(experts * pieces, r, -1)


def from_pieces(rows, pieces):
    if pieces == 1:
        return rows
    both, r, c = rows.shape
    return rows.reshape(both // pieces, pieces, r, c).transpose(0, 2, 1, 3).reshape(both // pieces, r, -1)


def for_pieces(rows, pieces):
    return jnp.repeat(rows, pieces, axis=0) if pieces > 1 else rows


def gate_back(gating, pulled, routes):
    inner_sum = gating * (pulled - jnp.sum(gating * pulled, axis=1, keepdims=True))
    one_hot = (routes[:, :, None] == jnp.arange(EXPERTS, dtype=jnp.int32)[None, None, :]).astype(F32)
    return jnp.sum(one_hot * inner_sum[:, :, None], axis=1).astype(BF16)


def per_device(
    tokens,
    segment_ids,
    attn_routes,
    ffn_routes,
    attn_gain,
    ffn_gain,
    routers,
    query_weight,
    output_weight,
    key_value_weight,
    gate_weight,
    up_weight,
    down_weight,
    cotangent,
):
    rows_here = tokens.shape[0]
    expert_count = lax.axis_size("expert")
    tensor_count = lax.axis_size("tensor")
    pieces = expert_count // EXPERTS
    column_count = D // tensor_count
    expert_index = lax.axis_index("expert")
    tensor_index = lax.axis_index("tensor")
    own = (expert_index // pieces).astype(F32)
    head_width = query_weight.shape[2]
    head_count = head_width // HD

    def cols(whole):
        return lax.dynamic_slice_in_dim(whole, tensor_index * column_count, column_count, whole.ndim - 1)

    def group_tokens(token_cols, places):
        return for_pieces(mm(places, token_cols).astype(BF16).reshape(EXPERTS, CAP, -1), pieces)

    def group_choices(choice_rows, places):
        return to_pieces(mm(places, choice_rows).astype(BF16).reshape(EXPERTS, CAP, -1), pieces)

    def choices_of(back, places):
        return mm_tn(places, from_pieces(back, pieces).reshape(SLOTS, -1)).astype(BF16)

    def sums_of(back, places):
        stride = back.shape[1]
        back = back.reshape(EXPERTS, pieces, stride, column_count)
        if pieces > 1:
            total = sum(mm_tn(places, back[:, p].reshape(EXPERTS * stride, -1)) for p in range(pieces))
        else:
            total = mm_tn(places, back.reshape(EXPERTS * stride, -1))
        return total

    def notes_of(*scalars):
        rows = jnp.stack([v.reshape(expert_count, CAP) for v in scalars], axis=1)
        return jnp.pad(rows, ((0, 0), (0, NOTES - len(scalars)), (0, column_count - CAP)))

    def read_notes(back, places, count, first=CAP):
        noted = back[:, first : first + count, :CAP].astype(F32)
        noted = noted.reshape(EXPERTS, pieces, count, CAP).sum(1).transpose(0, 2, 1).reshape(SLOTS, count)
        return mm_tn(places, noted.astype(BF16)).reshape(TOPK, rows_here, count)

    def exchange(away, b):
        return lax.ppermute(away, "expert", [(i, i ^ (1 << b)) for i in range(expert_count)])

    attn_slots, ffn_slots = slot_numbers(attn_routes), slot_numbers(ffn_routes)

    slots = jnp.stack([attn_slots, ffn_slots, spaced(attn_slots, 256), spaced(ffn_slots, 256)])
    segments = segment_ids[None]
    (rows_one, query_map, window, pair_map, keys, values, attn_gate_blocks, facts, heads, queries, log_total,
     gate_row, rate_one, output_map) = front(
        tokens, attn_gain[None], slots, attn_routes.T, ffn_routes.T, routers.T, segments,
        to_pieces(query_weight, pieces), key_value_weight, to_pieces(output_weight, pieces), collective_id=0)
    rows_one, attn_slots, ffn_slots, tokens, attn_gain, ffn_gain, routers, cotangent = lax.optimization_barrier(
        (rows_one, attn_slots, ffn_slots, tokens, attn_gain, ffn_gain, routers, cotangent))
    routers_one, routers_two = routers[:, :EXPERTS], routers[:, EXPERTS:]
    gain_one = attn_gain.astype(F32)
    gain_two = cols(ffn_gain.astype(F32))
    dy_cols = cols(cotangent)
    token_cols = cols(tokens).astype(F32)
    attn_places, ffn_places = place_matrix(attn_slots), place_matrix(ffn_slots)
    rows_one = rows_one.reshape(-1, D)
    normed_cols = lax.dynamic_slice(
        window, (2, 0, tensor_index * column_count), (1, rows_here, column_count)).reshape(rows_here, column_count)
    window = window.reshape(-1, D)
    attn_back, heads_rows = scatter_rows(
        to_pieces(heads.reshape(EXPERTS, CAP, -1), pieces), output_map, attn_gate_blocks, collective_id=1)
    heads_rows = heads_rows.reshape(expert_count * CAP, -1)
    state = token_cols + sums_of(attn_back, token_matrix(attn_slots))

    mean_two = lax.psum(jnp.sum(state * state, axis=1, keepdims=True), "tensor") / D
    rate_two = lax.rsqrt(mean_two + eps)
    normed_two = (state * rate_two * gain_two).astype(BF16)
    gate_map, up_map, down_map = gate_weight[0], up_weight[0], down_weight[0]
    ffn_back, rows_two, rows_dy, hidden, gate_low, up_low = feed_forward(
        normed_two, cotangent, ffn_slots[None], facts, routers.T, gate_map, up_map, down_map, collective_id=2)
    normed_two_grad = sums_of(ffn_back, token_matrix(ffn_slots, 2 * CAP + NOTES))
    ffn_pull, ffn_gates, moments, own_logits = (
        note.T for note in jnp.moveaxis(read_notes(ffn_back, ffn_places, 4, 2 * CAP), 2, 0))
    ffn_logit_grad = gate_back(ffn_gates, ffn_pull, ffn_routes)
    normed_two_grad = normed_two_grad + mm_nt(
        ffn_logit_grad, lax.dynamic_slice_in_dim(routers_two, tensor_index * column_count, column_count, 0))
    ffn_router_cols = mm_tn(normed_two, ffn_logit_grad)
    ffn_gain_cols = jnp.sum(normed_two_grad * state * rate_two, axis=0)
    ahead = normed_two_grad * gain_two
    chosen_grad = jnp.sum(
        jnp.where(ffn_routes[:, :, None] == jnp.arange(EXPERTS, dtype=jnp.int32), ffn_logit_grad[:, None].astype(F32), 0.0),
        axis=2)
    centre = jnp.sum(moments + chosen_grad * own_logits, axis=1, keepdims=True) / (rate_two * D)
    state_grad = dy_cols.astype(F32) + rate_two * ahead - state * rate_two * rate_two * rate_two * centre

    unused_rows, heads_grad, heads_grad_rows, output_grad = gather_rows(
        group_tokens(state_grad.astype(BF16), token_matrix(attn_slots)), output_map, gate=attn_gate_blocks,
        others=heads_rows.reshape(expert_count, CAP, -1), collective_id=4)
    heads_grad_rows = heads_grad_rows.reshape(expert_count * CAP, -1)
    attn_notes = notes_of(jnp.sum(heads_grad_rows.astype(F32) * heads_rows.astype(F32), axis=1))
    query_back, key_back, value_back, output_grad = attend_back(
        attn_slots[None], from_pieces(heads_grad, pieces).reshape(SLOTS, -1), queries, keys, values, log_total,
        segments, output_grad, collective_id=6)
    output_grad = from_pieces(output_grad, pieces).astype(F32)
    normed_back, unused_rows, owed, query_grad, pair_part, pair_came = scatter_rows(
        to_pieces(query_back.reshape(EXPERTS, CAP, -1), pieces), query_map, notes=attn_notes,
        windows=[key_back, value_back, pair_map, rows_one, window], collective_id=5)
    pair_part = (pair_part.astype(F32) + pair_came.astype(F32)).astype(BF16)
    pair_part, query_grad, rows_two, hidden = lax.optimization_barrier((pair_part, query_grad, rows_two, hidden))
    quarter = D // 4
    pair_came = jnp.concatenate(
        [exchange(pair_part[quarter:, :head_width], 1), exchange(pair_part[quarter:, head_width:], 0)], axis=1)
    query_grad = swap(query_grad)
    gate_grad = mm_tn(rows_two, gate_low)
    up_grad = mm_tn(rows_two, up_low)
    pair_came, hidden, gate_grad, up_grad = lax.optimization_barrier((pair_came, hidden, gate_grad, up_grad))
    pair_part = pair_part[:quarter].astype(F32) + pair_came.astype(F32)
    for b in range(2, expert_count.bit_length() - 1):
        rest = pair_part.shape[0] // 2
        pair_part = pair_part.astype(BF16)
        if b == 2:
            pair_part, hidden = lax.optimization_barrier((pair_part, hidden))
        pair_part = pair_part[:rest].astype(F32) + exchange(pair_part[rest:], b).astype(F32)
    down_grad = mm_tn(hidden, rows_dy)
    normed_back, owed, down_grad = lax.optimization_barrier((normed_back, owed, down_grad))
    normed_grad = sums_of(normed_back, token_matrix(attn_slots, CAP + NOTES)) + owed.astype(F32)
    attn_pull = read_notes(normed_back, attn_places, 1)[:, :, 0].T
    attn_gates = gate_row.reshape(TOPK, rows_here).T
    attn_logit_grad = gate_back(attn_gates, attn_pull, attn_routes)
    normed_grad = normed_grad + mm_nt(
        attn_logit_grad, lax.dynamic_slice_in_dim(routers_one, tensor_index * column_count, column_count, 0))
    attn_router_cols = mm_tn(normed_cols, attn_logit_grad)
    attn_gain_cols = jnp.sum(normed_grad * token_cols * rate_one, axis=0)
    ahead_one = normed_grad * cols(gain_one)
    centre_one = jnp.sum(ahead_one * token_cols, axis=1, keepdims=True)
    centre_one = lax.psum(centre_one, "tensor") / D
    tokens_grad = state_grad + rate_one * ahead_one - token_cols * rate_one * rate_one * rate_one * centre_one
    tokens_grad = columns_together(tokens_grad.astype(BF16)).astype(F32)

    small = jnp.concatenate(
        [attn_router_cols.T, ffn_router_cols.T, attn_gain_cols[None], ffn_gain_cols[None],
         jnp.zeros((6, column_count), F32)], axis=0)
    query_grad = from_pieces(query_grad, pieces).astype(F32)
    small, pair_part, query_grad, tokens_grad = lax.optimization_barrier((small, pair_part, query_grad, tokens_grad))
    small = small_sums(small, collective_id=3).T
    key_value_grad = pair_part.reshape(D // expert_count, 2, -1).transpose(1, 0, 2)
    ffn_out = sums_of(ffn_back, token_matrix(ffn_slots, 2 * CAP + NOTES, CAP))
    mixed = (state + ffn_out).astype(BF16)
    return (
        mixed,
        tokens_grad,
        small[:, 2 * EXPERTS],
        small[:, 2 * EXPERTS + 1],
        small[:, : 2 * EXPERTS],
        query_grad,
        output_grad,
        key_value_grad,
        gate_grad[None],
        up_grad[None],
        down_grad[None],
    )


def solution(mesh):
    in_specs = (
        P("expert", None),
        P(),
        P("expert", None),
        P("expert", None),
        P(),
        P(),
        P(),
        P(None, "expert", "tensor"),
        P(None, "expert", "tensor"),
        P(None, "expert", "tensor"),
        P("expert", None, "tensor"),
        P("expert", None, "tensor"),
        P("expert", "tensor", None),
        P("expert", None),
    )
    out_specs = (
        P("expert", "tensor"),
        P("expert", None),
        P("expert"),
        P("expert"),
        P("expert", None),
        P(None, "expert", "tensor"),
        P(None, "expert", "tensor"),
        P(None, "expert", "tensor"),
        P("expert", None, "tensor"),
        P("expert", None, "tensor"),
        P("expert", "tensor", None),
    )
    return jax.shard_map(
        per_device, mesh=mesh, in_specs=in_specs, out_specs=out_specs, check_vma=False
    )
```

```python
import functools
import math

import jax
import jax.numpy as jnp
from jax import lax
from jax.experimental import pallas as pl
from jax.experimental.pallas import tpu as pltpu
from jax.sharding import PartitionSpec as P

D = 2048
HD = 128
EXPERTS = 8
TOPK = 2
WINDOW = 1024
CAP = 160
SLOTS = EXPERTS * CAP

eps = 1e-06
masked_value = -1e30
SCALE = HD ** (-0.5)
LOG2E = math.log2(math.e)
Q_ROWS = 256
NOTES = 16
F32 = jnp.float32
BF16 = jnp.bfloat16
MESH = pl.DeviceIdType.MESH
VMEM = pl.BlockSpec(memory_space=pltpu.VMEM)
ANY = pl.BlockSpec(memory_space=pl.ANY)


def remote(src, dst, send, recv, **device):
    return pltpu.make_async_remote_copy(
        src_ref=src, dst_ref=dst, send_sem=send, recv_sem=recv, device_id=device, device_id_type=MESH)


def meet(experts, bits):
    e, t = lax.axis_index("expert"), lax.axis_index("tensor")
    barrier = pltpu.get_barrier_semaphore()

    @pl.loop(1, experts)
    def _(s):
        pl.semaphore_signal(barrier, inc=1, device_id={"expert": e ^ s}, device_id_type=MESH)

    for b in range(bits):
        pl.semaphore_signal(barrier, inc=1, device_id={"tensor": t ^ (1 << b)}, device_id_type=MESH)
    pl.semaphore_wait(barrier, experts - 1 + bits)


def partners(e, experts, near):
    if near:
        return lambda s: e ^ s
    return lambda s: e ^ ((experts - s) & (experts - 1))


def low_bit(d):
    return (d & -d).bit_length() - 1


def gather_kernel(experts, bits, near, multiply, scale, *refs):
    refs = list(refs)
    x = refs.pop(0)
    w = refs.pop(0) if multiply else None
    gate = refs.pop(0) if scale else None
    others = refs.pop(0) if scale else None
    rows = refs.pop(0)
    back = refs.pop(0) if multiply else None
    product = refs.pop(0) if scale else None
    map_grad = refs.pop(0) if scale else None
    y = refs.pop(0) if multiply else None
    z_send, z_recv, t_send, t_recv = refs[:4]
    refs = refs[4:]
    if multiply:
        y_send, y_recv = refs[:2]
    e, t = lax.axis_index("expert"), lax.axis_index("tensor")
    partner = partners(e, experts, near)
    width = x.shape[2]
    tensor = 1 << bits

    def cols(d):
        return pl.ds(pl.multiple_of((t ^ d) * width, 128), width)

    def arrive(j):
        return remote(x.at[j], rows.at[e, :, cols(0)], z_send.at[j], z_recv.at[e], expert=j)

    def arrived(j):
        return remote(x.at[j], rows.at[j, :, cols(0)], z_send.at[j], z_recv.at[j], expert=j)

    def pass_on(j, d, b):
        place = rows.at[j, :, cols(d)]
        far = d | (1 << b)
        return remote(place, place, t_send.at[j, far], t_recv.at[j, far], tensor=t ^ (1 << b))

    def passed(j, d):
        place = rows.at[j, :, cols(d)]
        return remote(place, place, t_send.at[j, d], t_recv.at[j, d], tensor=t ^ (1 << low_bit(d)))

    def hand_back(j):
        return remote(y.at[j], back.at[e], y_send.at[j], y_recv.at[e], expert=j)

    def handed(j):
        return remote(y.at[j], back.at[j], y_send.at[j], y_recv.at[j], expert=j)

    meet(experts, bits)

    @pl.loop(1, experts)
    def _(s):
        arrive(partner(s)).start()

    rows[e, :, cols(0)] = x[e]

    @pl.loop(0, experts + bits)
    def _(i):
        @pl.when(i < experts)
        def _():
            j = partner(i)

            @pl.when(i > 0)
            def _():
                arrived(j).wait_recv()

            for b in reversed(range(bits)):
                pass_on(j, 0, b).start()

        for k in range(1, bits + 1):
            @pl.when((i >= k) & (i < experts + k))
            def _():
                m = i - k
                j = partner(m)
                bit = bits - k
                for d in range(1, tensor):
                    if low_bit(d) == bit:
                        passed(j, d).wait_recv()
                        for b in reversed(range(bit)):
                            pass_on(j, d, b).start()
                if k == bits and multiply:
                    out = jnp.dot(rows[j], w[...], preferred_element_type=F32)
                    if scale:
                        product[j] = out.astype(BF16)
                        out = out * gate[j]
                    y[j] = out.astype(BF16)

                    @pl.when(m == 0)
                    def _():
                        back[e] = y[e]

                    @pl.when(m > 0)
                    def _():
                        hand_back(j).start()

    if scale:
        cap, f = others.shape[1], others.shape[2]
        share = map_grad.shape[1]
        scaled = (others[...].astype(F32) * gate[...]).astype(BF16).reshape(experts * cap, f)

        @pl.loop(0, experts)
        def _(j):
            some = rows[:, :, pl.ds(pl.multiple_of(j * share, share), share)].reshape(experts * cap, share)
            map_grad[j] = lax.dot_general(
                some, scaled, (((0,), (0,)), ((), ())), preferred_element_type=F32).astype(BF16)

    @pl.loop(1, experts)
    def _(s):
        j = partner(s)
        arrived(j).wait_send()
        if multiply:
            handed(j).wait_recv()
            handed(j).wait_send()

    @pl.loop(0, experts)
    def _(j):
        for d in range(1, tensor):
            passed(j, d).wait_send()


def gather_rows(x, w=None, gate=None, others=None, near=True, collective_id=0):
    experts, tensor = lax.axis_size("expert"), lax.axis_size("tensor")
    bits = tensor.bit_length() - 1
    cap, width = x.shape[1], x.shape[2]
    multiply = w is not None
    f = w.shape[-1] if multiply else 0
    ins, specs = [x], [VMEM]
    outs = [jax.ShapeDtypeStruct((experts, cap, width * tensor), BF16)]
    scratch = []
    if multiply:
        ins.append(w)
        specs.append(VMEM)
        outs.append(jax.ShapeDtypeStruct((experts, cap, f), BF16))
    if gate is not None:
        ins += [gate, others]
        specs += [VMEM, VMEM]
        outs.append(jax.ShapeDtypeStruct((experts, cap, f), BF16))
        outs.append(jax.ShapeDtypeStruct((experts, D // experts, f), BF16))
    if multiply:
        scratch.append(pltpu.VMEM((experts, cap, f), BF16))
    scratch += [pltpu.SemaphoreType.DMA((experts,))] * 2 + [pltpu.SemaphoreType.DMA((experts, tensor))] * 2
    if multiply:
        scratch += [pltpu.SemaphoreType.DMA((experts,))] * 2
    return pl.pallas_call(
        functools.partial(gather_kernel, experts, bits, near, multiply, gate is not None),
        out_shape=outs,
        in_specs=specs,
        out_specs=[VMEM] * len(outs),
        scratch_shapes=scratch,
        compiler_params=pltpu.CompilerParams(
            collective_id=collective_id, has_side_effects=True, vmem_limit_bytes=48 * 2**20),
        cost_estimate=pl.CostEstimate(flops=10**11, bytes_accessed=10**7, transcendentals=0),
    )(*ins)


def place_matrices(slots_ref, spread, gathered):
    count, choices = spread.shape
    spread[...] = (lax.broadcasted_iota(jnp.int32, (count, choices), 0) == slots_ref[0:1, :]).astype(F32).astype(BF16)
    gathered[...] = spread[...].T


def mask_bias(segments, bias):
    blocks, span, _ = bias.shape
    here = blocks * Q_ROWS
    e, experts = lax.axis_index("expert"), lax.axis_size("expert")
    parts = []
    for back in range(WINDOW // here, -1, -1):
        device = lax.rem(e + experts - back, experts)
        part = segments[:, pl.ds(pl.multiple_of(device * here, 128), here)]
        parts.append(jnp.where(e >= back, part, -1))
    query_ids = parts[-1]
    key_row = jnp.concatenate(parts, axis=1).astype(F32)
    key_ids = jnp.concatenate([key_row, jnp.zeros((7, WINDOW + here), F32)], axis=0).T[:, 0:1].astype(jnp.int32)

    for block in range(blocks):
        first = block * Q_ROWS
        query_place = lax.broadcasted_iota(jnp.int32, (span, Q_ROWS), 1) + WINDOW
        distance = query_place - lax.broadcasted_iota(jnp.int32, (span, Q_ROWS), 0)
        same = key_ids[first : first + span] == query_ids[:, first : first + Q_ROWS]
        allowed = (distance >= 0) & (distance < WINDOW) & same
        part = jnp.where(allowed, 0.0, masked_value)
        for k in range(TOPK):
            bias[block, :, pl.ds(k * Q_ROWS, Q_ROWS)] = part


def of_block(choices, block, lanes):
    rows = choices.shape[0] // TOPK
    return jnp.concatenate([choices[pl.ds(k * rows + block * Q_ROWS, Q_ROWS), lanes] for k in range(TOPK)], axis=0)


def attend(back, keys_ref, values_ref, grouped, queries_ref, lse, spread, gathered, bias, packed, heads):
    blocks, span, _ = bias.shape
    rows = queries_ref.shape[0] // TOPK
    pieces, of_piece = back.shape[0] // EXPERTS, back.shape[2] // HD

    @pl.loop(0, queries_ref.shape[1] // HD)
    def _(head):
        lanes = pl.ds(pl.multiple_of(head * HD, HD), HD)
        inner = pl.ds(pl.multiple_of(lax.rem(head, of_piece) * HD, HD), HD)
        for q in range(EXPERTS):
            packed[pl.ds(q * CAP, CAP), :] = back[q * pieces + lax.div(head, of_piece), :, inner]
        queries_ref[:, lanes] = jnp.dot(gathered[...], packed[...], preferred_element_type=F32).astype(BF16)
        for block in range(blocks):
            place = pl.ds(block * Q_ROWS, span)
            queries = of_block(queries_ref, block, lanes)
            scores = lax.dot_general(
                keys_ref[place, lanes], queries, (((1,), (1,)), ((), ())), preferred_element_type=F32)
            scores = scores * (SCALE * LOG2E) + bias[block]
            top = jnp.max(scores, axis=0, keepdims=True)
            probs = jnp.exp2(scores - top)
            total = jnp.sum(probs, axis=0, keepdims=True)
            out = lax.dot_general(
                values_ref[place, lanes], probs.astype(BF16), (((0,), (0,)), ((), ())), preferred_element_type=F32)
            out = (out * (1.0 / total)).T.astype(BF16)
            for k in range(TOPK):
                heads[pl.ds(k * rows + block * Q_ROWS, Q_ROWS), :] = out[k * Q_ROWS : (k + 1) * Q_ROWS]
            lse[head, :, pl.ds(block * TOPK * Q_ROWS, TOPK * Q_ROWS)] = top + jnp.log2(total)
        grouped[:, lanes] = jnp.dot(spread[...], heads[...], preferred_element_type=F32).astype(BF16)


def attend_back_kernel(experts, *refs):
    (slots, back, queries_ref, keys_ref, values_ref, lse, segments, part_grad,
     grouped, key_grad, value_grad, map_grad,
     spread, gathered, bias, key_acc, value_acc, query_grad, head_grad,
     g_send, g_recv, own_sem) = refs
    e = lax.axis_index("expert")
    blocks, span, _ = bias.shape
    here = queries_ref.shape[0] // TOPK
    def grad_from(j):
        return remote(part_grad.at[j], map_grad.at[j], g_send.at[j], g_recv.at[j], expert=j)

    barrier = pltpu.get_barrier_semaphore()

    @pl.loop(1, experts)
    def _(s):
        pl.semaphore_signal(barrier, inc=1, device_id={"expert": e ^ s}, device_id_type=MESH)

    own = pltpu.make_async_copy(part_grad.at[e], map_grad.at[e], own_sem)
    own.start()
    pl.semaphore_wait(barrier, experts - 1)

    @pl.loop(1, experts)
    def _(s):
        j = e ^ s
        remote(part_grad.at[j], map_grad.at[e], g_send.at[j], g_recv.at[e], expert=j).start()

    place_matrices(slots, spread, gathered)
    mask_bias(segments, bias)

    @pl.loop(0, queries_ref.shape[1] // HD)
    def _(head):
        lanes = pl.ds(pl.multiple_of(head * HD, HD), HD)
        head_grad[...] = jnp.dot(gathered[...], back[:, lanes], preferred_element_type=F32).astype(BF16)
        key_acc[...] = jnp.zeros_like(key_acc)
        value_acc[...] = jnp.zeros_like(value_acc)
        for block in range(blocks):
            queries = of_block(queries_ref, block, lanes)
            grads = of_block(head_grad, block, slice(None))
            place = pl.ds(block * Q_ROWS, span)
            keys, values = keys_ref[place, lanes], values_ref[place, lanes]
            scores = lax.dot_general(keys, queries, (((1,), (1,)), ((), ())), preferred_element_type=F32)
            probs = jnp.exp2(scores * (SCALE * LOG2E) + bias[block]
                             - lse[head, :, pl.ds(block * TOPK * Q_ROWS, TOPK * Q_ROWS)])
            pulled = lax.dot_general(values, grads, (((1,), (1,)), ((), ())), preferred_element_type=F32)
            pulled = probs * pulled
            inner = jnp.sum(pulled, axis=0, keepdims=True)
            score_grad = (pulled - probs * inner).astype(BF16)
            value_acc[place, :] += jnp.dot(probs.astype(BF16), grads, preferred_element_type=F32)
            key_acc[place, :] += jnp.dot(score_grad, queries, preferred_element_type=F32)
            out = lax.dot_general(keys, score_grad, (((0,), (0,)), ((), ())), preferred_element_type=F32)
            out = (out * SCALE).T.astype(BF16)
            for k in range(TOPK):
                query_grad[pl.ds(k * here + block * Q_ROWS, Q_ROWS), :] = out[k * Q_ROWS : (k + 1) * Q_ROWS]
        grouped[:, lanes] = jnp.dot(spread[...], query_grad[...], preferred_element_type=F32).astype(BF16)
        key_grad[:, lanes] = (key_acc[...] * SCALE).astype(BF16)
        value_grad[:, lanes] = value_acc[...].astype(BF16)

    own.wait()

    @pl.loop(1, experts)
    def _(s):
        grad_from(e ^ s).wait_recv()
        grad_from(e ^ s).wait_send()


def attend_back(slots, back, queries, keys, values, lse, segments, map_grad, collective_id):
    experts = lax.axis_size("expert")
    choices, (count, width), span = queries.shape[0], back.shape, keys.shape[0]
    blocks = choices // TOPK // Q_ROWS
    dma = pltpu.SemaphoreType.DMA
    return pl.pallas_call(
        functools.partial(attend_back_kernel, experts),
        out_shape=[
            jax.ShapeDtypeStruct((count, width), BF16),
            jax.ShapeDtypeStruct((span, width), BF16),
            jax.ShapeDtypeStruct((span, width), BF16),
            jax.ShapeDtypeStruct(map_grad.shape, BF16),
        ],
        in_specs=[VMEM] * 7 + [ANY],
        out_specs=[VMEM] * 3 + [ANY],
        scratch_shapes=[
            pltpu.VMEM((count, choices), BF16),
            pltpu.VMEM((choices, count), BF16),
            pltpu.VMEM((blocks, WINDOW + Q_ROWS, TOPK * Q_ROWS), F32),
            pltpu.VMEM((span, HD), F32),
            pltpu.VMEM((span, HD), F32),
            pltpu.VMEM((choices, HD), BF16),
            pltpu.VMEM((choices, HD), BF16),
        ] + [dma((experts,))] * 2 + [dma],
        compiler_params=pltpu.CompilerParams(
            collective_id=collective_id, has_side_effects=True, vmem_limit_bytes=56 * 2**20),
        cost_estimate=pl.CostEstimate(flops=10**11, bytes_accessed=10**7, transcendentals=0),
    )(slots, back, queries, keys, values, lse, segments, map_grad)


def fact_column(facts, k):
    return jnp.concatenate([facts, jnp.zeros((120, 256), F32)], axis=0).T[:CAP, k : k + 1]


def front_kernel(experts, bits, *refs):
    (tokens, gain, slots, routes, next_routes, routers, segments, w_in, kv_in, wo_in,
     rows, w, window, kv, keys, values, gates, facts_in, grouped, queries, lse, gate_row, rate_out, wo,
     back, x, y, facts, spread, gathered, bias, packed, heads,
     f_send, f_recv, v_send, v_recv, z_send, z_recv, t_send, t_recv, y_send, y_recv, w_send, w_recv, k_send, k_recv, n_send, n_recv, own_sem) = refs
    e, t = lax.axis_index("expert"), lax.axis_index("tensor")
    partner = partners(e, experts, True)
    width = x.shape[1]
    cap = rows.shape[1]
    here = tokens.shape[0]
    tensor = 1 << bits
    expert_bits = experts.bit_length() - 1
    pieces = experts * cap // x.shape[0]

    def x_part(j):
        return pl.ds(pl.multiple_of((j // pieces) * cap, cap), cap)

    def cols(d):
        return pl.ds(pl.multiple_of((t ^ d) * width, 128), width)

    def part(j):
        return pl.ds(j * (w.shape[0] // experts), w.shape[0] // experts)

    def block(q, d):
        if isinstance(q, int):
            return window.at[q - experts, :, cols(d)]
        return rows.at[q, :, cols(d)]

    def pass_on(q, d, b):
        far = d | (1 << b)
        return remote(block(q, d), block(q, d), t_send.at[q, far], t_recv.at[q, far], tensor=t ^ (1 << b))

    def passed(q, d):
        return remote(block(q, d), block(q, d), t_send.at[q, d], t_recv.at[q, d], tensor=t ^ (1 << low_bit(d)))

    def stage(q, k):
        bit = bits - k
        for d in range(1, tensor):
            if low_bit(d) == bit:
                passed(q, d).wait_recv()
                for b in reversed(range(bit)):
                    pass_on(q, d, b).start()

    def arrived(j):
        return remote(x.at[x_part(j)], rows.at[j, :, cols(0)], z_send.at[j], z_recv.at[j], expert=j)

    def handed(j):
        return remote(y.at[j], back.at[j], y_send.at[j], y_recv.at[j], expert=j)

    def chunk(d):
        return kv.at[:, part(e ^ d), :]

    def pass_chunk(d, b):
        far = d | (1 << b)
        return remote(chunk(d), chunk(d), k_send.at[far], k_recv.at[far], expert=e ^ (1 << b))

    def passed_chunk(d):
        return remote(chunk(d), chunk(d), k_send.at[d], k_recv.at[d], expert=e ^ (1 << low_bit(d)))

    def chunks(bit):
        for d in range(1, experts):
            if low_bit(d) == bit:
                passed_chunk(d).wait_recv()
                for b in reversed(range(bit)):
                    pass_chunk(d, b).start()

    def two_on(way):
        return remote(window.at[2, :, cols(0)], window.at[0, :, cols(0)], n_send.at[0], n_recv.at[0],
                      expert=lax.rem(e + experts + 2 * way, experts))

    def across():
        return remote(window.at[2 - 2 * (e & 1), :, cols(0)], window.at[1, :, cols(0)], n_send.at[1], n_recv.at[1],
                      expert=e ^ 1)

    own_kv = pltpu.make_async_copy(kv_in, chunk(0), own_sem.at[0])
    own_w = pltpu.make_async_copy(w_in.at[e], w.at[part(e)], own_sem.at[1])
    own_kv.start()
    own_w.start()
    meet(experts, bits)
    for b in reversed(range(expert_bits)):
        remote(kv_in, chunk(0), k_send.at[1 << b], k_recv.at[1 << b], expert=e ^ (1 << b)).start()

    state = tokens[...].astype(F32)
    rate = lax.rsqrt(jnp.mean(state * state, axis=1, keepdims=True) + eps)
    rate_out[...] = rate
    window[2] = (state * rate * gain[...].astype(F32)).astype(BF16)

    @pl.when(e < experts - 2)
    def _():
        two_on(1).start()

    @pl.when(e < 2)
    def _():
        window[0] = jnp.zeros((here, tensor * width), BF16)

    place = lax.broadcasted_iota(jnp.int32, (x.shape[0], here), 0)
    chosen = (place == slots[0:1, pl.ds(0, here)]) | (place == slots[0:1, pl.ds(here, here)])
    x[...] = jnp.dot(chosen.astype(F32).astype(BF16), window[2, :, cols(0)], preferred_element_type=F32).astype(BF16)

    @pl.loop(1, experts)
    def _(s):
        j = partner(s)
        remote(x.at[x_part(j)], rows.at[e, :, cols(0)], z_send.at[j], z_recv.at[e], expert=j).start()

    @pl.loop(1, experts)
    def _(s):
        j = partner(s)
        remote(w_in.at[j], w.at[part(e)], w_send.at[j], w_recv.at[e], expert=j).start()

    rows[e, :, cols(0)] = x[x_part(e), :]

    logits = lax.dot_general(routers[...], window[2], (((1,), (1,)), ((), ())), preferred_element_type=F32)
    row = lax.broadcasted_iota(jnp.int32, logits.shape, 0)
    first, second = (jnp.sum(jnp.where(row == routes[k : k + 1, :], logits, 0.0), axis=0, keepdims=True) for k in (0, 1))
    top = jnp.maximum(first, second)
    first, second = jnp.exp(first - top), jnp.exp(second - top)
    gate = jnp.concatenate([first / (first + second), second / (first + second)], axis=1)
    gate_row[...] = gate
    other = jnp.concatenate([next_routes[1:2, :], next_routes[0:1, :]], axis=1).astype(F32)
    high = gate.astype(BF16).astype(F32)
    middle = (gate - high).astype(BF16).astype(F32)
    empty = jnp.zeros((13, 2 * here), F32)
    tables = [jnp.concatenate([high, middle, gate - high - middle, empty], axis=0).astype(BF16),
              jnp.concatenate([other, empty, empty[:2]], axis=0).astype(BF16)]
    for q in range(EXPERTS):
        place = lax.broadcasted_iota(jnp.int32, (256, 2 * here), 0) + q * 256
        fact = [lax.dot_general(table, (place == slots[2 + k : 3 + k, :]).astype(F32).astype(BF16),
                                (((1,), (1,)), ((), ())), preferred_element_type=F32) for k, table in enumerate(tables)]
        row = lax.broadcasted_iota(jnp.int32, (8, 256), 0)
        facts[q] = jnp.where(row == 0, fact[0][0:1] + fact[0][1:2] + fact[0][2:3], jnp.where(row == 1, fact[1][0:1], 0.0))

    @pl.loop(1, experts)
    def _(s):
        j = partner(s)
        remote(facts.at[j // pieces], facts_in.at[e], f_send.at[j], f_recv.at[e], expert=j).start()

    facts_in[e] = facts[e // pieces]
    chunks(expert_bits - 1)
    place_matrices(slots, spread, gathered)
    mask_bias(segments, bias)

    @pl.loop(0, experts + bits)
    def _(i):
        @pl.when(i < experts)
        def _():
            j = partner(i)

            @pl.when(i > 0)
            def _():
                arrived(j).wait_recv()

            for b in reversed(range(bits)):
                pass_on(j, 0, b).start()

        for k in range(1, bits + 1):
            @pl.when((i >= k) & (i < experts + k))
            def _():
                stage(partner(i - k), k)

        @pl.when(i == experts // 2)
        def _():
            @pl.when(e >= 2)
            def _():
                two_on(-1).wait_recv()

            across().start()
            for b in reversed(range(bits)):
                pass_on(experts, 0, b).start()

    for bit in reversed(range(1, expert_bits - 1)):
        chunks(bit)
    across().wait_recv()
    for b in reversed(range(bits)):
        pass_on(experts + 1, 0, b).start()
    own_w.wait()

    @pl.loop(1, experts)
    def _(s):
        q = partner(s)
        remote(w_in.at[q], w.at[part(q)], w_send.at[q], w_recv.at[q], expert=q).wait_recv()

    @pl.loop(0, experts)
    def _(i):
        j = partner(lax.rem(i + 1, experts))
        y[j] = jnp.dot(rows[j], w[...], preferred_element_type=F32).astype(BF16)

        @pl.when(i < experts - 1)
        def _():
            remote(y.at[j], back.at[e], y_send.at[j], y_recv.at[e], expert=j).start()

    back[e] = y[e]

    def map_from(j):
        return remote(wo_in.at[j], wo.at[part(j)], v_send.at[j], v_recv.at[j], expert=j)

    own_wo = pltpu.make_async_copy(wo_in.at[e], wo.at[part(e)], own_sem.at[2])
    own_wo.start()

    @pl.loop(1, experts)
    def _(s):
        j = partner(s)
        remote(wo_in.at[j], wo.at[part(e)], v_send.at[j], v_recv.at[e], expert=j).start()

    for k in range(1, bits + 1):
        for q in range(2):
            stage(experts + q, k)
    chunks(0)
    own_kv.wait()
    for q in range(3):
        for c, out in enumerate((keys, values)):
            out[pl.ds(q * here, here), :] = jnp.dot(window[q], kv[c], preferred_element_type=F32).astype(BF16)

    @pl.loop(1, experts)
    def _(s):
        j = partner(s)
        fact_from = remote(facts.at[j // pieces], facts_in.at[j], f_send.at[j], f_recv.at[j], expert=j)
        fact_from.wait_recv()
        fact_from.wait_send()

    @pl.loop(0, experts)
    def _(j):
        gates[j] = fact_column(facts_in[j], 0)

    @pl.loop(1, experts)
    def _(s):
        handed(partner(s)).wait_recv()

    attend(back, keys, values, grouped, queries, lse, spread, gathered, bias, packed, heads)
    own_wo.wait()

    @pl.loop(1, experts)
    def _(s):
        j = partner(s)
        arrived(j).wait_send()
        handed(j).wait_send()
        remote(w_in.at[j], w.at[part(j)], w_send.at[j], w_recv.at[j], expert=j).wait_send()
        map_from(j).wait_recv()
        map_from(j).wait_send()

    for d in range(1, experts):
        passed_chunk(d).wait_send()
    @pl.when(e < experts - 2)
    def _():
        two_on(1).wait_send()

    across().wait_send()
    for q in range(2):
        for d in range(1, tensor):
            passed(experts + q, d).wait_send()

    @pl.loop(0, experts)
    def _(j):
        for d in range(1, tensor):
            passed(j, d).wait_send()


def front(tokens, gain, slots, routes, next_routes, routers, segments, w, kv, wo, collective_id):
    experts, tensor = lax.axis_size("expert"), lax.axis_size("tensor")
    bits = tensor.bit_length() - 1
    here = tokens.shape[0]
    f, f_kv = w.shape[2], kv.shape[2]
    dma = pltpu.SemaphoreType.DMA
    outs = [
        ((experts, CAP, D), BF16),
        ((D, f), BF16),
        ((3, here, D), BF16),
        ((2, D, f_kv), BF16),
        ((3 * here, f_kv), BF16),
        ((3 * here, f_kv), BF16),
        ((experts, CAP, 1), F32),
        ((experts, 8, 256), F32),
        ((SLOTS, f_kv), BF16),
        ((TOPK * here, f_kv), BF16),
        ((f_kv // HD, 1, TOPK * here), F32),
        ((1, TOPK * here), F32),
        ((here, 1), F32),
        ((D, f), BF16),
    ]
    return pl.pallas_call(
        functools.partial(front_kernel, experts, bits),
        out_shape=[jax.ShapeDtypeStruct(*out) for out in outs],
        in_specs=[VMEM] * 7 + [ANY] * 3,
        out_specs=[VMEM] * 13 + [ANY],
        scratch_shapes=[
            pltpu.VMEM((experts, CAP, f), BF16),
            pltpu.VMEM((SLOTS, D // tensor), BF16),
            pltpu.VMEM((experts, CAP, f), BF16),
            pltpu.VMEM((EXPERTS, 8, 256), F32),
            pltpu.VMEM((SLOTS, TOPK * here), BF16),
            pltpu.VMEM((TOPK * here, SLOTS), BF16),
            pltpu.VMEM((here // Q_ROWS, WINDOW + Q_ROWS, TOPK * Q_ROWS), F32),
            pltpu.VMEM((SLOTS, HD), BF16),
            pltpu.VMEM((TOPK * here, HD), BF16),
        ] + [dma((experts,))] * 6 + [dma((experts + 2, tensor))] * 2 + [dma((experts,))] * 6
        + [dma((2,))] * 2 + [dma((3,))],
        compiler_params=pltpu.CompilerParams(
            collective_id=collective_id, has_side_effects=True, vmem_limit_bytes=63 * 2**20),
        cost_estimate=pl.CostEstimate(flops=10**11, bytes_accessed=10**7, transcendentals=0),
    )(tokens, gain, slots, routes, next_routes, routers, segments, w, kv, wo)


def scatter_kernel(experts, bits, depth, near, scale, noted, *refs):
    refs = list(refs)
    h_in, w = refs[:2]
    refs = refs[2:]
    gate = refs.pop(0) if scale else None
    notes = refs.pop(0) if noted else None
    if depth:
        key_grad, value_grad, kv_in, rows_in, window_in = refs[:5]
        refs = refs[5:]
    back, h = refs[:2]
    refs = refs[2:]
    if depth:
        owed, map_grad, pair_kept, pair_came = refs[:4]
        refs = refs[4:]
    keep, sent, got, y, t_send, t_recv, y_send, y_recv, h_send, h_recv = refs[:10]
    if depth:
        (kv, rows, window, n_keep, n_sent, n_got, n_in, n_y, n_back, own, total_grad, pair_away,
         n_send, n_recv, o_send, o_recv, p_send, p_recv, l_sem) = refs[10:]
    e, t = lax.axis_index("expert"), lax.axis_index("tensor")
    partner = partners(e, experts, near)
    tensor = 1 << bits
    cap, width = h.shape[1], y.shape[2]
    body = pl.ds(0, cap)
    foot = pl.ds(cap, NOTES)

    def slice_at(d):
        return pl.ds(pl.multiple_of((t ^ d) * width, 128), width)

    def handed(j):
        return remote(y.at[j], back.at[j], y_send.at[j], y_recv.at[j], expert=j)

    def give(j, d):
        return remote(sent.at[j, d - 1], got.at[j, d - 1], t_send.at[j, d], t_recv.at[j, d], tensor=t ^ (1 << low_bit(d)))

    def owe(d):
        return remote(n_sent.at[d - 1], n_got.at[d - 1], n_send.at[d], n_recv.at[d], tensor=t ^ (1 << low_bit(d)))

    def across(c):
        grad = (key_grad, value_grad)[c]
        here = grad.shape[0] // 3
        return remote(grad.at[pl.ds(here, here)], n_in.at[c], o_send.at[c], o_recv.at[c], expert=e ^ 1)

    def two_back(way):
        return remote(n_y, n_back, o_send.at[2], o_recv.at[2], expert=lax.rem(e + experts - 2 * way, experts))

    def own_stage(k):
        for d in range(tensor - 1, -1, -1):
            if d % (1 << k) == 0:
                came = d | (1 << (k - 1))
                owe(came).wait_recv()
                total = n_keep[d // 2] + n_got[came - 1].astype(F32)
                if k == bits:
                    owed[...] = total.astype(BF16)
                elif d & (1 << k):
                    n_sent[d - 1] = total.astype(BF16)
                    owe(d).start()
                else:
                    n_keep[d // 2] = total

    order = [list(range(experts.bit_length() - 1)) for _ in range(2)]
    order[1][:2] = [1, 0]

    def pair_product(p, c):
        distance = 0
        for i, b in enumerate(reversed(order[c])):
            distance += ((p >> i) & 1) * (1 << b)
        some = window[:, shares(e ^ distance)]
        return lax.dot_general(some, (key_grad, value_grad)[c][...], (((0,), (0,)), ((), ())),
                               preferred_element_type=F32).astype(BF16)

    def pair_chunk(p, c):
        f = key_grad.shape[1]
        place, lanes = shares(p), pl.ds(c * f, f)
        return remote(pair_away.at[place, lanes], pair_came.at[place, lanes], p_send.at[c, p], p_recv.at[c, p],
                      expert=e ^ (1 << order[c][0]))

    def shares(q):
        share = map_grad.shape[1]
        return pl.ds(pl.multiple_of(q * share, share), share)

    def row_from(j):
        return remote(h_in.at[j], h.at[j], h_send.at[j], h_recv.at[j], expert=j)

    if depth:
        loads = [pltpu.make_async_copy(a, b, l_sem.at[i])
                 for i, (a, b) in enumerate(((window_in, window), (rows_in, rows), (kv_in, kv)))]
        for load in loads:
            load.start()
    meet(experts, bits)

    @pl.loop(1, experts)
    def _(s):
        j = partner(s)
        remote(h_in.at[j], h.at[e], h_send.at[j], h_recv.at[e], expert=j).start()

    h[e] = h_in[e]
    if depth:
        here = n_in.shape[1]
        f = key_grad.shape[1]
        for c in range(2):
            across(c).start()
        loads[0].wait()

        @pl.loop(0, experts // 2)
        def _(p):
            for c in range(2):
                pair_away[shares(p), pl.ds(c * f, f)] = pair_product(p + experts // 2, c)
                pair_chunk(p, c).start()

        passing = (e & 1).astype(F32)
        for c, grad in enumerate((key_grad, value_grad)):
            across(c).wait_recv()
            came = n_in[c].astype(F32)
            n_y[c] = (grad[pl.ds(0, here), :].astype(F32) + passing * came).astype(BF16)
            own[c] = grad[pl.ds(2 * here, here), :].astype(F32) + (1.0 - passing) * came
        @pl.when(e >= 2)
        def _():
            two_back(1).start()

        @pl.when(e >= experts - 2)
        def _():
            n_back[...] = jnp.zeros_like(n_back)

        @pl.loop(0, experts // 2)
        def _(p):
            for c in range(2):
                pair_kept[shares(p), pl.ds(c * f, f)] = pair_product(p, c)

    @pl.loop(0, experts + bits)
    def _(i):
        @pl.when(i < experts)
        def _():
            j = partner(i)
            slot = lax.rem(i, bits + 1)

            @pl.when(i > 0)
            def _():
                row_from(j).wait_recv()

            for d in range(tensor - 1, -1, -1):
                part = lax.dot_general(
                    h[j], w[slice_at(d), :], (((1,), (1,)), ((), ())), preferred_element_type=F32)
                if scale:
                    part = part * gate[j]
                if d & 1:
                    sent[j, d - 1, body, :] = part.astype(BF16)
                    if noted:
                        sent[j, d - 1, foot, :] = notes[j].astype(BF16)
                    give(j, d).start()
                else:
                    keep[slot, d // 2, body, :] = part
                    if noted:
                        keep[slot, d // 2, foot, :] = notes[j]

        for k in range(1, bits + 1):
            @pl.when((i >= k) & (i < experts + k))
            def _():
                m = i - k
                slot = lax.rem(m, bits + 1)
                j = partner(m)
                for d in range(tensor - 1, -1, -1):
                    if d % (1 << k) == 0:
                        came = d | (1 << (k - 1))
                        give(j, came).wait_recv()
                        total = keep[slot, d // 2] + got[j, came - 1].astype(F32)
                        if k == bits:
                            y[j] = total.astype(BF16)
                        elif d & (1 << k):
                            sent[j, d - 1] = total.astype(BF16)
                            give(j, d).start()
                        else:
                            keep[slot, d // 2] = total
                if k == bits:
                    @pl.when(m == 0)
                    def _():
                        back[e] = y[e]

                    @pl.when(m > 0)
                    def _():
                        remote(y.at[j], back.at[e], y_send.at[j], y_recv.at[e], expert=j).start()

        if depth:
            @pl.when(i == experts - 1)
            def _():
                @pl.when(e < experts - 2)
                def _():
                    two_back(-1).wait_recv()

                loads[2].wait()
                for c in range(2):
                    total_grad[c] = (own[c] + n_back[c].astype(F32)).astype(BF16)
                for d in range(tensor - 1, -1, -1):
                    part = None
                    for c in range(2):
                        term = lax.dot_general(total_grad[c], kv[c, slice_at(d), :], (((1,), (1,)), ((), ())),
                                               preferred_element_type=F32)
                        part = term if part is None else part + term
                    if d & 1:
                        n_sent[d - 1] = part.astype(BF16)
                        owe(d).start()
                    else:
                        n_keep[d // 2] = part

            @pl.when(i == experts)
            def _():
                own_stage(1)

    if depth:
        for k in range(2, bits + 1):
            own_stage(k)
        loads[1].wait()

        @pl.loop(0, experts)
        def _(i):
            map_grad[i] = lax.dot_general(
                rows[:, shares(i)], h[...].reshape(experts * cap, h.shape[2]), (((0,), (0,)), ((), ())),
                preferred_element_type=F32).astype(BF16)

    @pl.loop(1, experts)
    def _(s):
        j = partner(s)
        row_from(j).wait_send()
        handed(j).wait_recv()
        handed(j).wait_send()

    @pl.loop(0, experts)
    def _(j):
        for d in range(1, tensor):
            give(j, d).wait_send()

    if depth:
        for d in range(1, tensor):
            owe(d).wait_send()
        for c in range(2):
            across(c).wait_send()

        @pl.when(e >= 2)
        def _():
            two_back(1).wait_send()

        @pl.loop(0, experts // 2)
        def _(p):
            for c in range(2):
                pair_chunk(p, c).wait_recv()
                pair_chunk(p, c).wait_send()


def scatter_rows(h, w, gate=None, notes=None, windows=None, near=True, collective_id=0):
    experts, tensor = lax.axis_size("expert"), lax.axis_size("tensor")
    bits = tensor.bit_length() - 1
    high = CAP + (NOTES if notes is not None else 0)
    width, f = D // tensor, w.shape[1]
    dma = pltpu.SemaphoreType.DMA
    ins = [a for a in (h, w, gate, notes) if a is not None]
    outs = [jax.ShapeDtypeStruct((experts, high, width), BF16), jax.ShapeDtypeStruct(h.shape, BF16)]
    scratch = [
        pltpu.VMEM((bits + 1, tensor // 2, high, width), F32),
        pltpu.VMEM((experts, tensor - 1, high, width), BF16),
        pltpu.VMEM((experts, tensor - 1, high, width), BF16),
        pltpu.VMEM((experts, high, width), BF16),
    ] + [dma((experts, tensor))] * 2 + [dma((experts,))] * 4
    if windows is not None:
        ins += windows
        here = windows[0].shape[0] // 3
        outs.append(jax.ShapeDtypeStruct((here, width), BF16))
        outs.append(jax.ShapeDtypeStruct((experts, D // experts, f), BF16))
        outs += [jax.ShapeDtypeStruct((D // 2, 2 * windows[0].shape[1]), BF16)] * 2
        pair = (2, here, windows[0].shape[1])
        scratch += [
            pltpu.VMEM(windows[2].shape, BF16),
            pltpu.VMEM(windows[3].shape, BF16),
            pltpu.VMEM(windows[4].shape, BF16),
            pltpu.VMEM((tensor // 2, here, width), F32),
            pltpu.VMEM((tensor - 1, here, width), BF16),
            pltpu.VMEM((tensor - 1, here, width), BF16),
            pltpu.VMEM(pair, BF16),
            pltpu.VMEM(pair, BF16),
            pltpu.VMEM(pair, BF16),
            pltpu.VMEM(pair, F32),
            pltpu.VMEM(pair, BF16),
            pltpu.VMEM((D // 2, 2 * windows[0].shape[1]), BF16),
        ] + [dma((tensor,))] * 2 + [dma((3,))] * 2 + [dma((2, experts))] * 2 + [dma((3,))]
    return pl.pallas_call(
        functools.partial(scatter_kernel, experts, bits, windows is not None, near, gate is not None, notes is not None),
        out_shape=outs,
        in_specs=[VMEM] * (len(ins) - 3) + [VMEM if windows is None else ANY] * 3,
        out_specs=[VMEM] * (len(outs) - 1) + [VMEM if windows is None else ANY],
        scratch_shapes=scratch,
        compiler_params=pltpu.CompilerParams(
            collective_id=collective_id, has_side_effects=True, vmem_limit_bytes=63 * 2**20),
        cost_estimate=pl.CostEstimate(flops=10**11, bytes_accessed=10**7, transcendentals=0),
    )(*ins)


def ffn_kernel(experts, bits, pieces, *refs):
    (x_cols, dy_all, slots, facts, routers, gate_in, up_in, down_in,
     back, rows_out, dys_out, hidden_out, gate_out, up_out,
     x, dy, dy_near, land, gate_map, up_map, down_map, gate_pre, up_pre, hidden_grad, gates, pulls, moments, own_logits, low, sent, got, keep,
     z_send, z_recv, t_send, t_recv, r_send, r_recv, y_send, y_recv, w_sem, o_sem) = refs
    e, t = lax.axis_index("expert"), lax.axis_index("tensor")
    tensor = 1 << bits
    pairs = experts // 2
    width = x.shape[1]
    pair_rows = 2 * CAP
    sources = (x, dy)
    results = ((low.at[0], hidden_out), (low.at[1], gate_out), (low.at[2], up_out))

    def first_block(u):
        s = (lax.rem(u, pairs - 1) + 1) * lax.div(u + pairs - 1, pairs)
        return ((e >> 1) ^ s) * 2

    def block(j):
        return pl.ds(pl.multiple_of(j * CAP, CAP), CAP)

    def pair(j):
        return pl.ds(pl.multiple_of(j * CAP, pair_rows), pair_rows)

    def cols(d):
        return pl.ds(pl.multiple_of((t ^ d) * width, 128), width)

    def arrive(a, j):
        return remote(sources[a].at[block(j // pieces)], land.at[a, block(e), cols(0)], z_send.at[a, j], z_recv.at[a, e],
                      expert=j)

    def arrived(a, j):
        return remote(sources[a].at[block(j // pieces)], land.at[a, block(j), cols(0)], z_send.at[a, j], z_recv.at[a, j],
                      expert=j)

    def pass_on(a, j, d, b):
        place, far = land.at[a, block(j), cols(d)], d | (1 << b)
        return remote(place, place, t_send.at[a, j, far], t_recv.at[a, j, far], tensor=t ^ (1 << b))

    def passed(a, j, d):
        place = land.at[a, block(j), cols(d)]
        return remote(place, place, t_send.at[a, j, d], t_recv.at[a, j, d], tensor=t ^ (1 << low_bit(d)))

    def stage(j, k, arrays=(0, 1)):
        for q in range(2):
            for a in arrays:
                for d in range(1, tensor):
                    if low_bit(d) == bits - k:
                        passed(a, j + q, d).wait_recv()
                        for b in reversed(range(bits - k)):
                            pass_on(a, j + q, d, b).start()

    def place_of(u, q):
        return 2 * (u & 1) + q

    def give(u, q, d):
        j = first_block(u) + q
        return remote(sent.at[place_of(u, q), d - 1], got.at[j, d - 1], r_send.at[place_of(u, q), d - 1],
                      r_recv.at[j, d - 1], tensor=t ^ (1 << low_bit(d)))

    final = tensor // 2 - 1

    def hand_back(j):
        return remote(got.at[j, final], back.at[e], y_send.at[j], y_recv.at[e], expert=j)

    def handed(j):
        return remote(got.at[j, final], back.at[j], y_send.at[j], y_recv.at[j], expert=j)

    def sum_stage(u, k, blocks=(0, 1)):
        j = first_block(u)
        for q in blocks:
            for d in range(tensor - 1, -1, -1):
                if d % (1 << k) == 0:
                    came = d | (1 << (k - 1))
                    give(u, q, came).wait_recv()
                    total = keep[q, d // 2] + got[j + q, came - 1].astype(F32)
                    if k == bits:
                        got[j + q, final] = total.astype(BF16)
                    elif d & (1 << k):
                        sent[place_of(u, q), d - 1] = total.astype(BF16)
                        give(u, q, d).start()
                    else:
                        keep[q, d // 2] = total

    def finish(u):
        j = first_block(u)
        for k in range(2, bits):
            sum_stage(u, k)
        for q in range(2):
            sum_stage(u, bits, (q,))

            @pl.when(j + q == e)
            def _():
                back[e] = got[e, final]

            @pl.when(j + q != e)
            def _():
                hand_back(j + q).start()

    def to_memory(j):
        copies = [pltpu.make_async_copy(land.at[a, pair(j)], out.at[pair(j)], o_sem.at[a])
                  for a, out in enumerate((rows_out, dys_out))]
        return copies

    def results_to_memory(j):
        return [pltpu.make_async_copy(source, out.at[pair(j)], o_sem.at[2 + i])
                for i, (source, out) in enumerate(results)]

    weights = [pltpu.make_async_copy(a, b, w_sem.at[i])
               for i, (a, b) in enumerate(((gate_in, gate_map), (up_in, up_map), (down_in, down_map)))]
    for copy in weights:
        copy.start()
    here = x_cols.shape[0]
    place = lax.broadcasted_iota(jnp.int32, (x.shape[0], here), 0)
    chosen = (place == slots[:, pl.ds(0, here)]) | (place == slots[:, pl.ds(here, here)])
    chosen = chosen.astype(F32).astype(BF16)
    x[...] = jnp.dot(chosen, x_cols[...], preferred_element_type=F32).astype(BF16)
    dy[...] = jnp.dot(chosen, dy_all[:, cols(0)], preferred_element_type=F32).astype(BF16)

    even = [d for d in range(2, tensor, 2)]

    def near_block(n):
        return first_block((n // 2) * (pairs - 1)) + n % 2

    for n in range(4):
        place = lax.broadcasted_iota(jnp.int32, (CAP, here), 0) + (near_block(n) // pieces) * CAP
        mine = (place == slots[:, pl.ds(0, here)]) | (place == slots[:, pl.ds(here, here)])
        mine = mine.astype(F32).astype(BF16)
        for i, d in enumerate(even):
            dy_near[n, i] = jnp.dot(mine, dy_all[:, cols(d)], preferred_element_type=F32).astype(BF16)

    def straight(n, i):
        j, d = near_block(n), even[i]
        return remote(dy_near.at[n, i], land.at[1, block(e), cols(d)], t_send.at[1, j, d], t_recv.at[1, e, d], expert=j)

    def came_straight(j, d):
        return remote(land.at[1, block(j), cols(d)], land.at[1, block(j), cols(d)], t_send.at[1, j, d], t_recv.at[1, j, d],
                      expert=j)

    meet(experts, bits)
    for a in range(2):
        arrive(a, e ^ 1).start()
    for n in range(2):
        @pl.when(near_block(n) != e)
        def _():
            for i in range(len(even)):
                straight(n, i).start()

    def send_pair(u):
        for q in range(2):
            for a in range(2):
                arrive(a, first_block(u) + q).start()

    def forward_pair(u):
        for q in range(2):
            for a in range(2):
                arrived(a, first_block(u) + q).wait_recv()
                for b in reversed(range(bits)):
                    pass_on(a, first_block(u) + q, 0, b).start()

    def forward_near(j):
        for a in range(2):
            arrived(a, j).wait_recv()
            for b in reversed(range(1 if a else bits)):
                pass_on(a, j, 0, b).start()
        for d in even:
            came_straight(j, d).wait_recv()
            pass_on(1, j, d, 0).start()

    send_pair(1)
    own = first_block(0)
    for a in range(2):
        land[a, block(e), cols(0)] = sources[a][block(e // pieces), :]
        for b in reversed(range(1 if a else bits)):
            pass_on(a, e, 0, b).start()
    for i, d in enumerate(even):
        land[1, block(e), cols(d)] = dy_near[e & 1, i]
        pass_on(1, e, d, 0).start()
    foot = pl.ds(pair_rows, NOTES)
    for d in range(tensor):
        for q in range(4):
            if d:
                sent[q, d - 1, foot, :] = jnp.zeros((NOTES, width), BF16)
        for q in range(2):
            if d % 2 == 0:
                keep[q, d // 2, foot, :] = jnp.zeros((NOTES, width), F32)
    forward_near(e ^ 1)
    for k in range(1, bits):
        stage(own, k, (0,))
    for copy in weights:
        copy.wait()

    @pl.loop(0, pairs)
    def _(u):
        j = first_block(u)
        stage(j, bits)
        for copy in to_memory(j):
            copy.start()
        rows = land[0, pair(j), :]
        gate_pre[...] = jnp.dot(rows, gate_map[...], preferred_element_type=F32)
        up_pre[...] = jnp.dot(rows, up_map[...], preferred_element_type=F32)
        logits = lax.dot_general(rows, routers[...], (((1,), (1,)), ((), ())), preferred_element_type=F32)
        lane = lax.broadcasted_iota(jnp.int32, logits.shape, 1)
        mine = jnp.sum(jnp.where(lane == EXPERTS + e // pieces, logits, 0.0), axis=1, keepdims=True)
        other = jnp.concatenate([fact_column(facts[j + q], 1) for q in range(2)], axis=0) + EXPERTS
        rival = jnp.sum(jnp.where(lane.astype(F32) == other, logits, 0.0), axis=1, keepdims=True)
        own_logits[...] = mine
        top = jnp.maximum(mine, rival)
        mine, rival = jnp.exp(mine - top), jnp.exp(rival - top)
        gates[...] = mine / (mine + rival)

        @pl.when(u < pairs - 2)
        def _():
            forward_pair(u + 1)
            send_pair(u + 2)

        @pl.when(u == pairs - 3)
        def _():
            for n in range(2, 4):
                for i in range(len(even)):
                    straight(n, i).start()

        @pl.when(u == pairs - 2)
        def _():
            for q in range(2):
                forward_near(first_block(u + 1) + q)

        hidden_grad[...] = lax.dot_general(
            land[1, pair(j), :], down_map[...], (((1,), (1,)), ((), ())), preferred_element_type=F32)

        @pl.when(u > 0)
        def _():
            for copy in results_to_memory(j):
                copy.wait()

        @pl.loop(0, pair_rows // 32)
        def _(r):
            some = pl.ds(pl.multiple_of(r * 32, 32), 32)
            gate_here, up_here = gate_pre[some, :], up_pre[some, :]
            weight = gates[some, :]
            sigma = 1.0 / (1.0 + jnp.exp(-gate_here))
            silu = gate_here * sigma
            hidden = silu * up_here
            grad = hidden_grad[some, :]
            pulls[some, :] = jnp.sum(hidden * grad, axis=1, keepdims=True)
            grad = grad * weight
            low[0, some, :] = (hidden * weight).astype(BF16)
            gate_low = (grad * up_here * (sigma * (1.0 + gate_here * (1.0 - sigma)))).astype(BF16)
            up_low = (grad * silu).astype(BF16)
            low[1, some, :] = gate_low
            low[2, some, :] = up_low
            moments[some, :] = jnp.sum(
                gate_low.astype(F32) * gate_here + up_low.astype(F32) * up_here, axis=1, keepdims=True)

        for copy in results_to_memory(j):
            copy.start()

        @pl.when(u > 0)
        def _():
            finish(u - 1)

        @pl.when(u > 1)
        def _():
            for q in range(2):
                for d in range(1, tensor):
                    give(u - 2, q, d).wait_send()

        noted = []
        for q in range(2):
            some = pl.ds(q * CAP, CAP)
            lane = lax.broadcasted_iota(jnp.int32, (CAP, 128), 1)
            shared = tensor * pieces
            column = jnp.where(lane == 0, pulls[some, :], jnp.where(lane == 1, gates[some, :] / shared, 0.0))
            column = jnp.where(lane == 2, moments[some, :], jnp.where(lane == 3, own_logits[some, :] / shared, column))
            column = jnp.concatenate([column, jnp.zeros((256 - CAP, 128), F32)], axis=0)
            noted.append(column.T[:NOTES])
        for d in range(tensor - 1, -1, -1):
            grad = lax.dot_general(low[1], gate_map[cols(d), :], (((1,), (1,)), ((), ())), preferred_element_type=F32)
            grad += lax.dot_general(low[2], up_map[cols(d), :], (((1,), (1,)), ((), ())), preferred_element_type=F32)
            out = jnp.dot(low[0], down_map[:, cols(d)], preferred_element_type=F32)
            for q in range(2):
                part = pl.ds(q * CAP, CAP)
                parts = [(pl.ds(0, CAP), slice(None), grad[q * CAP : (q + 1) * CAP]),
                         (pl.ds(CAP, CAP), slice(None), out[q * CAP : (q + 1) * CAP]),
                         (foot, pl.ds(0, 256), noted[q])]
                for place, lanes, value in parts:
                    if d & 1:
                        sent[place_of(u, q), d - 1, place, lanes] = value.astype(BF16)
                    else:
                        keep[q, d // 2, place, lanes] = value
                if d & 1:
                    give(u, q, d).start()
        sum_stage(u, 1)

        @pl.when(u < pairs - 1)
        def _():
            for k in range(1, bits):
                stage(first_block(u + 1), k, (0,))

                @pl.when(u < pairs - 2)
                def _():
                    stage(first_block(u + 1), k, (1,))

        for copy in to_memory(j):
            copy.wait()

    finish(pairs - 1)
    for copy in results_to_memory(0):
        copy.wait()
    for u in range(max(pairs - 2, 0), pairs):
        for q in range(2):
            for d in range(1, tensor):
                give(u, q, d).wait_send()

    @pl.loop(1, experts)
    def _(s):
        j = e ^ s
        for a in range(2):
            arrived(a, j).wait_send()
        handed(j).wait_recv()
        handed(j).wait_send()

    @pl.loop(0, experts)
    def _(j):
        for a in range(2):
            for d in range(1, tensor):
                if a == 0 or d & 1:
                    passed(a, j, d).wait_send()

        @pl.when(j != e)
        def _():
            for d in even:
                passed(1, j, d).wait_send()


def feed_forward(x, dy, slots, facts, routers, gate_map, up_map, down_map, collective_id):
    experts, tensor = lax.axis_size("expert"), lax.axis_size("tensor")
    bits = tensor.bit_length() - 1
    width, hidden = x.shape[1], gate_map.shape[1]
    high = 2 * CAP + NOTES
    count = experts * CAP
    dma = pltpu.SemaphoreType.DMA
    return pl.pallas_call(
        functools.partial(ffn_kernel, experts, bits, experts // EXPERTS),
        out_shape=[jax.ShapeDtypeStruct((experts, high, width), BF16)]
        + [jax.ShapeDtypeStruct((count, D), BF16)] * 2 + [jax.ShapeDtypeStruct((count, hidden), BF16)] * 3,
        in_specs=[VMEM] * 5 + [ANY] * 3,
        out_specs=[VMEM] + [ANY] * 5,
        scratch_shapes=[
            pltpu.VMEM((SLOTS, width), BF16),
            pltpu.VMEM((SLOTS, width), BF16),
            pltpu.VMEM((4, tensor // 2 - 1, CAP, width), BF16),
            pltpu.VMEM((2, count, D), BF16),
            pltpu.VMEM((D, hidden), BF16),
            pltpu.VMEM((D, hidden), BF16),
            pltpu.VMEM((hidden, D), BF16),
            pltpu.VMEM((2 * CAP, hidden), F32),
            pltpu.VMEM((2 * CAP, hidden), F32),
            pltpu.VMEM((2 * CAP, hidden), F32),
            pltpu.VMEM((2 * CAP, 1), F32),
            pltpu.VMEM((2 * CAP, 1), F32),
            pltpu.VMEM((2 * CAP, 1), F32),
            pltpu.VMEM((2 * CAP, 1), F32),
            pltpu.VMEM((3, 2 * CAP, hidden), BF16),
            pltpu.VMEM((4, tensor - 1, high, width), BF16),
            pltpu.VMEM((experts, tensor - 1, high, width), BF16),
            pltpu.VMEM((2, tensor // 2, high, width), F32),
        ] + [dma((2, experts))] * 2 + [dma((2, experts, tensor))] * 2
        + [dma((4, tensor - 1)), dma((experts, tensor - 1))] + [dma((experts,))] * 2 + [dma((3,)), dma((5,))],
        compiler_params=pltpu.CompilerParams(
            collective_id=collective_id, has_side_effects=True, vmem_limit_bytes=63 * 2**20),
        cost_estimate=pl.CostEstimate(flops=10**11, bytes_accessed=10**7, transcendentals=0),
    )(x, dy, slots, facts, routers, gate_map, up_map, down_map)


def small_kernel(experts, tensor, part, out, came, s_send, s_recv, b_send, b_recv):
    e, t = lax.axis_index("expert"), lax.axis_index("tensor")
    owners = experts // tensor
    width = out.shape[1]
    place = t * owners

    def to_owner(c):
        return remote(part.at[:, pl.ds(c * width, width)], came.at[e], s_send.at[c], s_recv.at[e], expert=place + c)

    barrier = pltpu.get_barrier_semaphore()

    @pl.loop(1, experts)
    def _(s):
        pl.semaphore_signal(barrier, inc=1, device_id={"expert": e ^ s}, device_id_type=MESH)

    @pl.loop(1, tensor)
    def _(s):
        pl.semaphore_signal(barrier, inc=1, device_id={"tensor": t ^ s}, device_id_type=MESH)

    pl.semaphore_wait(barrier, experts + tensor - 2)
    for c in range(owners):
        @pl.when(e != place + c)
        def _():
            to_owner(c).start()

        @pl.when(e == place + c)
        def _():
            came[e] = part[:, c * width : (c + 1) * width]

    @pl.when(e // owners == t)
    def _():
        @pl.loop(1, experts)
        def _(s):
            j = e ^ s
            remote(came.at[j], came.at[j], s_send.at[0], s_recv.at[j], expert=j).wait_recv()

        total = came[0]
        for j in range(1, experts):
            total += came[j]
        out[...] = total

        @pl.loop(1, tensor)
        def _(s):
            remote(out, out, b_send.at[s], b_recv, tensor=t ^ s).start()

        @pl.loop(1, tensor)
        def _(s):
            remote(out, out, b_send.at[s], b_recv, tensor=t ^ s).wait_send()

    @pl.when(e // owners != t)
    def _():
        remote(out, out, b_send.at[0], b_recv, tensor=e // owners).wait_recv()

    for c in range(owners):
        @pl.when(e != place + c)
        def _():
            to_owner(c).wait_send()


def small_sums(part, collective_id):
    experts, tensor = lax.axis_size("expert"), lax.axis_size("tensor")
    n, width = part.shape[0], D // experts
    dma = pltpu.SemaphoreType.DMA
    return pl.pallas_call(
        functools.partial(small_kernel, experts, tensor),
        out_shape=jax.ShapeDtypeStruct((n, width), F32),
        in_specs=[VMEM],
        out_specs=VMEM,
        scratch_shapes=[pltpu.VMEM((experts, n, width), F32), dma((experts // tensor,)), dma((experts,)), dma((tensor,)),
                        dma],
        compiler_params=pltpu.CompilerParams(collective_id=collective_id, has_side_effects=True),
        cost_estimate=pl.CostEstimate(flops=10**10, bytes_accessed=10**5, transcendentals=0),
    )(part)


def dot(left, right, dims):
    return lax.dot_general(left, right, ((dims[0], dims[1]), ((), ())), preferred_element_type=F32)


def mm(left, right):
    return dot(left, right, ((1,), (0,)))


def mm_nt(left, right):
    return dot(left, right, ((1,), (1,)))


def mm_tn(left, right):
    return dot(left, right, ((0,), (0,)))


def swap(blocks):
    return lax.all_to_all(blocks, "expert", split_axis=0, concat_axis=0, tiled=True)


def columns_together(rows):
    return lax.all_gather(rows, "tensor", axis=1, tiled=True)


def columns_summed(rows):
    return lax.psum_scatter(rows, "tensor", scatter_dimension=1, tiled=True)


def slot_numbers(routes):
    flat = routes.T.reshape(-1)
    place = jnp.arange(flat.shape[0], dtype=jnp.int32)
    earlier = (flat[:, None] == flat[None, :]) & (place[None, :] < place[:, None])
    return flat * CAP + jnp.sum(earlier.astype(jnp.int32), axis=1)


def spaced(slots, stride):
    return slots + (slots // CAP) * (stride - CAP)


def place_matrix(slots):
    return (jnp.arange(SLOTS, dtype=jnp.int32)[:, None] == slots[None, :]).astype(BF16)


def token_matrix(slots, stride=CAP, first=0):
    wide = (spaced(slots, stride) + first).reshape(TOPK, -1)
    place = jnp.arange(EXPERTS * stride, dtype=jnp.int32)[:, None]
    return ((place == wide[0][None, :]) | (place == wide[1][None, :])).astype(BF16)


def to_pieces(rows, pieces):
    if pieces == 1:
        return rows
    experts, r, c = rows.shape
    return rows.reshape(experts, r, pieces, c // pieces).transpose(0, 2, 1, 3).reshape(experts * pieces, r, -1)


def from_pieces(rows, pieces):
    if pieces == 1:
        return rows
    both, r, c = rows.shape
    return rows.reshape(both // pieces, pieces, r, c).transpose(0, 2, 1, 3).reshape(both // pieces, r, -1)


def for_pieces(rows, pieces):
    return jnp.repeat(rows, pieces, axis=0) if pieces > 1 else rows


def gate_back(gating, pulled, routes):
    inner_sum = gating * (pulled - jnp.sum(gating * pulled, axis=1, keepdims=True))
    one_hot = (routes[:, :, None] == jnp.arange(EXPERTS, dtype=jnp.int32)[None, None, :]).astype(F32)
    return jnp.sum(one_hot * inner_sum[:, :, None], axis=1).astype(BF16)


def per_device(
    tokens,
    segment_ids,
    attn_routes,
    ffn_routes,
    attn_gain,
    ffn_gain,
    routers,
    query_weight,
    output_weight,
    key_value_weight,
    gate_weight,
    up_weight,
    down_weight,
    cotangent,
):
    rows_here = tokens.shape[0]
    expert_count = lax.axis_size("expert")
    tensor_count = lax.axis_size("tensor")
    pieces = expert_count // EXPERTS
    column_count = D // tensor_count
    expert_index = lax.axis_index("expert")
    tensor_index = lax.axis_index("tensor")
    own = (expert_index // pieces).astype(F32)
    head_width = query_weight.shape[2]
    head_count = head_width // HD

    def cols(whole):
        return lax.dynamic_slice_in_dim(whole, tensor_index * column_count, column_count, whole.ndim - 1)

    def group_tokens(token_cols, places):
        return for_pieces(mm(places, token_cols).astype(BF16).reshape(EXPERTS, CAP, -1), pieces)

    def group_choices(choice_rows, places):
        return to_pieces(mm(places, choice_rows).astype(BF16).reshape(EXPERTS, CAP, -1), pieces)

    def choices_of(back, places):
        return mm_tn(places, from_pieces(back, pieces).reshape(SLOTS, -1)).astype(BF16)

    def sums_of(back, places):
        stride = back.shape[1]
        back = back.reshape(EXPERTS, pieces, stride, column_count)
        if pieces > 1:
            total = sum(mm_tn(places, back[:, p].reshape(EXPERTS * stride, -1)) for p in range(pieces))
        else:
            total = mm_tn(places, back.reshape(EXPERTS * stride, -1))
        return total

    def notes_of(*scalars):
        rows = jnp.stack([v.reshape(expert_count, CAP) for v in scalars], axis=1)
        return jnp.pad(rows, ((0, 0), (0, NOTES - len(scalars)), (0, column_count - CAP)))

    def read_notes(back, places, count, first=CAP):
        noted = back[:, first : first + count, :CAP].astype(F32)
        noted = noted.reshape(EXPERTS, pieces, count, CAP).sum(1).transpose(0, 2, 1).reshape(SLOTS, count)
        return mm_tn(places, noted.astype(BF16)).reshape(TOPK, rows_here, count)

    def exchange(away, b):
        return lax.ppermute(away, "expert", [(i, i ^ (1 << b)) for i in range(expert_count)])

    attn_slots, ffn_slots = slot_numbers(attn_routes), slot_numbers(ffn_routes)

    slots = jnp.stack([attn_slots, ffn_slots, spaced(attn_slots, 256), spaced(ffn_slots, 256)])
    segments = segment_ids[None]
    (rows_one, query_map, window, pair_map, keys, values, attn_gate_blocks, facts, heads, queries, log_total,
     gate_row, rate_one, output_map) = front(
        tokens, attn_gain[None], slots, attn_routes.T, ffn_routes.T, routers.T, segments,
        to_pieces(query_weight, pieces), key_value_weight, to_pieces(output_weight, pieces), collective_id=0)
    rows_one, attn_slots, ffn_slots, tokens, attn_gain, ffn_gain, routers, cotangent = lax.optimization_barrier(
        (rows_one, attn_slots, ffn_slots, tokens, attn_gain, ffn_gain, routers, cotangent))
    routers_one, routers_two = routers[:, :EXPERTS], routers[:, EXPERTS:]
    gain_one = attn_gain.astype(F32)
    gain_two = cols(ffn_gain.astype(F32))
    dy_cols = cols(cotangent)
    token_cols = cols(tokens).astype(F32)
    attn_places, ffn_places = place_matrix(attn_slots), place_matrix(ffn_slots)
    rows_one = rows_one.reshape(-1, D)
    normed_cols = lax.dynamic_slice(
        window, (2, 0, tensor_index * column_count), (1, rows_here, column_count)).reshape(rows_here, column_count)
    window = window.reshape(-1, D)
    attn_back, heads_rows = scatter_rows(
        to_pieces(heads.reshape(EXPERTS, CAP, -1), pieces), output_map, attn_gate_blocks, collective_id=1)
    heads_rows = heads_rows.reshape(expert_count * CAP, -1)
    state = token_cols + sums_of(attn_back, token_matrix(attn_slots))

    mean_two = lax.psum(jnp.sum(state * state, axis=1, keepdims=True), "tensor") / D
    rate_two = lax.rsqrt(mean_two + eps)
    normed_two = (state * rate_two * gain_two).astype(BF16)
    gate_map, up_map, down_map = gate_weight[0], up_weight[0], down_weight[0]
    ffn_back, rows_two, rows_dy, hidden, gate_low, up_low = feed_forward(
        normed_two, cotangent, ffn_slots[None], facts, routers.T, gate_map, up_map, down_map, collective_id=2)
    normed_two_grad = sums_of(ffn_back, token_matrix(ffn_slots, 2 * CAP + NOTES))
    ffn_pull, ffn_gates, moments, own_logits = (
        note.T for note in jnp.moveaxis(read_notes(ffn_back, ffn_places, 4, 2 * CAP), 2, 0))
    ffn_logit_grad = gate_back(ffn_gates, ffn_pull, ffn_routes)
    normed_two_grad = normed_two_grad + mm_nt(
        ffn_logit_grad, lax.dynamic_slice_in_dim(routers_two, tensor_index * column_count, column_count, 0))
    ffn_router_cols = mm_tn(normed_two, ffn_logit_grad)
    ffn_gain_cols = jnp.sum(normed_two_grad * state * rate_two, axis=0)
    ahead = normed_two_grad * gain_two
    chosen_grad = jnp.sum(
        jnp.where(ffn_routes[:, :, None] == jnp.arange(EXPERTS, dtype=jnp.int32), ffn_logit_grad[:, None].astype(F32), 0.0),
        axis=2)
    centre = jnp.sum(moments + chosen_grad * own_logits, axis=1, keepdims=True) / (rate_two * D)
    state_grad = dy_cols.astype(F32) + rate_two * ahead - state * rate_two * rate_two * rate_two * centre

    unused_rows, heads_grad, heads_grad_rows, output_grad = gather_rows(
        group_tokens(state_grad.astype(BF16), token_matrix(attn_slots)), output_map, gate=attn_gate_blocks,
        others=heads_rows.reshape(expert_count, CAP, -1), collective_id=4)
    heads_grad_rows = heads_grad_rows.reshape(expert_count * CAP, -1)
    attn_notes = notes_of(jnp.sum(heads_grad_rows.astype(F32) * heads_rows.astype(F32), axis=1))
    query_back, key_back, value_back, output_grad = attend_back(
        attn_slots[None], from_pieces(heads_grad, pieces).reshape(SLOTS, -1), queries, keys, values, log_total,
        segments, output_grad, collective_id=6)
    output_grad = from_pieces(output_grad, pieces).astype(F32)
    normed_back, unused_rows, owed, query_grad, pair_part, pair_came = scatter_rows(
        to_pieces(query_back.reshape(EXPERTS, CAP, -1), pieces), query_map, notes=attn_notes,
        windows=[key_back, value_back, pair_map, rows_one, window], collective_id=5)
    pair_part = (pair_part.astype(F32) + pair_came.astype(F32)).astype(BF16)
    pair_part, query_grad, rows_two, hidden = lax.optimization_barrier((pair_part, query_grad, rows_two, hidden))
    quarter = D // 4
    pair_came = jnp.concatenate(
        [exchange(pair_part[quarter:, :head_width], 1), exchange(pair_part[quarter:, head_width:], 0)], axis=1)
    query_grad = swap(query_grad)
    gate_grad = mm_tn(rows_two, gate_low)
    up_grad = mm_tn(rows_two, up_low)
    pair_came, hidden, gate_grad, up_grad = lax.optimization_barrier((pair_came, hidden, gate_grad, up_grad))
    pair_part = pair_part[:quarter].astype(F32) + pair_came.astype(F32)
    for b in range(2, expert_count.bit_length() - 1):
        rest = pair_part.shape[0] // 2
        pair_part = pair_part.astype(BF16)
        if b == 2:
            pair_part, hidden = lax.optimization_barrier((pair_part, hidden))
        pair_part = pair_part[:rest].astype(F32) + exchange(pair_part[rest:], b).astype(F32)
    down_grad = mm_tn(hidden, rows_dy)
    normed_back, owed, down_grad = lax.optimization_barrier((normed_back, owed, down_grad))
    normed_grad = sums_of(normed_back, token_matrix(attn_slots, CAP + NOTES)) + owed.astype(F32)
    attn_pull = read_notes(normed_back, attn_places, 1)[:, :, 0].T
    attn_gates = gate_row.reshape(TOPK, rows_here).T
    attn_logit_grad = gate_back(attn_gates, attn_pull, attn_routes)
    normed_grad = normed_grad + mm_nt(
        attn_logit_grad, lax.dynamic_slice_in_dim(routers_one, tensor_index * column_count, column_count, 0))
    attn_router_cols = mm_tn(normed_cols, attn_logit_grad)
    attn_gain_cols = jnp.sum(normed_grad * token_cols * rate_one, axis=0)
    ahead_one = normed_grad * cols(gain_one)
    centre_one = jnp.sum(ahead_one * token_cols, axis=1, keepdims=True)
    centre_one = lax.psum(centre_one, "tensor") / D
    tokens_grad = state_grad + rate_one * ahead_one - token_cols * rate_one * rate_one * rate_one * centre_one
    tokens_grad = columns_together(tokens_grad.astype(BF16)).astype(F32)

    small = jnp.concatenate(
        [attn_router_cols.T, ffn_router_cols.T, attn_gain_cols[None], ffn_gain_cols[None],
         jnp.zeros((6, column_count), F32)], axis=0)
    query_grad = from_pieces(query_grad, pieces).astype(F32)
    small, pair_part, query_grad, tokens_grad = lax.optimization_barrier((small, pair_part, query_grad, tokens_grad))
    small = small_sums(small, collective_id=3).T
    key_value_grad = pair_part.reshape(D // expert_count, 2, -1).transpose(1, 0, 2)
    ffn_out = sums_of(ffn_back, token_matrix(ffn_slots, 2 * CAP + NOTES, CAP))
    mixed = (state + ffn_out).astype(BF16)
    return (
        mixed,
        tokens_grad,
        small[:, 2 * EXPERTS],
        small[:, 2 * EXPERTS + 1],
        small[:, : 2 * EXPERTS],
        query_grad,
        output_grad,
        key_value_grad,
        gate_grad[None],
        up_grad[None],
        down_grad[None],
    )


def solution(mesh):
    in_specs = (
        P("expert", None),
        P(),
        P("expert", None),
        P("expert", None),
        P(),
        P(),
        P(),
        P(None, "expert", "tensor"),
        P(None, "expert", "tensor"),
        P(None, "expert", "tensor"),
        P("expert", None, "tensor"),
        P("expert", None, "tensor"),
        P("expert", "tensor", None),
        P("expert", None),
    )
    out_specs = (
        P("expert", "tensor"),
        P("expert", None),
        P("expert"),
        P("expert"),
        P("expert", None),
        P(None, "expert", "tensor"),
        P(None, "expert", "tensor"),
        P(None, "expert", "tensor"),
        P("expert", None, "tensor"),
        P("expert", None, "tensor"),
        P("expert", "tensor", None),
    )
    return jax.shard_map(
        per_device, mesh=mesh, in_specs=in_specs, out_specs=out_specs, check_vma=False
    )
```
